32 devices in a mesh: gx: 4 (over y, x), gy: 8 (over z, core).
Axes of the slice: x: 2, y: 2, z: 4, core: 2. Of those that a mesh axis runs over, the one named last changes fastest.
Arguments:
- momentum_dist: float32 [19, 32, 128, 512], P(None, 'gx', 'gy'), may hold values from 0.2 to 0.8
- order_dist: float32 [19, 32, 128, 512], P(None, 'gx', 'gy'), may hold values from -0.25 to 0.25
- offsets: int32 [4], replicated, may hold values from 64 to 79, as said below
Outputs:
- next_momentum: float32 [19, 32, 128, 512], P(None, 'gx', 'gy')
- next_order: float32 [19, 32, 128, 512], P(None, 'gx', 'gy')
The draws below stay inside these ranges and needn't reach their ends.
Inputs may be any that keep to these rules, and one draw needn't show every extreme that they name: Every offsets[k] lies from 64 to 79; offsets[0] is 64 and offsets[3] is 79.
All inputs are finite; a program needn't handle non-finite values.
Results may differ from the reference program's by a relative error of at most 0.00002.
Values sent between devices are 32-bit elements; how exact they have to be, the bound alone decides.
No kernel may reach another device: no remote copies, remote signals or barrier semaphores. Data moves between devices by JAX's collectives and lax.ppermute only.
A program may use at most 128 MiB of HBM per device.

```python
import jax
import jax.numpy as jnp

CY = 16
NZ = 512
NX = 32
NY = 128


def draw_offsets(key, part):
    key = jax.random.fold_in(key, 5)
    middle_rests = jax.random.randint(key, (2,), 0, CY).astype(jnp.int32)
    remainders = jnp.concatenate([jnp.zeros((1,), jnp.int32), middle_rests, jnp.full((1,), CY - 1, jnp.int32)])
    return (NY // 2 + remainders).astype(jnp.int32)


def steps_of(rng, shape, pieces, low, high):
    level = 1.0
    for axis_at, shards_of in pieces:
        draws = jax.random.uniform(jax.random.fold_in(jax.random.fold_in(rng, 6), axis_at), (shards_of,), jnp.float32, low / len(pieces), high / len(pieces))
        level = level * jnp.repeat(jnp.exp(draws), shape[axis_at] // shards_of).reshape((-1,) + (1,) * (len(shape) - 1 - axis_at))
    return level


def setup_inputs(seed: int = 0) -> dict:
    streams_of = jax.random.split(jax.random.key(seed), 4)
    momentum_dist = jnp.clip(0.2 + 0.6 * jax.random.uniform(streams_of[0], (19, NX, NY, NZ), jnp.float32) ** steps_of(streams_of[0], (19, NX, NY, NZ), ((1, 4), (2, 8)), -0.2, 0.2), 0.2, 0.8)
    order_dist = jnp.clip(jax.random.uniform(streams_of[1], (19, NX, NY, NZ), jnp.float32, -0.25, 0.25) * steps_of(streams_of[1], (19, NX, NY, NZ), ((1, 4), (2, 8)), -0.4, 0.0), -0.25, 0.25)
    offsets = draw_offsets(jax.random.fold_in(streams_of[3], 71), 0)
    return {"momentum_dist": momentum_dist, "order_dist": order_dist, "offsets": offsets}


lattice_velocity = [(0, 0, 0), (1, 0, 0), (-1, 0, 0), (0, 1, 0), (0, -1, 0), (0, 0, 1), (0, 0, -1),
                    (1, 1, 0), (-1, -1, 0), (1, -1, 0), (-1, 1, 0), (1, 0, 1), (-1, 0, -1), (1, 0, -1), (-1, 0, 1),
                    (0, 1, 1), (0, -1, -1), (0, 1, -1), (0, -1, 1)]
lattice_weight = [1.0 / 3.0] + [1.0 / 18.0] * 6 + [1.0 / 36.0] * 12
relax_momentum = 0.8
relax_order = 0.9
bulk_quadratic = -0.0625
bulk_quartic = 0.0625
interface_kappa = 0.04
plane_speed = 0.04
rising = [1, 7, 9, 11, 13]
falling = [2, 8, 10, 12, 14]


def tables(chosen):
    weight = jnp.asarray([lattice_weight[c] for c in chosen], jnp.float32).reshape(-1, 1, 1, 1)
    directions = [jnp.asarray([float(lattice_velocity[c][axis_place]) for c in chosen], jnp.float32).reshape(-1, 1, 1, 1) for axis_place in range(3)]
    return weight, directions


def equilibria(density, order_field, potential, velocity, weight, directions):
    projection = directions[0] * velocity[0] + directions[1] * velocity[1] + directions[2] * velocity[2]
    speed_square = velocity[0] * velocity[0] + velocity[1] * velocity[1] + velocity[2] * velocity[2]
    shape_term = 3.0 * projection + 4.5 * projection * projection - 1.5 * speed_square
    moment_eq = weight * density * (1.0 + shape_term)
    order_eq = weight * (3.0 * potential + order_field * shape_term)
    return moment_eq, order_eq, projection


def collide(momentum, order, order_field, potential, gradient_parts):
    weight, directions = tables(list(range(19)))
    density = jnp.sum(momentum, axis=0)
    force_parts = [potential * part_value for part_value in gradient_parts]
    velocity = [(jnp.sum(directions[axis_place] * momentum, axis=0) + 0.5 * force_parts[axis_place]) / density for axis_place in range(3)]
    moment_eq, order_eq, projection = equilibria(density, order_field, potential, velocity, weight, directions)
    order_eq = jnp.concatenate([(order_field - jnp.sum(order_eq[1:], axis=0))[None], order_eq[1:]], 0)
    force_projection = directions[0] * force_parts[0] + directions[1] * force_parts[1] + directions[2] * force_parts[2]
    velocity_force = velocity[0] * force_parts[0] + velocity[1] * force_parts[1] + velocity[2] * force_parts[2]
    source = (1.0 - 0.5 / relax_momentum) * weight * (3.0 * (force_projection - velocity_force) + 9.0 * projection * force_projection)
    moment_post = momentum - (momentum - moment_eq) / relax_momentum + source
    order_post = order - (order - order_eq) / relax_order
    return moment_post, order_post, moment_eq, order_eq, density, velocity


def jump_terms(chosen, density, order_field, potential, velocity, velocity_jump, base_moment, base_order):
    weight, directions = tables(chosen)
    shifted_velocity = [velocity[0], velocity[1] + velocity_jump, velocity[2]]
    moment_shift, order_shift, projection = equilibria(density, order_field, potential, shifted_velocity, weight, directions)
    return moment_shift - base_moment, order_shift - base_order


def shear_rows(grid_field, shifts, near_weight, far_weight):
    span = grid_field.shape[1]
    positions = jnp.mod(jnp.arange(span, dtype=jnp.int32)[None, :] + shifts[:, None], span).astype(jnp.int32)
    positions = jnp.broadcast_to(positions[:, :, None], grid_field.shape)
    near_values = jnp.take_along_axis(grid_field, positions, axis=1)
    far_values = jnp.take_along_axis(grid_field, jnp.mod(positions + 1, span).astype(jnp.int32), axis=1)
    return near_weight[:, None, None] * near_values + far_weight[:, None, None] * far_values


def reference(momentum_dist, order_dist, offsets):
    quarter = NX // 4
    x_index = jnp.arange(NX, dtype=jnp.int32)
    fractions = (2.0 * jnp.arange(4, dtype=jnp.float32) + 1.0) / 8.0
    lower_mask = x_index % quarter == 0
    lower_plane = (x_index // quarter) % 4
    upper_mask = (x_index + 1) % quarter == 0
    upper_plane = ((x_index + 1) // quarter) % 4
    low_shift = jnp.where(lower_mask, offsets[lower_plane], 0).astype(jnp.int32)
    low_near = jnp.where(lower_mask, 1.0 - fractions[lower_plane], 1.0)
    low_far = jnp.where(lower_mask, fractions[lower_plane], 0.0)
    up_shift = jnp.where(upper_mask, -offsets[upper_plane] - 1, 0).astype(jnp.int32)
    up_near = jnp.where(upper_mask, fractions[upper_plane], 1.0)
    up_far = jnp.where(upper_mask, 1.0 - fractions[upper_plane], 0.0)

    order_field = jnp.sum(order_dist, axis=0)
    order_minus = shear_rows(jnp.roll(order_field, 1, 0), low_shift, low_near, low_far)
    order_plus = shear_rows(jnp.roll(order_field, -1, 0), up_shift, up_near, up_far)
    order_north = jnp.roll(order_field, -1, 1)
    order_south = jnp.roll(order_field, 1, 1)
    order_upper = jnp.roll(order_field, -1, 2)
    order_lower = jnp.roll(order_field, 1, 2)
    laplacian = (order_plus + order_minus) + (order_north + order_south) + (order_upper + order_lower) - 6.0 * order_field
    gradient_parts = [0.5 * (order_plus - order_minus), 0.5 * (order_north - order_south), 0.5 * (order_upper - order_lower)]
    potential = bulk_quadratic * order_field + bulk_quartic * order_field * order_field * order_field - interface_kappa * laplacian

    moment_post, order_post, moment_eq, order_eq, density, velocity = collide(momentum_dist, order_dist, order_field, potential, gradient_parts)

    for chosen, mask, velocity_jump in ((rising, upper_mask, -plane_speed), (falling, lower_mask, plane_speed)):
        moment_delta, order_delta = jump_terms(chosen, density, order_field, potential, velocity, velocity_jump, moment_post[jnp.asarray(chosen)] * 0.0 + moment_eq[jnp.asarray(chosen)], order_eq[jnp.asarray(chosen)])
        row_mask = mask[None, :, None, None]
        moment_post = moment_post.at[jnp.asarray(chosen)].set(jnp.where(row_mask, moment_post[jnp.asarray(chosen)] + moment_delta, moment_post[jnp.asarray(chosen)]))
        order_post = order_post.at[jnp.asarray(chosen)].set(jnp.where(row_mask, order_post[jnp.asarray(chosen)] + order_delta, order_post[jnp.asarray(chosen)]))

    def stream(post):
        arrived = []
        for component in range(19):
            step_x, step_y, step_z = lattice_velocity[component]
            shifted = jnp.roll(post[component], (step_x, step_z), axis=(0, 2))
            if step_x == 1:
                shifted = shear_rows(shifted, low_shift - step_y, low_near, low_far)
            elif step_x == -1:
                shifted = shear_rows(shifted, up_shift - step_y, up_near, up_far)
            else:
                shifted = jnp.roll(shifted, step_y, 1)
            arrived.append(shifted)
        return jnp.stack(arrived)

    return stream(moment_post), stream(order_post)
```

```python
import jax
import jax.numpy as jnp
from jax import lax
from jax.experimental import pallas as pl
from jax.experimental.pallas import tpu as pltpu
from jax.sharding import PartitionSpec as P

lattice_velocity = [
    (0, 0, 0),
    (1, 0, 0),
    (-1, 0, 0),
    (0, 1, 0),
    (0, -1, 0),
    (0, 0, 1),
    (0, 0, -1),
    (1, 1, 0),
    (-1, -1, 0),
    (1, -1, 0),
    (-1, 1, 0),
    (1, 0, 1),
    (-1, 0, -1),
    (1, 0, -1),
    (-1, 0, 1),
    (0, 1, 1),
    (0, -1, -1),
    (0, 1, -1),
    (0, -1, 1),
]
lattice_weight = [1.0 / 3.0] + [1.0 / 18.0] * 6 + [1.0 / 36.0] * 12
plane_speed = 0.04
rising = [1, 7, 9, 11, 13]
falling = [2, 8, 10, 12, 14]
north_going = [i for i in range(19) if lattice_velocity[i][1] == 1]
south_going = [i for i in range(19) if lattice_velocity[i][1] == -1]
f32 = jnp.float32
VMEM = pltpu.VMEM
LANES = 128


def spec_of(space):
    return pl.BlockSpec(memory_space=space)


def params(limit):
    return pltpu.CompilerParams(vmem_limit_bytes=limit)


def along(parts, c):
    total = None
    for sign, part in zip(c, parts):
        if sign == 0:
            continue
        if total is None:
            total = part if sign > 0 else -part
        else:
            total = total + part if sign > 0 else total - part
    return total


def signed_sum(load, axis):
    ups = [i for i in range(19) if lattice_velocity[i][axis] == 1]
    downs = [i for i in range(19) if lattice_velocity[i][axis] == -1]
    total = load(ups[0]) - load(downs[0])
    for i, j in zip(ups[1:], downs[1:]):
        total = total + (load(i) - load(j))
    return total


class Site:
    def __init__(self, load, phi, minus, plus, south, north, lower, upper):
        rho = load(0)
        for i in range(1, 19):
            rho = rho + load(i)
        momentum = [signed_sum(load, axis) for axis in range(3)]
        lap = (plus + minus) + (north + south) + (upper + lower) - 6.0 * phi
        mu = phi * (0.0625 * (phi * phi) - 0.0625) - 0.04 * lap
        half_mu = 0.5 * mu
        force = [half_mu * (plus - minus), half_mu * (north - south), half_mu * (upper - lower)]
        inverse = 1.0 / rho
        u = [(j + 0.5 * k) * inverse for j, k in zip(momentum, force)]
        uu = u[0] * u[0] + u[1] * u[1] + u[2] * u[2]
        uf = u[0] * force[0] + u[1] * force[1] + u[2] * force[2]
        self.rho, self.phi, self.mu, self.u, self.force, self.uu = rho, phi, mu, u, force, uu
        self.r = 1.25 * rho
        self.k = self.r * (1.0 - 1.5 * uu) - 1.125 * uf
        self.g_scale = phi * (1.0 / 0.9)
        self.g_base = (3.0 / 0.9) * mu - 1.5 * (self.g_scale * uu)

    def pair_f(self, i):
        p, q = along(self.u, lattice_velocity[i]), along(self.force, lattice_velocity[i])
        w = lattice_weight[i]
        rp = self.r * p
        even = w * (self.k + p * (4.5 * rp + 3.375 * q))
        odd = (3.0 * w) * rp + (1.125 * w) * q
        return even, odd

    def pair_g(self, i):
        p = along(self.u, lattice_velocity[i])
        w = lattice_weight[i]
        gp = self.g_scale * p
        return w * (self.g_base + 4.5 * (gp * p)), (3.0 * w) * gp

    def jump(self, i, delta):
        cy = lattice_velocity[i][1]
        uy = self.u[1]
        if cy == 0:
            return delta * (-3.0 * uy) - (1.5 * delta * delta)
        p = along(self.u, lattice_velocity[i])
        return delta * (3.0 * cy + (9.0 * cy) * p - 3.0 * uy) + (3.0 * delta * delta)


def z_moved(value, step):
    if step == 0:
        return value
    return pltpu.roll(value, step % value.shape[-1], value.ndim - 1)


class Shear:
    def __init__(self, raw, wide, rows):
        self.raw, self.wide, self.rows = raw, wide, rows

    def clear(self):
        self.raw[...] = jnp.zeros_like(self.raw)
        self.wide[...] = jnp.zeros_like(self.wide)

    def put(self, value, up, near, far):
        n = self.rows
        for k in range(self.raw.shape[0]):
            self.raw[k, 8 : 8 + n] = value[:, LANES * k : LANES * k + LANES]
        for k in range(self.raw.shape[0]):
            if up:
                self.wide[k, n : n + n + 8] = (
                    near * self.raw[k, 0 : n + 8] + far * self.raw[k, 1 : n + 9]
                )
            else:
                self.wide[k, n + 8 : n + n + 16] = (
                    near * self.raw[k, 7 : n + 15] + far * self.raw[k, 8 : n + 16]
                )

    def take(self, up, block, rest, cy, store):
        n = self.rows
        if up:
            start = (n + 8 if block == 0 else 8) + rest - cy
        else:
            start = (n + 8 if block == 0 else n + n + 8) - rest - cy
        for k in range(self.raw.shape[0]):
            store(k, self.wide[k, pl.ds(start, n)])


def lane_store(ref, lead):
    def store(k, value):
        ref[(*lead, slice(None), slice(LANES * k, LANES * k + LANES))] = value

    return store


def shear_scratch(rows, cols):
    return [
        VMEM((cols // LANES, rows + 16, LANES), f32),
        VMEM((cols // LANES, 3 * rows + 16, LANES), f32),
    ]


def phi_kernel(
    ints, floats, g_ref, phi_ref, ra, rb, fa, fb, north, south, buf, sems, raw, wide
):
    layers, rows = buf.shape[1], buf.shape[2]
    order = [layers - 1, 0] + list(range(1, layers - 1))
    copies = {
        x: pltpu.make_async_copy(g_ref.at[:, pl.ds(x, 1)], buf.at[:, pl.ds(x, 1)], sems.at[x])
        for x in order
    }
    for x in order:
        copies[x].start()
    shear = Shear(raw, wide, rows)
    shear.clear()
    for x in order:
        copies[x].wait()
        total = buf[0, x]
        for i in range(1, 19):
            total = total + buf[i, x]
        phi_ref[x] = total
        north[x : x + 1] = total[rows - 1 : rows]
        south[x : x + 1] = total[0:1]
        if x == layers - 1:
            shear.put(total, True, floats[0], floats[1])
            shear.take(True, 0, ints[0], 0, lane_store(ra, ()))
            shear.take(True, 1, ints[0], 0, lane_store(rb, ()))
        if x == 0:
            shear.clear()
            shear.put(total, False, floats[2], floats[3])
            shear.take(False, 0, ints[1], 0, lane_store(fa, ()))
            shear.take(False, 1, ints[1], 0, lane_store(fb, ()))


def with_halo(ref, layer, below, above):
    rows = layer.shape[0]
    ref[8 : 8 + rows] = layer
    ref[7:8] = below
    ref[8 + rows : 9 + rows] = above


def face_kernel(
    ints,
    floats,
    f_ref,
    g_ref,
    phi_ref,
    ra,
    rb,
    fa,
    fb,
    from_south,
    from_north,
    mate,
    direct,
    across,
    joint,
    corner_near_up,
    corner_far_up,
    corner_near_low,
    corner_far_low,
    fbuf,
    gbuf,
    sems,
    halo,
    post,
    raw,
    wide,
):
    layers, rows, cols = phi_ref.shape
    faces = (layers - 1, 0)
    copies = []
    for s, x in enumerate(faces):
        copies.append(
            (
                pltpu.make_async_copy(f_ref.at[:, pl.ds(x, 1)], fbuf.at[:, pl.ds(s, 1)], sems.at[s, 0]),
                pltpu.make_async_copy(g_ref.at[:, pl.ds(x, 1)], gbuf.at[:, pl.ds(s, 1)], sems.at[s, 1]),
            )
        )
    for pair in copies:
        for copy in pair:
            copy.start()
    shear = Shear(raw, wide, rows)
    odd = ints[2] == 1
    for s, x in enumerate(faces):
        up = s == 0
        phi = phi_ref[x]
        with_halo(halo, phi, from_south[x : x + 1], from_north[x : x + 1])
        delta = floats[4] if up else floats[5]
        near, far = (floats[0], floats[1]) if up else (floats[2], floats[3])
        rest = ints[0] if up else ints[1]
        for copy in copies[s]:
            copy.wait()
        for h in range(0, rows, 8):
            span = slice(h, h + 8)
            phi_h = phi_ref[x, span]
            if up:
                minus, plus = phi_ref[x - 1, span], fa[span] + fb[span]
            else:
                minus, plus = ra[span] + rb[span], phi_ref[x + 1, span]
            site = Site(
                lambda i: fbuf[i, s, span],
                phi_h,
                minus,
                plus,
                halo[7 + h : 15 + h],
                halo[9 + h : 17 + h],
                z_moved(phi_h, 1),
                z_moved(phi_h, -1),
            )
            for j in range(5):
                i = rising[j] if up else falling[j]
                w = lattice_weight[i]
                change = w * site.jump(i, delta)
                even, odd_part = site.pair_f(i)
                value = even + odd_part - 0.25 * fbuf[i, s, span] + site.rho * change
                post[j, span] = z_moved(value, lattice_velocity[i][2])
                even, odd_part = site.pair_g(i)
                value = even + odd_part - (1.0 / 9.0) * gbuf[i, s, span] + phi_h * change
                post[5 + j, span] = z_moved(value, lattice_velocity[i][2])
        shear.clear()
        for j in range(10):
            i = (rising if up else falling)[j % 5]
            cy = lattice_velocity[i][1]
            shear.put(post[j], up, near, far)

            @pl.when(odd)
            def _():
                shear.take(up, 0, rest, cy, lane_store(direct if up else joint, (j,)))
                shear.take(up, 1, rest, cy, lane_store(mate if up else across, (j,)))

            @pl.when(jnp.logical_not(odd))
            def _():
                shear.take(up, 0, rest, cy, lane_store(joint if up else direct, (j,)))
                shear.take(up, 1, rest, cy, lane_store(across if up else mate, (j,)))

            slot = j // 5
            if cy == 1:
                gate = jnp.where(rest == (0 if up else rows - 1), near, 0.0)
                target = corner_near_up if up else corner_near_low
                target[slot : slot + 1] = gate * post[j, rows - 1 : rows]
            if cy == -1:
                gate = jnp.where(rest == (rows - 1 if up else 0), far, 0.0)
                target = corner_far_up if up else corner_far_low
                target[slot : slot + 1] = gate * post[j, 0:1]


def bulk_kernel(
    after,
    f_ref,
    g_ref,
    phi_ref,
    ra,
    rb,
    fa,
    fb,
    from_south,
    from_north,
    next_f,
    next_g,
    north,
    south,
    wide_phi,
    halo,
):
    layers, rows, cols = phi_ref.shape
    wide_phi[0] = ra[...] + rb[...]
    wide_phi[layers + 1] = fa[...] + fb[...]
    for x in range(layers):
        wide_phi[x + 1] = phi_ref[x]

    def layer(x, carry):
        with_halo(halo, phi_ref[x], from_south[pl.ds(x, 1)], from_north[pl.ds(x, 1)])
        beyond = lax.rem(x + 1, layers)
        before = lax.rem(x + layers - 1, layers)
        for h in range(0, rows, 8):
            span = slice(h, h + 8)
            phi_h = phi_ref[x, span]
            site = Site(
                lambda i: f_ref[i, x, span],
                phi_h,
                wide_phi[x, span],
                wide_phi[x + 2, span],
                halo[7 + h : 15 + h],
                halo[9 + h : 17 + h],
                z_moved(phi_h, 1),
                z_moved(phi_h, -1),
            )

            def emit(out, slot, i, value):
                cx, cy, cz = lattice_velocity[i]
                value = z_moved(value, cz)
                at = beyond if cx == 1 else before if cx == -1 else x
                if cy == 0:
                    out[i, at, span] = value
                elif cy == 1:
                    if h + 8 < rows:
                        out[i, at, h + 1 : h + 9] = value
                    else:
                        out[i, at, h + 1 : h + 8] = value[0:7]
                        north[slot * 5 + north_going.index(i), pl.ds(x, 1)] = value[7:8]
                else:
                    if h > 0:
                        out[i, at, h - 1 : h + 7] = value
                    else:
                        out[i, at, 0:7] = value[1:8]
                        south[slot * 5 + south_going.index(i), pl.ds(x, 1)] = value[0:1]

            emit(next_f, 0, 0, lattice_weight[0] * site.k - 0.25 * f_ref[0, x, span])
            rest_g = (phi_h - 2.0 * site.mu - 0.5 * (phi_h * site.uu)) * (1.0 / 0.9)
            emit(next_g, 1, 0, rest_g - (1.0 / 9.0) * g_ref[0, x, span])
            for i in range(1, 19, 2):
                even, odd = site.pair_f(i)
                emit(next_f, 0, i, (even + odd) - 0.25 * f_ref[i, x, span])
                emit(next_f, 0, i + 1, (even - odd) - 0.25 * f_ref[i + 1, x, span])
                even, odd = site.pair_g(i)
                emit(next_g, 1, i, (even + odd) - (1.0 / 9.0) * g_ref[i, x, span])
                emit(next_g, 1, i + 1, (even - odd) - (1.0 / 9.0) * g_ref[i + 1, x, span])
        return carry

    lax.fori_loop(0, layers, layer, 0)


def rim_kernel(from_south, from_north, f_in, g_in, f_out, g_out, buf, sems):
    layers, rows = f_out.shape[1], f_out.shape[2]
    jobs = []
    for side, (chosen, recv) in enumerate(((north_going, from_south), (south_going, from_north))):
        first = 0 if side == 0 else rows - 8
        for family, out in enumerate((f_out, g_out)):
            for j, i in enumerate(chosen):
                slot = side * 10 + family * 5 + j
                tile = out.at[i, :, pl.ds(first, 8)]
                jobs.append((slot, i, side, recv, family * 5 + j, tile))
    for slot, i, side, recv, row, tile in jobs:
        pltpu.make_async_copy(tile, buf.at[slot], sems.at[slot]).start()
    for slot, i, side, recv, row, tile in jobs:
        pltpu.make_async_copy(tile, buf.at[slot], sems.at[slot]).wait()
        cx = lattice_velocity[i][0]
        at = 0 if side == 0 else 7
        for x in range(layers):
            if 0 <= x + cx < layers:
                buf[slot, x + cx, at : at + 1] = recv[row, x : x + 1]
        pltpu.make_async_copy(buf.at[slot], tile, sems.at[slot]).start()
    for slot, i, side, recv, row, tile in jobs:
        pltpu.make_async_copy(buf.at[slot], tile, sems.at[slot]).wait()


def face_fill_kernel(
    ints,
    direct,
    across,
    joint,
    near_up,
    far_up,
    near_low,
    far_low,
    f_in,
    g_in,
    f_out,
    g_out,
    low,
    high,
    sems,
):
    layers, rows = f_out.shape[1], f_out.shape[2]
    odd = ints[2] == 1

    @pl.when(odd)
    def _():
        low[...] = direct[...] + across[...]
        high[...] = joint[...]

    @pl.when(jnp.logical_not(odd))
    def _():
        low[...] = joint[...]
        high[...] = direct[...] + across[...]

    copies = []
    for family, out in enumerate((f_out, g_out)):
        for j in range(5):
            slot = family * 5 + j
            for buf, chosen, near, far, x in (
                (low, rising, near_up, far_up, 0),
                (high, falling, near_low, far_low, layers - 1),
            ):
                cy = lattice_velocity[chosen[j]][1]
                if cy == 1:
                    buf[slot, 0:1] = buf[slot, 0:1] + near[family : family + 1]
                if cy == -1:
                    buf[slot, rows - 1 : rows] = buf[slot, rows - 1 : rows] + far[family : family + 1]
                copy = pltpu.make_async_copy(
                    buf.at[slot], out.at[chosen[j], x], sems.at[0 if x == 0 else 1, slot]
                )
                copy.start()
                copies.append(copy)
    for copy in copies:
        copy.wait()


def on_device(momentum_dist, order_dist, offsets):
    layers, rows, cols = momentum_dist.shape[1:]
    count_x, count_y = lax.axis_size("gx"), lax.axis_size("gy")
    per_plane = count_x // 4
    half = count_y // 2
    a, c = lax.axis_index("gx"), lax.axis_index("gy")

    def plane_of(column):
        is_plane = column % per_plane == 0
        plane = column // per_plane % 4
        rest = jnp.where(is_plane, jnp.clip(offsets[plane] - half * rows, 0, rows - 1), 0)
        return is_plane, (2.0 * plane.astype(f32) + 1.0) / 8.0, rest

    up_is, up_part, up_rest = plane_of((a + 1) % count_x)
    low_is, low_part, low_rest = plane_of(a)
    ints = jnp.stack([up_rest, low_rest, c % 2]).astype(jnp.int32)
    floats = jnp.stack(
        [
            jnp.where(up_is, 1.0 - up_part, 1.0),
            jnp.where(up_is, up_part, 0.0),
            jnp.where(low_is, low_part, 0.0),
            jnp.where(low_is, 1.0 - low_part, 1.0),
            jnp.where(up_is, -plane_speed, 0.0),
            jnp.where(low_is, plane_speed, 0.0),
        ]
    ).astype(f32)

    def hop(value, target):
        perm = []
        for x in range(count_x):
            for y in range(count_y):
                tx, ty = target(x, y)
                perm.append((x * count_y + y, tx % count_x * count_y + ty % count_y))
        return lax.ppermute(value, ("gx", "gy"), perm)

    def base_up(x):
        return half if (x + 1) % per_plane == 0 else 0

    def base_low(x):
        return half if x % per_plane == 0 else 0

    def hop_up(value, extra):
        return hop(value, lambda x, y: (x + 1, y - base_up(x) - extra))

    def hop_low(value, extra):
        return hop(value, lambda x, y: (x - 1, y + base_low(x) + extra))

    def hop_parity(value, odd_up, extra):
        def target(x, y):
            if (y % 2 == 1) == odd_up:
                return (x + 1, y - base_up(x) - extra)
            return (x - 1, y + base_low(x) + extra)

        return hop(value, target)

    def hop_y(value, step):
        return hop(value, lambda x, y: (x, y + step))

    smem, vmem, hbm = spec_of(pltpu.SMEM), spec_of(VMEM), spec_of(pl.ANY)
    plane = jax.ShapeDtypeStruct((rows, cols), f32)
    edge = jax.ShapeDtypeStruct((layers, cols), f32)
    phi, ra, rb, fa, fb, to_north, to_south = pl.pallas_call(
        phi_kernel,
        out_shape=[jax.ShapeDtypeStruct((layers, rows, cols), f32)] + [plane] * 4 + [edge] * 2,
        in_specs=[smem, smem, hbm],
        out_specs=[vmem] * 7,
        scratch_shapes=[
            VMEM((19, layers, rows, cols), f32),
            pltpu.SemaphoreType.DMA((layers,)),
            *shear_scratch(rows, cols),
        ],
        compiler_params=params(24 << 20),
        name="order_field",
    )(ints, floats, order_dist)

    ra, rb = hop_up(ra, 0), hop_up(rb, 1)
    fa, fb = hop_low(fa, 0), hop_low(fb, 1)
    phi_south, phi_north = hop_y(to_north, 1), hop_y(to_south, -1)
    field_parts = (phi, ra, rb, fa, fb, phi_south, phi_north)

    ten = jax.ShapeDtypeStruct((10, rows, cols), f32)
    two = jax.ShapeDtypeStruct((2, cols), f32)
    mate, direct, across, joint, near_up, far_up, near_low, far_low = pl.pallas_call(
        face_kernel,
        out_shape=[ten] * 4 + [two] * 4,
        in_specs=[smem, smem, hbm, hbm] + [vmem] * 7,
        out_specs=[vmem] * 8,
        scratch_shapes=[
            VMEM((19, 2, rows, cols), f32),
            VMEM((19, 2, rows, cols), f32),
            pltpu.SemaphoreType.DMA((2, 2)),
            VMEM((rows + 16, cols), f32),
            VMEM((10, rows, cols), f32),
            *shear_scratch(rows, cols),
        ],
        compiler_params=params(24 << 20),
        name="faces",
    )(ints, floats, momentum_dist, order_dist, *field_parts)

    mate = hop(mate, lambda x, y: (x, y ^ 1))
    direct = hop_parity(direct, True, 0)
    across = hop_parity(across, False, 1)
    near_up, far_up = hop_up(near_up, -1), hop_up(far_up, 2)
    near_low, far_low = hop_low(near_low, 2), hop_low(far_low, -1)
    joint = joint + mate
    after = joint
    joint = hop_parity(joint, False, 0)

    side = jax.ShapeDtypeStruct((10, layers, cols), f32)
    whole = jax.ShapeDtypeStruct(momentum_dist.shape, f32)
    next_f, next_g, to_north, to_south = pl.pallas_call(
        bulk_kernel,
        out_shape=[whole, whole, side, side],
        in_specs=[hbm] + [vmem] * 9,
        out_specs=[vmem] * 4,
        scratch_shapes=[
            VMEM((layers + 2, rows, cols), f32),
            VMEM((rows + 16, cols), f32),
        ],
        compiler_params=params(48 << 20),
        name="bulk",
    )(after, momentum_dist, order_dist, *field_parts)
    from_south, from_north = hop_y(to_north, 1), hop_y(to_south, -1)

    next_f, next_g = pl.pallas_call(
        rim_kernel,
        out_shape=[whole, whole],
        in_specs=[vmem, vmem, hbm, hbm],
        out_specs=[hbm, hbm],
        scratch_shapes=[VMEM((20, layers, 8, cols), f32), pltpu.SemaphoreType.DMA((20,))],
        input_output_aliases={2: 0, 3: 1},
        compiler_params=params(24 << 20),
        name="y_rims",
    )(from_south, from_north, next_f, next_g)

    return pl.pallas_call(
        face_fill_kernel,
        out_shape=[whole, whole],
        in_specs=[smem] + [vmem] * 7 + [hbm, hbm],
        out_specs=[hbm, hbm],
        scratch_shapes=[
            VMEM((10, rows, cols), f32),
            VMEM((10, rows, cols), f32),
            pltpu.SemaphoreType.DMA((2, 10)),
        ],
        input_output_aliases={8: 0, 9: 1},
        compiler_params=params(24 << 20),
        name="x_faces",
    )(ints, direct, across, joint, near_up, far_up, near_low, far_low, next_f, next_g)


def solution(mesh):
    return jax.shard_map(
        on_device,
        mesh=mesh,
        in_specs=(P(None, "gx", "gy", None), P(None, "gx", "gy", None), P()),
        out_specs=(P(None, "gx", "gy", None), P(None, "gx", "gy", None)),
        check_vma=False,
    )
```

```python
import functools

import jax
import jax.numpy as jnp
from jax import lax
from jax.experimental import pallas as pl
from jax.experimental.pallas import tpu as pltpu
from jax.sharding import PartitionSpec as P

lattice_velocity = [
    (0, 0, 0),
    (1, 0, 0),
    (-1, 0, 0),
    (0, 1, 0),
    (0, -1, 0),
    (0, 0, 1),
    (0, 0, -1),
    (1, 1, 0),
    (-1, -1, 0),
    (1, -1, 0),
    (-1, 1, 0),
    (1, 0, 1),
    (-1, 0, -1),
    (1, 0, -1),
    (-1, 0, 1),
    (0, 1, 1),
    (0, -1, -1),
    (0, 1, -1),
    (0, -1, 1),
]
lattice_weight = [1.0 / 3.0] + [1.0 / 18.0] * 6 + [1.0 / 36.0] * 12
plane_speed = 0.04
rising = [1, 7, 9, 11, 13]
falling = [2, 8, 10, 12, 14]
north_going = [i for i in range(19) if lattice_velocity[i][1] == 1]
south_going = [i for i in range(19) if lattice_velocity[i][1] == -1]
f32 = jnp.float32
VMEM = pltpu.VMEM
LANES = 128


def z_moved(value, step):
    if step == 0:
        return value
    return pltpu.roll(value, step % value.shape[-1], value.ndim - 1)


def spec_of(space):
    return pl.BlockSpec(memory_space=space)


def params(limit):
    return pltpu.CompilerParams(vmem_limit_bytes=limit)


def along(parts, c):
    total = None
    for sign, part in zip(c, parts):
        if sign == 0:
            continue
        if total is None:
            total = part if sign > 0 else -part
        else:
            total = total + part if sign > 0 else total - part
    return total


def signed_sum(load, axis):
    ups = [i for i in range(19) if lattice_velocity[i][axis] == 1]
    downs = [i for i in range(19) if lattice_velocity[i][axis] == -1]
    total = load(ups[0]) - load(downs[0])
    for i, j in zip(ups[1:], downs[1:]):
        total = total + (load(i) - load(j))
    return total


def moments_of(load):
    rho = load(0)
    for i in range(1, 19):
        rho = rho + load(i)
    return [rho] + [signed_sum(load, axis) for axis in range(3)]


class Site:
    def __init__(self, moments, phi, minus, plus, south, north):
        rho, momentum = moments[0], moments[1:]
        lower, upper = z_moved(phi, 1), z_moved(phi, -1)
        lap = (plus + minus) + (north + south) + (upper + lower) - 6.0 * phi
        mu = phi * (0.0625 * (phi * phi) - 0.0625) - 0.04 * lap
        half_mu = 0.5 * mu
        force = [half_mu * (plus - minus), half_mu * (north - south), half_mu * (upper - lower)]
        inverse = 1.0 / rho
        u = [(j + 0.5 * k) * inverse for j, k in zip(momentum, force)]
        uu = u[0] * u[0] + u[1] * u[1] + u[2] * u[2]
        uf = u[0] * force[0] + u[1] * force[1] + u[2] * force[2]
        self.rho, self.phi, self.mu, self.u, self.force, self.uu = rho, phi, mu, u, force, uu
        self.r = 1.25 * rho
        self.k = self.r * (1.0 - 1.5 * uu) - 1.125 * uf
        self.g_scale = phi * (1.0 / 0.9)
        self.g_base = (3.0 / 0.9) * mu - 1.5 * (self.g_scale * uu)

    def pair_f(self, i):
        p, q = along(self.u, lattice_velocity[i]), along(self.force, lattice_velocity[i])
        w = lattice_weight[i]
        rp = self.r * p
        even = w * (self.k + p * (4.5 * rp + 3.375 * q))
        odd = (3.0 * w) * rp + (1.125 * w) * q
        return even, odd

    def pair_g(self, i):
        p = along(self.u, lattice_velocity[i])
        w = lattice_weight[i]
        gp = self.g_scale * p
        return w * (self.g_base + 4.5 * (gp * p)), (3.0 * w) * gp

    def jump(self, i, delta):
        cy = lattice_velocity[i][1]
        uy = self.u[1]
        if cy == 0:
            return delta * (-3.0 * uy) - (1.5 * delta * delta)
        p = along(self.u, lattice_velocity[i])
        return delta * (3.0 * cy + (9.0 * cy) * p - 3.0 * uy) + (3.0 * delta * delta)


class Shear:
    def __init__(self, raw, wide, rows):
        self.raw, self.wide, self.rows = raw, wide, rows

    def clear(self):
        self.raw[...] = jnp.zeros_like(self.raw)
        self.wide[...] = jnp.zeros_like(self.wide)

    def put(self, value, up, near, far):
        n = self.rows
        for k in range(self.raw.shape[0]):
            self.raw[k, 8 : 8 + n] = value[:, LANES * k : LANES * k + LANES]
        for k in range(self.raw.shape[0]):
            if up:
                self.wide[k, n : n + n + 8] = (
                    near * self.raw[k, 0 : n + 8] + far * self.raw[k, 1 : n + 9]
                )
            else:
                self.wide[k, n + 8 : n + n + 16] = (
                    near * self.raw[k, 7 : n + 15] + far * self.raw[k, 8 : n + 16]
                )

    def add_row(self, at, row):
        for k in range(self.raw.shape[0]):
            lanes = slice(LANES * k, LANES * k + LANES)
            self.wide[k, at : at + 1] = self.wide[k, at : at + 1] + row[:, lanes]

    def take(self, up, block, rest, cy, ref, j):
        n = self.rows
        if up:
            start = (n + 8 if block == 0 else 8) + rest - cy
        else:
            start = (n + 8 if block == 0 else n + n + 8) - rest - cy
        for k in range(self.raw.shape[0]):
            ref[j, :, LANES * k : LANES * k + LANES] = self.wide[k, pl.ds(start, n)]


class Planes:
    def __init__(self, offsets, rows, sizes):
        count_x, count_y = sizes
        per_plane, half = count_x // 4, count_y // 2
        a = lax.axis_index("gx")
        self.odd = lax.rem(lax.axis_index("gy"), 2) == 1

        def plane_of(column):
            is_plane = lax.rem(column, per_plane) == 0
            plane = lax.rem(lax.div(column, per_plane), 4)
            rest = jnp.where(is_plane, jnp.clip(offsets[plane] - half * rows, 0, rows - 1), 0)
            return is_plane, (2.0 * plane.astype(f32) + 1.0) * 0.125, rest

        up_is, up_part, self.up_rest = plane_of(lax.rem(a + 1, count_x))
        low_is, low_part, self.low_rest = plane_of(a)
        self.up_near = jnp.where(up_is, 1.0 - up_part, 1.0)
        self.up_far = jnp.where(up_is, up_part, 0.0)
        self.low_near = jnp.where(low_is, low_part, 0.0)
        self.low_far = jnp.where(low_is, 1.0 - low_part, 1.0)
        self.up_jump = jnp.where(up_is, -plane_speed, 0.0)
        self.low_jump = jnp.where(low_is, plane_speed, 0.0)


def order_sum(load):
    total = load(0)
    for i in range(1, 19):
        total = total + load(i)
    return total


def phi_faces_kernel(g_ref, top, bottom, buf, sems):
    layers = g_ref.shape[1]
    copies = [
        pltpu.make_async_copy(g_ref.at[:, x], buf.at[s], sems.at[s])
        for s, x in enumerate((layers - 1, 0))
    ]
    for copy in copies:
        copy.start()
    for s, (copy, out) in enumerate(zip(copies, (top, bottom))):
        copy.wait()
        out[...] = order_sum(lambda i: buf[s, i])


def phi_kernel(f_ref, g_ref, top, bottom, phi_ref, to_north, to_south, fbuf, sems):
    layers, rows = phi_ref.shape[0], phi_ref.shape[1]
    faces = (layers - 1, 0)
    copies = [
        pltpu.make_async_copy(f_ref.at[:, x], fbuf.at[:, s], sems.at[s])
        for s, x in enumerate(faces)
    ]
    for copy in copies:
        copy.start()
    phi_ref[layers - 1] = top[...]
    phi_ref[0] = bottom[...]
    for x in range(layers):
        if 0 < x < layers - 1:
            phi_ref[x] = order_sum(lambda i: g_ref[i, x])
        to_north[x : x + 1] = phi_ref[x, rows - 1 : rows]
        to_south[x : x + 1] = phi_ref[x, 0:1]
    for s, x in enumerate(faces):
        copies[s].wait()
        for out, edge, inner, chosen in (
            (to_north, rows - 1, rows - 2, (7, 10)),
            (to_south, 0, 1, (9, 8)),
        ):
            out[layers + s : layers + s + 1] = phi_ref[x, inner : inner + 1]
            at = layers + 2 + 6 * s
            i = chosen[s]
            out[at : at + 1] = fbuf[i, s, edge : edge + 1]
            out[at + 1 : at + 2] = g_ref[i, x, edge : edge + 1]
            for k, part in enumerate(moments_of(lambda i: fbuf[i, s, edge : edge + 1])):
                out[at + 2 + k : at + 3 + k] = part
    for out in (to_north, to_south):
        out[layers + 14 : layers + 16] = jnp.zeros((2, out.shape[1]), f32)


def with_halo(ref, layer, below, above):
    rows = layer.shape[0]
    ref[8 : 8 + rows] = layer
    ref[7:8] = below
    ref[8 + rows : 9 + rows] = above


def corner_values(cells, planes, phi_ref, south_msg, north_msg, minus_wide, plus_wide):
    layers, rows, cols = phi_ref.shape
    cells[...] = jnp.ones_like(cells)
    for row in range(4):
        msg = south_msg if row < 2 else north_msg
        x = layers - 1 if row % 2 == 0 else 0
        beside = rows + (layers - 2 if row % 2 == 0 else 1)
        wide_row = 7 if row < 2 else rows + 8
        at = rows + layers
        first = at + 2 + 6 * (row % 2)
        far_phi = msg[at + row % 2 : at + row % 2 + 1]
        own_phi = phi_ref[x, 0:1] if row < 2 else phi_ref[x, rows - 1 : rows]
        parts = [msg[first + k : first + k + 1] for k in range(6)]
        parts.append(msg[rows + x : rows + x + 1])
        if row % 2 == 0:
            parts += [msg[beside : beside + 1], plus_wide[wide_row : wide_row + 1]]
        else:
            parts += [minus_wide[wide_row : wide_row + 1], msg[beside : beside + 1]]
        parts += [far_phi, own_phi] if row < 2 else [own_phi, far_phi]
        for k, part in enumerate(parts):
            cells[k, row : row + 1] = part
    place = lax.broadcasted_iota(jnp.int32, (8, cols), 0)
    is_top = (place == 0) | (place == 2)
    sx = jnp.where(is_top, 1.0, -1.0)
    sy = jnp.where(place < 2, 1.0, -1.0)
    delta = jnp.where(is_top, planes.up_jump, planes.low_jump)
    site = Site([cells[k] for k in range(2, 6)], *[cells[k] for k in range(6, 11)])
    w = lattice_weight[7]
    p = sx * site.u[0] + sy * site.u[1]
    q = sx * site.force[0] + sy * site.force[1]
    change = delta * (3.0 * sy + 9.0 * (sy * p) - 3.0 * site.u[1]) + 3.0 * (delta * delta)
    rp, gp = site.r * p, site.g_scale * p
    f_post = w * (site.k + p * (4.5 * rp + 3.375 * q) + 3.0 * rp + 1.125 * q + site.rho * change)
    g_post = w * (site.g_base + 4.5 * (gp * p) + 3.0 * gp + site.phi * change)
    return f_post - 0.25 * cells[0], g_post - (1.0 / 9.0) * cells[1]


def face_kernel(
    sizes,
    offsets,
    f_ref,
    g_ref,
    phi_ref,
    rise,
    fall,
    south_msg,
    north_msg,
    mate,
    direct,
    across,
    joint,
    minus_out,
    plus_out,
    minus_wide,
    plus_wide,
    window,
    halo,
    post,
    cells,
    corners,
    raw,
    wide,
):
    layers, rows, cols = phi_ref.shape
    planes = Planes(offsets, rows, sizes)
    shear = Shear(raw, wide, rows)
    window[...] = jnp.zeros_like(window)
    for up in (True, False):
        if up:
            first, second = rise, north_msg
            near, far, start = planes.low_far, planes.low_near, planes.low_rest
        else:
            first, second = south_msg, fall
            near, far, start = planes.up_far, planes.up_near, rows - 1 - planes.up_rest
        target = minus_wide if up else plus_wide
        for k in range(window.shape[0]):
            lanes = slice(LANES * k, LANES * k + LANES)
            window[k, 8 : 8 + rows] = first[0:rows, lanes]
            window[k, 8 + rows : 8 + 2 * rows] = second[0:rows, lanes]
            target[:, lanes] = (
                near * window[k, pl.ds(start, rows + 16)]
                + far * window[k, pl.ds(start + 1, rows + 16)]
            )
    minus_out[...] = minus_wide[8 : 8 + rows]
    plus_out[...] = plus_wide[8 : 8 + rows]
    corners[0], corners[1] = corner_values(
        cells, planes, phi_ref, south_msg, north_msg, minus_wide, plus_wide
    )
    for up in (True, False):
        x = layers - 1 if up else 0
        with_halo(
            halo, phi_ref[x], south_msg[rows + x : rows + x + 1], north_msg[rows + x : rows + x + 1]
        )
        if up:
            near, far, rest, delta = planes.up_near, planes.up_far, planes.up_rest, planes.up_jump
        else:
            near, far, rest, delta = planes.low_near, planes.low_far, planes.low_rest, planes.low_jump
        for h in range(0, rows, 8):
            span = slice(h, h + 8)
            phi_h = phi_ref[x, span]
            if up:
                minus, plus = phi_ref[x - 1, span], plus_wide[8 + h : 16 + h]
            else:
                minus, plus = minus_wide[8 + h : 16 + h], phi_ref[x + 1, span]
            site = Site(
                moments_of(lambda i: f_ref[i, x, span]),
                phi_h,
                minus,
                plus,
                halo[7 + h : 15 + h],
                halo[9 + h : 17 + h],
            )
            for j in range(5):
                i = rising[j] if up else falling[j]
                cz = lattice_velocity[i][2]
                change = lattice_weight[i] * site.jump(i, delta)
                even, odd = site.pair_f(i)
                value = even + odd - 0.25 * f_ref[i, x, span] + site.rho * change
                post[j, span] = z_moved(value, cz)
                even, odd = site.pair_g(i)
                value = even + odd - (1.0 / 9.0) * g_ref[i, x, span] + phi_h * change
                post[5 + j, span] = z_moved(value, cz)
        shear.clear()
        for j in range(10):
            cy = lattice_velocity[(rising if up else falling)[j % 5]][1]
            shear.put(post[j], up, near, far)
            corner = (0 if up else 1) + (0 if cy == 1 else 2)
            if cy == 1:
                gate = jnp.where(rest == (0 if up else rows - 1), near, 0.0)
                at = rows + 7 if up else rows + 8
            if cy == -1:
                gate = jnp.where(rest == (rows - 1 if up else 0), far, 0.0)
                at = 2 * rows + 7 if up else 2 * rows + 8
            if cy != 0:
                shear.add_row(at, gate * corners[j // 5, corner : corner + 1])

            @pl.when(planes.odd)
            def _():
                shear.take(up, 0, rest, cy, direct if up else joint, j)
                shear.take(up, 1, rest, cy, mate if up else across, j)

            @pl.when(jnp.logical_not(planes.odd))
            def _():
                shear.take(up, 0, rest, cy, joint if up else direct, j)
                shear.take(up, 1, rest, cy, across if up else mate, j)


def rim_kernel(f_ref, g_ref, phi_ref, minus, plus, south_msg, north_msg, north, south, line):
    layers, rows, cols = phi_ref.shape
    for edge, out, chosen in ((rows - 1, north, north_going), (0, south, south_going)):
        phi = phi_ref[:, edge, :]
        with_halo(line, phi, minus[edge : edge + 1], plus[edge : edge + 1])
        if edge == 0:
            below, above = south_msg[rows : rows + layers], phi_ref[:, 1, :]
        else:
            below, above = phi_ref[:, rows - 2, :], north_msg[rows : rows + layers]
        site = Site(
            moments_of(lambda i: f_ref[i, :, edge, :]),
            phi,
            line[7 : 7 + layers],
            line[9 : 9 + layers],
            below,
            above,
        )
        for j, i in enumerate(chosen):
            cz = lattice_velocity[i][2]
            even, odd = site.pair_f(i)
            out[j] = z_moved(even + odd - 0.25 * f_ref[i, :, edge, :], cz)
            even, odd = site.pair_g(i)
            out[5 + j] = z_moved(even + odd - (1.0 / 9.0) * g_ref[i, :, edge, :], cz)


def bulk_kernel(
    after,
    f_ref,
    g_ref,
    phi_ref,
    minus,
    plus,
    south_msg,
    north_msg,
    south_rim,
    north_rim,
    next_f,
    next_g,
    wide_phi,
    halo,
):
    layers, rows, cols = phi_ref.shape
    wide_phi[0] = minus[...]
    wide_phi[layers + 1] = plus[...]
    for x in range(layers):
        wide_phi[x + 1] = phi_ref[x]

    def layer(x, carry):
        with_halo(halo, phi_ref[x], south_msg[pl.ds(rows + x, 1)], north_msg[pl.ds(rows + x, 1)])
        beyond = lax.rem(x + 1, layers)
        before = lax.rem(x + layers - 1, layers)
        for h in range(0, rows, 8):
            span = slice(h, h + 8)
            phi_h = phi_ref[x, span]
            site = Site(
                moments_of(lambda i: f_ref[i, x, span]),
                phi_h,
                wide_phi[x, span],
                wide_phi[x + 2, span],
                halo[7 + h : 15 + h],
                halo[9 + h : 17 + h],
            )

            def emit(out, slot, i, value):
                cx, cy, cz = lattice_velocity[i]
                value = z_moved(value, cz)
                at = beyond if cx == 1 else before if cx == -1 else x
                if cy == 0:
                    out[i, at, span] = value
                elif cy == 1:
                    if h == 0:
                        rim = slot * 5 + north_going.index(i)
                        out[i, at, 0:1] = south_rim[rim, pl.ds(x, 1)]
                    if h + 8 < rows:
                        out[i, at, h + 1 : h + 9] = value
                    else:
                        out[i, at, h + 1 : h + 8] = value[0:7]
                else:
                    if h + 8 == rows:
                        rim = slot * 5 + south_going.index(i)
                        out[i, at, rows - 1 : rows] = north_rim[rim, pl.ds(x, 1)]
                    if h > 0:
                        out[i, at, h - 1 : h + 7] = value
                    else:
                        out[i, at, 0:7] = value[1:8]

            emit(next_f, 0, 0, lattice_weight[0] * site.k - 0.25 * f_ref[0, x, span])
            rest_g = (phi_h - 2.0 * site.mu - 0.5 * (phi_h * site.uu)) * (1.0 / 0.9)
            emit(next_g, 1, 0, rest_g - (1.0 / 9.0) * g_ref[0, x, span])
            for i in range(1, 19, 2):
                even, odd = site.pair_f(i)
                emit(next_f, 0, i, (even + odd) - 0.25 * f_ref[i, x, span])
                emit(next_f, 0, i + 1, (even - odd) - 0.25 * f_ref[i + 1, x, span])
                even, odd = site.pair_g(i)
                emit(next_g, 1, i, (even + odd) - (1.0 / 9.0) * g_ref[i, x, span])
                emit(next_g, 1, i + 1, (even - odd) - (1.0 / 9.0) * g_ref[i + 1, x, span])
        return carry

    lax.fori_loop(0, layers, layer, 0)


def face_fill_kernel(direct, across, joint, f_in, g_in, f_out, g_out, low, high, sems):
    layers = f_out.shape[1]
    odd = lax.rem(lax.axis_index("gy"), 2) == 1

    @pl.when(odd)
    def _():
        low[...] = direct[...] + across[...]
        high[...] = joint[...]

    @pl.when(jnp.logical_not(odd))
    def _():
        low[...] = joint[...]
        high[...] = direct[...] + across[...]

    copies = []
    for family, out in enumerate((f_out, g_out)):
        for j in range(5):
            slot = family * 5 + j
            for side, buf, chosen, x in ((0, low, rising, 0), (1, high, falling, layers - 1)):
                copy = pltpu.make_async_copy(
                    buf.at[slot], out.at[chosen[j], x], sems.at[side, slot]
                )
                copy.start()
                copies.append(copy)
    for copy in copies:
        copy.wait()


def on_device(momentum_dist, order_dist, offsets):
    layers, rows, cols = momentum_dist.shape[1:]
    count_x, count_y = lax.axis_size("gx"), lax.axis_size("gy")
    per_plane = count_x // 4
    half = count_y // 2

    def hop(value, target):
        perm = []
        for x in range(count_x):
            for y in range(count_y):
                tx, ty = target(x, y)
                perm.append((x * count_y + y, tx % count_x * count_y + ty % count_y))
        return lax.ppermute(value, ("gx", "gy"), perm)

    def base_up(x):
        return half if (x + 1) % per_plane == 0 else 0

    def base_low(x):
        return half if x % per_plane == 0 else 0

    def hop_parity(value, odd_up, extra):
        def target(x, y):
            if (y % 2 == 1) == odd_up:
                return (x + 1, y - base_up(x) - extra)
            return (x - 1, y + base_low(x) + extra)

        return hop(value, target)

    def hop_y(value, step):
        return hop(value, lambda x, y: (x, y + step))

    smem, vmem, anywhere = spec_of(pltpu.SMEM), spec_of(VMEM), spec_of(pl.ANY)
    plane = jax.ShapeDtypeStruct((rows, cols), f32)
    top, bottom = pl.pallas_call(
        phi_faces_kernel,
        out_shape=[plane] * 2,
        in_specs=[anywhere],
        out_specs=[vmem] * 2,
        scratch_shapes=[VMEM((2, 19, rows, cols), f32), pltpu.SemaphoreType.DMA((2,))],
        compiler_params=params(60 << 20),
        name="phi_faces",
    )(order_dist)
    rise = hop(top, lambda x, y: (x + 1, y - base_up(x)))
    fall = hop(bottom, lambda x, y: (x - 1, y + base_low(x)))

    block = jax.ShapeDtypeStruct((layers + 16, cols), f32)
    phi, to_north, to_south = pl.pallas_call(
        phi_kernel,
        out_shape=[jax.ShapeDtypeStruct((layers, rows, cols), f32)] + [block] * 2,
        in_specs=[anywhere, vmem, vmem, vmem],
        out_specs=[vmem] * 3,
        scratch_shapes=[VMEM((19, 2, rows, cols), f32), pltpu.SemaphoreType.DMA((2,))],
        compiler_params=params(8 << 20),
        name="phi_all",
    )(momentum_dist, order_dist, top, bottom)
    south_msg = hop_y(jnp.concatenate([fall, to_north], 0), 1)
    north_msg = hop_y(jnp.concatenate([rise, to_south], 0), -1)

    ten = jax.ShapeDtypeStruct((10, rows, cols), f32)
    mate, direct, across, joint, minus, plus = pl.pallas_call(
        functools.partial(face_kernel, (count_x, count_y)),
        out_shape=[ten] * 4 + [plane] * 2,
        in_specs=[smem] + [vmem] * 7,
        out_specs=[vmem] * 6,
        scratch_shapes=[
            VMEM((rows + 16, cols), f32),
            VMEM((rows + 16, cols), f32),
            VMEM((cols // LANES, 2 * rows + 16, LANES), f32),
            VMEM((rows + 16, cols), f32),
            VMEM((10, rows, cols), f32),
            VMEM((11, 8, cols), f32),
            VMEM((2, 8, cols), f32),
            VMEM((cols // LANES, rows + 16, LANES), f32),
            VMEM((cols // LANES, 3 * rows + 16, LANES), f32),
        ],
        compiler_params=params(24 << 20),
        name="x_faces",
    )(offsets, momentum_dist, order_dist, phi, rise, fall, south_msg, north_msg)

    mate = hop(mate, lambda x, y: (x, y ^ 1))
    direct = hop_parity(direct, True, 0)

    side = jax.ShapeDtypeStruct((10, layers, cols), f32)
    around = (phi, minus, plus, south_msg, north_msg)
    to_north, to_south = pl.pallas_call(
        rim_kernel,
        out_shape=[side] * 2,
        in_specs=[vmem] * 7,
        out_specs=[vmem] * 2,
        scratch_shapes=[VMEM((layers + 16, cols), f32)],
        compiler_params=params(24 << 20),
        name="y_rims",
    )(momentum_dist, order_dist, *around)
    south_rim, north_rim = hop_y(to_north, 1), hop_y(to_south, -1)
    across = hop_parity(across, False, 1)
    joint = joint + mate
    after = joint
    joint = hop_parity(joint, False, 0)

    whole = jax.ShapeDtypeStruct(momentum_dist.shape, f32)
    next_f, next_g = pl.pallas_call(
        bulk_kernel,
        out_shape=[whole, whole],
        in_specs=[anywhere] + [vmem] * 9,
        out_specs=[vmem] * 2,
        scratch_shapes=[
            VMEM((layers + 2, rows, cols), f32),
            VMEM((rows + 16, cols), f32),
        ],
        compiler_params=params(48 << 20),
        name="bulk",
    )(after, momentum_dist, order_dist, *around, south_rim, north_rim)

    return pl.pallas_call(
        face_fill_kernel,
        out_shape=[whole, whole],
        in_specs=[vmem] * 3 + [anywhere, anywhere],
        out_specs=[anywhere, anywhere],
        scratch_shapes=[
            VMEM((10, rows, cols), f32),
            VMEM((10, rows, cols), f32),
            pltpu.SemaphoreType.DMA((2, 10)),
        ],
        input_output_aliases={3: 0, 4: 1},
        compiler_params=params(24 << 20),
        name="x_fill",
    )(direct, across, joint, next_f, next_g)


def solution(mesh):
    return jax.shard_map(
        on_device,
        mesh=mesh,
        in_specs=(P(None, "gx", "gy", None), P(None, "gx", "gy", None), P()),
        out_specs=(P(None, "gx", "gy", None), P(None, "gx", "gy", None)),
        check_vma=False,
    )
```

```python
import functools

import jax
import jax.numpy as jnp
from jax import lax
from jax.experimental import pallas as pl
from jax.experimental.pallas import tpu as pltpu
from jax.sharding import PartitionSpec as P

lattice_velocity = [
    (0, 0, 0),
    (1, 0, 0),
    (-1, 0, 0),
    (0, 1, 0),
    (0, -1, 0),
    (0, 0, 1),
    (0, 0, -1),
    (1, 1, 0),
    (-1, -1, 0),
    (1, -1, 0),
    (-1, 1, 0),
    (1, 0, 1),
    (-1, 0, -1),
    (1, 0, -1),
    (-1, 0, 1),
    (0, 1, 1),
    (0, -1, -1),
    (0, 1, -1),
    (0, -1, 1),
]
lattice_weight = [1.0 / 3.0] + [1.0 / 18.0] * 6 + [1.0 / 36.0] * 12
plane_speed = 0.04
rising = [1, 7, 9, 11, 13]
falling = [2, 8, 10, 12, 14]
north_going = [i for i in range(19) if lattice_velocity[i][1] == 1]
south_going = [i for i in range(19) if lattice_velocity[i][1] == -1]
f32 = jnp.float32
VMEM = pltpu.VMEM
LANES = 128


def z_moved(value, step):
    if step == 0:
        return value
    return pltpu.roll(value, step % value.shape[-1], value.ndim - 1)


def spec_of(space):
    return pl.BlockSpec(memory_space=space)


def params(limit):
    return pltpu.CompilerParams(vmem_limit_bytes=limit)


def along(parts, c):
    total = None
    for sign, part in zip(c, parts):
        if sign == 0:
            continue
        if total is None:
            total = part if sign > 0 else -part
        else:
            total = total + part if sign > 0 else total - part
    return total


def signed_sum(load, axis):
    ups = [i for i in range(19) if lattice_velocity[i][axis] == 1]
    downs = [i for i in range(19) if lattice_velocity[i][axis] == -1]
    total = load(ups[0]) - load(downs[0])
    for i, j in zip(ups[1:], downs[1:]):
        total = total + (load(i) - load(j))
    return total


def moments_of(load):
    rho = load(0)
    for i in range(1, 19):
        rho = rho + load(i)
    return [rho] + [signed_sum(load, axis) for axis in range(3)]


class Site:
    def __init__(self, moments, phi, minus, plus, south, north):
        rho, momentum = moments[0], moments[1:]
        lower, upper = z_moved(phi, 1), z_moved(phi, -1)
        lap = (plus + minus) + (north + south) + (upper + lower) - 6.0 * phi
        mu = phi * (0.0625 * (phi * phi) - 0.0625) - 0.04 * lap
        half_mu = 0.5 * mu
        force = [half_mu * (plus - minus), half_mu * (north - south), half_mu * (upper - lower)]
        inverse = 1.0 / rho
        u = [(j + 0.5 * k) * inverse for j, k in zip(momentum, force)]
        uu = u[0] * u[0] + u[1] * u[1] + u[2] * u[2]
        uf = u[0] * force[0] + u[1] * force[1] + u[2] * force[2]
        self.rho, self.phi, self.mu, self.u, self.force, self.uu = rho, phi, mu, u, force, uu
        self.r = 1.25 * rho
        self.k = self.r * (1.0 - 1.5 * uu) - 1.125 * uf
        self.g_scale = phi * (1.0 / 0.9)
        self.g_base = (3.0 / 0.9) * mu - 1.5 * (self.g_scale * uu)

    def pair_f(self, i):
        p, q = along(self.u, lattice_velocity[i]), along(self.force, lattice_velocity[i])
        w = lattice_weight[i]
        rp = self.r * p
        even = w * (self.k + p * (4.5 * rp + 3.375 * q))
        odd = (3.0 * w) * rp + (1.125 * w) * q
        return even, odd

    def pair_g(self, i):
        p = along(self.u, lattice_velocity[i])
        w = lattice_weight[i]
        gp = self.g_scale * p
        return w * (self.g_base + 4.5 * (gp * p)), (3.0 * w) * gp

    def jump(self, i, delta):
        cy = lattice_velocity[i][1]
        uy = self.u[1]
        if cy == 0:
            return delta * (-3.0 * uy) - (1.5 * delta * delta)
        p = along(self.u, lattice_velocity[i])
        return delta * (3.0 * cy + (9.0 * cy) * p - 3.0 * uy) + (3.0 * delta * delta)


class Shear:
    def __init__(self, raw, wide, rows):
        self.raw, self.wide, self.rows = raw, wide, rows

    def clear(self):
        self.raw[...] = jnp.zeros_like(self.raw)
        self.wide[...] = jnp.zeros_like(self.wide)

    def put(self, value, up, near, far):
        n = self.rows
        for k in range(self.raw.shape[0]):
            self.raw[k, 8 : 8 + n] = value[:, LANES * k : LANES * k + LANES]
        for k in range(self.raw.shape[0]):
            if up:
                self.wide[k, n : n + n + 8] = (
                    near * self.raw[k, 0 : n + 8] + far * self.raw[k, 1 : n + 9]
                )
            else:
                self.wide[k, n + 8 : n + n + 16] = (
                    near * self.raw[k, 7 : n + 15] + far * self.raw[k, 8 : n + 16]
                )

    def add_row(self, at, row):
        for k in range(self.raw.shape[0]):
            lanes = slice(LANES * k, LANES * k + LANES)
            self.wide[k, at : at + 1] = self.wide[k, at : at + 1] + row[:, lanes]

    def take(self, up, block, rest, cy, ref, j):
        n = self.rows
        if up:
            start = (n + 8 if block == 0 else 8) + rest - cy
        else:
            start = (n + 8 if block == 0 else n + n + 8) - rest - cy
        for k in range(self.raw.shape[0]):
            ref[j, 0:n, LANES * k : LANES * k + LANES] = self.wide[k, pl.ds(start, n)]


class Planes:
    def __init__(self, offsets, rows, sizes):
        count_x, count_y = sizes
        per_plane, half = count_x // 4, count_y // 2
        a = lax.axis_index("gx")
        self.odd = lax.rem(lax.axis_index("gy"), 2) == 1

        def plane_of(column):
            is_plane = lax.rem(column, per_plane) == 0
            plane = lax.rem(lax.div(column, per_plane), 4)
            rest = jnp.where(is_plane, jnp.clip(offsets[plane] - half * rows, 0, rows - 1), 0)
            return is_plane, (2.0 * plane.astype(f32) + 1.0) * 0.125, rest

        up_is, up_part, self.up_rest = plane_of(lax.rem(a + 1, count_x))
        low_is, low_part, self.low_rest = plane_of(a)
        self.up_near = jnp.where(up_is, 1.0 - up_part, 1.0)
        self.up_far = jnp.where(up_is, up_part, 0.0)
        self.low_near = jnp.where(low_is, low_part, 0.0)
        self.low_far = jnp.where(low_is, 1.0 - low_part, 1.0)
        self.up_jump = jnp.where(up_is, -plane_speed, 0.0)
        self.low_jump = jnp.where(low_is, plane_speed, 0.0)


def order_sum(load):
    total = load(0)
    for i in range(1, 19):
        total = total + load(i)
    return total


def phi_kernel(f_ref, g_ref, top, bottom, phi_ref, to_north, to_south, fbuf, gbuf, sems):
    layers, rows = phi_ref.shape[0], phi_ref.shape[1]
    faces = (layers - 1, 0)
    f_copies = [
        pltpu.make_async_copy(f_ref.at[:, x], fbuf.at[:, s], sems.at[layers + s])
        for s, x in enumerate(faces)
    ]
    g_copies = [
        pltpu.make_async_copy(g_ref.at[:, x], gbuf.at[:, x], sems.at[x]) for x in range(layers)
    ]
    for copy in f_copies + g_copies:
        copy.start()
    phi_ref[layers - 1] = top[...]
    phi_ref[0] = bottom[...]
    edges = ((to_north, rows - 1, rows - 2, (7, 10)), (to_south, 0, 1, (9, 8)))
    for s, x in enumerate(faces):
        f_copies[s].wait()
        for out, edge, inner, chosen in edges:
            out[layers + s : layers + s + 1] = phi_ref[x, inner : inner + 1]
            at = layers + 2 + 6 * s
            out[at : at + 1] = fbuf[chosen[s], s, edge : edge + 1]
            for k, part in enumerate(moments_of(lambda i: fbuf[i, s, edge : edge + 1])):
                out[at + 2 + k : at + 3 + k] = part
    for x in range(layers):
        g_copies[x].wait()
        if 0 < x < layers - 1:
            phi_ref[x] = order_sum(lambda i: gbuf[i, x])
        to_north[x : x + 1] = phi_ref[x, rows - 1 : rows]
        to_south[x : x + 1] = phi_ref[x, 0:1]
    for s, x in enumerate(faces):
        for out, edge, inner, chosen in edges:
            at = layers + 3 + 6 * s
            out[at : at + 1] = gbuf[chosen[s], x, edge : edge + 1]
    for out in (to_north, to_south):
        out[layers + 14 : layers + 16] = jnp.zeros((2, out.shape[1]), f32)


def with_halo(ref, layer, below, above):
    rows = layer.shape[0]
    ref[8 : 8 + rows] = layer
    ref[7:8] = below
    ref[8 + rows : 9 + rows] = above


def corner_values(cells, planes, phi_ref, south_msg, north_msg, minus_wide, plus_wide):
    layers, rows, cols = phi_ref.shape
    cells[...] = jnp.ones_like(cells)
    for row in range(4):
        msg = south_msg if row < 2 else north_msg
        x = layers - 1 if row % 2 == 0 else 0
        beside = rows + (layers - 2 if row % 2 == 0 else 1)
        wide_row = 7 if row < 2 else rows + 8
        at = rows + layers
        first = at + 2 + 6 * (row % 2)
        far_phi = msg[at + row % 2 : at + row % 2 + 1]
        own_phi = phi_ref[x, 0:1] if row < 2 else phi_ref[x, rows - 1 : rows]
        parts = [msg[first + k : first + k + 1] for k in range(6)]
        parts.append(msg[rows + x : rows + x + 1])
        if row % 2 == 0:
            parts += [msg[beside : beside + 1], plus_wide[wide_row : wide_row + 1]]
        else:
            parts += [minus_wide[wide_row : wide_row + 1], msg[beside : beside + 1]]
        parts += [far_phi, own_phi] if row < 2 else [own_phi, far_phi]
        for k, part in enumerate(parts):
            cells[k, row : row + 1] = part
    place = lax.broadcasted_iota(jnp.int32, (8, cols), 0)
    is_top = (place == 0) | (place == 2)
    sx = jnp.where(is_top, 1.0, -1.0)
    sy = jnp.where(place < 2, 1.0, -1.0)
    delta = jnp.where(is_top, planes.up_jump, planes.low_jump)
    site = Site([cells[k] for k in range(2, 6)], *[cells[k] for k in range(6, 11)])
    w = lattice_weight[7]
    p = sx * site.u[0] + sy * site.u[1]
    q = sx * site.force[0] + sy * site.force[1]
    change = delta * (3.0 * sy + 9.0 * (sy * p) - 3.0 * site.u[1]) + 3.0 * (delta * delta)
    rp, gp = site.r * p, site.g_scale * p
    f_post = w * (site.k + p * (4.5 * rp + 3.375 * q) + 3.0 * rp + 1.125 * q + site.rho * change)
    g_post = w * (site.g_base + 4.5 * (gp * p) + 3.0 * gp + site.phi * change)
    return f_post - 0.25 * cells[0], g_post - (1.0 / 9.0) * cells[1]


def rim_values(f_ref, g_ref, phi_ref, minus, plus, south_msg, north_msg, line, edge, chosen, store):
    layers, rows, cols = phi_ref.shape
    phi = phi_ref[:, edge, :]
    with_halo(line, phi, minus[edge : edge + 1], plus[edge : edge + 1])
    if edge == 0:
        below, above = south_msg[rows : rows + layers], phi_ref[:, 1, :]
    else:
        below, above = phi_ref[:, rows - 2, :], north_msg[rows : rows + layers]
    site = Site(
        moments_of(lambda i: f_ref[i, :, edge, :]),
        phi,
        line[7 : 7 + layers],
        line[9 : 9 + layers],
        below,
        above,
    )
    for j, i in enumerate(chosen):
        cz = lattice_velocity[i][2]
        even, odd = site.pair_f(i)
        store(j, z_moved(even + odd - 0.25 * f_ref[i, :, edge, :], cz))
        even, odd = site.pair_g(i)
        store(5 + j, z_moved(even + odd - (1.0 / 9.0) * g_ref[i, :, edge, :], cz))


def face_kernel(
    sizes,
    offsets,
    f_ref,
    g_ref,
    phi_ref,
    rise,
    fall,
    south_msg,
    north_msg,
    mate,
    direct,
    across,
    joint,
    cross,
    minus_out,
    plus_out,
    minus_wide,
    plus_wide,
    window,
    halo,
    line,
    post,
    cells,
    corners,
    raw,
    wide,
):
    layers, rows, cols = phi_ref.shape
    planes = Planes(offsets, rows, sizes)
    shear = Shear(raw, wide, rows)
    window[...] = jnp.zeros_like(window)
    for up in (True, False):
        if up:
            first, second = rise, north_msg
            near, far, start = planes.low_far, planes.low_near, planes.low_rest
        else:
            first, second = south_msg, fall
            near, far, start = planes.up_far, planes.up_near, rows - 1 - planes.up_rest
        target = minus_wide if up else plus_wide
        for k in range(window.shape[0]):
            lanes = slice(LANES * k, LANES * k + LANES)
            window[k, 8 : 8 + rows] = first[0:rows, lanes]
            window[k, 8 + rows : 8 + 2 * rows] = second[0:rows, lanes]
            target[:, lanes] = (
                near * window[k, pl.ds(start, rows + 16)]
                + far * window[k, pl.ds(start + 1, rows + 16)]
            )
    minus_out[...] = minus_wide[8 : 8 + rows]
    plus_out[...] = plus_wide[8 : 8 + rows]
    corners[0], corners[1] = corner_values(
        cells, planes, phi_ref, south_msg, north_msg, minus_wide, plus_wide
    )
    for edge, chosen in ((rows - 1, north_going), (0, south_going)):
        to_mate = planes.odd if edge == 0 else jnp.logical_not(planes.odd)

        def store(slot, value):
            @pl.when(to_mate)
            def _():
                mate[slot, rows : rows + layers] = value

            @pl.when(jnp.logical_not(to_mate))
            def _():
                cross[slot] = value

        rim_values(
            f_ref,
            g_ref,
            phi_ref,
            minus_out,
            plus_out,
            south_msg,
            north_msg,
            line,
            edge,
            chosen,
            store,
        )
    for up in (True, False):
        x = layers - 1 if up else 0
        with_halo(
            halo, phi_ref[x], south_msg[rows + x : rows + x + 1], north_msg[rows + x : rows + x + 1]
        )
        if up:
            near, far, rest, delta = planes.up_near, planes.up_far, planes.up_rest, planes.up_jump
        else:
            near, far, rest, delta = planes.low_near, planes.low_far, planes.low_rest, planes.low_jump
        for h in range(0, rows, 8):
            span = slice(h, h + 8)
            phi_h = phi_ref[x, span]
            if up:
                minus, plus = phi_ref[x - 1, span], plus_wide[8 + h : 16 + h]
            else:
                minus, plus = minus_wide[8 + h : 16 + h], phi_ref[x + 1, span]
            site = Site(
                moments_of(lambda i: f_ref[i, x, span]),
                phi_h,
                minus,
                plus,
                halo[7 + h : 15 + h],
                halo[9 + h : 17 + h],
            )
            for j in range(5):
                i = rising[j] if up else falling[j]
                cz = lattice_velocity[i][2]
                change = lattice_weight[i] * site.jump(i, delta)
                even, odd = site.pair_f(i)
                value = even + odd - 0.25 * f_ref[i, x, span] + site.rho * change
                post[j, span] = z_moved(value, cz)
                even, odd = site.pair_g(i)
                value = even + odd - (1.0 / 9.0) * g_ref[i, x, span] + phi_h * change
                post[5 + j, span] = z_moved(value, cz)
        shear.clear()
        for j in range(10):
            cy = lattice_velocity[(rising if up else falling)[j % 5]][1]
            shear.put(post[j], up, near, far)
            corner = (0 if up else 1) + (0 if cy == 1 else 2)
            if cy == 1:
                gate = jnp.where(rest == (0 if up else rows - 1), near, 0.0)
                at = rows + 7 if up else rows + 8
            if cy == -1:
                gate = jnp.where(rest == (rows - 1 if up else 0), far, 0.0)
                at = 2 * rows + 7 if up else 2 * rows + 8
            if cy != 0:
                shear.add_row(at, gate * corners[j // 5, corner : corner + 1])

            @pl.when(planes.odd)
            def _():
                shear.take(up, 0, rest, cy, direct if up else joint, j)
                shear.take(up, 1, rest, cy, mate if up else across, j)

            @pl.when(jnp.logical_not(planes.odd))
            def _():
                shear.take(up, 0, rest, cy, joint if up else direct, j)
                shear.take(up, 1, rest, cy, across if up else mate, j)


def bulk_kernel(
    after,
    f_ref,
    g_ref,
    phi_ref,
    minus,
    plus,
    south_msg,
    north_msg,
    mate_rim,
    cross_rim,
    next_f,
    next_g,
    wide_phi,
    halo,
):
    layers, rows, cols = phi_ref.shape
    is_odd = lax.rem(lax.axis_index("gy"), 2) == 1
    wide_phi[0] = minus[...]
    wide_phi[layers + 1] = plus[...]
    for x in range(layers):
        wide_phi[x + 1] = phi_ref[x]

    def layer(x, carry):
        with_halo(halo, phi_ref[x], south_msg[pl.ds(rows + x, 1)], north_msg[pl.ds(rows + x, 1)])
        beyond = lax.rem(x + 1, layers)
        before = lax.rem(x + layers - 1, layers)
        for h in range(0, rows, 8):
            span = slice(h, h + 8)
            phi_h = phi_ref[x, span]
            site = Site(
                moments_of(lambda i: f_ref[i, x, span]),
                phi_h,
                wide_phi[x, span],
                wide_phi[x + 2, span],
                halo[7 + h : 15 + h],
                halo[9 + h : 17 + h],
            )

            def emit(out, slot, i, value):
                cx, cy, cz = lattice_velocity[i]
                value = z_moved(value, cz)
                at = beyond if cx == 1 else before if cx == -1 else x
                if cy == 0:
                    out[i, at, span] = value
                elif cy == 1:
                    if h == 0:
                        rim = slot * 5 + north_going.index(i)
                        out[i, at, 0:1] = jnp.where(
                            is_odd, mate_rim[rim, pl.ds(rows + x, 1)], cross_rim[rim, pl.ds(x, 1)]
                        )
                    if h + 8 < rows:
                        out[i, at, h + 1 : h + 9] = value
                    else:
                        out[i, at, h + 1 : h + 8] = value[0:7]
                else:
                    if h + 8 == rows:
                        rim = slot * 5 + south_going.index(i)
                        out[i, at, rows - 1 : rows] = jnp.where(
                            is_odd, cross_rim[rim, pl.ds(x, 1)], mate_rim[rim, pl.ds(rows + x, 1)]
                        )
                    if h > 0:
                        out[i, at, h - 1 : h + 7] = value
                    else:
                        out[i, at, 0:7] = value[1:8]

            emit(next_f, 0, 0, lattice_weight[0] * site.k - 0.25 * f_ref[0, x, span])
            rest_g = (phi_h - 2.0 * site.mu - 0.5 * (phi_h * site.uu)) * (1.0 / 0.9)
            emit(next_g, 1, 0, rest_g - (1.0 / 9.0) * g_ref[0, x, span])
            for i in range(1, 19, 2):
                even, odd = site.pair_f(i)
                emit(next_f, 0, i, (even + odd) - 0.25 * f_ref[i, x, span])
                emit(next_f, 0, i + 1, (even - odd) - 0.25 * f_ref[i + 1, x, span])
                even, odd = site.pair_g(i)
                emit(next_g, 1, i, (even + odd) - (1.0 / 9.0) * g_ref[i, x, span])
                emit(next_g, 1, i + 1, (even - odd) - (1.0 / 9.0) * g_ref[i + 1, x, span])
        return carry

    lax.fori_loop(0, layers, layer, 0)


def face_fill_kernel(direct, across, joint, f_in, g_in, f_out, g_out, low, high, sems):
    layers = f_out.shape[1]
    odd = lax.rem(lax.axis_index("gy"), 2) == 1

    @pl.when(odd)
    def _():
        low[...] = direct[...] + across[...]
        high[...] = joint[...]

    @pl.when(jnp.logical_not(odd))
    def _():
        low[...] = joint[...]
        high[...] = direct[...] + across[...]

    copies = []
    for family, out in enumerate((f_out, g_out)):
        for j in range(5):
            slot = family * 5 + j
            for side, buf, chosen, x in ((0, low, rising, 0), (1, high, falling, layers - 1)):
                copy = pltpu.make_async_copy(
                    buf.at[slot], out.at[chosen[j], x], sems.at[side, slot]
                )
                copy.start()
                copies.append(copy)
    for copy in copies:
        copy.wait()


def on_device(momentum_dist, order_dist, offsets):
    layers, rows, cols = momentum_dist.shape[1:]
    count_x, count_y = lax.axis_size("gx"), lax.axis_size("gy")
    per_plane = count_x // 4
    half = count_y // 2

    def hop(value, target):
        perm = []
        for x in range(count_x):
            for y in range(count_y):
                tx, ty = target(x, y)
                perm.append((x * count_y + y, tx % count_x * count_y + ty % count_y))
        return lax.ppermute(value, ("gx", "gy"), perm)

    def base_up(x):
        return half if (x + 1) % per_plane == 0 else 0

    def base_low(x):
        return half if x % per_plane == 0 else 0

    def hop_parity(value, odd_up, extra):
        def target(x, y):
            if (y % 2 == 1) == odd_up:
                return (x + 1, y - base_up(x) - extra)
            return (x - 1, y + base_low(x) + extra)

        return hop(value, target)

    def hop_y(value, step):
        return hop(value, lambda x, y: (x, y + step))

    smem, vmem, anywhere = spec_of(pltpu.SMEM), spec_of(VMEM), spec_of(pl.ANY)
    plane = jax.ShapeDtypeStruct((rows, cols), f32)
    top, bottom = jnp.sum(order_dist[:, layers - 1], axis=0), jnp.sum(order_dist[:, 0], axis=0)
    rise = hop(top, lambda x, y: (x + 1, y - base_up(x)))
    fall = hop(bottom, lambda x, y: (x - 1, y + base_low(x)))

    block = jax.ShapeDtypeStruct((layers + 16, cols), f32)
    phi, to_north, to_south = pl.pallas_call(
        phi_kernel,
        out_shape=[jax.ShapeDtypeStruct((layers, rows, cols), f32)] + [block] * 2,
        in_specs=[anywhere, anywhere, vmem, vmem],
        out_specs=[vmem] * 3,
        scratch_shapes=[
            VMEM((19, 2, rows, cols), f32),
            VMEM((19, layers, rows, cols), f32),
            pltpu.SemaphoreType.DMA((layers + 2,)),
        ],
        compiler_params=params(52 << 20),
        name="phi_all",
    )(momentum_dist, order_dist, top, bottom)
    south_msg = hop_y(jnp.concatenate([fall, to_north], 0), 1)
    north_msg = hop_y(jnp.concatenate([rise, to_south], 0), -1)

    ten = jax.ShapeDtypeStruct((10, rows, cols), f32)
    side = jax.ShapeDtypeStruct((10, layers, cols), f32)
    ten_side = jax.ShapeDtypeStruct((10, rows + layers, cols), f32)
    mate, direct, across, joint, cross, minus, plus = pl.pallas_call(
        functools.partial(face_kernel, (count_x, count_y)),
        out_shape=[ten_side] + [ten] * 3 + [side] + [plane] * 2,
        in_specs=[smem] + [vmem] * 7,
        out_specs=[vmem] * 7,
        scratch_shapes=[
            VMEM((rows + 16, cols), f32),
            VMEM((rows + 16, cols), f32),
            VMEM((cols // LANES, 2 * rows + 16, LANES), f32),
            VMEM((rows + 16, cols), f32),
            VMEM((layers + 16, cols), f32),
            VMEM((10, rows, cols), f32),
            VMEM((11, 8, cols), f32),
            VMEM((2, 8, cols), f32),
            VMEM((cols // LANES, rows + 16, LANES), f32),
            VMEM((cols // LANES, 3 * rows + 16, LANES), f32),
        ],
        compiler_params=params(24 << 20),
        name="faces",
    )(offsets, momentum_dist, order_dist, phi, rise, fall, south_msg, north_msg)

    mate = hop(mate, lambda x, y: (x, y ^ 1))
    cross = hop(cross, lambda x, y: (x, y + 1 if y % 2 == 1 else y - 1))
    direct = hop_parity(direct, True, 0)
    across = hop_parity(across, False, 1)
    joint, cross = lax.optimization_barrier((joint + mate[:, :rows], cross))
    after = joint
    joint = hop_parity(joint, False, 0)
    around = (phi, minus, plus, south_msg, north_msg)

    whole = jax.ShapeDtypeStruct(momentum_dist.shape, f32)
    next_f, next_g = pl.pallas_call(
        bulk_kernel,
        out_shape=[whole, whole],
        in_specs=[anywhere] + [vmem] * 9,
        out_specs=[vmem] * 2,
        scratch_shapes=[
            VMEM((layers + 2, rows, cols), f32),
            VMEM((rows + 16, cols), f32),
        ],
        compiler_params=params(48 << 20),
        name="bulk",
    )(after, momentum_dist, order_dist, *around, mate, cross)

    return pl.pallas_call(
        face_fill_kernel,
        out_shape=[whole, whole],
        in_specs=[vmem] * 3 + [anywhere, anywhere],
        out_specs=[anywhere, anywhere],
        scratch_shapes=[
            VMEM((10, rows, cols), f32),
            VMEM((10, rows, cols), f32),
            pltpu.SemaphoreType.DMA((2, 10)),
        ],
        input_output_aliases={3: 0, 4: 1},
        compiler_params=params(24 << 20),
        name="x_fill",
    )(direct, across, joint, next_f, next_g)


def solution(mesh):
    return jax.shard_map(
        on_device,
        mesh=mesh,
        in_specs=(P(None, "gx", "gy", None), P(None, "gx", "gy", None), P()),
        out_specs=(P(None, "gx", "gy", None), P(None, "gx", "gy", None)),
        check_vma=False,
    )
```

```python
import functools

import jax
import jax.numpy as jnp
from jax import lax
from jax.experimental import pallas as pl
from jax.experimental.pallas import tpu as pltpu
from jax.sharding import PartitionSpec as P

lattice_velocity = [
    (0, 0, 0),
    (1, 0, 0),
    (-1, 0, 0),
    (0, 1, 0),
    (0, -1, 0),
    (0, 0, 1),
    (0, 0, -1),
    (1, 1, 0),
    (-1, -1, 0),
    (1, -1, 0),
    (-1, 1, 0),
    (1, 0, 1),
    (-1, 0, -1),
    (1, 0, -1),
    (-1, 0, 1),
    (0, 1, 1),
    (0, -1, -1),
    (0, 1, -1),
    (0, -1, 1),
]
lattice_weight = [1.0 / 3.0] + [1.0 / 18.0] * 6 + [1.0 / 36.0] * 12
plane_speed = 0.04
rising = [1, 7, 9, 11, 13]
falling = [2, 8, 10, 12, 14]
north_going = [i for i in range(19) if lattice_velocity[i][1] == 1]
south_going = [i for i in range(19) if lattice_velocity[i][1] == -1]
f32 = jnp.float32
VMEM = pltpu.VMEM
LANES = 128


def z_moved(value, step):
    if step == 0:
        return value
    return pltpu.roll(value, step % value.shape[-1], value.ndim - 1)


def spec_of(space):
    return pl.BlockSpec(memory_space=space)


def params(limit):
    return pltpu.CompilerParams(vmem_limit_bytes=limit)


def along(parts, c):
    total = None
    for sign, part in zip(c, parts):
        if sign == 0:
            continue
        if total is None:
            total = part if sign > 0 else -part
        else:
            total = total + part if sign > 0 else total - part
    return total


def signed_sum(load, axis):
    ups = [i for i in range(19) if lattice_velocity[i][axis] == 1]
    downs = [i for i in range(19) if lattice_velocity[i][axis] == -1]
    total = load(ups[0]) - load(downs[0])
    for i, j in zip(ups[1:], downs[1:]):
        total = total + (load(i) - load(j))
    return total


def moments_of(load):
    rho = load(0)
    for i in range(1, 19):
        rho = rho + load(i)
    return [rho] + [signed_sum(load, axis) for axis in range(3)]


class Site:
    def __init__(self, moments, phi, minus, plus, south, north):
        rho, momentum = moments[0], moments[1:]
        lower, upper = z_moved(phi, 1), z_moved(phi, -1)
        lap = (plus + minus) + (north + south) + (upper + lower) - 6.0 * phi
        mu = phi * (0.0625 * (phi * phi) - 0.0625) - 0.04 * lap
        half_mu = 0.5 * mu
        force = [half_mu * (plus - minus), half_mu * (north - south), half_mu * (upper - lower)]
        inverse = 1.0 / rho
        u = [(j + 0.5 * k) * inverse for j, k in zip(momentum, force)]
        uu = u[0] * u[0] + u[1] * u[1] + u[2] * u[2]
        uf = u[0] * force[0] + u[1] * force[1] + u[2] * force[2]
        self.rho, self.phi, self.mu, self.u, self.force, self.uu = rho, phi, mu, u, force, uu
        self.r = 1.25 * rho
        self.k = self.r * (1.0 - 1.5 * uu) - 1.125 * uf
        self.g_scale = phi * (1.0 / 0.9)
        self.g_base = (3.0 / 0.9) * mu - 1.5 * (self.g_scale * uu)

    def pair_f(self, i):
        p, q = along(self.u, lattice_velocity[i]), along(self.force, lattice_velocity[i])
        w = lattice_weight[i]
        rp = self.r * p
        even = w * (self.k + p * (4.5 * rp + 3.375 * q))
        odd = (3.0 * w) * rp + (1.125 * w) * q
        return even, odd

    def pair_g(self, i):
        p = along(self.u, lattice_velocity[i])
        w = lattice_weight[i]
        gp = self.g_scale * p
        return w * (self.g_base + 4.5 * (gp * p)), (3.0 * w) * gp

    def jump(self, i, delta):
        cy = lattice_velocity[i][1]
        uy = self.u[1]
        if cy == 0:
            return delta * (-3.0 * uy) - (1.5 * delta * delta)
        p = along(self.u, lattice_velocity[i])
        return delta * (3.0 * cy + (9.0 * cy) * p - 3.0 * uy) + (3.0 * delta * delta)


class Shear:
    def __init__(self, raw, wide, rows):
        self.raw, self.wide, self.rows = raw, wide, rows

    def clear(self):
        self.raw[...] = jnp.zeros_like(self.raw)
        self.wide[...] = jnp.zeros_like(self.wide)

    def put(self, value, up, near, far):
        n = self.rows
        for k in range(self.raw.shape[0]):
            self.raw[k, 8 : 8 + n] = value[:, LANES * k : LANES * k + LANES]
        for k in range(self.raw.shape[0]):
            if up:
                self.wide[k, n : n + n + 8] = (
                    near * self.raw[k, 0 : n + 8] + far * self.raw[k, 1 : n + 9]
                )
            else:
                self.wide[k, n + 8 : n + n + 16] = (
                    near * self.raw[k, 7 : n + 15] + far * self.raw[k, 8 : n + 16]
                )

    def add_row(self, at, row):
        for k in range(self.raw.shape[0]):
            lanes = slice(LANES * k, LANES * k + LANES)
            self.wide[k, at : at + 1] = self.wide[k, at : at + 1] + row[:, lanes]

    def take(self, up, block, rest, cy, ref, j):
        n = self.rows
        if up:
            start = (n + 8 if block == 0 else 8) + rest - cy
        else:
            start = (n + 8 if block == 0 else n + n + 8) - rest - cy
        for k in range(self.raw.shape[0]):
            ref[j, 0:n, LANES * k : LANES * k + LANES] = self.wide[k, pl.ds(start, n)]


class Planes:
    def __init__(self, offsets, rows, sizes):
        count_x, count_y = sizes
        per_plane, half = count_x // 4, count_y // 2
        a = lax.axis_index("gx")
        self.odd = lax.rem(lax.axis_index("gy"), 2) == 1

        def plane_of(column):
            is_plane = lax.rem(column, per_plane) == 0
            plane = lax.rem(lax.div(column, per_plane), 4)
            rest = jnp.where(is_plane, jnp.clip(offsets[plane] - half * rows, 0, rows - 1), 0)
            return is_plane, (2.0 * plane.astype(f32) + 1.0) * 0.125, rest

        up_is, up_part, self.up_rest = plane_of(lax.rem(a + 1, count_x))
        low_is, low_part, self.low_rest = plane_of(a)
        self.up_near = jnp.where(up_is, 1.0 - up_part, 1.0)
        self.up_far = jnp.where(up_is, up_part, 0.0)
        self.low_near = jnp.where(low_is, low_part, 0.0)
        self.low_far = jnp.where(low_is, 1.0 - low_part, 1.0)
        self.up_jump = jnp.where(up_is, -plane_speed, 0.0)
        self.low_jump = jnp.where(low_is, plane_speed, 0.0)


def order_sum(load):
    total = load(0)
    for i in range(1, 19):
        total = total + load(i)
    return total


def phi_kernel(f_ref, g_ref, top, bottom, phi_ref, to_north, to_south, fbuf, gbuf, sems):
    layers, rows = phi_ref.shape[0], phi_ref.shape[1]
    faces = (layers - 1, 0)
    f_copies = [
        pltpu.make_async_copy(f_ref.at[:, x], fbuf.at[:, s], sems.at[layers + s])
        for s, x in enumerate(faces)
    ]
    g_copies = [
        pltpu.make_async_copy(g_ref.at[:, x], gbuf.at[:, x], sems.at[x]) for x in range(layers)
    ]
    for copy in f_copies + g_copies:
        copy.start()
    phi_ref[layers - 1] = top[...]
    phi_ref[0] = bottom[...]
    edges = ((to_north, rows - 1, rows - 2, (7, 10)), (to_south, 0, 1, (9, 8)))
    for s, x in enumerate(faces):
        f_copies[s].wait()
        for out, edge, inner, chosen in edges:
            out[layers + s : layers + s + 1] = phi_ref[x, inner : inner + 1]
            at = layers + 2 + 6 * s
            out[at : at + 1] = fbuf[chosen[s], s, edge : edge + 1]
            for k, part in enumerate(moments_of(lambda i: fbuf[i, s, edge : edge + 1])):
                out[at + 2 + k : at + 3 + k] = part
    for x in range(layers):
        g_copies[x].wait()
        if 0 < x < layers - 1:
            phi_ref[x] = order_sum(lambda i: gbuf[i, x])
        to_north[x : x + 1] = phi_ref[x, rows - 1 : rows]
        to_south[x : x + 1] = phi_ref[x, 0:1]
    for s, x in enumerate(faces):
        for out, edge, inner, chosen in edges:
            at = layers + 3 + 6 * s
            out[at : at + 1] = gbuf[chosen[s], x, edge : edge + 1]
    for out in (to_north, to_south):
        out[layers + 14 : layers + 16] = jnp.zeros((2, out.shape[1]), f32)


def with_halo(ref, layer, below, above):
    rows = layer.shape[0]
    ref[8 : 8 + rows] = layer
    ref[7:8] = below
    ref[8 + rows : 9 + rows] = above


def corner_values(cells, planes, phi_ref, south_msg, north_msg, minus_wide, plus_wide):
    layers, rows, cols = phi_ref.shape
    cells[...] = jnp.ones_like(cells)
    for row in range(4):
        msg = south_msg if row < 2 else north_msg
        x = layers - 1 if row % 2 == 0 else 0
        beside = rows + (layers - 2 if row % 2 == 0 else 1)
        wide_row = 7 if row < 2 else rows + 8
        at = rows + layers
        first = at + 2 + 6 * (row % 2)
        far_phi = msg[at + row % 2 : at + row % 2 + 1]
        own_phi = phi_ref[x, 0:1] if row < 2 else phi_ref[x, rows - 1 : rows]
        parts = [msg[first + k : first + k + 1] for k in range(6)]
        parts.append(msg[rows + x : rows + x + 1])
        if row % 2 == 0:
            parts += [msg[beside : beside + 1], plus_wide[wide_row : wide_row + 1]]
        else:
            parts += [minus_wide[wide_row : wide_row + 1], msg[beside : beside + 1]]
        parts += [far_phi, own_phi] if row < 2 else [own_phi, far_phi]
        for k, part in enumerate(parts):
            cells[k, row : row + 1] = part
    place = lax.broadcasted_iota(jnp.int32, (8, cols), 0)
    is_top = (place == 0) | (place == 2)
    sx = jnp.where(is_top, 1.0, -1.0)
    sy = jnp.where(place < 2, 1.0, -1.0)
    delta = jnp.where(is_top, planes.up_jump, planes.low_jump)
    site = Site([cells[k] for k in range(2, 6)], *[cells[k] for k in range(6, 11)])
    w = lattice_weight[7]
    p = sx * site.u[0] + sy * site.u[1]
    q = sx * site.force[0] + sy * site.force[1]
    change = delta * (3.0 * sy + 9.0 * (sy * p) - 3.0 * site.u[1]) + 3.0 * (delta * delta)
    rp, gp = site.r * p, site.g_scale * p
    f_post = w * (site.k + p * (4.5 * rp + 3.375 * q) + 3.0 * rp + 1.125 * q + site.rho * change)
    g_post = w * (site.g_base + 4.5 * (gp * p) + 3.0 * gp + site.phi * change)
    return f_post - 0.25 * cells[0], g_post - (1.0 / 9.0) * cells[1]


def moment_kernel(f_ref, g_ref, faces, rims):
    layers, rows = f_ref.shape[1], f_ref.shape[2]
    for s, x in enumerate((layers - 1, 0)):
        for k, part in enumerate(moments_of(lambda i: f_ref[i, x])):
            faces[s, k] = part
    for s, (edge, chosen) in enumerate(((rows - 1, north_going), (0, south_going))):
        for k, part in enumerate(moments_of(lambda i: f_ref[i, :, edge, :])):
            rims[s, k] = part
        for j, i in enumerate(chosen):
            rims[s, 4 + j] = f_ref[i, :, edge, :]
            rims[s, 9 + j] = g_ref[i, :, edge, :]


def rim_values(rims, s, phi_ref, minus, plus, south_msg, north_msg, line, edge, chosen, store):
    layers, rows, cols = phi_ref.shape
    phi = phi_ref[:, edge, :]
    with_halo(line, phi, minus[edge : edge + 1], plus[edge : edge + 1])
    if edge == 0:
        below, above = south_msg[rows : rows + layers], phi_ref[:, 1, :]
    else:
        below, above = phi_ref[:, rows - 2, :], north_msg[rows : rows + layers]
    site = Site(
        [rims[s, k] for k in range(4)],
        phi,
        line[7 : 7 + layers],
        line[9 : 9 + layers],
        below,
        above,
    )
    for j, i in enumerate(chosen):
        cz = lattice_velocity[i][2]
        even, odd = site.pair_f(i)
        store(j, z_moved(even + odd - 0.25 * rims[s, 4 + j], cz))
        even, odd = site.pair_g(i)
        store(5 + j, z_moved(even + odd - (1.0 / 9.0) * rims[s, 9 + j], cz))


def face_kernel(
    sizes,
    offsets,
    f_ref,
    g_ref,
    face_moments,
    rims,
    phi_ref,
    rise,
    fall,
    south_msg,
    north_msg,
    mate,
    direct,
    across,
    joint,
    cross,
    minus_out,
    plus_out,
    minus_wide,
    plus_wide,
    window,
    halo,
    line,
    post,
    cells,
    corners,
    raw,
    wide,
):
    layers, rows, cols = phi_ref.shape
    planes = Planes(offsets, rows, sizes)
    shear = Shear(raw, wide, rows)
    window[...] = jnp.zeros_like(window)
    for up in (True, False):
        if up:
            first, second = rise, north_msg
            near, far, start = planes.low_far, planes.low_near, planes.low_rest
        else:
            first, second = south_msg, fall
            near, far, start = planes.up_far, planes.up_near, rows - 1 - planes.up_rest
        target = minus_wide if up else plus_wide
        for k in range(window.shape[0]):
            lanes = slice(LANES * k, LANES * k + LANES)
            window[k, 8 : 8 + rows] = first[0:rows, lanes]
            window[k, 8 + rows : 8 + 2 * rows] = second[0:rows, lanes]
            target[:, lanes] = (
                near * window[k, pl.ds(start, rows + 16)]
                + far * window[k, pl.ds(start + 1, rows + 16)]
            )
    minus_out[...] = minus_wide[8 : 8 + rows]
    plus_out[...] = plus_wide[8 : 8 + rows]
    corners[0], corners[1] = corner_values(
        cells, planes, phi_ref, south_msg, north_msg, minus_wide, plus_wide
    )
    for s, (edge, chosen) in enumerate(((rows - 1, north_going), (0, south_going))):
        to_mate = planes.odd if edge == 0 else jnp.logical_not(planes.odd)

        def store(slot, value):
            @pl.when(to_mate)
            def _():
                mate[slot, rows : rows + layers] = value

            @pl.when(jnp.logical_not(to_mate))
            def _():
                cross[slot] = value

        rim_values(
            rims,
            s,
            phi_ref,
            minus_out,
            plus_out,
            south_msg,
            north_msg,
            line,
            edge,
            chosen,
            store,
        )
    for up in (True, False):
        x = layers - 1 if up else 0
        with_halo(
            halo, phi_ref[x], south_msg[rows + x : rows + x + 1], north_msg[rows + x : rows + x + 1]
        )
        if up:
            near, far, rest, delta = planes.up_near, planes.up_far, planes.up_rest, planes.up_jump
        else:
            near, far, rest, delta = planes.low_near, planes.low_far, planes.low_rest, planes.low_jump
        for h in range(0, rows, 8):
            span = slice(h, h + 8)
            phi_h = phi_ref[x, span]
            if up:
                minus, plus = phi_ref[x - 1, span], plus_wide[8 + h : 16 + h]
            else:
                minus, plus = minus_wide[8 + h : 16 + h], phi_ref[x + 1, span]
            site = Site(
                [face_moments[0 if up else 1, k, span] for k in range(4)],
                phi_h,
                minus,
                plus,
                halo[7 + h : 15 + h],
                halo[9 + h : 17 + h],
            )
            for j in range(5):
                i = rising[j] if up else falling[j]
                cz = lattice_velocity[i][2]
                change = lattice_weight[i] * site.jump(i, delta)
                even, odd = site.pair_f(i)
                value = even + odd - 0.25 * f_ref[i, x, span] + site.rho * change
                post[j, span] = z_moved(value, cz)
                even, odd = site.pair_g(i)
                value = even + odd - (1.0 / 9.0) * g_ref[i, x, span] + phi_h * change
                post[5 + j, span] = z_moved(value, cz)
        shear.clear()
        for j in range(10):
            cy = lattice_velocity[(rising if up else falling)[j % 5]][1]
            shear.put(post[j], up, near, far)
            corner = (0 if up else 1) + (0 if cy == 1 else 2)
            if cy == 1:
                gate = jnp.where(rest == (0 if up else rows - 1), near, 0.0)
                at = rows + 7 if up else rows + 8
            if cy == -1:
                gate = jnp.where(rest == (rows - 1 if up else 0), far, 0.0)
                at = 2 * rows + 7 if up else 2 * rows + 8
            if cy != 0:
                shear.add_row(at, gate * corners[j // 5, corner : corner + 1])

            @pl.when(planes.odd)
            def _():
                shear.take(up, 0, rest, cy, direct if up else joint, j)
                shear.take(up, 1, rest, cy, mate if up else across, j)

            @pl.when(jnp.logical_not(planes.odd))
            def _():
                shear.take(up, 0, rest, cy, joint if up else direct, j)
                shear.take(up, 1, rest, cy, across if up else mate, j)


def bulk_kernel(
    after,
    f_ref,
    g_ref,
    phi_ref,
    minus,
    plus,
    south_msg,
    north_msg,
    mate_rim,
    cross_rim,
    next_f,
    next_g,
    wide_phi,
    halo,
):
    layers, rows, cols = phi_ref.shape
    is_odd = lax.rem(lax.axis_index("gy"), 2) == 1
    wide_phi[0] = minus[...]
    wide_phi[layers + 1] = plus[...]
    for x in range(layers):
        wide_phi[x + 1] = phi_ref[x]

    def layer(x, carry):
        with_halo(halo, phi_ref[x], south_msg[pl.ds(rows + x, 1)], north_msg[pl.ds(rows + x, 1)])
        beyond = lax.rem(x + 1, layers)
        before = lax.rem(x + layers - 1, layers)
        for h in range(0, rows, 8):
            span = slice(h, h + 8)
            phi_h = phi_ref[x, span]
            site = Site(
                moments_of(lambda i: f_ref[i, x, span]),
                phi_h,
                wide_phi[x, span],
                wide_phi[x + 2, span],
                halo[7 + h : 15 + h],
                halo[9 + h : 17 + h],
            )

            def emit(out, slot, i, value):
                cx, cy, cz = lattice_velocity[i]
                value = z_moved(value, cz)
                at = beyond if cx == 1 else before if cx == -1 else x
                if cy == 0:
                    out[i, at, span] = value
                elif cy == 1:
                    if h == 0:
                        rim = slot * 5 + north_going.index(i)
                        out[i, at, 0:1] = jnp.where(
                            is_odd, mate_rim[rim, pl.ds(rows + x, 1)], cross_rim[rim, pl.ds(x, 1)]
                        )
                    if h + 8 < rows:
                        out[i, at, h + 1 : h + 9] = value
                    else:
                        out[i, at, h + 1 : h + 8] = value[0:7]
                else:
                    if h + 8 == rows:
                        rim = slot * 5 + south_going.index(i)
                        out[i, at, rows - 1 : rows] = jnp.where(
                            is_odd, cross_rim[rim, pl.ds(x, 1)], mate_rim[rim, pl.ds(rows + x, 1)]
                        )
                    if h > 0:
                        out[i, at, h - 1 : h + 7] = value
                    else:
                        out[i, at, 0:7] = value[1:8]

            emit(next_f, 0, 0, lattice_weight[0] * site.k - 0.25 * f_ref[0, x, span])
            rest_g = (phi_h - 2.0 * site.mu - 0.5 * (phi_h * site.uu)) * (1.0 / 0.9)
            emit(next_g, 1, 0, rest_g - (1.0 / 9.0) * g_ref[0, x, span])
            for i in range(1, 19, 2):
                even, odd = site.pair_f(i)
                emit(next_f, 0, i, (even + odd) - 0.25 * f_ref[i, x, span])
                emit(next_f, 0, i + 1, (even - odd) - 0.25 * f_ref[i + 1, x, span])
                even, odd = site.pair_g(i)
                emit(next_g, 1, i, (even + odd) - (1.0 / 9.0) * g_ref[i, x, span])
                emit(next_g, 1, i + 1, (even - odd) - (1.0 / 9.0) * g_ref[i + 1, x, span])
        return carry

    lax.fori_loop(0, layers, layer, 0)


def face_fill_kernel(direct, across, joint, f_in, g_in, f_out, g_out, low, high, sems):
    layers = f_out.shape[1]
    odd = lax.rem(lax.axis_index("gy"), 2) == 1

    @pl.when(odd)
    def _():
        low[...] = direct[...] + across[...]
        high[...] = joint[...]

    @pl.when(jnp.logical_not(odd))
    def _():
        low[...] = joint[...]
        high[...] = direct[...] + across[...]

    copies = []
    for family, out in enumerate((f_out, g_out)):
        for j in range(5):
            slot = family * 5 + j
            for side, buf, chosen, x in ((0, low, rising, 0), (1, high, falling, layers - 1)):
                copy = pltpu.make_async_copy(
                    buf.at[slot], out.at[chosen[j], x], sems.at[side, slot]
                )
                copy.start()
                copies.append(copy)
    for copy in copies:
        copy.wait()


def on_device(momentum_dist, order_dist, offsets):
    layers, rows, cols = momentum_dist.shape[1:]
    count_x, count_y = lax.axis_size("gx"), lax.axis_size("gy")
    per_plane = count_x // 4
    half = count_y // 2

    def hop(value, target):
        perm = []
        for x in range(count_x):
            for y in range(count_y):
                tx, ty = target(x, y)
                perm.append((x * count_y + y, tx % count_x * count_y + ty % count_y))
        return lax.ppermute(value, ("gx", "gy"), perm)

    def base_up(x):
        return half if (x + 1) % per_plane == 0 else 0

    def base_low(x):
        return half if x % per_plane == 0 else 0

    def hop_parity(value, odd_up, extra):
        def target(x, y):
            if (y % 2 == 1) == odd_up:
                return (x + 1, y - base_up(x) - extra)
            return (x - 1, y + base_low(x) + extra)

        return hop(value, target)

    def hop_y(value, step):
        return hop(value, lambda x, y: (x, y + step))

    smem, vmem, anywhere = spec_of(pltpu.SMEM), spec_of(VMEM), spec_of(pl.ANY)
    plane = jax.ShapeDtypeStruct((rows, cols), f32)
    top, bottom = jnp.sum(order_dist[:, layers - 1], axis=0), jnp.sum(order_dist[:, 0], axis=0)
    rise = hop(top, lambda x, y: (x + 1, y - base_up(x)))
    fall = hop(bottom, lambda x, y: (x - 1, y + base_low(x)))

    block = jax.ShapeDtypeStruct((layers + 16, cols), f32)
    phi, to_north, to_south = pl.pallas_call(
        phi_kernel,
        out_shape=[jax.ShapeDtypeStruct((layers, rows, cols), f32)] + [block] * 2,
        in_specs=[anywhere, anywhere, vmem, vmem],
        out_specs=[vmem] * 3,
        scratch_shapes=[
            VMEM((19, 2, rows, cols), f32),
            VMEM((19, layers, rows, cols), f32),
            pltpu.SemaphoreType.DMA((layers + 2,)),
        ],
        compiler_params=params(52 << 20),
        name="phi_all",
    )(momentum_dist, order_dist, top, bottom)
    south_msg = hop_y(jnp.concatenate([fall, to_north], 0), 1)
    north_msg = hop_y(jnp.concatenate([rise, to_south], 0), -1)

    face_moments, rims = pl.pallas_call(
        moment_kernel,
        out_shape=[
            jax.ShapeDtypeStruct((2, 4, rows, cols), f32),
            jax.ShapeDtypeStruct((2, 14, layers, cols), f32),
        ],
        in_specs=[vmem] * 2,
        out_specs=[vmem] * 2,
        compiler_params=params(16 << 20),
        name="moments",
    )(momentum_dist, order_dist)

    ten = jax.ShapeDtypeStruct((10, rows, cols), f32)
    side = jax.ShapeDtypeStruct((10, layers, cols), f32)
    ten_side = jax.ShapeDtypeStruct((10, rows + layers, cols), f32)
    mate, direct, across, joint, cross, minus, plus = pl.pallas_call(
        functools.partial(face_kernel, (count_x, count_y)),
        out_shape=[ten_side] + [ten] * 3 + [side] + [plane] * 2,
        in_specs=[smem] + [vmem] * 9,
        out_specs=[vmem] * 7,
        scratch_shapes=[
            VMEM((rows + 16, cols), f32),
            VMEM((rows + 16, cols), f32),
            VMEM((cols // LANES, 2 * rows + 16, LANES), f32),
            VMEM((rows + 16, cols), f32),
            VMEM((layers + 16, cols), f32),
            VMEM((10, rows, cols), f32),
            VMEM((11, 8, cols), f32),
            VMEM((2, 8, cols), f32),
            VMEM((cols // LANES, rows + 16, LANES), f32),
            VMEM((cols // LANES, 3 * rows + 16, LANES), f32),
        ],
        compiler_params=params(24 << 20),
        name="faces",
    )(
        offsets,
        momentum_dist,
        order_dist,
        face_moments,
        rims,
        phi,
        rise,
        fall,
        south_msg,
        north_msg,
    )

    mate = hop(mate, lambda x, y: (x, y ^ 1))
    cross = hop(cross, lambda x, y: (x, y + 1 if y % 2 == 1 else y - 1))
    direct = hop_parity(direct, True, 0)
    across = hop_parity(across, False, 1)
    joint, cross = lax.optimization_barrier((joint + mate[:, :rows], cross))
    after = joint
    joint = hop_parity(joint, False, 0)
    around = (phi, minus, plus, south_msg, north_msg)

    whole = jax.ShapeDtypeStruct(momentum_dist.shape, f32)
    next_f, next_g = pl.pallas_call(
        bulk_kernel,
        out_shape=[whole, whole],
        in_specs=[anywhere] + [vmem] * 9,
        out_specs=[vmem] * 2,
        scratch_shapes=[
            VMEM((layers + 2, rows, cols), f32),
            VMEM((rows + 16, cols), f32),
        ],
        compiler_params=params(48 << 20),
        name="bulk",
    )(after, momentum_dist, order_dist, *around, mate, cross)

    return pl.pallas_call(
        face_fill_kernel,
        out_shape=[whole, whole],
        in_specs=[vmem] * 3 + [anywhere, anywhere],
        out_specs=[anywhere, anywhere],
        scratch_shapes=[
            VMEM((10, rows, cols), f32),
            VMEM((10, rows, cols), f32),
            pltpu.SemaphoreType.DMA((2, 10)),
        ],
        input_output_aliases={3: 0, 4: 1},
        compiler_params=params(24 << 20),
        name="x_fill",
    )(direct, across, joint, next_f, next_g)


def solution(mesh):
    return jax.shard_map(
        on_device,
        mesh=mesh,
        in_specs=(P(None, "gx", "gy", None), P(None, "gx", "gy", None), P()),
        out_specs=(P(None, "gx", "gy", None), P(None, "gx", "gy", None)),
        check_vma=False,
    )
```

```python
import functools

import jax
import jax.numpy as jnp
from jax import lax
from jax.experimental import pallas as pl
from jax.experimental.pallas import tpu as pltpu
from jax.sharding import PartitionSpec as P

lattice_velocity = [
    (0, 0, 0),
    (1, 0, 0),
    (-1, 0, 0),
    (0, 1, 0),
    (0, -1, 0),
    (0, 0, 1),
    (0, 0, -1),
    (1, 1, 0),
    (-1, -1, 0),
    (1, -1, 0),
    (-1, 1, 0),
    (1, 0, 1),
    (-1, 0, -1),
    (1, 0, -1),
    (-1, 0, 1),
    (0, 1, 1),
    (0, -1, -1),
    (0, 1, -1),
    (0, -1, 1),
]
lattice_weight = [1.0 / 3.0] + [1.0 / 18.0] * 6 + [1.0 / 36.0] * 12
plane_speed = 0.04
rising = [1, 7, 9, 11, 13]
falling = [2, 8, 10, 12, 14]
north_going = [i for i in range(19) if lattice_velocity[i][1] == 1]
south_going = [i for i in range(19) if lattice_velocity[i][1] == -1]
f32 = jnp.float32
VMEM = pltpu.VMEM
LANES = 128


def z_moved(value, step):
    if step == 0:
        return value
    return pltpu.roll(value, step % value.shape[-1], value.ndim - 1)


def spec_of(space):
    return pl.BlockSpec(memory_space=space)


def params(limit):
    return pltpu.CompilerParams(vmem_limit_bytes=limit)


def along(parts, c):
    total = None
    for sign, part in zip(c, parts):
        if sign == 0:
            continue
        if total is None:
            total = part if sign > 0 else -part
        else:
            total = total + part if sign > 0 else total - part
    return total


def signed_sum(load, axis):
    ups = [i for i in range(19) if lattice_velocity[i][axis] == 1]
    downs = [i for i in range(19) if lattice_velocity[i][axis] == -1]
    total = load(ups[0]) - load(downs[0])
    for i, j in zip(ups[1:], downs[1:]):
        total = total + (load(i) - load(j))
    return total


def moments_of(load):
    rho = load(0)
    for i in range(1, 19):
        rho = rho + load(i)
    return [rho] + [signed_sum(load, axis) for axis in range(3)]


class Site:
    def __init__(self, moments, phi, minus, plus, south, north):
        rho, momentum = moments[0], moments[1:]
        lower, upper = z_moved(phi, 1), z_moved(phi, -1)
        lap = (plus + minus) + (north + south) + (upper + lower) - 6.0 * phi
        mu = phi * (0.0625 * (phi * phi) - 0.0625) - 0.04 * lap
        half_mu = 0.5 * mu
        force = [half_mu * (plus - minus), half_mu * (north - south), half_mu * (upper - lower)]
        inverse = 1.0 / rho
        u = [(j + 0.5 * k) * inverse for j, k in zip(momentum, force)]
        uu = u[0] * u[0] + u[1] * u[1] + u[2] * u[2]
        uf = u[0] * force[0] + u[1] * force[1] + u[2] * force[2]
        self.rho, self.phi, self.mu, self.u, self.force, self.uu = rho, phi, mu, u, force, uu
        self.r = 1.25 * rho
        self.k = self.r * (1.0 - 1.5 * uu) - 1.125 * uf
        self.g_scale = phi * (1.0 / 0.9)
        self.g_base = (3.0 / 0.9) * mu - 1.5 * (self.g_scale * uu)

    def pair_f(self, i):
        p, q = along(self.u, lattice_velocity[i]), along(self.force, lattice_velocity[i])
        w = lattice_weight[i]
        rp = self.r * p
        even = w * (self.k + p * (4.5 * rp + 3.375 * q))
        odd = (3.0 * w) * rp + (1.125 * w) * q
        return even, odd

    def pair_g(self, i):
        p = along(self.u, lattice_velocity[i])
        w = lattice_weight[i]
        gp = self.g_scale * p
        return w * (self.g_base + 4.5 * (gp * p)), (3.0 * w) * gp

    def jump(self, i, delta):
        cy = lattice_velocity[i][1]
        uy = self.u[1]
        if cy == 0:
            return delta * (-3.0 * uy) - (1.5 * delta * delta)
        p = along(self.u, lattice_velocity[i])
        return delta * (3.0 * cy + (9.0 * cy) * p - 3.0 * uy) + (3.0 * delta * delta)


class Shear:
    def __init__(self, raw, wide, rows):
        self.raw, self.wide, self.rows = raw, wide, rows

    def clear(self):
        self.raw[...] = jnp.zeros_like(self.raw)
        self.wide[...] = jnp.zeros_like(self.wide)

    def put(self, value, up, near, far):
        n = self.rows
        for k in range(self.raw.shape[0]):
            self.raw[k, 8 : 8 + n] = value[:, LANES * k : LANES * k + LANES]
        for k in range(self.raw.shape[0]):
            if up:
                self.wide[k, n : n + n + 8] = (
                    near * self.raw[k, 0 : n + 8] + far * self.raw[k, 1 : n + 9]
                )
            else:
                self.wide[k, n + 8 : n + n + 16] = (
                    near * self.raw[k, 7 : n + 15] + far * self.raw[k, 8 : n + 16]
                )

    def add_row(self, at, row):
        for k in range(self.raw.shape[0]):
            lanes = slice(LANES * k, LANES * k + LANES)
            self.wide[k, at : at + 1] = self.wide[k, at : at + 1] + row[:, lanes]

    def take(self, up, block, rest, cy, ref, j):
        n = self.rows
        if up:
            start = (n + 8 if block == 0 else 8) + rest - cy
        else:
            start = (n + 8 if block == 0 else n + n + 8) - rest - cy
        for k in range(self.raw.shape[0]):
            ref[j, 0:n, LANES * k : LANES * k + LANES] = self.wide[k, pl.ds(start, n)]


class Planes:
    def __init__(self, offsets, rows, sizes):
        count_x, count_y = sizes
        per_plane, half = count_x // 4, count_y // 2
        a = lax.axis_index("gx")
        self.odd = lax.rem(lax.axis_index("gy"), 2) == 1

        def plane_of(column):
            is_plane = lax.rem(column, per_plane) == 0
            plane = lax.rem(lax.div(column, per_plane), 4)
            rest = jnp.where(is_plane, jnp.clip(offsets[plane] - half * rows, 0, rows - 1), 0)
            return is_plane, (2.0 * plane.astype(f32) + 1.0) * 0.125, rest

        up_is, up_part, self.up_rest = plane_of(lax.rem(a + 1, count_x))
        low_is, low_part, self.low_rest = plane_of(a)
        self.up_near = jnp.where(up_is, 1.0 - up_part, 1.0)
        self.up_far = jnp.where(up_is, up_part, 0.0)
        self.low_near = jnp.where(low_is, low_part, 0.0)
        self.low_far = jnp.where(low_is, 1.0 - low_part, 1.0)
        self.up_jump = jnp.where(up_is, -plane_speed, 0.0)
        self.low_jump = jnp.where(low_is, plane_speed, 0.0)


def order_sum(load):
    total = load(0)
    for i in range(1, 19):
        total = total + load(i)
    return total


def phi_kernel(f_ref, g_ref, top, bottom, phi_ref, to_north, to_south, fbuf, gbuf, sems):
    layers, rows = phi_ref.shape[0], phi_ref.shape[1]
    faces = (layers - 1, 0)
    f_copies = [
        pltpu.make_async_copy(f_ref.at[:, x], fbuf.at[:, s], sems.at[layers + s])
        for s, x in enumerate(faces)
    ]
    g_copies = [
        pltpu.make_async_copy(g_ref.at[:, x], gbuf.at[:, x], sems.at[x]) for x in range(layers)
    ]
    for copy in f_copies + g_copies:
        copy.start()
    phi_ref[layers - 1] = top[...]
    phi_ref[0] = bottom[...]
    edges = ((to_north, rows - 1, rows - 2, (7, 10)), (to_south, 0, 1, (9, 8)))
    for s, x in enumerate(faces):
        f_copies[s].wait()
        for out, edge, inner, chosen in edges:
            out[layers + s : layers + s + 1] = phi_ref[x, inner : inner + 1]
            at = layers + 2 + 6 * s
            out[at : at + 1] = fbuf[chosen[s], s, edge : edge + 1]
            for k, part in enumerate(moments_of(lambda i: fbuf[i, s, edge : edge + 1])):
                out[at + 2 + k : at + 3 + k] = part
    for x in range(layers):
        g_copies[x].wait()
        if 0 < x < layers - 1:
            phi_ref[x] = order_sum(lambda i: gbuf[i, x])
        to_north[x : x + 1] = phi_ref[x, rows - 1 : rows]
        to_south[x : x + 1] = phi_ref[x, 0:1]
    for s, x in enumerate(faces):
        for out, edge, inner, chosen in edges:
            at = layers + 3 + 6 * s
            out[at : at + 1] = gbuf[chosen[s], x, edge : edge + 1]
    for out in (to_north, to_south):
        out[layers + 14 : layers + 16] = jnp.zeros((2, out.shape[1]), f32)


def with_halo(ref, layer, below, above):
    rows = layer.shape[0]
    ref[8 : 8 + rows] = layer
    ref[7:8] = below
    ref[8 + rows : 9 + rows] = above


def corner_values(cells, planes, phi_ref, south_msg, north_msg, minus_wide, plus_wide):
    layers, rows, cols = phi_ref.shape
    cells[...] = jnp.ones_like(cells)
    for row in range(4):
        msg = south_msg if row < 2 else north_msg
        x = layers - 1 if row % 2 == 0 else 0
        beside = rows + (layers - 2 if row % 2 == 0 else 1)
        wide_row = 7 if row < 2 else rows + 8
        at = rows + layers
        first = at + 2 + 6 * (row % 2)
        far_phi = msg[at + row % 2 : at + row % 2 + 1]
        own_phi = phi_ref[x, 0:1] if row < 2 else phi_ref[x, rows - 1 : rows]
        parts = [msg[first + k : first + k + 1] for k in range(6)]
        parts.append(msg[rows + x : rows + x + 1])
        if row % 2 == 0:
            parts += [msg[beside : beside + 1], plus_wide[wide_row : wide_row + 1]]
        else:
            parts += [minus_wide[wide_row : wide_row + 1], msg[beside : beside + 1]]
        parts += [far_phi, own_phi] if row < 2 else [own_phi, far_phi]
        for k, part in enumerate(parts):
            cells[k, row : row + 1] = part
    place = lax.broadcasted_iota(jnp.int32, (8, cols), 0)
    is_top = (place == 0) | (place == 2)
    sx = jnp.where(is_top, 1.0, -1.0)
    sy = jnp.where(place < 2, 1.0, -1.0)
    delta = jnp.where(is_top, planes.up_jump, planes.low_jump)
    site = Site([cells[k] for k in range(2, 6)], *[cells[k] for k in range(6, 11)])
    w = lattice_weight[7]
    p = sx * site.u[0] + sy * site.u[1]
    q = sx * site.force[0] + sy * site.force[1]
    change = delta * (3.0 * sy + 9.0 * (sy * p) - 3.0 * site.u[1]) + 3.0 * (delta * delta)
    rp, gp = site.r * p, site.g_scale * p
    f_post = w * (site.k + p * (4.5 * rp + 3.375 * q) + 3.0 * rp + 1.125 * q + site.rho * change)
    g_post = w * (site.g_base + 4.5 * (gp * p) + 3.0 * gp + site.phi * change)
    return f_post - 0.25 * cells[0], g_post - (1.0 / 9.0) * cells[1]


def moment_kernel(f_ref, g_ref, faces, rims):
    layers, rows = f_ref.shape[1], f_ref.shape[2]
    for s, x in enumerate((layers - 1, 0)):
        for k, part in enumerate(moments_of(lambda i: f_ref[i, x])):
            faces[s, k] = part
    for s, (edge, chosen) in enumerate(((rows - 1, north_going), (0, south_going))):
        for k, part in enumerate(moments_of(lambda i: f_ref[i, :, edge, :])):
            rims[s, k] = part
        for j, i in enumerate(chosen):
            rims[s, 4 + j] = f_ref[i, :, edge, :]
            rims[s, 9 + j] = g_ref[i, :, edge, :]


def half_rows(rows, first):
    return slice(0, rows // 2) if first else slice(rows // 2, rows)


def seam_rows(rows, up):
    return slice(rows // 2 - 2, rows // 2) if up else slice(rows // 2, rows // 2 + 2)


def rim_values(rims, s, phi_ref, minus, plus, south_msg, north_msg, line, edge, chosen, store):
    layers, rows, cols = phi_ref.shape
    phi = phi_ref[:, edge, :]
    with_halo(line, phi, minus[edge : edge + 1], plus[edge : edge + 1])
    if edge == 0:
        below, above = south_msg[rows : rows + layers], phi_ref[:, 1, :]
    else:
        below, above = phi_ref[:, rows - 2, :], north_msg[rows : rows + layers]
    site = Site(
        [rims[s, k] for k in range(4)],
        phi,
        line[7 : 7 + layers],
        line[9 : 9 + layers],
        below,
        above,
    )
    for j, i in enumerate(chosen):
        cz = lattice_velocity[i][2]
        even, odd = site.pair_f(i)
        store(j, z_moved(even + odd - 0.25 * rims[s, 4 + j], cz))
        even, odd = site.pair_g(i)
        store(5 + j, z_moved(even + odd - (1.0 / 9.0) * rims[s, 9 + j], cz))


def face_kernel(
    sizes,
    offsets,
    f_ref,
    g_ref,
    face_moments,
    rims,
    phi_ref,
    rise,
    fall,
    south_msg,
    north_msg,
    mate,
    direct,
    direct_short,
    across,
    across_short,
    joint,
    cross,
    minus_out,
    plus_out,
    minus_wide,
    plus_wide,
    window,
    halo,
    line,
    post,
    cells,
    corners,
    raw,
    wide,
):
    layers, rows, cols = phi_ref.shape
    planes = Planes(offsets, rows, sizes)
    shear = Shear(raw, wide, rows)
    window[...] = jnp.zeros_like(window)
    for up in (True, False):
        if up:
            first, second = rise, north_msg
            near, far, start = planes.low_far, planes.low_near, planes.low_rest
        else:
            first, second = south_msg, fall
            near, far, start = planes.up_far, planes.up_near, rows - 1 - planes.up_rest
        target = minus_wide if up else plus_wide
        for k in range(window.shape[0]):
            lanes = slice(LANES * k, LANES * k + LANES)
            window[k, 8 : 8 + rows] = first[0:rows, lanes]
            window[k, 8 + rows : 8 + 2 * rows] = second[0:rows, lanes]
            target[:, lanes] = (
                near * window[k, pl.ds(start, rows + 16)]
                + far * window[k, pl.ds(start + 1, rows + 16)]
            )
    minus_out[...] = minus_wide[8 : 8 + rows]
    plus_out[...] = plus_wide[8 : 8 + rows]
    corners[0], corners[1] = corner_values(
        cells, planes, phi_ref, south_msg, north_msg, minus_wide, plus_wide
    )
    for s, (edge, chosen) in enumerate(((rows - 1, north_going), (0, south_going))):
        to_mate = planes.odd if edge == 0 else jnp.logical_not(planes.odd)

        def store(slot, value):
            @pl.when(to_mate)
            def _():
                mate[slot, rows : rows + layers] = value

            @pl.when(jnp.logical_not(to_mate))
            def _():
                cross[slot] = value

        rim_values(
            rims,
            s,
            phi_ref,
            minus_out,
            plus_out,
            south_msg,
            north_msg,
            line,
            edge,
            chosen,
            store,
        )
    for up in (True, False):
        x = layers - 1 if up else 0
        with_halo(
            halo, phi_ref[x], south_msg[rows + x : rows + x + 1], north_msg[rows + x : rows + x + 1]
        )
        if up:
            near, far, rest, delta = planes.up_near, planes.up_far, planes.up_rest, planes.up_jump
        else:
            near, far, rest, delta = planes.low_near, planes.low_far, planes.low_rest, planes.low_jump
        for h in range(0, rows, 8):
            span = slice(h, h + 8)
            phi_h = phi_ref[x, span]
            if up:
                minus, plus = phi_ref[x - 1, span], plus_wide[8 + h : 16 + h]
            else:
                minus, plus = minus_wide[8 + h : 16 + h], phi_ref[x + 1, span]
            site = Site(
                [face_moments[0 if up else 1, k, span] for k in range(4)],
                phi_h,
                minus,
                plus,
                halo[7 + h : 15 + h],
                halo[9 + h : 17 + h],
            )
            for j in range(5):
                i = rising[j] if up else falling[j]
                cz = lattice_velocity[i][2]
                change = lattice_weight[i] * site.jump(i, delta)
                even, odd = site.pair_f(i)
                value = even + odd - 0.25 * f_ref[i, x, span] + site.rho * change
                post[j, span] = z_moved(value, cz)
                even, odd = site.pair_g(i)
                value = even + odd - (1.0 / 9.0) * g_ref[i, x, span] + phi_h * change
                post[5 + j, span] = z_moved(value, cz)
        shear.clear()
        for j in range(10):
            cy = lattice_velocity[(rising if up else falling)[j % 5]][1]
            shear.put(post[j], up, near, far)
            corner = (0 if up else 1) + (0 if cy == 1 else 2)
            if cy == 1:
                gate = jnp.where(rest == (0 if up else rows - 1), near, 0.0)
                at = rows + 7 if up else rows + 8
            if cy == -1:
                gate = jnp.where(rest == (rows - 1 if up else 0), far, 0.0)
                at = 2 * rows + 7 if up else 2 * rows + 8
            if cy != 0:
                shear.add_row(at, gate * corners[j // 5, corner : corner + 1])

            @pl.when(planes.odd)
            def _():
                shear.take(up, 0, rest, cy, direct if up else joint, j)
                shear.take(up, 1, rest, cy, mate if up else across, j)

            @pl.when(jnp.logical_not(planes.odd))
            def _():
                shear.take(up, 0, rest, cy, joint if up else direct, j)
                shear.take(up, 1, rest, cy, across if up else mate, j)

    def shorten(direct_up, across_up):
        for j in range(10):
            direct_short[j] = direct[j, half_rows(rows, direct_up)]
            across_short[part * j : part * j + part] = across[j, half_rows(rows, not across_up)]
            across_short[seam + 2 * j : seam + 2 * j + 2] = across[j, seam_rows(rows, across_up)]

    part = rows // 2
    seam = 10 * part
    across_short[seam + 20 : seam + 24] = jnp.zeros((4, cols), f32)
    pl.when(planes.odd)(lambda: shorten(True, False))
    pl.when(jnp.logical_not(planes.odd))(lambda: shorten(False, True))


def bulk_kernel(
    after,
    f_ref,
    g_ref,
    phi_ref,
    minus,
    plus,
    south_msg,
    north_msg,
    mate_rim,
    cross_rim,
    next_f,
    next_g,
    wide_phi,
    halo,
):
    layers, rows, cols = phi_ref.shape
    is_odd = lax.rem(lax.axis_index("gy"), 2) == 1
    wide_phi[0] = minus[...]
    wide_phi[layers + 1] = plus[...]
    for x in range(layers):
        wide_phi[x + 1] = phi_ref[x]

    def layer(x, carry):
        with_halo(halo, phi_ref[x], south_msg[pl.ds(rows + x, 1)], north_msg[pl.ds(rows + x, 1)])
        beyond = lax.rem(x + 1, layers)
        before = lax.rem(x + layers - 1, layers)
        for h in range(0, rows, 8):
            span = slice(h, h + 8)
            phi_h = phi_ref[x, span]
            site = Site(
                moments_of(lambda i: f_ref[i, x, span]),
                phi_h,
                wide_phi[x, span],
                wide_phi[x + 2, span],
                halo[7 + h : 15 + h],
                halo[9 + h : 17 + h],
            )

            def emit(out, slot, i, value):
                cx, cy, cz = lattice_velocity[i]
                value = z_moved(value, cz)
                at = beyond if cx == 1 else before if cx == -1 else x
                if cy == 0:
                    out[i, at, span] = value
                elif cy == 1:
                    if h == 0:
                        rim = slot * 5 + north_going.index(i)
                        out[i, at, 0:1] = jnp.where(
                            is_odd, mate_rim[rim, pl.ds(rows + x, 1)], cross_rim[rim, pl.ds(x, 1)]
                        )
                    if h + 8 < rows:
                        out[i, at, h + 1 : h + 9] = value
                    else:
                        out[i, at, h + 1 : h + 8] = value[0:7]
                else:
                    if h + 8 == rows:
                        rim = slot * 5 + south_going.index(i)
                        out[i, at, rows - 1 : rows] = jnp.where(
                            is_odd, cross_rim[rim, pl.ds(x, 1)], mate_rim[rim, pl.ds(rows + x, 1)]
                        )
                    if h > 0:
                        out[i, at, h - 1 : h + 7] = value
                    else:
                        out[i, at, 0:7] = value[1:8]

            emit(next_f, 0, 0, lattice_weight[0] * site.k - 0.25 * f_ref[0, x, span])
            rest_g = (phi_h - 2.0 * site.mu - 0.5 * (phi_h * site.uu)) * (1.0 / 0.9)
            emit(next_g, 1, 0, rest_g - (1.0 / 9.0) * g_ref[0, x, span])
            for i in range(1, 19, 2):
                even, odd = site.pair_f(i)
                emit(next_f, 0, i, (even + odd) - 0.25 * f_ref[i, x, span])
                emit(next_f, 0, i + 1, (even - odd) - 0.25 * f_ref[i + 1, x, span])
                even, odd = site.pair_g(i)
                emit(next_g, 1, i, (even + odd) - (1.0 / 9.0) * g_ref[i, x, span])
                emit(next_g, 1, i + 1, (even - odd) - (1.0 / 9.0) * g_ref[i + 1, x, span])
        return carry

    lax.fori_loop(0, layers, layer, 0)


def face_fill_kernel(
    sizes,
    offsets,
    direct,
    direct_short,
    across,
    across_short,
    joint,
    f_in,
    g_in,
    f_out,
    g_out,
    low,
    high,
    sems,
):
    layers, rows = f_out.shape[1], f_out.shape[2]
    planes = Planes(offsets, rows, sizes)
    part = rows // 2
    seam = 10 * part

    def merge(out, rest, up):
        is_long = rest > part
        near, other, between = half_rows(rows, up), half_rows(rows, not up), seam_rows(rows, up)

        @pl.when(is_long)
        def _():
            out[...] = across[...]
            for j in range(10):
                out[j, near] = out[j, near] + direct_short[j]

        @pl.when(jnp.logical_not(is_long))
        def _():
            out[...] = direct[...]
            for j in range(10):
                out[j, other] = out[j, other] + across_short[part * j : part * j + part]
                at = seam + 2 * j
                out[j, between] = out[j, between] + across_short[at : at + 2]

    @pl.when(planes.odd)
    def _():
        merge(low, planes.low_rest, True)
        high[...] = joint[...]

    @pl.when(jnp.logical_not(planes.odd))
    def _():
        low[...] = joint[...]
        merge(high, planes.up_rest, False)

    copies = []
    for family, out in enumerate((f_out, g_out)):
        for j in range(5):
            slot = family * 5 + j
            for side, buf, chosen, x in ((0, low, rising, 0), (1, high, falling, layers - 1)):
                copy = pltpu.make_async_copy(
                    buf.at[slot], out.at[chosen[j], x], sems.at[side, slot]
                )
                copy.start()
                copies.append(copy)
    for copy in copies:
        copy.wait()


def on_device(momentum_dist, order_dist, offsets):
    layers, rows, cols = momentum_dist.shape[1:]
    count_x, count_y = lax.axis_size("gx"), lax.axis_size("gy")
    per_plane = count_x // 4
    half = count_y // 2

    def hop(value, target):
        perm = []
        for x in range(count_x):
            for y in range(count_y):
                tx, ty = target(x, y)
                perm.append((x * count_y + y, tx % count_x * count_y + ty % count_y))
        return lax.ppermute(value, ("gx", "gy"), perm)

    def base_up(x):
        return half if (x + 1) % per_plane == 0 else 0

    def base_low(x):
        return half if x % per_plane == 0 else 0

    def hop_parity(value, odd_up, extra):
        def target(x, y):
            if (y % 2 == 1) == odd_up:
                return (x + 1, y - base_up(x) - extra)
            return (x - 1, y + base_low(x) + extra)

        return hop(value, target)

    def hop_y(value, step):
        return hop(value, lambda x, y: (x, y + step))

    smem, vmem, anywhere = spec_of(pltpu.SMEM), spec_of(VMEM), spec_of(pl.ANY)
    plane = jax.ShapeDtypeStruct((rows, cols), f32)
    top, bottom = jnp.sum(order_dist[:, layers - 1], axis=0), jnp.sum(order_dist[:, 0], axis=0)
    rise = hop(top, lambda x, y: (x + 1, y - base_up(x)))
    fall = hop(bottom, lambda x, y: (x - 1, y + base_low(x)))

    block = jax.ShapeDtypeStruct((layers + 16, cols), f32)
    phi, to_north, to_south = pl.pallas_call(
        phi_kernel,
        out_shape=[jax.ShapeDtypeStruct((layers, rows, cols), f32)] + [block] * 2,
        in_specs=[anywhere, anywhere, vmem, vmem],
        out_specs=[vmem] * 3,
        scratch_shapes=[
            VMEM((19, 2, rows, cols), f32),
            VMEM((19, layers, rows, cols), f32),
            pltpu.SemaphoreType.DMA((layers + 2,)),
        ],
        compiler_params=params(52 << 20),
        name="phi_all",
    )(momentum_dist, order_dist, top, bottom)
    south_msg = hop_y(jnp.concatenate([fall, to_north], 0), 1)
    north_msg = hop_y(jnp.concatenate([rise, to_south], 0), -1)

    face_moments, rims = pl.pallas_call(
        moment_kernel,
        out_shape=[
            jax.ShapeDtypeStruct((2, 4, rows, cols), f32),
            jax.ShapeDtypeStruct((2, 14, layers, cols), f32),
        ],
        in_specs=[vmem] * 2,
        out_specs=[vmem] * 2,
        compiler_params=params(16 << 20),
        name="moments",
    )(momentum_dist, order_dist)

    part = rows // 2
    ten = jax.ShapeDtypeStruct((10, rows, cols), f32)
    ten_short = jax.ShapeDtypeStruct((10, part, cols), f32)
    ten_seam = jax.ShapeDtypeStruct((10 * part + 24, cols), f32)
    side = jax.ShapeDtypeStruct((10, layers, cols), f32)
    ten_side = jax.ShapeDtypeStruct((10, rows + layers, cols), f32)
    *outgoing, minus, plus = pl.pallas_call(
        functools.partial(face_kernel, (count_x, count_y)),
        out_shape=[ten_side, ten, ten_short, ten, ten_seam, ten, side] + [plane] * 2,
        in_specs=[smem] + [vmem] * 9,
        out_specs=[vmem] * 9,
        scratch_shapes=[
            VMEM((rows + 16, cols), f32),
            VMEM((rows + 16, cols), f32),
            VMEM((cols // LANES, 2 * rows + 16, LANES), f32),
            VMEM((rows + 16, cols), f32),
            VMEM((layers + 16, cols), f32),
            VMEM((10, rows, cols), f32),
            VMEM((11, 8, cols), f32),
            VMEM((2, 8, cols), f32),
            VMEM((cols // LANES, rows + 16, LANES), f32),
            VMEM((cols // LANES, 3 * rows + 16, LANES), f32),
        ],
        compiler_params=params(24 << 20),
        name="faces",
    )(
        offsets,
        momentum_dist,
        order_dist,
        face_moments,
        rims,
        phi,
        rise,
        fall,
        south_msg,
        north_msg,
    )
    around = (phi, minus, plus, south_msg, north_msg)
    whole = jax.ShapeDtypeStruct(momentum_dist.shape, f32)

    def finish(long_planes, mate, direct, direct_short, across, across_short, joint, cross):

        def is_long(x):
            return x % per_plane == 0 and x // per_plane % 4 in long_planes

        def hop_some(value, odd_up, extra, long):
            pairs = []
            for x in range(count_x):
                for y in range(count_y):
                    up = (y % 2 == 1) == odd_up
                    tx = (x + 1 if up else x - 1) % count_x
                    if is_long(tx if up else x) != long:
                        continue
                    ty = y - base_up(x) - extra if up else y + base_low(x) + extra
                    pairs.append((x * count_y + y, tx * count_y + ty % count_y))
            return lax.ppermute(value, ("gx", "gy"), pairs)

        mate = hop(mate, lambda x, y: (x, y ^ 1))
        cross = hop(cross, lambda x, y: (x, y + 1 if y % 2 == 1 else y - 1))
        direct = hop_some(direct, True, 0, False)
        direct_short = hop_some(direct_short, True, 0, True)
        across = hop_some(across, False, 1, True)
        across_short = hop_some(across_short, False, 1, False)
        joint, cross = lax.optimization_barrier((joint + mate[:, :rows], cross))
        after = joint
        joint = hop_parity(joint, False, 0)

        next_f, next_g = pl.pallas_call(
            bulk_kernel,
            out_shape=[whole, whole],
            in_specs=[anywhere] + [vmem] * 9,
            out_specs=[vmem] * 2,
            scratch_shapes=[
                VMEM((layers + 2, rows, cols), f32),
                VMEM((rows + 16, cols), f32),
            ],
            compiler_params=params(48 << 20),
            name="bulk",
        )(after, momentum_dist, order_dist, *around, mate, cross)

        return pl.pallas_call(
            functools.partial(face_fill_kernel, (count_x, count_y)),
            out_shape=[whole, whole],
            in_specs=[smem] + [vmem] * 5 + [anywhere, anywhere],
            out_specs=[anywhere, anywhere],
            scratch_shapes=[
                VMEM((10, rows, cols), f32),
                VMEM((10, rows, cols), f32),
                pltpu.SemaphoreType.DMA((2, 10)),
            ],
            input_output_aliases={6: 0, 7: 1},
            compiler_params=params(24 << 20),
            name="x_fill",
        )(offsets, direct, direct_short, across, across_short, joint, next_f, next_g)

    is_long = [(offsets[k] - half * rows > part).astype(jnp.int32) for k in (1, 2)]
    branches = [
        functools.partial(finish, {3} | ({1} if k & 2 else set()) | ({2} if k & 1 else set()))
        for k in range(4)
    ]
    return lax.switch(2 * is_long[0] + is_long[1], branches, *outgoing)


def solution(mesh):
    return jax.shard_map(
        on_device,
        mesh=mesh,
        in_specs=(P(None, "gx", "gy", None), P(None, "gx", "gy", None), P()),
        out_specs=(P(None, "gx", "gy", None), P(None, "gx", "gy", None)),
        check_vma=False,
    )
```

```python
import functools

import jax
import jax.numpy as jnp
from jax import lax
from jax.experimental import pallas as pl
from jax.experimental.pallas import tpu as pltpu
from jax.sharding import PartitionSpec as P

lattice_velocity = [
    (0, 0, 0),
    (1, 0, 0),
    (-1, 0, 0),
    (0, 1, 0),
    (0, -1, 0),
    (0, 0, 1),
    (0, 0, -1),
    (1, 1, 0),
    (-1, -1, 0),
    (1, -1, 0),
    (-1, 1, 0),
    (1, 0, 1),
    (-1, 0, -1),
    (1, 0, -1),
    (-1, 0, 1),
    (0, 1, 1),
    (0, -1, -1),
    (0, 1, -1),
    (0, -1, 1),
]
lattice_weight = [1.0 / 3.0] + [1.0 / 18.0] * 6 + [1.0 / 36.0] * 12
plane_speed = 0.04
rising = [1, 7, 9, 11, 13]
falling = [2, 8, 10, 12, 14]
north_going = [i for i in range(19) if lattice_velocity[i][1] == 1]
south_going = [i for i in range(19) if lattice_velocity[i][1] == -1]
f32 = jnp.float32
VMEM = pltpu.VMEM
LANES = 128


def z_moved(value, step):
    if step == 0:
        return value
    return pltpu.roll(value, step % value.shape[-1], value.ndim - 1)


def spec_of(space):
    return pl.BlockSpec(memory_space=space)


def params(limit):
    return pltpu.CompilerParams(vmem_limit_bytes=limit)


def along(parts, c):
    total = None
    for sign, part in zip(c, parts):
        if sign == 0:
            continue
        if total is None:
            total = part if sign > 0 else -part
        else:
            total = total + part if sign > 0 else total - part
    return total


def signed_sum(load, axis):
    ups = [i for i in range(19) if lattice_velocity[i][axis] == 1]
    downs = [i for i in range(19) if lattice_velocity[i][axis] == -1]
    total = load(ups[0]) - load(downs[0])
    for i, j in zip(ups[1:], downs[1:]):
        total = total + (load(i) - load(j))
    return total


def moments_of(load):
    rho = load(0)
    for i in range(1, 19):
        rho = rho + load(i)
    return [rho] + [signed_sum(load, axis) for axis in range(3)]


class Site:
    def __init__(self, moments, phi, minus, plus, south, north):
        rho, momentum = moments[0], moments[1:]
        lower, upper = z_moved(phi, 1), z_moved(phi, -1)
        lap = (plus + minus) + (north + south) + (upper + lower) - 6.0 * phi
        mu = phi * (0.0625 * (phi * phi) - 0.0625) - 0.04 * lap
        half_mu = 0.5 * mu
        force = [half_mu * (plus - minus), half_mu * (north - south), half_mu * (upper - lower)]
        inverse = 1.0 / rho
        u = [(j + 0.5 * k) * inverse for j, k in zip(momentum, force)]
        uu = u[0] * u[0] + u[1] * u[1] + u[2] * u[2]
        uf = u[0] * force[0] + u[1] * force[1] + u[2] * force[2]
        self.rho, self.phi, self.mu, self.u, self.force, self.uu = rho, phi, mu, u, force, uu
        self.r = 1.25 * rho
        self.k = self.r * (1.0 - 1.5 * uu) - 1.125 * uf
        self.g_scale = phi * (1.0 / 0.9)
        self.g_base = (3.0 / 0.9) * mu - 1.5 * (self.g_scale * uu)

    def pair_f(self, i):
        p, q = along(self.u, lattice_velocity[i]), along(self.force, lattice_velocity[i])
        w = lattice_weight[i]
        rp = self.r * p
        even = w * (self.k + p * (4.5 * rp + 3.375 * q))
        odd = (3.0 * w) * rp + (1.125 * w) * q
        return even, odd

    def pair_g(self, i):
        p = along(self.u, lattice_velocity[i])
        w = lattice_weight[i]
        gp = self.g_scale * p
        return w * (self.g_base + 4.5 * (gp * p)), (3.0 * w) * gp

    def jump(self, i, delta):
        cy = lattice_velocity[i][1]
        uy = self.u[1]
        if cy == 0:
            return delta * (-3.0 * uy) - (1.5 * delta * delta)
        p = along(self.u, lattice_velocity[i])
        return delta * (3.0 * cy + (9.0 * cy) * p - 3.0 * uy) + (3.0 * delta * delta)


class Shear:
    def __init__(self, raw, wide, rows):
        self.raw, self.wide, self.rows = raw, wide, rows

    def clear(self):
        self.raw[...] = jnp.zeros_like(self.raw)
        self.wide[...] = jnp.zeros_like(self.wide)

    def put(self, value, up, near, far):
        n = self.rows
        for k in range(self.raw.shape[0]):
            self.raw[k, 8 : 8 + n] = value[:, LANES * k : LANES * k + LANES]
        for k in range(self.raw.shape[0]):
            if up:
                self.wide[k, n : n + n + 8] = (
                    near * self.raw[k, 0 : n + 8] + far * self.raw[k, 1 : n + 9]
                )
            else:
                self.wide[k, n + 8 : n + n + 16] = (
                    near * self.raw[k, 7 : n + 15] + far * self.raw[k, 8 : n + 16]
                )

    def add_row(self, at, row):
        for k in range(self.raw.shape[0]):
            lanes = slice(LANES * k, LANES * k + LANES)
            self.wide[k, at : at + 1] = self.wide[k, at : at + 1] + row[:, lanes]

    def take(self, up, block, rest, cy, ref, j):
        n = self.rows
        if up:
            start = (n + 8 if block == 0 else 8) + rest - cy
        else:
            start = (n + 8 if block == 0 else n + n + 8) - rest - cy
        for k in range(self.raw.shape[0]):
            ref[j, 0:n, LANES * k : LANES * k + LANES] = self.wide[k, pl.ds(start, n)]


class Planes:
    def __init__(self, offsets, rows, sizes):
        count_x, count_y = sizes
        per_plane, half = count_x // 4, count_y // 2
        a = lax.axis_index("gx")
        self.odd = lax.rem(lax.axis_index("gy"), 2) == 1

        def plane_of(column):
            is_plane = lax.rem(column, per_plane) == 0
            plane = lax.rem(lax.div(column, per_plane), 4)
            rest = jnp.where(is_plane, jnp.clip(offsets[plane] - half * rows, 0, rows - 1), 0)
            return is_plane, (2.0 * plane.astype(f32) + 1.0) * 0.125, rest

        up_is, up_part, self.up_rest = plane_of(lax.rem(a + 1, count_x))
        low_is, low_part, self.low_rest = plane_of(a)
        self.up_near = jnp.where(up_is, 1.0 - up_part, 1.0)
        self.up_far = jnp.where(up_is, up_part, 0.0)
        self.low_near = jnp.where(low_is, low_part, 0.0)
        self.low_far = jnp.where(low_is, 1.0 - low_part, 1.0)
        self.up_jump = jnp.where(up_is, -plane_speed, 0.0)
        self.low_jump = jnp.where(low_is, plane_speed, 0.0)


def order_sum(load):
    total = load(0)
    for i in range(1, 19):
        total = total + load(i)
    return total


def phi_kernel(f_ref, g_ref, top, bottom, phi_ref, to_north, to_south, gbuf, fbuf, sems):
    layers, rows = phi_ref.shape[0], phi_ref.shape[1]
    faces = (layers - 1, 0)
    f_copies = [
        pltpu.make_async_copy(f_ref.at[:, x], fbuf.at[:, s], sems.at[layers + s])
        for s, x in enumerate(faces)
    ]
    g_copies = [
        pltpu.make_async_copy(g_ref.at[:, x], gbuf.at[:, x], sems.at[x]) for x in range(layers)
    ]
    for copy in f_copies + g_copies:
        copy.start()
    phi_ref[layers - 1] = top[...]
    phi_ref[0] = bottom[...]
    edges = ((to_north, rows - 1, rows - 2, (7, 10)), (to_south, 0, 1, (9, 8)))
    for s, x in enumerate(faces):
        f_copies[s].wait()
        for out, edge, inner, chosen in edges:
            out[layers + s : layers + s + 1] = phi_ref[x, inner : inner + 1]
            at = layers + 2 + 6 * s
            out[at : at + 1] = fbuf[chosen[s], s, edge : edge + 1]
            for k, part in enumerate(moments_of(lambda i: fbuf[i, s, edge : edge + 1])):
                out[at + 2 + k : at + 3 + k] = part
    for x in range(layers):
        g_copies[x].wait()
        if 0 < x < layers - 1:
            phi_ref[x] = order_sum(lambda i: gbuf[i, x])
        to_north[x : x + 1] = phi_ref[x, rows - 1 : rows]
        to_south[x : x + 1] = phi_ref[x, 0:1]
    for s, x in enumerate(faces):
        for out, edge, inner, chosen in edges:
            at = layers + 3 + 6 * s
            out[at : at + 1] = gbuf[chosen[s], x, edge : edge + 1]
    for out in (to_north, to_south):
        out[layers + 14 : layers + 16] = jnp.zeros((2, out.shape[1]), f32)


def with_halo(ref, layer, below, above):
    rows = layer.shape[0]
    ref[8 : 8 + rows] = layer
    ref[7:8] = below
    ref[8 + rows : 9 + rows] = above


def corner_values(cells, planes, phi_ref, south_msg, north_msg, minus_wide, plus_wide):
    layers, rows, cols = phi_ref.shape
    cells[...] = jnp.ones_like(cells)
    for row in range(4):
        msg = south_msg if row < 2 else north_msg
        x = layers - 1 if row % 2 == 0 else 0
        beside = rows + (layers - 2 if row % 2 == 0 else 1)
        wide_row = 7 if row < 2 else rows + 8
        at = rows + layers
        first = at + 2 + 6 * (row % 2)
        far_phi = msg[at + row % 2 : at + row % 2 + 1]
        own_phi = phi_ref[x, 0:1] if row < 2 else phi_ref[x, rows - 1 : rows]
        parts = [msg[first + k : first + k + 1] for k in range(6)]
        parts.append(msg[rows + x : rows + x + 1])
        if row % 2 == 0:
            parts += [msg[beside : beside + 1], plus_wide[wide_row : wide_row + 1]]
        else:
            parts += [minus_wide[wide_row : wide_row + 1], msg[beside : beside + 1]]
        parts += [far_phi, own_phi] if row < 2 else [own_phi, far_phi]
        for k, part in enumerate(parts):
            cells[k, row : row + 1] = part
    place = lax.broadcasted_iota(jnp.int32, (8, cols), 0)
    is_top = (place == 0) | (place == 2)
    sx = jnp.where(is_top, 1.0, -1.0)
    sy = jnp.where(place < 2, 1.0, -1.0)
    delta = jnp.where(is_top, planes.up_jump, planes.low_jump)
    site = Site([cells[k] for k in range(2, 6)], *[cells[k] for k in range(6, 11)])
    w = lattice_weight[7]
    p = sx * site.u[0] + sy * site.u[1]
    q = sx * site.force[0] + sy * site.force[1]
    change = delta * (3.0 * sy + 9.0 * (sy * p) - 3.0 * site.u[1]) + 3.0 * (delta * delta)
    rp, gp = site.r * p, site.g_scale * p
    f_post = w * (site.k + p * (4.5 * rp + 3.375 * q) + 3.0 * rp + 1.125 * q + site.rho * change)
    g_post = w * (site.g_base + 4.5 * (gp * p) + 3.0 * gp + site.phi * change)
    return f_post - 0.25 * cells[0], g_post - (1.0 / 9.0) * cells[1]


def moment_kernel(after_north, after_south, f_ref, g_ref, faces, rims):
    layers, rows = f_ref.shape[1], f_ref.shape[2]
    for s, x in enumerate((layers - 1, 0)):
        for k, part in enumerate(moments_of(lambda i: f_ref[i, x])):
            faces[s, k] = part
    for s, (edge, chosen) in enumerate(((rows - 1, north_going), (0, south_going))):
        for k, part in enumerate(moments_of(lambda i: f_ref[i, :, edge, :])):
            rims[s, k] = part
        for j, i in enumerate(chosen):
            rims[s, 4 + j] = f_ref[i, :, edge, :]
            rims[s, 9 + j] = g_ref[i, :, edge, :]


def half_rows(rows, first):
    return slice(0, rows // 2) if first else slice(rows // 2, rows)


def seam_rows(rows, up):
    return slice(rows // 2 - 2, rows // 2) if up else slice(rows // 2, rows // 2 + 2)


def rim_values(rims, s, phi_ref, minus, plus, south_msg, north_msg, line, edge, chosen, out):
    layers, rows, cols = phi_ref.shape
    phi = phi_ref[:, edge, :]
    with_halo(line, phi, minus[edge : edge + 1], plus[edge : edge + 1])
    if edge == 0:
        below, above = south_msg[rows : rows + layers], phi_ref[:, 1, :]
    else:
        below, above = phi_ref[:, rows - 2, :], north_msg[rows : rows + layers]
    site = Site(
        [rims[s, k] for k in range(4)],
        phi,
        line[7 : 7 + layers],
        line[9 : 9 + layers],
        below,
        above,
    )
    for j, i in enumerate(chosen):
        cz = lattice_velocity[i][2]
        even, odd = site.pair_f(i)
        out[s, j] = z_moved(even + odd - 0.25 * rims[s, 4 + j], cz)
        even, odd = site.pair_g(i)
        out[s, 5 + j] = z_moved(even + odd - (1.0 / 9.0) * rims[s, 9 + j], cz)


def face_kernel(
    sizes,
    offsets,
    f_ref,
    g_ref,
    face_moments,
    rims,
    phi_ref,
    rise,
    fall,
    south_msg,
    north_msg,
    mate,
    direct,
    direct_short,
    across,
    across_short,
    joint,
    cross,
    minus_out,
    plus_out,
    minus_wide,
    plus_wide,
    window,
    halo,
    line,
    rim_post,
    post,
    cells,
    corners,
    raw,
    wide,
):
    layers, rows, cols = phi_ref.shape
    planes = Planes(offsets, rows, sizes)
    shear = Shear(raw, wide, rows)
    window[...] = jnp.zeros_like(window)
    for up in (True, False):
        if up:
            first, second = rise, north_msg
            near, far, start = planes.low_far, planes.low_near, planes.low_rest
        else:
            first, second = south_msg, fall
            near, far, start = planes.up_far, planes.up_near, rows - 1 - planes.up_rest
        target = minus_wide if up else plus_wide
        for k in range(window.shape[0]):
            lanes = slice(LANES * k, LANES * k + LANES)
            window[k, 8 : 8 + rows] = first[0:rows, lanes]
            window[k, 8 + rows : 8 + 2 * rows] = second[0:rows, lanes]
            target[:, lanes] = (
                near * window[k, pl.ds(start, rows + 16)]
                + far * window[k, pl.ds(start + 1, rows + 16)]
            )
    minus_out[...] = minus_wide[8 : 8 + rows]
    plus_out[...] = plus_wide[8 : 8 + rows]
    corners[0], corners[1] = corner_values(
        cells, planes, phi_ref, south_msg, north_msg, minus_wide, plus_wide
    )
    for s, (edge, chosen) in enumerate(((rows - 1, north_going), (0, south_going))):
        rim_values(
            rims,
            s,
            phi_ref,
            minus_out,
            plus_out,
            south_msg,
            north_msg,
            line,
            edge,
            chosen,
            rim_post,
        )
    for side, up in enumerate((True, False)):
        x = layers - 1 if up else 0
        delta = planes.up_jump if up else planes.low_jump
        with_halo(
            halo, phi_ref[x], south_msg[rows + x : rows + x + 1], north_msg[rows + x : rows + x + 1]
        )
        for h in range(0, rows, 8):
            span = slice(h, h + 8)
            phi_h = phi_ref[x, span]
            if up:
                minus, plus = phi_ref[x - 1, span], plus_wide[8 + h : 16 + h]
            else:
                minus, plus = minus_wide[8 + h : 16 + h], phi_ref[x + 1, span]
            site = Site(
                [face_moments[side, k, span] for k in range(4)],
                phi_h,
                minus,
                plus,
                halo[7 + h : 15 + h],
                halo[9 + h : 17 + h],
            )
            for j, i in enumerate(rising if up else falling):
                cz = lattice_velocity[i][2]
                change = lattice_weight[i] * site.jump(i, delta)
                even, odd = site.pair_f(i)
                value = even + odd - 0.25 * f_ref[i, x, span] + site.rho * change
                post[side, j, span] = z_moved(value, cz)
                even, odd = site.pair_g(i)
                value = even + odd - (1.0 / 9.0) * g_ref[i, x, span] + phi_h * change
                post[side, 5 + j, span] = z_moved(value, cz)

    part = rows // 2
    seam = 10 * part

    def hand_out(is_odd):
        for side, up in enumerate((True, False)):
            if up:
                near, far, rest = planes.up_near, planes.up_far, planes.up_rest
            else:
                near, far, rest = planes.low_near, planes.low_far, planes.low_rest
            first, second = (direct, mate) if up == is_odd else (joint, across)
            shear.clear()
            for j in range(10):
                cy = lattice_velocity[(rising if up else falling)[j % 5]][1]
                shear.put(post[side, j], up, near, far)
                corner = side + (0 if cy == 1 else 2)
                if cy == 1:
                    gate = jnp.where(rest == (0 if up else rows - 1), near, 0.0)
                    at = rows + 7 if up else rows + 8
                if cy == -1:
                    gate = jnp.where(rest == (rows - 1 if up else 0), far, 0.0)
                    at = 2 * rows + 7 if up else 2 * rows + 8
                if cy != 0:
                    shear.add_row(at, gate * corners[j // 5, corner : corner + 1])
                shear.take(up, 0, rest, cy, first, j)
                shear.take(up, 1, rest, cy, second, j)
        for j in range(10):
            mate[j, rows : rows + layers] = rim_post[1 if is_odd else 0, j]
            cross[j] = rim_post[0 if is_odd else 1, j]
            direct_short[j] = direct[j, half_rows(rows, is_odd)]
            across_short[part * j : part * j + part] = across[j, half_rows(rows, is_odd)]
            across_short[seam + 2 * j : seam + 2 * j + 2] = across[j, seam_rows(rows, not is_odd)]
        across_short[seam + 20 : seam + 24] = jnp.zeros((4, cols), f32)

    pl.when(planes.odd)(lambda: hand_out(True))
    pl.when(jnp.logical_not(planes.odd))(lambda: hand_out(False))


def bulk_kernel(
    after,
    f_ref,
    g_ref,
    phi_ref,
    minus,
    plus,
    south_msg,
    north_msg,
    mate_rim,
    cross_rim,
    next_f,
    next_g,
    wide_phi,
    halo,
):
    layers, rows, cols = phi_ref.shape
    is_odd = lax.rem(lax.axis_index("gy"), 2) == 1
    wide_phi[0] = minus[...]
    wide_phi[layers + 1] = plus[...]
    for x in range(layers):
        wide_phi[x + 1] = phi_ref[x]

    def layer(x, carry):
        with_halo(halo, phi_ref[x], south_msg[pl.ds(rows + x, 1)], north_msg[pl.ds(rows + x, 1)])
        beyond = lax.rem(x + 1, layers)
        before = lax.rem(x + layers - 1, layers)
        for h in range(0, rows, 8):
            span = slice(h, h + 8)
            phi_h = phi_ref[x, span]
            site = Site(
                moments_of(lambda i: f_ref[i, x, span]),
                phi_h,
                wide_phi[x, span],
                wide_phi[x + 2, span],
                halo[7 + h : 15 + h],
                halo[9 + h : 17 + h],
            )

            def emit(out, slot, i, value):
                cx, cy, cz = lattice_velocity[i]
                value = z_moved(value, cz)
                at = beyond if cx == 1 else before if cx == -1 else x
                if cy == 0:
                    out[i, at, span] = value
                elif cy == 1:
                    if h == 0:
                        rim = slot * 5 + north_going.index(i)
                        out[i, at, 0:1] = jnp.where(
                            is_odd, mate_rim[rim, pl.ds(rows + x, 1)], cross_rim[rim, pl.ds(x, 1)]
                        )
                    if h + 8 < rows:
                        out[i, at, h + 1 : h + 9] = value
                    else:
                        out[i, at, h + 1 : h + 8] = value[0:7]
                else:
                    if h + 8 == rows:
                        rim = slot * 5 + south_going.index(i)
                        out[i, at, rows - 1 : rows] = jnp.where(
                            is_odd, cross_rim[rim, pl.ds(x, 1)], mate_rim[rim, pl.ds(rows + x, 1)]
                        )
                    if h > 0:
                        out[i, at, h - 1 : h + 7] = value
                    else:
                        out[i, at, 0:7] = value[1:8]

            emit(next_f, 0, 0, lattice_weight[0] * site.k - 0.25 * f_ref[0, x, span])
            rest_g = (phi_h - 2.0 * site.mu - 0.5 * (phi_h * site.uu)) * (1.0 / 0.9)
            emit(next_g, 1, 0, rest_g - (1.0 / 9.0) * g_ref[0, x, span])
            for i in range(1, 19, 2):
                even, odd = site.pair_f(i)
                emit(next_f, 0, i, (even + odd) - 0.25 * f_ref[i, x, span])
                emit(next_f, 0, i + 1, (even - odd) - 0.25 * f_ref[i + 1, x, span])
                even, odd = site.pair_g(i)
                emit(next_g, 1, i, (even + odd) - (1.0 / 9.0) * g_ref[i, x, span])
                emit(next_g, 1, i + 1, (even - odd) - (1.0 / 9.0) * g_ref[i + 1, x, span])
        return carry

    lax.fori_loop(0, layers, layer, 0)


def put_faces(buf, out_f, out_g, chosen, x, sems):
    copies = [
        pltpu.make_async_copy(buf.at[5 * family + j], out.at[i, x], sems.at[5 * family + j])
        for family, out in enumerate((out_f, out_g))
        for j, i in enumerate(chosen)
    ]
    for copy in copies:
        copy.start()
    for copy in copies:
        copy.wait()


def merge_fill_kernel(
    sizes,
    offsets,
    direct,
    direct_short,
    across,
    across_short,
    f_in,
    g_in,
    f_out,
    g_out,
    buf,
    sems,
):
    layers, rows = f_out.shape[1], f_out.shape[2]
    planes = Planes(offsets, rows, sizes)
    part = rows // 2
    seam = 10 * part

    def merge(rest, up):
        is_long = rest > part
        near, other, between = half_rows(rows, up), half_rows(rows, not up), seam_rows(rows, up)

        @pl.when(is_long)
        def _():
            buf[...] = across[...]
            for j in range(10):
                buf[j, near] = buf[j, near] + direct_short[j]

        @pl.when(jnp.logical_not(is_long))
        def _():
            buf[...] = direct[...]
            for j in range(10):
                buf[j, other] = buf[j, other] + across_short[part * j : part * j + part]
                at = seam + 2 * j
                buf[j, between] = buf[j, between] + across_short[at : at + 2]

        if up:
            put_faces(buf, f_out, g_out, rising, 0, sems)
        else:
            put_faces(buf, f_out, g_out, falling, layers - 1, sems)

    pl.when(planes.odd)(lambda: merge(planes.low_rest, True))
    pl.when(jnp.logical_not(planes.odd))(lambda: merge(planes.up_rest, False))


def joint_fill_kernel(joint, f_in, g_in, f_out, g_out, sems):
    odd = lax.rem(lax.axis_index("gy"), 2) == 1
    layers = f_out.shape[1]
    pl.when(odd)(lambda: put_faces(joint, f_out, g_out, falling, layers - 1, sems))
    pl.when(jnp.logical_not(odd))(lambda: put_faces(joint, f_out, g_out, rising, 0, sems))


def on_device(momentum_dist, order_dist, offsets):
    layers, rows, cols = momentum_dist.shape[1:]
    count_x, count_y = lax.axis_size("gx"), lax.axis_size("gy")
    per_plane = count_x // 4
    half = count_y // 2

    def hop(value, target):
        perm = []
        for x in range(count_x):
            for y in range(count_y):
                tx, ty = target(x, y)
                perm.append((x * count_y + y, tx % count_x * count_y + ty % count_y))
        return lax.ppermute(value, ("gx", "gy"), perm)

    def base_up(x):
        return half if (x + 1) % per_plane == 0 else 0

    def base_low(x):
        return half if x % per_plane == 0 else 0

    def hop_parity(value, odd_up, extra):
        def target(x, y):
            if (y % 2 == 1) == odd_up:
                return (x + 1, y - base_up(x) - extra)
            return (x - 1, y + base_low(x) + extra)

        return hop(value, target)

    def hop_y(value, step):
        return hop(value, lambda x, y: (x, y + step))

    smem, vmem, anywhere = spec_of(pltpu.SMEM), spec_of(VMEM), spec_of(pl.ANY)
    plane = jax.ShapeDtypeStruct((rows, cols), f32)
    top, bottom = jnp.sum(order_dist[:, layers - 1], axis=0), jnp.sum(order_dist[:, 0], axis=0)
    rise = hop(top, lambda x, y: (x + 1, y - base_up(x)))
    fall = hop(bottom, lambda x, y: (x - 1, y + base_low(x)))

    block = jax.ShapeDtypeStruct((layers + 16, cols), f32)
    phi, to_north, to_south, order_near = pl.pallas_call(
        phi_kernel,
        out_shape=[jax.ShapeDtypeStruct((layers, rows, cols), f32)]
        + [block] * 2
        + [jax.ShapeDtypeStruct(order_dist.shape, f32)],
        in_specs=[anywhere, anywhere, vmem, vmem],
        out_specs=[vmem] * 4,
        scratch_shapes=[
            VMEM((19, 2, rows, cols), f32),
            pltpu.SemaphoreType.DMA((layers + 2,)),
        ],
        compiler_params=params(52 << 20),
        name="phi_all",
    )(momentum_dist, order_dist, top, bottom)
    to_north = jnp.concatenate([fall, to_north], 0)
    to_south = jnp.concatenate([rise, to_south], 0)
    south_msg, north_msg = hop_y(to_north, 1), hop_y(to_south, -1)

    face_moments, rims = pl.pallas_call(
        moment_kernel,
        out_shape=[
            jax.ShapeDtypeStruct((2, 4, rows, cols), f32),
            jax.ShapeDtypeStruct((2, 14, layers, cols), f32),
        ],
        in_specs=[anywhere, anywhere, vmem, vmem],
        out_specs=[vmem] * 2,
        compiler_params=params(16 << 20),
        name="moments",
    )(to_north, to_south, momentum_dist, order_near)

    part = rows // 2
    ten = jax.ShapeDtypeStruct((10, rows, cols), f32)
    ten_short = jax.ShapeDtypeStruct((10, part, cols), f32)
    ten_seam = jax.ShapeDtypeStruct((10 * part + 24, cols), f32)
    side = jax.ShapeDtypeStruct((10, layers, cols), f32)
    ten_side = jax.ShapeDtypeStruct((10, rows + layers, cols), f32)
    *outgoing, minus, plus = pl.pallas_call(
        functools.partial(face_kernel, (count_x, count_y)),
        out_shape=[ten_side, ten, ten_short, ten, ten_seam, ten, side] + [plane] * 2,
        in_specs=[smem] + [vmem] * 9,
        out_specs=[vmem] * 9,
        scratch_shapes=[
            VMEM((rows + 16, cols), f32),
            VMEM((rows + 16, cols), f32),
            VMEM((cols // LANES, 2 * rows + 16, LANES), f32),
            VMEM((rows + 16, cols), f32),
            VMEM((layers + 16, cols), f32),
            VMEM((2, 10, layers, cols), f32),
            VMEM((2, 10, rows, cols), f32),
            VMEM((11, 8, cols), f32),
            VMEM((2, 8, cols), f32),
            VMEM((cols // LANES, rows + 16, LANES), f32),
            VMEM((cols // LANES, 3 * rows + 16, LANES), f32),
        ],
        compiler_params=params(24 << 20),
        name="faces",
    )(
        offsets,
        momentum_dist,
        order_near,
        face_moments,
        rims,
        phi,
        rise,
        fall,
        south_msg,
        north_msg,
    )
    around = (phi, minus, plus, south_msg, north_msg)
    whole = jax.ShapeDtypeStruct(momentum_dist.shape, f32)

    def finish(long_planes, mate, direct, direct_short, across, across_short, joint, cross):

        def is_long(x):
            return x % per_plane == 0 and x // per_plane % 4 in long_planes

        def hop_some(value, odd_up, extra, long):
            pairs = []
            for x in range(count_x):
                for y in range(count_y):
                    up = (y % 2 == 1) == odd_up
                    tx = (x + 1 if up else x - 1) % count_x
                    if is_long(tx if up else x) != long:
                        continue
                    ty = y - base_up(x) - extra if up else y + base_low(x) + extra
                    pairs.append((x * count_y + y, tx * count_y + ty % count_y))
            return lax.ppermute(value, ("gx", "gy"), pairs)

        cross = hop(cross, lambda x, y: (x, y + 1 if y % 2 == 1 else y - 1))
        mate = hop(mate, lambda x, y: (x, y ^ 1))
        direct = hop_some(direct, True, 0, False)
        direct_short = hop_some(direct_short, True, 0, True)
        across = hop_some(across, False, 1, True)
        across_short = hop_some(across_short, False, 1, False)
        joint = joint + mate[:, :rows]
        after = joint
        joint = hop_parity(joint, False, 0)

        next_f, next_g = pl.pallas_call(
            bulk_kernel,
            out_shape=[whole, whole],
            in_specs=[anywhere] + [vmem] * 9,
            out_specs=[vmem] * 2,
            scratch_shapes=[
                VMEM((layers + 2, rows, cols), f32),
                VMEM((rows + 16, cols), f32),
            ],
            compiler_params=params(48 << 20),
            name="bulk",
        )(after, momentum_dist, order_near, *around, mate, cross)

        next_f, next_g = pl.pallas_call(
            functools.partial(merge_fill_kernel, (count_x, count_y)),
            out_shape=[whole, whole],
            in_specs=[smem] + [vmem] * 4 + [anywhere, anywhere],
            out_specs=[anywhere, anywhere],
            scratch_shapes=[VMEM((10, rows, cols), f32), pltpu.SemaphoreType.DMA((10,))],
            input_output_aliases={5: 0, 6: 1},
            compiler_params=params(24 << 20),
            name="merge_fill",
        )(offsets, direct, direct_short, across, across_short, next_f, next_g)

        return pl.pallas_call(
            joint_fill_kernel,
            out_shape=[whole, whole],
            in_specs=[vmem, anywhere, anywhere],
            out_specs=[anywhere, anywhere],
            scratch_shapes=[pltpu.SemaphoreType.DMA((10,))],
            input_output_aliases={1: 0, 2: 1},
            compiler_params=params(24 << 20),
            name="joint_fill",
        )(joint, next_f, next_g)

    is_long = [(offsets[k] - half * rows > part).astype(jnp.int32) for k in (1, 2)]
    branches = [
        functools.partial(finish, {3} | ({1} if k & 2 else set()) | ({2} if k & 1 else set()))
        for k in range(4)
    ]
    return lax.switch(2 * is_long[0] + is_long[1], branches, *outgoing)


def solution(mesh):
    return jax.shard_map(
        on_device,
        mesh=mesh,
        in_specs=(P(None, "gx", "gy", None), P(None, "gx", "gy", None), P()),
        out_specs=(P(None, "gx", "gy", None), P(None, "gx", "gy", None)),
        check_vma=False,
    )
```

```python
import functools

import jax
import jax.numpy as jnp
from jax import lax
from jax.experimental import pallas as pl
from jax.experimental.pallas import tpu as pltpu
from jax.sharding import PartitionSpec as P

lattice_velocity = [
    (0, 0, 0),
    (1, 0, 0),
    (-1, 0, 0),
    (0, 1, 0),
    (0, -1, 0),
    (0, 0, 1),
    (0, 0, -1),
    (1, 1, 0),
    (-1, -1, 0),
    (1, -1, 0),
    (-1, 1, 0),
    (1, 0, 1),
    (-1, 0, -1),
    (1, 0, -1),
    (-1, 0, 1),
    (0, 1, 1),
    (0, -1, -1),
    (0, 1, -1),
    (0, -1, 1),
]
lattice_weight = [1.0 / 3.0] + [1.0 / 18.0] * 6 + [1.0 / 36.0] * 12
plane_speed = 0.04
rising = [1, 7, 9, 11, 13]
falling = [2, 8, 10, 12, 14]
north_going = [i for i in range(19) if lattice_velocity[i][1] == 1]
south_going = [i for i in range(19) if lattice_velocity[i][1] == -1]
f32 = jnp.float32
VMEM = pltpu.VMEM
LANES = 128


def z_moved(value, step):
    if step == 0:
        return value
    return pltpu.roll(value, step % value.shape[-1], value.ndim - 1)


def spec_of(space):
    return pl.BlockSpec(memory_space=space)


def params(limit):
    return pltpu.CompilerParams(vmem_limit_bytes=limit)


def along(parts, c):
    total = None
    for sign, part in zip(c, parts):
        if sign == 0:
            continue
        if total is None:
            total = part if sign > 0 else -part
        else:
            total = total + part if sign > 0 else total - part
    return total


def signed_sum(load, axis):
    ups = [i for i in range(19) if lattice_velocity[i][axis] == 1]
    downs = [i for i in range(19) if lattice_velocity[i][axis] == -1]
    total = load(ups[0]) - load(downs[0])
    for i, j in zip(ups[1:], downs[1:]):
        total = total + (load(i) - load(j))
    return total


def moments_of(load):
    rho = load(0)
    for i in range(1, 19):
        rho = rho + load(i)
    return [rho] + [signed_sum(load, axis) for axis in range(3)]


class Site:
    def __init__(self, moments, phi, minus, plus, south, north):
        rho, momentum = moments[0], moments[1:]
        lower, upper = z_moved(phi, 1), z_moved(phi, -1)
        lap = (plus + minus) + (north + south) + (upper + lower) - 6.0 * phi
        mu = phi * (0.0625 * (phi * phi) - 0.0625) - 0.04 * lap
        half_mu = 0.5 * mu
        force = [half_mu * (plus - minus), half_mu * (north - south), half_mu * (upper - lower)]
        inverse = 1.0 / rho
        u = [(j + 0.5 * k) * inverse for j, k in zip(momentum, force)]
        uu = u[0] * u[0] + u[1] * u[1] + u[2] * u[2]
        uf = u[0] * force[0] + u[1] * force[1] + u[2] * force[2]
        self.rho, self.phi, self.mu, self.u, self.force, self.uu = rho, phi, mu, u, force, uu
        self.r = 1.25 * rho
        self.k = self.r * (1.0 - 1.5 * uu) - 1.125 * uf
        self.g_scale = phi * (1.0 / 0.9)
        self.g_base = (3.0 / 0.9) * mu - 1.5 * (self.g_scale * uu)

    def pair_f(self, i):
        p, q = along(self.u, lattice_velocity[i]), along(self.force, lattice_velocity[i])
        w = lattice_weight[i]
        rp = self.r * p
        even = w * (self.k + p * (4.5 * rp + 3.375 * q))
        odd = (3.0 * w) * rp + (1.125 * w) * q
        return even, odd

    def pair_g(self, i):
        p = along(self.u, lattice_velocity[i])
        w = lattice_weight[i]
        gp = self.g_scale * p
        return w * (self.g_base + 4.5 * (gp * p)), (3.0 * w) * gp

    def jump(self, i, delta):
        cy = lattice_velocity[i][1]
        uy = self.u[1]
        if cy == 0:
            return delta * (-3.0 * uy) - (1.5 * delta * delta)
        p = along(self.u, lattice_velocity[i])
        return delta * (3.0 * cy + (9.0 * cy) * p - 3.0 * uy) + (3.0 * delta * delta)


class Shear:
    def __init__(self, raw, wide, rows):
        self.raw, self.wide, self.rows = raw, wide, rows

    def clear(self):
        self.raw[...] = jnp.zeros_like(self.raw)
        self.wide[...] = jnp.zeros_like(self.wide)

    def put(self, value, up, near, far):
        n = self.rows
        for k in range(self.raw.shape[0]):
            self.raw[k, 8 : 8 + n] = value[:, LANES * k : LANES * k + LANES]
        for k in range(self.raw.shape[0]):
            if up:
                self.wide[k, n : n + n + 8] = (
                    near * self.raw[k, 0 : n + 8] + far * self.raw[k, 1 : n + 9]
                )
            else:
                self.wide[k, n + 8 : n + n + 16] = (
                    near * self.raw[k, 7 : n + 15] + far * self.raw[k, 8 : n + 16]
                )

    def add_row(self, at, row):
        for k in range(self.raw.shape[0]):
            lanes = slice(LANES * k, LANES * k + LANES)
            self.wide[k, at : at + 1] = self.wide[k, at : at + 1] + row[:, lanes]

    def take(self, up, block, rest, cy, ref, j):
        n = self.rows
        if up:
            start = (n + 8 if block == 0 else 8) + rest - cy
        else:
            start = (n + 8 if block == 0 else n + n + 8) - rest - cy
        for k in range(self.raw.shape[0]):
            ref[j, 0:n, LANES * k : LANES * k + LANES] = self.wide[k, pl.ds(start, n)]


class Planes:
    def __init__(self, offsets, rows, sizes):
        count_x, count_y = sizes
        per_plane, half = count_x // 4, count_y // 2
        a = lax.axis_index("gx")
        self.odd = lax.rem(lax.axis_index("gy"), 2) == 1

        def plane_of(column):
            is_plane = lax.rem(column, per_plane) == 0
            plane = lax.rem(lax.div(column, per_plane), 4)
            rest = jnp.where(is_plane, jnp.clip(offsets[plane] - half * rows, 0, rows - 1), 0)
            return is_plane, (2.0 * plane.astype(f32) + 1.0) * 0.125, rest

        up_is, up_part, self.up_rest = plane_of(lax.rem(a + 1, count_x))
        low_is, low_part, self.low_rest = plane_of(a)
        self.up_near = jnp.where(up_is, 1.0 - up_part, 1.0)
        self.up_far = jnp.where(up_is, up_part, 0.0)
        self.low_near = jnp.where(low_is, low_part, 0.0)
        self.low_far = jnp.where(low_is, 1.0 - low_part, 1.0)
        self.up_jump = jnp.where(up_is, -plane_speed, 0.0)
        self.low_jump = jnp.where(low_is, plane_speed, 0.0)


def order_sum(load):
    total = load(0)
    for i in range(1, 19):
        total = total + load(i)
    return total


def phi_kernel(f_ref, g_ref, top, bottom, phi_ref, to_north, to_south, gbuf, fbuf, sems):
    layers, rows = phi_ref.shape[0], phi_ref.shape[1]
    faces = (layers - 1, 0)
    f_copies = [
        pltpu.make_async_copy(f_ref.at[:, x], fbuf.at[:, s], sems.at[layers + s])
        for s, x in enumerate(faces)
    ]
    g_copies = [
        pltpu.make_async_copy(g_ref.at[:, x], gbuf.at[:, x], sems.at[x]) for x in range(layers)
    ]
    for copy in f_copies + g_copies:
        copy.start()
    phi_ref[layers - 1] = top[...]
    phi_ref[0] = bottom[...]
    edges = ((to_north, rows - 1, rows - 2, (7, 10)), (to_south, 0, 1, (9, 8)))
    for s, x in enumerate(faces):
        f_copies[s].wait()
        for out, edge, inner, chosen in edges:
            out[layers + s : layers + s + 1] = phi_ref[x, inner : inner + 1]
            at = layers + 2 + 6 * s
            out[at : at + 1] = fbuf[chosen[s], s, edge : edge + 1]
            for k, part in enumerate(moments_of(lambda i: fbuf[i, s, edge : edge + 1])):
                out[at + 2 + k : at + 3 + k] = part
    for x in range(layers):
        g_copies[x].wait()
        if 0 < x < layers - 1:
            phi_ref[x] = order_sum(lambda i: gbuf[i, x])
        to_north[x : x + 1] = phi_ref[x, rows - 1 : rows]
        to_south[x : x + 1] = phi_ref[x, 0:1]
    for s, x in enumerate(faces):
        for out, edge, inner, chosen in edges:
            at = layers + 3 + 6 * s
            out[at : at + 1] = gbuf[chosen[s], x, edge : edge + 1]
    for out in (to_north, to_south):
        out[layers + 14 : layers + 16] = jnp.zeros((2, out.shape[1]), f32)


def with_halo(ref, layer, below, above):
    rows = layer.shape[0]
    ref[8 : 8 + rows] = layer
    ref[7:8] = below
    ref[8 + rows : 9 + rows] = above


def corner_values(cells, planes, phi_ref, south_msg, north_msg, minus_wide, plus_wide):
    layers, rows, cols = phi_ref.shape
    cells[...] = jnp.ones_like(cells)
    for row in range(4):
        msg = south_msg if row < 2 else north_msg
        x = layers - 1 if row % 2 == 0 else 0
        beside = rows + (layers - 2 if row % 2 == 0 else 1)
        wide_row = 7 if row < 2 else rows + 8
        at = rows + layers
        first = at + 2 + 6 * (row % 2)
        far_phi = msg[at + row % 2 : at + row % 2 + 1]
        own_phi = phi_ref[x, 0:1] if row < 2 else phi_ref[x, rows - 1 : rows]
        parts = [msg[first + k : first + k + 1] for k in range(6)]
        parts.append(msg[rows + x : rows + x + 1])
        if row % 2 == 0:
            parts += [msg[beside : beside + 1], plus_wide[wide_row : wide_row + 1]]
        else:
            parts += [minus_wide[wide_row : wide_row + 1], msg[beside : beside + 1]]
        parts += [far_phi, own_phi] if row < 2 else [own_phi, far_phi]
        for k, part in enumerate(parts):
            cells[k, row : row + 1] = part
    place = lax.broadcasted_iota(jnp.int32, (8, cols), 0)
    is_top = (place == 0) | (place == 2)
    sx = jnp.where(is_top, 1.0, -1.0)
    sy = jnp.where(place < 2, 1.0, -1.0)
    delta = jnp.where(is_top, planes.up_jump, planes.low_jump)
    site = Site([cells[k] for k in range(2, 6)], *[cells[k] for k in range(6, 11)])
    w = lattice_weight[7]
    p = sx * site.u[0] + sy * site.u[1]
    q = sx * site.force[0] + sy * site.force[1]
    change = delta * (3.0 * sy + 9.0 * (sy * p) - 3.0 * site.u[1]) + 3.0 * (delta * delta)
    rp, gp = site.r * p, site.g_scale * p
    f_post = w * (site.k + p * (4.5 * rp + 3.375 * q) + 3.0 * rp + 1.125 * q + site.rho * change)
    g_post = w * (site.g_base + 4.5 * (gp * p) + 3.0 * gp + site.phi * change)
    return f_post - 0.25 * cells[0], g_post - (1.0 / 9.0) * cells[1]


def moment_kernel(
    base,
    after_north,
    after_south,
    offsets,
    f_ref,
    g_ref,
    phi_ref,
    faces,
    raw_north,
    raw_south,
    index,
):
    layers, rows = f_ref.shape[1], f_ref.shape[2]
    is_long = [(offsets[k] - base > rows // 2).astype(jnp.int32) for k in (1, 2)]
    index[0] = 2 * is_long[0] + is_long[1]
    for s, x in enumerate((layers - 1, 0)):
        for k, part in enumerate(moments_of(lambda i: f_ref[i, x])):
            faces[s, k] = part
    for out, edge, inner, chosen in (
        (raw_north, rows - 1, rows - 2, north_going),
        (raw_south, 0, 1, south_going),
    ):
        parts = moments_of(lambda i: f_ref[i, :, edge, :])
        parts += [f_ref[i, :, edge, :] for i in chosen] + [g_ref[i, :, edge, :] for i in chosen]
        parts.append(phi_ref[:, inner, :])
        for k, part in enumerate(parts):
            out[layers * k : layers * k + layers] = part


def half_rows(rows, first):
    return slice(0, rows // 2) if first else slice(rows // 2, rows)


def seam_rows(rows, up):
    return slice(rows // 2 - 2, rows // 2) if up else slice(rows // 2, rows // 2 + 2)


def rim_values(planes, raw, msg, phi_ref, minus_wide, plus_wide, line, south, out):
    layers, rows, cols = phi_ref.shape

    def piece(k):
        return raw[layers * k : layers * k + layers]

    extra = 15 * layers
    beside, relayed = raw[extra : extra + 1], raw[extra + 1 : extra + 2]
    row = 7 if south else rows + 8
    minus, plus = minus_wide[row : row + 1], plus_wide[row : row + 1]
    low_rest, up_rest = planes.low_rest, planes.up_rest
    if south:
        minus = minus + jnp.where(low_rest == 0, planes.low_far, 0.0) * beside
        plus = plus + jnp.where(up_rest == rows - 1, planes.up_far, 0.0) * relayed
    else:
        minus = minus + jnp.where(low_rest == rows - 1, planes.low_near, 0.0) * relayed
        plus = plus + jnp.where(up_rest == 0, planes.up_near, 0.0) * beside
    phi = msg[rows : rows + layers]
    with_halo(line, phi, minus, plus)
    if south:
        below, above = piece(14), phi_ref[:, 0, :]
    else:
        below, above = phi_ref[:, rows - 1, :], piece(14)
    site = Site(
        [piece(k) for k in range(4)],
        phi,
        line[7 : 7 + layers],
        line[9 : 9 + layers],
        below,
        above,
    )
    for j, i in enumerate(north_going if south else south_going):
        cz = lattice_velocity[i][2]
        even, odd = site.pair_f(i)
        out[j] = z_moved(even + odd - 0.25 * piece(4 + j), cz)
        even, odd = site.pair_g(i)
        out[5 + j] = z_moved(even + odd - (1.0 / 9.0) * piece(9 + j), cz)


def face_kernel(
    sizes,
    offsets,
    f_ref,
    g_ref,
    face_moments,
    phi_ref,
    rise,
    fall,
    south_msg,
    north_msg,
    mate,
    direct,
    direct_short,
    across,
    across_short,
    joint,
    minus_wide,
    plus_wide,
    window,
    halo,
    post,
    cells,
    corners,
    raw,
    wide,
):
    layers, rows, cols = phi_ref.shape
    planes = Planes(offsets, rows, sizes)
    shear = Shear(raw, wide, rows)
    window[...] = jnp.zeros_like(window)
    for up in (True, False):
        if up:
            first, second = rise, north_msg
            near, far, start = planes.low_far, planes.low_near, planes.low_rest
        else:
            first, second = south_msg, fall
            near, far, start = planes.up_far, planes.up_near, rows - 1 - planes.up_rest
        target = minus_wide if up else plus_wide
        for k in range(window.shape[0]):
            lanes = slice(LANES * k, LANES * k + LANES)
            window[k, 8 : 8 + rows] = first[0:rows, lanes]
            window[k, 8 + rows : 8 + 2 * rows] = second[0:rows, lanes]
            target[:, lanes] = (
                near * window[k, pl.ds(start, rows + 16)]
                + far * window[k, pl.ds(start + 1, rows + 16)]
            )
    corners[0], corners[1] = corner_values(
        cells, planes, phi_ref, south_msg, north_msg, minus_wide, plus_wide
    )
    for side, up in enumerate((True, False)):
        x = layers - 1 if up else 0
        delta = planes.up_jump if up else planes.low_jump
        with_halo(
            halo, phi_ref[x], south_msg[rows + x : rows + x + 1], north_msg[rows + x : rows + x + 1]
        )
        for h in range(0, rows, 8):
            span = slice(h, h + 8)
            phi_h = phi_ref[x, span]
            if up:
                minus, plus = phi_ref[x - 1, span], plus_wide[8 + h : 16 + h]
            else:
                minus, plus = minus_wide[8 + h : 16 + h], phi_ref[x + 1, span]
            site = Site(
                [face_moments[side, k, span] for k in range(4)],
                phi_h,
                minus,
                plus,
                halo[7 + h : 15 + h],
                halo[9 + h : 17 + h],
            )
            for j, i in enumerate(rising if up else falling):
                cz = lattice_velocity[i][2]
                change = lattice_weight[i] * site.jump(i, delta)
                even, odd = site.pair_f(i)
                value = even + odd - 0.25 * f_ref[i, x, span] + site.rho * change
                post[side, j, span] = z_moved(value, cz)
                even, odd = site.pair_g(i)
                value = even + odd - (1.0 / 9.0) * g_ref[i, x, span] + phi_h * change
                post[side, 5 + j, span] = z_moved(value, cz)

    part = rows // 2
    seam = 10 * part

    def hand_out(is_odd):
        for side, up in enumerate((True, False)):
            if up:
                near, far, rest = planes.up_near, planes.up_far, planes.up_rest
            else:
                near, far, rest = planes.low_near, planes.low_far, planes.low_rest
            first, second = (direct, mate) if up == is_odd else (joint, across)
            shear.clear()
            for j in range(10):
                cy = lattice_velocity[(rising if up else falling)[j % 5]][1]
                shear.put(post[side, j], up, near, far)
                corner = side + (0 if cy == 1 else 2)
                if cy == 1:
                    gate = jnp.where(rest == (0 if up else rows - 1), near, 0.0)
                    at = rows + 7 if up else rows + 8
                if cy == -1:
                    gate = jnp.where(rest == (rows - 1 if up else 0), far, 0.0)
                    at = 2 * rows + 7 if up else 2 * rows + 8
                if cy != 0:
                    shear.add_row(at, gate * corners[j // 5, corner : corner + 1])
                shear.take(up, 0, rest, cy, first, j)
                shear.take(up, 1, rest, cy, second, j)
        for j in range(10):
            direct_short[j] = direct[j, half_rows(rows, is_odd)]
            across_short[part * j : part * j + part] = across[j, half_rows(rows, is_odd)]
            across_short[seam + 2 * j : seam + 2 * j + 2] = across[j, seam_rows(rows, not is_odd)]
        across_short[seam + 20 : seam + 24] = jnp.zeros((4, cols), f32)

    pl.when(planes.odd)(lambda: hand_out(True))
    pl.when(jnp.logical_not(planes.odd))(lambda: hand_out(False))


def bulk_kernel(
    sizes,
    after,
    offsets,
    f_ref,
    g_ref,
    phi_ref,
    minus,
    plus,
    south_msg,
    north_msg,
    south_raw,
    north_raw,
    next_f,
    next_g,
    wide_phi,
    halo,
    line,
    south_rim,
    north_rim,
):
    layers, rows, cols = phi_ref.shape
    planes = Planes(offsets, rows, sizes)
    rim_values(planes, south_raw, south_msg, phi_ref, minus, plus, line, True, south_rim)
    rim_values(planes, north_raw, north_msg, phi_ref, minus, plus, line, False, north_rim)
    wide_phi[0] = minus[8 : 8 + rows]
    wide_phi[layers + 1] = plus[8 : 8 + rows]
    for x in range(layers):
        wide_phi[x + 1] = phi_ref[x]

    def layer(x, carry):
        with_halo(halo, phi_ref[x], south_msg[pl.ds(rows + x, 1)], north_msg[pl.ds(rows + x, 1)])
        beyond = lax.rem(x + 1, layers)
        before = lax.rem(x + layers - 1, layers)
        for h in range(0, rows, 8):
            span = slice(h, h + 8)
            phi_h = phi_ref[x, span]
            site = Site(
                moments_of(lambda i: f_ref[i, x, span]),
                phi_h,
                wide_phi[x, span],
                wide_phi[x + 2, span],
                halo[7 + h : 15 + h],
                halo[9 + h : 17 + h],
            )

            def emit(out, slot, i, value):
                cx, cy, cz = lattice_velocity[i]
                value = z_moved(value, cz)
                at = beyond if cx == 1 else before if cx == -1 else x
                if cy == 0:
                    out[i, at, span] = value
                elif cy == 1:
                    if h == 0:
                        rim = slot * 5 + north_going.index(i)
                        out[i, at, 0:1] = south_rim[rim, pl.ds(x, 1)]
                    if h + 8 < rows:
                        out[i, at, h + 1 : h + 9] = value
                    else:
                        out[i, at, h + 1 : h + 8] = value[0:7]
                else:
                    if h + 8 == rows:
                        rim = slot * 5 + south_going.index(i)
                        out[i, at, rows - 1 : rows] = north_rim[rim, pl.ds(x, 1)]
                    if h > 0:
                        out[i, at, h - 1 : h + 7] = value
                    else:
                        out[i, at, 0:7] = value[1:8]

            emit(next_f, 0, 0, lattice_weight[0] * site.k - 0.25 * f_ref[0, x, span])
            rest_g = (phi_h - 2.0 * site.mu - 0.5 * (phi_h * site.uu)) * (1.0 / 0.9)
            emit(next_g, 1, 0, rest_g - (1.0 / 9.0) * g_ref[0, x, span])
            for i in range(1, 19, 2):
                even, odd = site.pair_f(i)
                emit(next_f, 0, i, (even + odd) - 0.25 * f_ref[i, x, span])
                emit(next_f, 0, i + 1, (even - odd) - 0.25 * f_ref[i + 1, x, span])
                even, odd = site.pair_g(i)
                emit(next_g, 1, i, (even + odd) - (1.0 / 9.0) * g_ref[i, x, span])
                emit(next_g, 1, i + 1, (even - odd) - (1.0 / 9.0) * g_ref[i + 1, x, span])
        return carry

    lax.fori_loop(0, layers, layer, 0)


def put_faces(buf, out_f, out_g, chosen, x, sems):
    copies = [
        pltpu.make_async_copy(buf.at[5 * family + j], out.at[i, x], sems.at[5 * family + j])
        for family, out in enumerate((out_f, out_g))
        for j, i in enumerate(chosen)
    ]
    for copy in copies:
        copy.start()
    for copy in copies:
        copy.wait()


def merge_fill_kernel(
    sizes,
    offsets,
    direct,
    direct_short,
    across,
    across_short,
    f_in,
    g_in,
    f_out,
    g_out,
    buf,
    sems,
):
    layers, rows = f_out.shape[1], f_out.shape[2]
    planes = Planes(offsets, rows, sizes)
    part = rows // 2
    seam = 10 * part

    def merge(rest, up):
        is_long = rest > part
        near, other, between = half_rows(rows, up), half_rows(rows, not up), seam_rows(rows, up)

        @pl.when(is_long)
        def _():
            buf[...] = across[...]
            for j in range(10):
                buf[j, near] = buf[j, near] + direct_short[j]

        @pl.when(jnp.logical_not(is_long))
        def _():
            buf[...] = direct[...]
            for j in range(10):
                buf[j, other] = buf[j, other] + across_short[part * j : part * j + part]
                at = seam + 2 * j
                buf[j, between] = buf[j, between] + across_short[at : at + 2]

        if up:
            put_faces(buf, f_out, g_out, rising, 0, sems)
        else:
            put_faces(buf, f_out, g_out, falling, layers - 1, sems)

    pl.when(planes.odd)(lambda: merge(planes.low_rest, True))
    pl.when(jnp.logical_not(planes.odd))(lambda: merge(planes.up_rest, False))


def joint_fill_kernel(joint, f_in, g_in, f_out, g_out, sems):
    odd = lax.rem(lax.axis_index("gy"), 2) == 1
    layers = f_out.shape[1]
    pl.when(odd)(lambda: put_faces(joint, f_out, g_out, falling, layers - 1, sems))
    pl.when(jnp.logical_not(odd))(lambda: put_faces(joint, f_out, g_out, rising, 0, sems))


def on_device(momentum_dist, order_dist, offsets):
    layers, rows, cols = momentum_dist.shape[1:]
    count_x, count_y = lax.axis_size("gx"), lax.axis_size("gy")
    per_plane = count_x // 4
    half = count_y // 2

    def hop(value, target):
        perm = []
        for x in range(count_x):
            for y in range(count_y):
                tx, ty = target(x, y)
                perm.append((x * count_y + y, tx % count_x * count_y + ty % count_y))
        return lax.ppermute(value, ("gx", "gy"), perm)

    def base_up(x):
        return half if (x + 1) % per_plane == 0 else 0

    def base_low(x):
        return half if x % per_plane == 0 else 0

    def hop_parity(value, odd_up, extra):
        def target(x, y):
            if (y % 2 == 1) == odd_up:
                return (x + 1, y - base_up(x) - extra)
            return (x - 1, y + base_low(x) + extra)

        return hop(value, target)

    def hop_y(value, step):
        return hop(value, lambda x, y: (x, y + step))

    smem, vmem, anywhere = spec_of(pltpu.SMEM), spec_of(VMEM), spec_of(pl.ANY)
    plane = jax.ShapeDtypeStruct((rows, cols), f32)
    top, bottom = jnp.sum(order_dist[:, layers - 1], axis=0), jnp.sum(order_dist[:, 0], axis=0)
    rise = hop(top, lambda x, y: (x + 1, y - base_up(x)))
    fall = hop(bottom, lambda x, y: (x - 1, y + base_low(x)))

    part = rows // 2
    block = jax.ShapeDtypeStruct((layers + 16, cols), f32)
    phi, to_north, to_south, order_near = pl.pallas_call(
        phi_kernel,
        out_shape=[jax.ShapeDtypeStruct((layers, rows, cols), f32)]
        + [block] * 2
        + [jax.ShapeDtypeStruct(order_dist.shape, f32)],
        in_specs=[anywhere, anywhere, vmem, vmem],
        out_specs=[vmem] * 4,
        scratch_shapes=[
            VMEM((19, 2, rows, cols), f32),
            pltpu.SemaphoreType.DMA((layers + 2,)),
        ],
        compiler_params=params(52 << 20),
        name="phi_all",
    )(momentum_dist, order_dist, top, bottom)
    to_north = jnp.concatenate([fall, to_north], 0)
    to_south = jnp.concatenate([rise, to_south], 0)
    south_msg, north_msg = hop_y(to_north, 1), hop_y(to_south, -1)

    raw = jax.ShapeDtypeStruct((15 * layers, cols), f32)
    face_moments, raw_north, raw_south, index = pl.pallas_call(
        functools.partial(moment_kernel, half * rows),
        out_shape=[
            jax.ShapeDtypeStruct((2, 4, rows, cols), f32),
            raw,
            raw,
            jax.ShapeDtypeStruct((1,), jnp.int32),
        ],
        in_specs=[anywhere, anywhere, smem] + [vmem] * 3,
        out_specs=[vmem] * 3 + [smem],
        compiler_params=params(16 << 20),
        name="moments",
    )(to_north, to_south, offsets, momentum_dist, order_near, phi)
    blank = jnp.zeros((6, cols), f32)
    raw_north = jnp.concatenate([raw_north, rise[rows - 1 :], south_msg[rows - 1 : rows], blank], 0)
    raw_south = jnp.concatenate([raw_south, fall[:1], north_msg[:1], blank], 0)

    ten = jax.ShapeDtypeStruct((10, rows, cols), f32)
    ten_short = jax.ShapeDtypeStruct((10, part, cols), f32)
    ten_seam = jax.ShapeDtypeStruct((10 * part + 24, cols), f32)
    wide = jax.ShapeDtypeStruct((rows + 16, cols), f32)
    whole = jax.ShapeDtypeStruct(momentum_dist.shape, f32)

    def finish(long_planes):

        def is_long(x):
            return x % per_plane == 0 and x // per_plane % 4 in long_planes

        def hop_some(value, odd_up, extra, long):
            pairs = []
            for x in range(count_x):
                for y in range(count_y):
                    up = (y % 2 == 1) == odd_up
                    tx = (x + 1 if up else x - 1) % count_x
                    if is_long(tx if up else x) != long:
                        continue
                    ty = y - base_up(x) - extra if up else y + base_low(x) + extra
                    pairs.append((x * count_y + y, tx * count_y + ty % count_y))
            return lax.ppermute(value, ("gx", "gy"), pairs)

        south_raw, north_raw = hop_y(raw_north, 1), hop_y(raw_south, -1)
        mate, direct, direct_short, across, across_short, joint, minus, plus = pl.pallas_call(
            functools.partial(face_kernel, (count_x, count_y)),
            out_shape=[ten, ten, ten_short, ten, ten_seam, ten] + [wide] * 2,
            in_specs=[smem] + [vmem] * 8,
            out_specs=[vmem] * 8,
            scratch_shapes=[
                VMEM((cols // LANES, 2 * rows + 16, LANES), f32),
                VMEM((rows + 16, cols), f32),
                VMEM((2, 10, rows, cols), f32),
                VMEM((11, 8, cols), f32),
                VMEM((2, 8, cols), f32),
                VMEM((cols // LANES, rows + 16, LANES), f32),
                VMEM((cols // LANES, 3 * rows + 16, LANES), f32),
            ],
            compiler_params=params(24 << 20),
            name="faces",
        )(
            offsets,
            momentum_dist,
            order_near,
            face_moments,
            phi,
            rise,
            fall,
            south_msg,
            north_msg,
        )
        around = (phi, minus, plus, south_msg, north_msg)
        mate = hop(mate, lambda x, y: (x, y ^ 1))
        direct = hop_some(direct, True, 0, False)
        direct_short = hop_some(direct_short, True, 0, True)
        across = hop_some(across, False, 1, True)
        across_short = hop_some(across_short, False, 1, False)
        joint = joint + mate
        after = joint
        joint = hop_parity(joint, False, 0)

        next_f, next_g = pl.pallas_call(
            functools.partial(bulk_kernel, (count_x, count_y)),
            out_shape=[whole, whole],
            in_specs=[anywhere, smem] + [vmem] * 9,
            out_specs=[vmem] * 2,
            scratch_shapes=[
                VMEM((layers + 2, rows, cols), f32),
                VMEM((rows + 16, cols), f32),
                VMEM((layers + 16, cols), f32),
                VMEM((10, layers, cols), f32),
                VMEM((10, layers, cols), f32),
            ],
            compiler_params=params(48 << 20),
            name="bulk",
        )(after, offsets, momentum_dist, order_near, *around, south_raw, north_raw)

        next_f, next_g = pl.pallas_call(
            functools.partial(merge_fill_kernel, (count_x, count_y)),
            out_shape=[whole, whole],
            in_specs=[smem] + [vmem] * 4 + [anywhere, anywhere],
            out_specs=[anywhere, anywhere],
            scratch_shapes=[VMEM((10, rows, cols), f32), pltpu.SemaphoreType.DMA((10,))],
            input_output_aliases={5: 0, 6: 1},
            compiler_params=params(24 << 20),
            name="merge_fill",
        )(offsets, direct, direct_short, across, across_short, next_f, next_g)

        return pl.pallas_call(
            joint_fill_kernel,
            out_shape=[whole, whole],
            in_specs=[vmem, anywhere, anywhere],
            out_specs=[anywhere, anywhere],
            scratch_shapes=[pltpu.SemaphoreType.DMA((10,))],
            input_output_aliases={1: 0, 2: 1},
            compiler_params=params(24 << 20),
            name="joint_fill",
        )(joint, next_f, next_g)

    branches = [
        functools.partial(finish, {3} | ({1} if k & 2 else set()) | ({2} if k & 1 else set()))
        for k in range(4)
    ]
    return lax.switch(index[0], branches)


def solution(mesh):
    return jax.shard_map(
        on_device,
        mesh=mesh,
        in_specs=(P(None, "gx", "gy", None), P(None, "gx", "gy", None), P()),
        out_specs=(P(None, "gx", "gy", None), P(None, "gx", "gy", None)),
        check_vma=False,
    )
```

```python
import functools

import jax
import jax.numpy as jnp
from jax import lax
from jax.experimental import pallas as pl
from jax.experimental.pallas import tpu as pltpu
from jax.sharding import PartitionSpec as P

lattice_velocity = [
    (0, 0, 0),
    (1, 0, 0),
    (-1, 0, 0),
    (0, 1, 0),
    (0, -1, 0),
    (0, 0, 1),
    (0, 0, -1),
    (1, 1, 0),
    (-1, -1, 0),
    (1, -1, 0),
    (-1, 1, 0),
    (1, 0, 1),
    (-1, 0, -1),
    (1, 0, -1),
    (-1, 0, 1),
    (0, 1, 1),
    (0, -1, -1),
    (0, 1, -1),
    (0, -1, 1),
]
lattice_weight = [1.0 / 3.0] + [1.0 / 18.0] * 6 + [1.0 / 36.0] * 12
plane_speed = 0.04
rising = [1, 7, 9, 11, 13]
falling = [2, 8, 10, 12, 14]
north_going = [i for i in range(19) if lattice_velocity[i][1] == 1]
south_going = [i for i in range(19) if lattice_velocity[i][1] == -1]
f32 = jnp.float32
VMEM = pltpu.VMEM
LANES = 128


def z_moved(value, step):
    if step == 0:
        return value
    return pltpu.roll(value, step % value.shape[-1], value.ndim - 1)


def spec_of(space):
    return pl.BlockSpec(memory_space=space)


def params(limit):
    return pltpu.CompilerParams(vmem_limit_bytes=limit)


def along(parts, c):
    total = None
    for sign, part in zip(c, parts):
        if sign == 0:
            continue
        if total is None:
            total = part if sign > 0 else -part
        else:
            total = total + part if sign > 0 else total - part
    return total


def signed_sum(load, axis):
    ups = [i for i in range(19) if lattice_velocity[i][axis] == 1]
    downs = [i for i in range(19) if lattice_velocity[i][axis] == -1]
    total = load(ups[0]) - load(downs[0])
    for i, j in zip(ups[1:], downs[1:]):
        total = total + (load(i) - load(j))
    return total


def moments_of(load):
    rho = load(0)
    for i in range(1, 19):
        rho = rho + load(i)
    return [rho] + [signed_sum(load, axis) for axis in range(3)]


class Site:
    def __init__(self, moments, phi, minus, plus, south, north):
        rho, momentum = moments[0], moments[1:]
        lower, upper = z_moved(phi, 1), z_moved(phi, -1)
        lap = (plus + minus) + (north + south) + (upper + lower) - 6.0 * phi
        mu = phi * (0.0625 * (phi * phi) - 0.0625) - 0.04 * lap
        half_mu = 0.5 * mu
        force = [half_mu * (plus - minus), half_mu * (north - south), half_mu * (upper - lower)]
        inverse = 1.0 / rho
        u = [(j + 0.5 * k) * inverse for j, k in zip(momentum, force)]
        uu = u[0] * u[0] + u[1] * u[1] + u[2] * u[2]
        uf = u[0] * force[0] + u[1] * force[1] + u[2] * force[2]
        self.rho, self.phi, self.mu, self.u, self.force, self.uu = rho, phi, mu, u, force, uu
        self.r = 1.25 * rho
        self.k = self.r * (1.0 - 1.5 * uu) - 1.125 * uf
        self.g_scale = phi * (1.0 / 0.9)
        self.g_base = (3.0 / 0.9) * mu - 1.5 * (self.g_scale * uu)

    def pair_f(self, i):
        p, q = along(self.u, lattice_velocity[i]), along(self.force, lattice_velocity[i])
        w = lattice_weight[i]
        rp = self.r * p
        even = w * (self.k + p * (4.5 * rp + 3.375 * q))
        odd = (3.0 * w) * rp + (1.125 * w) * q
        return even, odd

    def pair_g(self, i):
        p = along(self.u, lattice_velocity[i])
        w = lattice_weight[i]
        gp = self.g_scale * p
        return w * (self.g_base + 4.5 * (gp * p)), (3.0 * w) * gp

    def jump(self, i, delta):
        cy = lattice_velocity[i][1]
        uy = self.u[1]
        if cy == 0:
            return delta * (-3.0 * uy) - (1.5 * delta * delta)
        p = along(self.u, lattice_velocity[i])
        return delta * (3.0 * cy + (9.0 * cy) * p - 3.0 * uy) + (3.0 * delta * delta)


class Shear:
    def __init__(self, raw, wide, rows):
        self.raw, self.wide, self.rows = raw, wide, rows

    def clear(self):
        self.raw[...] = jnp.zeros_like(self.raw)
        self.wide[...] = jnp.zeros_like(self.wide)

    def put(self, value, up, near, far):
        n = self.rows
        for k in range(self.raw.shape[0]):
            self.raw[k, 8 : 8 + n] = value[:, LANES * k : LANES * k + LANES]
        for k in range(self.raw.shape[0]):
            if up:
                self.wide[k, n : n + n + 8] = (
                    near * self.raw[k, 0 : n + 8] + far * self.raw[k, 1 : n + 9]
                )
            else:
                self.wide[k, n + 8 : n + n + 16] = (
                    near * self.raw[k, 7 : n + 15] + far * self.raw[k, 8 : n + 16]
                )

    def add_row(self, at, row):
        for k in range(self.raw.shape[0]):
            lanes = slice(LANES * k, LANES * k + LANES)
            self.wide[k, at : at + 1] = self.wide[k, at : at + 1] + row[:, lanes]

    def take(self, up, block, rest, cy, ref, j):
        n = self.rows
        if up:
            start = (n + 8 if block == 0 else 8) + rest - cy
        else:
            start = (n + 8 if block == 0 else n + n + 8) - rest - cy
        for k in range(self.raw.shape[0]):
            ref[j, 0:n, LANES * k : LANES * k + LANES] = self.wide[k, pl.ds(start, n)]


class Planes:
    def __init__(self, offsets, rows, sizes):
        count_x, count_y = sizes
        per_plane, half = count_x // 4, count_y // 2
        a = lax.axis_index("gx")
        self.odd = lax.rem(lax.axis_index("gy"), 2) == 1

        def plane_of(column):
            is_plane = lax.rem(column, per_plane) == 0
            plane = lax.rem(lax.div(column, per_plane), 4)
            rest = jnp.where(is_plane, jnp.clip(offsets[plane] - half * rows, 0, rows - 1), 0)
            return is_plane, (2.0 * plane.astype(f32) + 1.0) * 0.125, rest

        up_is, up_part, self.up_rest = plane_of(lax.rem(a + 1, count_x))
        low_is, low_part, self.low_rest = plane_of(a)
        self.up_near = jnp.where(up_is, 1.0 - up_part, 1.0)
        self.up_far = jnp.where(up_is, up_part, 0.0)
        self.low_near = jnp.where(low_is, low_part, 0.0)
        self.low_far = jnp.where(low_is, 1.0 - low_part, 1.0)
        self.up_jump = jnp.where(up_is, -plane_speed, 0.0)
        self.low_jump = jnp.where(low_is, plane_speed, 0.0)


def order_sum(load):
    total = load(0)
    for i in range(1, 19):
        total = total + load(i)
    return total


def phi_kernel(f_ref, g_ref, top, bottom, phi_ref, to_north, to_south, gbuf, fbuf, sems):
    layers, rows = phi_ref.shape[0], phi_ref.shape[1]
    faces = (layers - 1, 0)
    f_copies = [
        pltpu.make_async_copy(f_ref.at[:, x], fbuf.at[:, s], sems.at[layers + s])
        for s, x in enumerate(faces)
    ]
    g_copies = [
        pltpu.make_async_copy(g_ref.at[:, x], gbuf.at[:, x], sems.at[x]) for x in range(layers)
    ]
    for copy in f_copies + g_copies:
        copy.start()
    phi_ref[layers - 1] = top[...]
    phi_ref[0] = bottom[...]
    edges = ((to_north, rows - 1, rows - 2, (7, 10)), (to_south, 0, 1, (9, 8)))
    for s, x in enumerate(faces):
        f_copies[s].wait()
        for out, edge, inner, chosen in edges:
            out[layers + s : layers + s + 1] = phi_ref[x, inner : inner + 1]
            at = layers + 2 + 6 * s
            out[at : at + 1] = fbuf[chosen[s], s, edge : edge + 1]
            for k, part in enumerate(moments_of(lambda i: fbuf[i, s, edge : edge + 1])):
                out[at + 2 + k : at + 3 + k] = part
    for x in range(layers):
        g_copies[x].wait()
        if 0 < x < layers - 1:
            phi_ref[x] = order_sum(lambda i: gbuf[i, x])
        to_north[x : x + 1] = phi_ref[x, rows - 1 : rows]
        to_south[x : x + 1] = phi_ref[x, 0:1]
    for s, x in enumerate(faces):
        for out, edge, inner, chosen in edges:
            at = layers + 3 + 6 * s
            out[at : at + 1] = gbuf[chosen[s], x, edge : edge + 1]
    for out in (to_north, to_south):
        out[layers + 14 : layers + 16] = jnp.zeros((2, out.shape[1]), f32)


def with_halo(ref, layer, below, above):
    rows = layer.shape[0]
    ref[8 : 8 + rows] = layer
    ref[7:8] = below
    ref[8 + rows : 9 + rows] = above


def corner_values(cells, planes, phi_ref, south_msg, north_msg, minus_wide, plus_wide):
    layers, rows, cols = phi_ref.shape
    cells[...] = jnp.ones_like(cells)
    for row in range(4):
        msg = south_msg if row < 2 else north_msg
        x = layers - 1 if row % 2 == 0 else 0
        beside = rows + (layers - 2 if row % 2 == 0 else 1)
        wide_row = 7 if row < 2 else rows + 8
        at = rows + layers
        first = at + 2 + 6 * (row % 2)
        far_phi = msg[at + row % 2 : at + row % 2 + 1]
        own_phi = phi_ref[x, 0:1] if row < 2 else phi_ref[x, rows - 1 : rows]
        parts = [msg[first + k : first + k + 1] for k in range(6)]
        parts.append(msg[rows + x : rows + x + 1])
        if row % 2 == 0:
            parts += [msg[beside : beside + 1], plus_wide[wide_row : wide_row + 1]]
        else:
            parts += [minus_wide[wide_row : wide_row + 1], msg[beside : beside + 1]]
        parts += [far_phi, own_phi] if row < 2 else [own_phi, far_phi]
        for k, part in enumerate(parts):
            cells[k, row : row + 1] = part
    place = lax.broadcasted_iota(jnp.int32, (8, cols), 0)
    is_top = (place == 0) | (place == 2)
    sx = jnp.where(is_top, 1.0, -1.0)
    sy = jnp.where(place < 2, 1.0, -1.0)
    delta = jnp.where(is_top, planes.up_jump, planes.low_jump)
    site = Site([cells[k] for k in range(2, 6)], *[cells[k] for k in range(6, 11)])
    w = lattice_weight[7]
    p = sx * site.u[0] + sy * site.u[1]
    q = sx * site.force[0] + sy * site.force[1]
    change = delta * (3.0 * sy + 9.0 * (sy * p) - 3.0 * site.u[1]) + 3.0 * (delta * delta)
    rp, gp = site.r * p, site.g_scale * p
    f_post = w * (site.k + p * (4.5 * rp + 3.375 * q) + 3.0 * rp + 1.125 * q + site.rho * change)
    g_post = w * (site.g_base + 4.5 * (gp * p) + 3.0 * gp + site.phi * change)
    return f_post - 0.25 * cells[0], g_post - (1.0 / 9.0) * cells[1]


def moment_kernel(
    base,
    after_north,
    after_south,
    offsets,
    f_ref,
    g_ref,
    phi_ref,
    faces,
    raw_north,
    raw_south,
    index,
):
    layers, rows = f_ref.shape[1], f_ref.shape[2]
    is_long = [(offsets[k] - base > rows // 2).astype(jnp.int32) for k in (1, 2)]
    index[0] = 2 * is_long[0] + is_long[1]
    for s, x in enumerate((layers - 1, 0)):
        for k, part in enumerate(moments_of(lambda i: f_ref[i, x])):
            faces[s, k] = part
    for out, edge, inner, chosen in (
        (raw_north, rows - 1, rows - 2, north_going),
        (raw_south, 0, 1, south_going),
    ):
        parts = moments_of(lambda i: f_ref[i, :, edge, :])
        parts += [f_ref[i, :, edge, :] for i in chosen] + [g_ref[i, :, edge, :] for i in chosen]
        parts.append(phi_ref[:, inner, :])
        for k, part in enumerate(parts):
            out[layers * k : layers * k + layers] = part


def half_rows(rows, first):
    return slice(0, rows // 2) if first else slice(rows // 2, rows)


def seam_rows(rows, up):
    return slice(rows // 2 - 2, rows // 2) if up else slice(rows // 2, rows // 2 + 2)


def rim_values(planes, raw, msg, phi_ref, minus_wide, plus_wide, line, south, out):
    layers, rows, cols = phi_ref.shape

    def piece(k):
        return raw[layers * k : layers * k + layers]

    extra = 15 * layers
    beside, relayed = raw[extra : extra + 1], raw[extra + 1 : extra + 2]
    row = 7 if south else rows + 8
    minus, plus = minus_wide[row : row + 1], plus_wide[row : row + 1]
    low_rest, up_rest = planes.low_rest, planes.up_rest
    if south:
        minus = minus + jnp.where(low_rest == 0, planes.low_far, 0.0) * beside
        plus = plus + jnp.where(up_rest == rows - 1, planes.up_far, 0.0) * relayed
    else:
        minus = minus + jnp.where(low_rest == rows - 1, planes.low_near, 0.0) * relayed
        plus = plus + jnp.where(up_rest == 0, planes.up_near, 0.0) * beside
    phi = msg[rows : rows + layers]
    with_halo(line, phi, minus, plus)
    if south:
        below, above = piece(14), phi_ref[:, 0, :]
    else:
        below, above = phi_ref[:, rows - 1, :], piece(14)
    site = Site(
        [piece(k) for k in range(4)],
        phi,
        line[7 : 7 + layers],
        line[9 : 9 + layers],
        below,
        above,
    )
    for j, i in enumerate(north_going if south else south_going):
        cz = lattice_velocity[i][2]
        even, odd = site.pair_f(i)
        out[j] = z_moved(even + odd - 0.25 * piece(4 + j), cz)
        even, odd = site.pair_g(i)
        out[5 + j] = z_moved(even + odd - (1.0 / 9.0) * piece(9 + j), cz)


def face_kernel(
    sizes,
    offsets,
    f_ref,
    g_ref,
    face_moments,
    phi_ref,
    rise,
    fall,
    south_msg,
    north_msg,
    mate,
    direct,
    direct_short,
    across,
    across_short,
    joint,
    minus_wide,
    plus_wide,
    window,
    halo,
    post,
    cells,
    corners,
    raw,
    wide,
):
    layers, rows, cols = phi_ref.shape
    planes = Planes(offsets, rows, sizes)
    shear = Shear(raw, wide, rows)
    window[...] = jnp.zeros_like(window)
    for up in (True, False):
        if up:
            first, second = rise, north_msg
            near, far, start = planes.low_far, planes.low_near, planes.low_rest
        else:
            first, second = south_msg, fall
            near, far, start = planes.up_far, planes.up_near, rows - 1 - planes.up_rest
        target = minus_wide if up else plus_wide
        for k in range(window.shape[0]):
            lanes = slice(LANES * k, LANES * k + LANES)
            window[k, 8 : 8 + rows] = first[0:rows, lanes]
            window[k, 8 + rows : 8 + 2 * rows] = second[0:rows, lanes]
            target[:, lanes] = (
                near * window[k, pl.ds(start, rows + 16)]
                + far * window[k, pl.ds(start + 1, rows + 16)]
            )
    corners[0], corners[1] = corner_values(
        cells, planes, phi_ref, south_msg, north_msg, minus_wide, plus_wide
    )
    for side, up in enumerate((True, False)):
        x = layers - 1 if up else 0
        delta = planes.up_jump if up else planes.low_jump
        with_halo(
            halo, phi_ref[x], south_msg[rows + x : rows + x + 1], north_msg[rows + x : rows + x + 1]
        )
        for h in range(0, rows, 8):
            span = slice(h, h + 8)
            phi_h = phi_ref[x, span]
            if up:
                minus, plus = phi_ref[x - 1, span], plus_wide[8 + h : 16 + h]
            else:
                minus, plus = minus_wide[8 + h : 16 + h], phi_ref[x + 1, span]
            site = Site(
                [face_moments[side, k, span] for k in range(4)],
                phi_h,
                minus,
                plus,
                halo[7 + h : 15 + h],
                halo[9 + h : 17 + h],
            )
            for j, i in enumerate(rising if up else falling):
                cz = lattice_velocity[i][2]
                change = lattice_weight[i] * site.jump(i, delta)
                even, odd = site.pair_f(i)
                value = even + odd - 0.25 * f_ref[i, x, span] + site.rho * change
                post[side, j, span] = z_moved(value, cz)
                even, odd = site.pair_g(i)
                value = even + odd - (1.0 / 9.0) * g_ref[i, x, span] + phi_h * change
                post[side, 5 + j, span] = z_moved(value, cz)

    part = rows // 2
    seam = 10 * part

    def hand_out(is_odd):
        for side, up in enumerate((True, False)):
            if up:
                near, far, rest = planes.up_near, planes.up_far, planes.up_rest
            else:
                near, far, rest = planes.low_near, planes.low_far, planes.low_rest
            first, second = (direct, mate) if up == is_odd else (joint, across)
            shear.clear()
            for j in range(10):
                cy = lattice_velocity[(rising if up else falling)[j % 5]][1]
                shear.put(post[side, j], up, near, far)
                corner = side + (0 if cy == 1 else 2)
                if cy == 1:
                    gate = jnp.where(rest == (0 if up else rows - 1), near, 0.0)
                    at = rows + 7 if up else rows + 8
                if cy == -1:
                    gate = jnp.where(rest == (rows - 1 if up else 0), far, 0.0)
                    at = 2 * rows + 7 if up else 2 * rows + 8
                if cy != 0:
                    shear.add_row(at, gate * corners[j // 5, corner : corner + 1])
                shear.take(up, 0, rest, cy, first, j)
                shear.take(up, 1, rest, cy, second, j)
        for j in range(10):
            direct_short[j] = direct[j, half_rows(rows, is_odd)]
            across_short[part * j : part * j + part] = across[j, half_rows(rows, is_odd)]
            across_short[seam + 2 * j : seam + 2 * j + 2] = across[j, seam_rows(rows, not is_odd)]
        across_short[seam + 20 : seam + 24] = jnp.zeros((4, cols), f32)

    pl.when(planes.odd)(lambda: hand_out(True))
    pl.when(jnp.logical_not(planes.odd))(lambda: hand_out(False))


def bulk_kernel(
    sizes,
    after,
    offsets,
    f_ref,
    g_ref,
    phi_ref,
    minus,
    plus,
    south_msg,
    north_msg,
    south_raw,
    north_raw,
    next_f,
    next_g,
    wide_phi,
    halo,
    line,
    south_rim,
    north_rim,
):
    layers, rows, cols = phi_ref.shape
    planes = Planes(offsets, rows, sizes)
    rim_values(planes, south_raw, south_msg, phi_ref, minus, plus, line, True, south_rim)
    rim_values(planes, north_raw, north_msg, phi_ref, minus, plus, line, False, north_rim)
    wide_phi[0] = minus[8 : 8 + rows]
    wide_phi[layers + 1] = plus[8 : 8 + rows]
    for x in range(layers):
        wide_phi[x + 1] = phi_ref[x]

    def layer(x, carry):
        with_halo(halo, phi_ref[x], south_msg[pl.ds(rows + x, 1)], north_msg[pl.ds(rows + x, 1)])
        beyond = lax.rem(x + 1, layers)
        before = lax.rem(x + layers - 1, layers)
        for h in range(0, rows, 8):
            span = slice(h, h + 8)
            phi_h = phi_ref[x, span]
            site = Site(
                moments_of(lambda i: f_ref[i, x, span]),
                phi_h,
                wide_phi[x, span],
                wide_phi[x + 2, span],
                halo[7 + h : 15 + h],
                halo[9 + h : 17 + h],
            )

            def emit(out, slot, i, value):
                cx, cy, cz = lattice_velocity[i]
                value = z_moved(value, cz)
                at = beyond if cx == 1 else before if cx == -1 else x
                if cy == 0:
                    out[i, at, span] = value
                elif cy == 1:
                    if h == 0:
                        rim = slot * 5 + north_going.index(i)
                        out[i, at, 0:1] = south_rim[rim, pl.ds(x, 1)]
                    if h + 8 < rows:
                        out[i, at, h + 1 : h + 9] = value
                    else:
                        out[i, at, h + 1 : h + 8] = value[0:7]
                else:
                    if h + 8 == rows:
                        rim = slot * 5 + south_going.index(i)
                        out[i, at, rows - 1 : rows] = north_rim[rim, pl.ds(x, 1)]
                    if h > 0:
                        out[i, at, h - 1 : h + 7] = value
                    else:
                        out[i, at, 0:7] = value[1:8]

            emit(next_f, 0, 0, lattice_weight[0] * site.k - 0.25 * f_ref[0, x, span])
            rest_g = (phi_h - 2.0 * site.mu - 0.5 * (phi_h * site.uu)) * (1.0 / 0.9)
            emit(next_g, 1, 0, rest_g - (1.0 / 9.0) * g_ref[0, x, span])
            for i in range(1, 19, 2):
                even, odd = site.pair_f(i)
                emit(next_f, 0, i, (even + odd) - 0.25 * f_ref[i, x, span])
                emit(next_f, 0, i + 1, (even - odd) - 0.25 * f_ref[i + 1, x, span])
                even, odd = site.pair_g(i)
                emit(next_g, 1, i, (even + odd) - (1.0 / 9.0) * g_ref[i, x, span])
                emit(next_g, 1, i + 1, (even - odd) - (1.0 / 9.0) * g_ref[i + 1, x, span])
        return carry

    lax.fori_loop(0, layers, layer, 0)


def put_faces(buf, out_f, out_g, chosen, x, sems):
    copies = [
        pltpu.make_async_copy(buf.at[5 * family + j], out.at[i, x], sems.at[5 * family + j])
        for family, out in enumerate((out_f, out_g))
        for j, i in enumerate(chosen)
    ]
    for copy in copies:
        copy.start()
    for copy in copies:
        copy.wait()


def merge_fill_kernel(
    sizes,
    offsets,
    direct,
    direct_short,
    across,
    across_short,
    f_in,
    g_in,
    f_out,
    g_out,
    buf,
    sems,
):
    layers, rows = f_out.shape[1], f_out.shape[2]
    planes = Planes(offsets, rows, sizes)
    part = rows // 2
    seam = 10 * part

    def merge(rest, up):
        is_long = rest > part
        near, other, between = half_rows(rows, up), half_rows(rows, not up), seam_rows(rows, up)

        @pl.when(is_long)
        def _():
            buf[...] = across[...]
            for j in range(10):
                buf[j, near] = buf[j, near] + direct_short[j]

        @pl.when(jnp.logical_not(is_long))
        def _():
            buf[...] = direct[...]
            for j in range(10):
                buf[j, other] = buf[j, other] + across_short[part * j : part * j + part]
                at = seam + 2 * j
                buf[j, between] = buf[j, between] + across_short[at : at + 2]

        if up:
            put_faces(buf, f_out, g_out, rising, 0, sems)
        else:
            put_faces(buf, f_out, g_out, falling, layers - 1, sems)

    pl.when(planes.odd)(lambda: merge(planes.low_rest, True))
    pl.when(jnp.logical_not(planes.odd))(lambda: merge(planes.up_rest, False))


def joint_fill_kernel(joint, f_in, g_in, f_out, g_out, sems):
    odd = lax.rem(lax.axis_index("gy"), 2) == 1
    layers = f_out.shape[1]
    pl.when(odd)(lambda: put_faces(joint, f_out, g_out, falling, layers - 1, sems))
    pl.when(jnp.logical_not(odd))(lambda: put_faces(joint, f_out, g_out, rising, 0, sems))


def on_device(momentum_dist, order_dist, offsets):
    layers, rows, cols = momentum_dist.shape[1:]
    count_x, count_y = lax.axis_size("gx"), lax.axis_size("gy")
    per_plane = count_x // 4
    half = count_y // 2

    def hop(value, target):
        perm = []
        for x in range(count_x):
            for y in range(count_y):
                tx, ty = target(x, y)
                perm.append((x * count_y + y, tx % count_x * count_y + ty % count_y))
        return lax.ppermute(value, ("gx", "gy"), perm)

    def base_up(x):
        return half if (x + 1) % per_plane == 0 else 0

    def base_low(x):
        return half if x % per_plane == 0 else 0

    def hop_parity(value, odd_up, extra):
        def target(x, y):
            if (y % 2 == 1) == odd_up:
                return (x + 1, y - base_up(x) - extra)
            return (x - 1, y + base_low(x) + extra)

        return hop(value, target)

    def hop_y(value, step):
        return hop(value, lambda x, y: (x, y + step))

    smem, vmem, anywhere = spec_of(pltpu.SMEM), spec_of(VMEM), spec_of(pl.ANY)
    plane = jax.ShapeDtypeStruct((rows, cols), f32)
    top, bottom = jnp.sum(order_dist[:, layers - 1], axis=0), jnp.sum(order_dist[:, 0], axis=0)
    rise = hop(top, lambda x, y: (x + 1, y - base_up(x)))
    fall = hop(bottom, lambda x, y: (x - 1, y + base_low(x)))

    part = rows // 2
    block = jax.ShapeDtypeStruct((layers + 16, cols), f32)
    phi, to_north, to_south, order_near = pl.pallas_call(
        phi_kernel,
        out_shape=[jax.ShapeDtypeStruct((layers, rows, cols), f32)]
        + [block] * 2
        + [jax.ShapeDtypeStruct(order_dist.shape, f32)],
        in_specs=[anywhere, anywhere, vmem, vmem],
        out_specs=[vmem] * 4,
        scratch_shapes=[
            VMEM((19, 2, rows, cols), f32),
            pltpu.SemaphoreType.DMA((layers + 2,)),
        ],
        compiler_params=params(52 << 20),
        name="phi_all",
    )(momentum_dist, order_dist, top, bottom)
    to_north = jnp.concatenate([fall, to_north], 0)
    to_south = jnp.concatenate([rise, to_south], 0)
    south_msg, north_msg = hop_y(to_north, 1), hop_y(to_south, -1)

    raw = jax.ShapeDtypeStruct((15 * layers, cols), f32)
    face_moments, raw_north, raw_south, index = pl.pallas_call(
        functools.partial(moment_kernel, half * rows),
        out_shape=[
            jax.ShapeDtypeStruct((2, 4, rows, cols), f32),
            raw,
            raw,
            jax.ShapeDtypeStruct((1,), jnp.int32),
        ],
        in_specs=[anywhere, anywhere, smem] + [vmem] * 3,
        out_specs=[vmem] * 3 + [smem],
        compiler_params=params(16 << 20),
        name="moments",
    )(to_north, to_south, offsets, momentum_dist, order_near, phi)
    blank = jnp.zeros((6, cols), f32)
    raw_north = jnp.concatenate([raw_north, rise[rows - 1 :], south_msg[rows - 1 : rows], blank], 0)
    raw_south = jnp.concatenate([raw_south, fall[:1], north_msg[:1], blank], 0)

    ten = jax.ShapeDtypeStruct((10, rows, cols), f32)
    ten_short = jax.ShapeDtypeStruct((10, part, cols), f32)
    ten_seam = jax.ShapeDtypeStruct((10 * part + 24, cols), f32)
    wide = jax.ShapeDtypeStruct((rows + 16, cols), f32)
    whole = jax.ShapeDtypeStruct(momentum_dist.shape, f32)

    def finish(long_planes):

        def is_long(x):
            return x % per_plane == 0 and x // per_plane % 4 in long_planes

        def hop_some(value, odd_up, extra, long):
            pairs = []
            for x in range(count_x):
                for y in range(count_y):
                    up = (y % 2 == 1) == odd_up
                    tx = (x + 1 if up else x - 1) % count_x
                    if is_long(tx if up else x) != long:
                        continue
                    ty = y - base_up(x) - extra if up else y + base_low(x) + extra
                    pairs.append((x * count_y + y, tx * count_y + ty % count_y))
            return lax.ppermute(value, ("gx", "gy"), pairs)

        south_raw, north_raw = hop_y(raw_north, 1), hop_y(raw_south, -1)
        mate, direct, direct_short, across, across_short, joint, minus, plus = pl.pallas_call(
            functools.partial(face_kernel, (count_x, count_y)),
            out_shape=[ten, ten, ten_short, ten, ten_seam, ten] + [wide] * 2,
            in_specs=[smem] + [vmem] * 8,
            out_specs=[vmem] * 8,
            scratch_shapes=[
                VMEM((cols // LANES, 2 * rows + 16, LANES), f32),
                VMEM((rows + 16, cols), f32),
                VMEM((2, 10, rows, cols), f32),
                VMEM((11, 8, cols), f32),
                VMEM((2, 8, cols), f32),
                VMEM((cols // LANES, rows + 16, LANES), f32),
                VMEM((cols // LANES, 3 * rows + 16, LANES), f32),
            ],
            compiler_params=params(24 << 20),
            name="faces",
        )(
            offsets,
            momentum_dist,
            order_near,
            face_moments,
            phi,
            rise,
            fall,
            south_msg,
            north_msg,
        )
        around = (phi, minus, plus, south_msg, north_msg)
        mate, south_raw, north_raw = lax.optimization_barrier((mate, south_raw, north_raw))
        mate = hop(mate, lambda x, y: (x, y ^ 1))
        direct = hop_some(direct, True, 0, False)
        direct_short = hop_some(direct_short, True, 0, True)
        across = hop_some(across, False, 1, True)
        across_short = hop_some(across_short, False, 1, False)
        joint = joint + mate
        after = joint
        joint = hop_parity(joint, False, 0)

        next_f, next_g = pl.pallas_call(
            functools.partial(bulk_kernel, (count_x, count_y)),
            out_shape=[whole, whole],
            in_specs=[anywhere, smem] + [vmem] * 9,
            out_specs=[vmem] * 2,
            scratch_shapes=[
                VMEM((layers + 2, rows, cols), f32),
                VMEM((rows + 16, cols), f32),
                VMEM((layers + 16, cols), f32),
                VMEM((10, layers, cols), f32),
                VMEM((10, layers, cols), f32),
            ],
            compiler_params=params(48 << 20),
            name="bulk",
        )(after, offsets, momentum_dist, order_near, *around, south_raw, north_raw)

        next_f, next_g = pl.pallas_call(
            functools.partial(merge_fill_kernel, (count_x, count_y)),
            out_shape=[whole, whole],
            in_specs=[smem] + [vmem] * 4 + [anywhere, anywhere],
            out_specs=[anywhere, anywhere],
            scratch_shapes=[VMEM((10, rows, cols), f32), pltpu.SemaphoreType.DMA((10,))],
            input_output_aliases={5: 0, 6: 1},
            compiler_params=params(24 << 20),
            name="merge_fill",
        )(offsets, direct, direct_short, across, across_short, next_f, next_g)

        return pl.pallas_call(
            joint_fill_kernel,
            out_shape=[whole, whole],
            in_specs=[vmem, anywhere, anywhere],
            out_specs=[anywhere, anywhere],
            scratch_shapes=[pltpu.SemaphoreType.DMA((10,))],
            input_output_aliases={1: 0, 2: 1},
            compiler_params=params(24 << 20),
            name="joint_fill",
        )(joint, next_f, next_g)

    branches = [
        functools.partial(finish, {3} | ({1} if k & 2 else set()) | ({2} if k & 1 else set()))
        for k in range(4)
    ]
    return lax.switch(index[0], branches)


def solution(mesh):
    return jax.shard_map(
        on_device,
        mesh=mesh,
        in_specs=(P(None, "gx", "gy", None), P(None, "gx", "gy", None), P()),
        out_specs=(P(None, "gx", "gy", None), P(None, "gx", "gy", None)),
        check_vma=False,
    )
```

```python
import functools

import jax
import jax.numpy as jnp
from jax import lax
from jax.experimental import pallas as pl
from jax.experimental.pallas import tpu as pltpu
from jax.sharding import PartitionSpec as P

lattice_velocity = [
    (0, 0, 0),
    (1, 0, 0),
    (-1, 0, 0),
    (0, 1, 0),
    (0, -1, 0),
    (0, 0, 1),
    (0, 0, -1),
    (1, 1, 0),
    (-1, -1, 0),
    (1, -1, 0),
    (-1, 1, 0),
    (1, 0, 1),
    (-1, 0, -1),
    (1, 0, -1),
    (-1, 0, 1),
    (0, 1, 1),
    (0, -1, -1),
    (0, 1, -1),
    (0, -1, 1),
]
lattice_weight = [1.0 / 3.0] + [1.0 / 18.0] * 6 + [1.0 / 36.0] * 12
plane_speed = 0.04
rising = [1, 7, 9, 11, 13]
falling = [2, 8, 10, 12, 14]
north_going = [i for i in range(19) if lattice_velocity[i][1] == 1]
south_going = [i for i in range(19) if lattice_velocity[i][1] == -1]
f32 = jnp.float32
VMEM = pltpu.VMEM
LANES = 128


def z_moved(value, step):
    if step == 0:
        return value
    return pltpu.roll(value, step % value.shape[-1], value.ndim - 1)


def spec_of(space):
    return pl.BlockSpec(memory_space=space)


def params(limit):
    return pltpu.CompilerParams(vmem_limit_bytes=limit)


def along(parts, c):
    total = None
    for sign, part in zip(c, parts):
        if sign == 0:
            continue
        if total is None:
            total = part if sign > 0 else -part
        else:
            total = total + part if sign > 0 else total - part
    return total


def signed_sum(load, axis):
    ups = [i for i in range(19) if lattice_velocity[i][axis] == 1]
    downs = [i for i in range(19) if lattice_velocity[i][axis] == -1]
    total = load(ups[0]) - load(downs[0])
    for i, j in zip(ups[1:], downs[1:]):
        total = total + (load(i) - load(j))
    return total


def moments_of(load):
    rho = load(0)
    for i in range(1, 19):
        rho = rho + load(i)
    return [rho] + [signed_sum(load, axis) for axis in range(3)]


class Site:
    def __init__(self, moments, phi, minus, plus, south, north):
        rho, momentum = moments[0], moments[1:]
        lower, upper = z_moved(phi, 1), z_moved(phi, -1)
        lap = (plus + minus) + (north + south) + (upper + lower) - 6.0 * phi
        mu = phi * (0.0625 * (phi * phi) - 0.0625) - 0.04 * lap
        half_mu = 0.5 * mu
        force = [half_mu * (plus - minus), half_mu * (north - south), half_mu * (upper - lower)]
        inverse = 1.0 / rho
        u = [(j + 0.5 * k) * inverse for j, k in zip(momentum, force)]
        uu = u[0] * u[0] + u[1] * u[1] + u[2] * u[2]
        uf = u[0] * force[0] + u[1] * force[1] + u[2] * force[2]
        self.rho, self.phi, self.mu, self.u, self.force, self.uu = rho, phi, mu, u, force, uu
        self.r = 1.25 * rho
        self.k = self.r * (1.0 - 1.5 * uu) - 1.125 * uf
        self.g_scale = phi * (1.0 / 0.9)
        self.g_base = (3.0 / 0.9) * mu - 1.5 * (self.g_scale * uu)

    def pair_f(self, i):
        p, q = along(self.u, lattice_velocity[i]), along(self.force, lattice_velocity[i])
        w = lattice_weight[i]
        rp = self.r * p
        even = w * (self.k + p * (4.5 * rp + 3.375 * q))
        odd = (3.0 * w) * rp + (1.125 * w) * q
        return even, odd

    def pair_g(self, i):
        p = along(self.u, lattice_velocity[i])
        w = lattice_weight[i]
        gp = self.g_scale * p
        return w * (self.g_base + 4.5 * (gp * p)), (3.0 * w) * gp

    def jump(self, i, delta):
        cy = lattice_velocity[i][1]
        uy = self.u[1]
        if cy == 0:
            return delta * (-3.0 * uy) - (1.5 * delta * delta)
        p = along(self.u, lattice_velocity[i])
        return delta * (3.0 * cy + (9.0 * cy) * p - 3.0 * uy) + (3.0 * delta * delta)


class Shear:
    def __init__(self, raw, wide, rows):
        self.raw, self.wide, self.rows = raw, wide, rows

    def clear(self):
        self.raw[...] = jnp.zeros_like(self.raw)
        self.wide[...] = jnp.zeros_like(self.wide)

    def put(self, value, up, near, far):
        n = self.rows
        for k in range(self.raw.shape[0]):
            self.raw[k, 8 : 8 + n] = value[:, LANES * k : LANES * k + LANES]
        for k in range(self.raw.shape[0]):
            if up:
                self.wide[k, n : n + n + 8] = (
                    near * self.raw[k, 0 : n + 8] + far * self.raw[k, 1 : n + 9]
                )
            else:
                self.wide[k, n + 8 : n + n + 16] = (
                    near * self.raw[k, 7 : n + 15] + far * self.raw[k, 8 : n + 16]
                )

    def add_row(self, at, row):
        for k in range(self.raw.shape[0]):
            lanes = slice(LANES * k, LANES * k + LANES)
            self.wide[k, at : at + 1] = self.wide[k, at : at + 1] + row[:, lanes]

    def take(self, up, block, rest, cy, ref, j):
        n = self.rows
        if up:
            start = (n + 8 if block == 0 else 8) + rest - cy
        else:
            start = (n + 8 if block == 0 else n + n + 8) - rest - cy
        for k in range(self.raw.shape[0]):
            ref[j, 0:n, LANES * k : LANES * k + LANES] = self.wide[k, pl.ds(start, n)]


class Planes:
    def __init__(self, offsets, rows, sizes):
        count_x, count_y = sizes
        per_plane, half = count_x // 4, count_y // 2
        a = lax.axis_index("gx")
        self.odd = lax.rem(lax.axis_index("gy"), 2) == 1

        def plane_of(column):
            is_plane = lax.rem(column, per_plane) == 0
            plane = lax.rem(lax.div(column, per_plane), 4)
            rest = jnp.where(is_plane, jnp.clip(offsets[plane] - half * rows, 0, rows - 1), 0)
            return is_plane, (2.0 * plane.astype(f32) + 1.0) * 0.125, rest

        up_is, up_part, self.up_rest = plane_of(lax.rem(a + 1, count_x))
        low_is, low_part, self.low_rest = plane_of(a)
        self.up_near = jnp.where(up_is, 1.0 - up_part, 1.0)
        self.up_far = jnp.where(up_is, up_part, 0.0)
        self.low_near = jnp.where(low_is, low_part, 0.0)
        self.low_far = jnp.where(low_is, 1.0 - low_part, 1.0)
        self.up_jump = jnp.where(up_is, -plane_speed, 0.0)
        self.low_jump = jnp.where(low_is, plane_speed, 0.0)


def order_sum(load):
    total = load(0)
    for i in range(1, 19):
        total = total + load(i)
    return total


def branch_kernel(part, base, g_ref, offsets, index):
    first, second = offsets[1] - base > part, offsets[2] - base > part
    index[0] = 2 * first.astype(jnp.int32) + second.astype(jnp.int32)


def phi_kernel(index, f_ref, g_ref, top, bottom, phi_ref, to_north, to_south, fbuf, sems):
    layers, rows = phi_ref.shape[0], phi_ref.shape[1]
    faces = (layers - 1, 0)
    copies = [
        pltpu.make_async_copy(f_ref.at[:, x], fbuf.at[:, s], sems.at[s])
        for s, x in enumerate(faces)
    ]
    for copy in copies:
        copy.start()
    phi_ref[layers - 1] = top[...]
    phi_ref[0] = bottom[...]
    for x in range(layers):
        if 0 < x < layers - 1:
            phi_ref[x] = order_sum(lambda i: g_ref[i, x])
        to_north[x : x + 1] = phi_ref[x, rows - 1 : rows]
        to_south[x : x + 1] = phi_ref[x, 0:1]
    for s, x in enumerate(faces):
        copies[s].wait()
        for out, edge, inner, chosen in (
            (to_north, rows - 1, rows - 2, (7, 10)),
            (to_south, 0, 1, (9, 8)),
        ):
            out[layers + s : layers + s + 1] = phi_ref[x, inner : inner + 1]
            at = layers + 2 + 6 * s
            out[at : at + 1] = fbuf[chosen[s], s, edge : edge + 1]
            out[at + 1 : at + 2] = g_ref[chosen[s], x, edge : edge + 1]
            for k, part in enumerate(moments_of(lambda i: fbuf[i, s, edge : edge + 1])):
                out[at + 2 + k : at + 3 + k] = part
    for out in (to_north, to_south):
        out[layers + 14 : layers + 16] = jnp.zeros((2, out.shape[1]), f32)


def with_halo(ref, layer, below, above):
    rows = layer.shape[0]
    ref[8 : 8 + rows] = layer
    ref[7:8] = below
    ref[8 + rows : 9 + rows] = above


def corner_values(cells, planes, phi_ref, south_msg, north_msg, minus_wide, plus_wide):
    layers, rows, cols = phi_ref.shape
    cells[...] = jnp.ones_like(cells)
    for row in range(4):
        msg = south_msg if row < 2 else north_msg
        x = layers - 1 if row % 2 == 0 else 0
        beside = rows + (layers - 2 if row % 2 == 0 else 1)
        wide_row = 7 if row < 2 else rows + 8
        at = rows + layers
        first = at + 2 + 6 * (row % 2)
        far_phi = msg[at + row % 2 : at + row % 2 + 1]
        own_phi = phi_ref[x, 0:1] if row < 2 else phi_ref[x, rows - 1 : rows]
        parts = [msg[first + k : first + k + 1] for k in range(6)]
        parts.append(msg[rows + x : rows + x + 1])
        if row % 2 == 0:
            parts += [msg[beside : beside + 1], plus_wide[wide_row : wide_row + 1]]
        else:
            parts += [minus_wide[wide_row : wide_row + 1], msg[beside : beside + 1]]
        parts += [far_phi, own_phi] if row < 2 else [own_phi, far_phi]
        for k, part in enumerate(parts):
            cells[k, row : row + 1] = part
    place = lax.broadcasted_iota(jnp.int32, (8, cols), 0)
    is_top = (place == 0) | (place == 2)
    sx = jnp.where(is_top, 1.0, -1.0)
    sy = jnp.where(place < 2, 1.0, -1.0)
    delta = jnp.where(is_top, planes.up_jump, planes.low_jump)
    site = Site([cells[k] for k in range(2, 6)], *[cells[k] for k in range(6, 11)])
    w = lattice_weight[7]
    p = sx * site.u[0] + sy * site.u[1]
    q = sx * site.force[0] + sy * site.force[1]
    change = delta * (3.0 * sy + 9.0 * (sy * p) - 3.0 * site.u[1]) + 3.0 * (delta * delta)
    rp, gp = site.r * p, site.g_scale * p
    f_post = w * (site.k + p * (4.5 * rp + 3.375 * q) + 3.0 * rp + 1.125 * q + site.rho * change)
    g_post = w * (site.g_base + 4.5 * (gp * p) + 3.0 * gp + site.phi * change)
    return f_post - 0.25 * cells[0], g_post - (1.0 / 9.0) * cells[1]


def moment_kernel(after_north, after_south, f_ref, g_ref, faces, rims):
    layers, rows = f_ref.shape[1], f_ref.shape[2]
    for s, x in enumerate((layers - 1, 0)):
        for k, part in enumerate(moments_of(lambda i: f_ref[i, x])):
            faces[s, k] = part
    for s, (edge, chosen) in enumerate(((rows - 1, north_going), (0, south_going))):
        for k, part in enumerate(moments_of(lambda i: f_ref[i, :, edge, :])):
            rims[s, k] = part
        for j, i in enumerate(chosen):
            rims[s, 4 + j] = f_ref[i, :, edge, :]
            rims[s, 9 + j] = g_ref[i, :, edge, :]


def half_rows(rows, first):
    return slice(0, rows // 2) if first else slice(rows // 2, rows)


def seam_rows(rows, up):
    return slice(rows // 2 - 2, rows // 2) if up else slice(rows // 2, rows // 2 + 2)


def rim_values(rims, s, phi_ref, minus, plus, south_msg, north_msg, line, edge, chosen, out):
    layers, rows, cols = phi_ref.shape
    phi = phi_ref[:, edge, :]
    with_halo(line, phi, minus[edge : edge + 1], plus[edge : edge + 1])
    if edge == 0:
        below, above = south_msg[rows : rows + layers], phi_ref[:, 1, :]
    else:
        below, above = phi_ref[:, rows - 2, :], north_msg[rows : rows + layers]
    site = Site(
        [rims[s, k] for k in range(4)],
        phi,
        line[7 : 7 + layers],
        line[9 : 9 + layers],
        below,
        above,
    )
    for j, i in enumerate(chosen):
        cz = lattice_velocity[i][2]
        even, odd = site.pair_f(i)
        out[s, j] = z_moved(even + odd - 0.25 * rims[s, 4 + j], cz)
        even, odd = site.pair_g(i)
        out[s, 5 + j] = z_moved(even + odd - (1.0 / 9.0) * rims[s, 9 + j], cz)


def face_kernel(
    sizes,
    offsets,
    f_ref,
    g_ref,
    face_moments,
    rims,
    phi_ref,
    rise,
    fall,
    south_msg,
    north_msg,
    mate,
    direct,
    direct_short,
    across,
    across_short,
    joint,
    cross,
    minus_out,
    plus_out,
    minus_wide,
    plus_wide,
    window,
    halo,
    line,
    rim_post,
    post,
    cells,
    corners,
    raw,
    wide,
):
    layers, rows, cols = phi_ref.shape
    planes = Planes(offsets, rows, sizes)
    shear = Shear(raw, wide, rows)
    window[...] = jnp.zeros_like(window)
    for up in (True, False):
        if up:
            first, second = rise, north_msg
            near, far, start = planes.low_far, planes.low_near, planes.low_rest
        else:
            first, second = south_msg, fall
            near, far, start = planes.up_far, planes.up_near, rows - 1 - planes.up_rest
        target = minus_wide if up else plus_wide
        for k in range(window.shape[0]):
            lanes = slice(LANES * k, LANES * k + LANES)
            window[k, 8 : 8 + rows] = first[0:rows, lanes]
            window[k, 8 + rows : 8 + 2 * rows] = second[0:rows, lanes]
            target[:, lanes] = (
                near * window[k, pl.ds(start, rows + 16)]
                + far * window[k, pl.ds(start + 1, rows + 16)]
            )
    minus_out[...] = minus_wide[8 : 8 + rows]
    plus_out[...] = plus_wide[8 : 8 + rows]
    corners[0], corners[1] = corner_values(
        cells, planes, phi_ref, south_msg, north_msg, minus_wide, plus_wide
    )
    for s, (edge, chosen) in enumerate(((rows - 1, north_going), (0, south_going))):
        rim_values(
            rims,
            s,
            phi_ref,
            minus_out,
            plus_out,
            south_msg,
            north_msg,
            line,
            edge,
            chosen,
            rim_post,
        )
    for side, up in enumerate((True, False)):
        x = layers - 1 if up else 0
        delta = planes.up_jump if up else planes.low_jump
        with_halo(
            halo, phi_ref[x], south_msg[rows + x : rows + x + 1], north_msg[rows + x : rows + x + 1]
        )
        for h in range(0, rows, 8):
            span = slice(h, h + 8)
            phi_h = phi_ref[x, span]
            if up:
                minus, plus = phi_ref[x - 1, span], plus_wide[8 + h : 16 + h]
            else:
                minus, plus = minus_wide[8 + h : 16 + h], phi_ref[x + 1, span]
            site = Site(
                [face_moments[side, k, span] for k in range(4)],
                phi_h,
                minus,
                plus,
                halo[7 + h : 15 + h],
                halo[9 + h : 17 + h],
            )
            for j, i in enumerate(rising if up else falling):
                cz = lattice_velocity[i][2]
                change = lattice_weight[i] * site.jump(i, delta)
                even, odd = site.pair_f(i)
                value = even + odd - 0.25 * f_ref[i, x, span] + site.rho * change
                post[side, j, span] = z_moved(value, cz)
                even, odd = site.pair_g(i)
                value = even + odd - (1.0 / 9.0) * g_ref[i, x, span] + phi_h * change
                post[side, 5 + j, span] = z_moved(value, cz)

    part = rows // 2
    seam = 10 * part

    def hand_out(is_odd):
        for side, up in enumerate((True, False)):
            if up:
                near, far, rest = planes.up_near, planes.up_far, planes.up_rest
            else:
                near, far, rest = planes.low_near, planes.low_far, planes.low_rest
            first, second = (direct, mate) if up == is_odd else (joint, across)
            shear.clear()
            for j in range(10):
                cy = lattice_velocity[(rising if up else falling)[j % 5]][1]
                shear.put(post[side, j], up, near, far)
                corner = side + (0 if cy == 1 else 2)
                if cy == 1:
                    gate = jnp.where(rest == (0 if up else rows - 1), near, 0.0)
                    at = rows + 7 if up else rows + 8
                if cy == -1:
                    gate = jnp.where(rest == (rows - 1 if up else 0), far, 0.0)
                    at = 2 * rows + 7 if up else 2 * rows + 8
                if cy != 0:
                    shear.add_row(at, gate * corners[j // 5, corner : corner + 1])
                shear.take(up, 0, rest, cy, first, j)
                shear.take(up, 1, rest, cy, second, j)
        for j in range(10):
            mate[j, rows : rows + layers] = rim_post[1 if is_odd else 0, j]
            cross[j] = rim_post[0 if is_odd else 1, j]
            direct_short[j] = direct[j, half_rows(rows, is_odd)]
            across_short[part * j : part * j + part] = across[j, half_rows(rows, is_odd)]
            across_short[seam + 2 * j : seam + 2 * j + 2] = across[j, seam_rows(rows, not is_odd)]
        across_short[seam + 20 : seam + 24] = jnp.zeros((4, cols), f32)

    pl.when(planes.odd)(lambda: hand_out(True))
    pl.when(jnp.logical_not(planes.odd))(lambda: hand_out(False))


def bulk_kernel(
    after,
    f_ref,
    g_ref,
    phi_ref,
    minus,
    plus,
    south_msg,
    north_msg,
    mate_rim,
    cross_rim,
    next_f,
    next_g,
    wide_phi,
    halo,
):
    layers, rows, cols = phi_ref.shape
    is_odd = lax.rem(lax.axis_index("gy"), 2) == 1
    wide_phi[0] = minus[...]
    wide_phi[layers + 1] = plus[...]
    for x in range(layers):
        wide_phi[x + 1] = phi_ref[x]

    def layer(x, carry):
        with_halo(halo, phi_ref[x], south_msg[pl.ds(rows + x, 1)], north_msg[pl.ds(rows + x, 1)])
        beyond = lax.rem(x + 1, layers)
        before = lax.rem(x + layers - 1, layers)
        for h in range(0, rows, 8):
            span = slice(h, h + 8)
            phi_h = phi_ref[x, span]
            site = Site(
                moments_of(lambda i: f_ref[i, x, span]),
                phi_h,
                wide_phi[x, span],
                wide_phi[x + 2, span],
                halo[7 + h : 15 + h],
                halo[9 + h : 17 + h],
            )

            def emit(out, slot, i, value):
                cx, cy, cz = lattice_velocity[i]
                value = z_moved(value, cz)
                at = beyond if cx == 1 else before if cx == -1 else x
                if cy == 0:
                    out[i, at, span] = value
                elif cy == 1:
                    if h == 0:
                        rim = slot * 5 + north_going.index(i)
                        out[i, at, 0:1] = jnp.where(
                            is_odd, mate_rim[rim, pl.ds(rows + x, 1)], cross_rim[rim, pl.ds(x, 1)]
                        )
                    if h + 8 < rows:
                        out[i, at, h + 1 : h + 9] = value
                    else:
                        out[i, at, h + 1 : h + 8] = value[0:7]
                else:
                    if h + 8 == rows:
                        rim = slot * 5 + south_going.index(i)
                        out[i, at, rows - 1 : rows] = jnp.where(
                            is_odd, cross_rim[rim, pl.ds(x, 1)], mate_rim[rim, pl.ds(rows + x, 1)]
                        )
                    if h > 0:
                        out[i, at, h - 1 : h + 7] = value
                    else:
                        out[i, at, 0:7] = value[1:8]

            emit(next_f, 0, 0, lattice_weight[0] * site.k - 0.25 * f_ref[0, x, span])
            rest_g = (phi_h - 2.0 * site.mu - 0.5 * (phi_h * site.uu)) * (1.0 / 0.9)
            emit(next_g, 1, 0, rest_g - (1.0 / 9.0) * g_ref[0, x, span])
            for i in range(1, 19, 2):
                even, odd = site.pair_f(i)
                emit(next_f, 0, i, (even + odd) - 0.25 * f_ref[i, x, span])
                emit(next_f, 0, i + 1, (even - odd) - 0.25 * f_ref[i + 1, x, span])
                even, odd = site.pair_g(i)
                emit(next_g, 1, i, (even + odd) - (1.0 / 9.0) * g_ref[i, x, span])
                emit(next_g, 1, i + 1, (even - odd) - (1.0 / 9.0) * g_ref[i + 1, x, span])
        return carry

    lax.fori_loop(0, layers, layer, 0)


def put_faces(buf, out_f, out_g, chosen, x, sems):
    copies = [
        pltpu.make_async_copy(buf.at[5 * family + j], out.at[i, x], sems.at[5 * family + j])
        for family, out in enumerate((out_f, out_g))
        for j, i in enumerate(chosen)
    ]
    for copy in copies:
        copy.start()
    for copy in copies:
        copy.wait()


def merge_fill_kernel(
    sizes,
    offsets,
    direct,
    direct_short,
    across,
    across_short,
    f_in,
    g_in,
    f_out,
    g_out,
    buf,
    sems,
):
    layers, rows = f_out.shape[1], f_out.shape[2]
    planes = Planes(offsets, rows, sizes)
    part = rows // 2
    seam = 10 * part

    def merge(rest, up):
        is_long = rest > part
        near, other, between = half_rows(rows, up), half_rows(rows, not up), seam_rows(rows, up)

        @pl.when(is_long)
        def _():
            buf[...] = across[...]
            for j in range(10):
                buf[j, near] = buf[j, near] + direct_short[j]

        @pl.when(jnp.logical_not(is_long))
        def _():
            buf[...] = direct[...]
            for j in range(10):
                buf[j, other] = buf[j, other] + across_short[part * j : part * j + part]
                at = seam + 2 * j
                buf[j, between] = buf[j, between] + across_short[at : at + 2]

        if up:
            put_faces(buf, f_out, g_out, rising, 0, sems)
        else:
            put_faces(buf, f_out, g_out, falling, layers - 1, sems)

    pl.when(planes.odd)(lambda: merge(planes.low_rest, True))
    pl.when(jnp.logical_not(planes.odd))(lambda: merge(planes.up_rest, False))


def joint_fill_kernel(joint, f_in, g_in, f_out, g_out, sems):
    odd = lax.rem(lax.axis_index("gy"), 2) == 1
    layers = f_out.shape[1]
    pl.when(odd)(lambda: put_faces(joint, f_out, g_out, falling, layers - 1, sems))
    pl.when(jnp.logical_not(odd))(lambda: put_faces(joint, f_out, g_out, rising, 0, sems))


def on_device(momentum_dist, order_dist, offsets):
    layers, rows, cols = momentum_dist.shape[1:]
    count_x, count_y = lax.axis_size("gx"), lax.axis_size("gy")
    per_plane = count_x // 4
    half = count_y // 2

    def hop(value, target):
        perm = []
        for x in range(count_x):
            for y in range(count_y):
                tx, ty = target(x, y)
                perm.append((x * count_y + y, tx % count_x * count_y + ty % count_y))
        return lax.ppermute(value, ("gx", "gy"), perm)

    def base_up(x):
        return half if (x + 1) % per_plane == 0 else 0

    def base_low(x):
        return half if x % per_plane == 0 else 0

    def hop_parity(value, odd_up, extra):
        def target(x, y):
            if (y % 2 == 1) == odd_up:
                return (x + 1, y - base_up(x) - extra)
            return (x - 1, y + base_low(x) + extra)

        return hop(value, target)

    def hop_y(value, step):
        return hop(value, lambda x, y: (x, y + step))

    smem, vmem, anywhere = spec_of(pltpu.SMEM), spec_of(VMEM), spec_of(pl.ANY)
    plane = jax.ShapeDtypeStruct((rows, cols), f32)
    top, bottom = jnp.sum(order_dist[:, layers - 1], axis=0), jnp.sum(order_dist[:, 0], axis=0)
    rise = hop(top, lambda x, y: (x + 1, y - base_up(x)))
    fall = hop(bottom, lambda x, y: (x - 1, y + base_low(x)))

    block = jax.ShapeDtypeStruct((layers + 16, cols), f32)
    part = rows // 2
    index = pl.pallas_call(
        functools.partial(branch_kernel, part, half * rows),
        out_shape=jax.ShapeDtypeStruct((1,), jnp.int32),
        in_specs=[anywhere, smem],
        out_specs=smem,
        compiler_params=params(50 << 20),
        name="branch",
    )(order_dist, offsets)
    phi, to_north, to_south = pl.pallas_call(
        phi_kernel,
        out_shape=[jax.ShapeDtypeStruct((layers, rows, cols), f32)] + [block] * 2,
        in_specs=[smem, anywhere, vmem, vmem, vmem],
        out_specs=[vmem] * 3,
        scratch_shapes=[VMEM((19, 2, rows, cols), f32), pltpu.SemaphoreType.DMA((2,))],
        compiler_params=params(8 << 20),
        name="phi_all",
    )(index, momentum_dist, order_dist, top, bottom)
    to_north = jnp.concatenate([fall, to_north], 0)
    to_south = jnp.concatenate([rise, to_south], 0)
    south_msg, north_msg = hop_y(to_north, 1), hop_y(to_south, -1)

    face_moments, rims = pl.pallas_call(
        moment_kernel,
        out_shape=[
            jax.ShapeDtypeStruct((2, 4, rows, cols), f32),
            jax.ShapeDtypeStruct((2, 14, layers, cols), f32),
        ],
        in_specs=[anywhere, anywhere, vmem, vmem],
        out_specs=[vmem] * 2,
        compiler_params=params(16 << 20),
        name="moments",
    )(to_north, to_south, momentum_dist, order_dist)

    ten = jax.ShapeDtypeStruct((10, rows, cols), f32)
    ten_short = jax.ShapeDtypeStruct((10, part, cols), f32)
    ten_seam = jax.ShapeDtypeStruct((10 * part + 24, cols), f32)
    side = jax.ShapeDtypeStruct((10, layers, cols), f32)
    ten_side = jax.ShapeDtypeStruct((10, rows + layers, cols), f32)
    *outgoing, minus, plus = pl.pallas_call(
        functools.partial(face_kernel, (count_x, count_y)),
        out_shape=[ten_side, ten, ten_short, ten, ten_seam, ten, side] + [plane] * 2,
        in_specs=[smem] + [vmem] * 9,
        out_specs=[vmem] * 9,
        scratch_shapes=[
            VMEM((rows + 16, cols), f32),
            VMEM((rows + 16, cols), f32),
            VMEM((cols // LANES, 2 * rows + 16, LANES), f32),
            VMEM((rows + 16, cols), f32),
            VMEM((layers + 16, cols), f32),
            VMEM((2, 10, layers, cols), f32),
            VMEM((2, 10, rows, cols), f32),
            VMEM((11, 8, cols), f32),
            VMEM((2, 8, cols), f32),
            VMEM((cols // LANES, rows + 16, LANES), f32),
            VMEM((cols // LANES, 3 * rows + 16, LANES), f32),
        ],
        compiler_params=params(24 << 20),
        name="faces",
    )(
        offsets,
        momentum_dist,
        order_dist,
        face_moments,
        rims,
        phi,
        rise,
        fall,
        south_msg,
        north_msg,
    )
    around = (phi, minus, plus, south_msg, north_msg)
    whole = jax.ShapeDtypeStruct(momentum_dist.shape, f32)

    def finish(long_planes, mate, direct, direct_short, across, across_short, joint, cross):

        def is_long(x):
            return x % per_plane == 0 and x // per_plane % 4 in long_planes

        def hop_some(value, odd_up, extra, long):
            pairs = []
            for x in range(count_x):
                for y in range(count_y):
                    up = (y % 2 == 1) == odd_up
                    tx = (x + 1 if up else x - 1) % count_x
                    if is_long(tx if up else x) != long:
                        continue
                    ty = y - base_up(x) - extra if up else y + base_low(x) + extra
                    pairs.append((x * count_y + y, tx * count_y + ty % count_y))
            return lax.ppermute(value, ("gx", "gy"), pairs)

        cross = hop(cross, lambda x, y: (x, y + 1 if y % 2 == 1 else y - 1))
        mate = hop(mate, lambda x, y: (x, y ^ 1))
        direct = hop_some(direct, True, 0, False)
        direct_short = hop_some(direct_short, True, 0, True)
        across = hop_some(across, False, 1, True)
        across_short = hop_some(across_short, False, 1, False)
        joint = joint + mate[:, :rows]
        after = joint
        joint = hop_parity(joint, False, 0)

        next_f, next_g = pl.pallas_call(
            bulk_kernel,
            out_shape=[whole, whole],
            in_specs=[anywhere] + [vmem] * 9,
            out_specs=[vmem] * 2,
            scratch_shapes=[
                VMEM((layers + 2, rows, cols), f32),
                VMEM((rows + 16, cols), f32),
            ],
            compiler_params=params(48 << 20),
            name="bulk",
        )(after, momentum_dist, order_dist, *around, mate, cross)

        next_f, next_g = pl.pallas_call(
            functools.partial(merge_fill_kernel, (count_x, count_y)),
            out_shape=[whole, whole],
            in_specs=[smem] + [vmem] * 4 + [anywhere, anywhere],
            out_specs=[anywhere, anywhere],
            scratch_shapes=[VMEM((10, rows, cols), f32), pltpu.SemaphoreType.DMA((10,))],
            input_output_aliases={5: 0, 6: 1},
            compiler_params=params(24 << 20),
            name="merge_fill",
        )(offsets, direct, direct_short, across, across_short, next_f, next_g)

        return pl.pallas_call(
            joint_fill_kernel,
            out_shape=[whole, whole],
            in_specs=[vmem, anywhere, anywhere],
            out_specs=[anywhere, anywhere],
            scratch_shapes=[pltpu.SemaphoreType.DMA((10,))],
            input_output_aliases={1: 0, 2: 1},
            compiler_params=params(24 << 20),
            name="joint_fill",
        )(joint, next_f, next_g)

    branches = [
        functools.partial(finish, {3} | ({1} if k & 2 else set()) | ({2} if k & 1 else set()))
        for k in range(4)
    ]
    return lax.switch(index[0], branches, *outgoing)


def solution(mesh):
    return jax.shard_map(
        on_device,
        mesh=mesh,
        in_specs=(P(None, "gx", "gy", None), P(None, "gx", "gy", None), P()),
        out_specs=(P(None, "gx", "gy", None), P(None, "gx", "gy", None)),
        check_vma=False,
    )
```

```python
import functools

import jax
import jax.numpy as jnp
from jax import lax
from jax.experimental import pallas as pl
from jax.experimental.pallas import tpu as pltpu
from jax.sharding import PartitionSpec as P

lattice_velocity = [
    (0, 0, 0),
    (1, 0, 0),
    (-1, 0, 0),
    (0, 1, 0),
    (0, -1, 0),
    (0, 0, 1),
    (0, 0, -1),
    (1, 1, 0),
    (-1, -1, 0),
    (1, -1, 0),
    (-1, 1, 0),
    (1, 0, 1),
    (-1, 0, -1),
    (1, 0, -1),
    (-1, 0, 1),
    (0, 1, 1),
    (0, -1, -1),
    (0, 1, -1),
    (0, -1, 1),
]
lattice_weight = [1.0 / 3.0] + [1.0 / 18.0] * 6 + [1.0 / 36.0] * 12
plane_speed = 0.04
rising = [1, 7, 9, 11, 13]
falling = [2, 8, 10, 12, 14]
north_going = [i for i in range(19) if lattice_velocity[i][1] == 1]
south_going = [i for i in range(19) if lattice_velocity[i][1] == -1]
f32 = jnp.float32
VMEM = pltpu.VMEM
LANES = 128


def z_moved(value, step):
    if step == 0:
        return value
    return pltpu.roll(value, step % value.shape[-1], value.ndim - 1)


def spec_of(space):
    return pl.BlockSpec(memory_space=space)


def params(limit):
    return pltpu.CompilerParams(vmem_limit_bytes=limit)


def along(parts, c):
    total = None
    for sign, part in zip(c, parts):
        if sign == 0:
            continue
        if total is None:
            total = part if sign > 0 else -part
        else:
            total = total + part if sign > 0 else total - part
    return total


def signed_sum(load, axis):
    ups = [i for i in range(19) if lattice_velocity[i][axis] == 1]
    downs = [i for i in range(19) if lattice_velocity[i][axis] == -1]
    total = load(ups[0]) - load(downs[0])
    for i, j in zip(ups[1:], downs[1:]):
        total = total + (load(i) - load(j))
    return total


def moments_of(load):
    rho = load(0)
    for i in range(1, 19):
        rho = rho + load(i)
    return [rho] + [signed_sum(load, axis) for axis in range(3)]


class Site:
    def __init__(self, moments, phi, minus, plus, south, north):
        rho, momentum = moments[0], moments[1:]
        lower, upper = z_moved(phi, 1), z_moved(phi, -1)
        lap = (plus + minus) + (north + south) + (upper + lower) - 6.0 * phi
        mu = phi * (0.0625 * (phi * phi) - 0.0625) - 0.04 * lap
        half_mu = 0.5 * mu
        force = [half_mu * (plus - minus), half_mu * (north - south), half_mu * (upper - lower)]
        inverse = 1.0 / rho
        u = [(j + 0.5 * k) * inverse for j, k in zip(momentum, force)]
        uu = u[0] * u[0] + u[1] * u[1] + u[2] * u[2]
        uf = u[0] * force[0] + u[1] * force[1] + u[2] * force[2]
        self.rho, self.phi, self.mu, self.u, self.force, self.uu = rho, phi, mu, u, force, uu
        self.r = 1.25 * rho
        self.k = self.r * (1.0 - 1.5 * uu) - 1.125 * uf
        self.g_scale = phi * (1.0 / 0.9)
        self.g_base = (3.0 / 0.9) * mu - 1.5 * (self.g_scale * uu)

    def pair_f(self, i):
        p, q = along(self.u, lattice_velocity[i]), along(self.force, lattice_velocity[i])
        w = lattice_weight[i]
        rp = self.r * p
        even = w * (self.k + p * (4.5 * rp + 3.375 * q))
        odd = (3.0 * w) * rp + (1.125 * w) * q
        return even, odd

    def pair_g(self, i):
        p = along(self.u, lattice_velocity[i])
        w = lattice_weight[i]
        gp = self.g_scale * p
        return w * (self.g_base + 4.5 * (gp * p)), (3.0 * w) * gp

    def jump(self, i, delta):
        cy = lattice_velocity[i][1]
        uy = self.u[1]
        if cy == 0:
            return delta * (-3.0 * uy) - (1.5 * delta * delta)
        p = along(self.u, lattice_velocity[i])
        return delta * (3.0 * cy + (9.0 * cy) * p - 3.0 * uy) + (3.0 * delta * delta)


class Shear:
    def __init__(self, raw, wide, rows):
        self.raw, self.wide, self.rows = raw, wide, rows

    def clear(self):
        self.raw[...] = jnp.zeros_like(self.raw)
        self.wide[...] = jnp.zeros_like(self.wide)

    def put(self, value, up, near, far):
        n = self.rows
        for k in range(self.raw.shape[0]):
            self.raw[k, 8 : 8 + n] = value[:, LANES * k : LANES * k + LANES]
        for k in range(self.raw.shape[0]):
            if up:
                self.wide[k, n : n + n + 8] = (
                    near * self.raw[k, 0 : n + 8] + far * self.raw[k, 1 : n + 9]
                )
            else:
                self.wide[k, n + 8 : n + n + 16] = (
                    near * self.raw[k, 7 : n + 15] + far * self.raw[k, 8 : n + 16]
                )

    def add_row(self, at, row):
        for k in range(self.raw.shape[0]):
            lanes = slice(LANES * k, LANES * k + LANES)
            self.wide[k, at : at + 1] = self.wide[k, at : at + 1] + row[:, lanes]

    def take(self, up, block, rest, cy, ref, j):
        n = self.rows
        if up:
            start = (n + 8 if block == 0 else 8) + rest - cy
        else:
            start = (n + 8 if block == 0 else n + n + 8) - rest - cy
        for k in range(self.raw.shape[0]):
            ref[j, 0:n, LANES * k : LANES * k + LANES] = self.wide[k, pl.ds(start, n)]


class Planes:
    def __init__(self, offsets, rows, sizes):
        count_x, count_y = sizes
        per_plane, half = count_x // 4, count_y // 2
        a = lax.axis_index("gx")
        self.odd = lax.rem(lax.axis_index("gy"), 2) == 1

        def plane_of(column):
            is_plane = lax.rem(column, per_plane) == 0
            plane = lax.rem(lax.div(column, per_plane), 4)
            rest = jnp.where(is_plane, jnp.clip(offsets[plane] - half * rows, 0, rows - 1), 0)
            return is_plane, (2.0 * plane.astype(f32) + 1.0) * 0.125, rest

        up_is, up_part, self.up_rest = plane_of(lax.rem(a + 1, count_x))
        low_is, low_part, self.low_rest = plane_of(a)
        self.up_near = jnp.where(up_is, 1.0 - up_part, 1.0)
        self.up_far = jnp.where(up_is, up_part, 0.0)
        self.low_near = jnp.where(low_is, low_part, 0.0)
        self.low_far = jnp.where(low_is, 1.0 - low_part, 1.0)
        self.up_jump = jnp.where(up_is, -plane_speed, 0.0)
        self.low_jump = jnp.where(low_is, plane_speed, 0.0)


def order_sum(load):
    total = load(0)
    for i in range(1, 19):
        total = total + load(i)
    return total


def phi_kernel(f_ref, g_ref, top, bottom, phi_ref, to_north, to_south, gbuf, fbuf, sems):
    layers, rows = phi_ref.shape[0], phi_ref.shape[1]
    faces = (layers - 1, 0)
    f_copies = [
        pltpu.make_async_copy(f_ref.at[:, x], fbuf.at[:, s], sems.at[layers + s])
        for s, x in enumerate(faces)
    ]
    g_copies = [
        pltpu.make_async_copy(g_ref.at[:, x], gbuf.at[:, x], sems.at[x]) for x in range(layers)
    ]
    for copy in f_copies + g_copies:
        copy.start()
    phi_ref[layers - 1] = top[...]
    phi_ref[0] = bottom[...]
    edges = ((to_north, rows - 1, rows - 2, (7, 10)), (to_south, 0, 1, (9, 8)))
    for s, x in enumerate(faces):
        f_copies[s].wait()
        for out, edge, inner, chosen in edges:
            out[layers + s : layers + s + 1] = phi_ref[x, inner : inner + 1]
            at = layers + 2 + 6 * s
            out[at : at + 1] = fbuf[chosen[s], s, edge : edge + 1]
            for k, part in enumerate(moments_of(lambda i: fbuf[i, s, edge : edge + 1])):
                out[at + 2 + k : at + 3 + k] = part
    for x in range(layers):
        g_copies[x].wait()
        if 0 < x < layers - 1:
            phi_ref[x] = order_sum(lambda i: gbuf[i, x])
        to_north[x : x + 1] = phi_ref[x, rows - 1 : rows]
        to_south[x : x + 1] = phi_ref[x, 0:1]
    for s, x in enumerate(faces):
        for out, edge, inner, chosen in edges:
            at = layers + 3 + 6 * s
            out[at : at + 1] = gbuf[chosen[s], x, edge : edge + 1]
    for out in (to_north, to_south):
        out[layers + 14 : layers + 16] = jnp.zeros((2, out.shape[1]), f32)


def with_halo(ref, layer, below, above):
    rows = layer.shape[0]
    ref[8 : 8 + rows] = layer
    ref[7:8] = below
    ref[8 + rows : 9 + rows] = above


def corner_values(cells, planes, phi_ref, south_msg, north_msg, minus_wide, plus_wide):
    layers, rows, cols = phi_ref.shape
    cells[...] = jnp.ones_like(cells)
    for row in range(4):
        msg = south_msg if row < 2 else north_msg
        x = layers - 1 if row % 2 == 0 else 0
        beside = rows + (layers - 2 if row % 2 == 0 else 1)
        wide_row = 7 if row < 2 else rows + 8
        at = rows + layers
        first = at + 2 + 6 * (row % 2)
        far_phi = msg[at + row % 2 : at + row % 2 + 1]
        own_phi = phi_ref[x, 0:1] if row < 2 else phi_ref[x, rows - 1 : rows]
        parts = [msg[first + k : first + k + 1] for k in range(6)]
        parts.append(msg[rows + x : rows + x + 1])
        if row % 2 == 0:
            parts += [msg[beside : beside + 1], plus_wide[wide_row : wide_row + 1]]
        else:
            parts += [minus_wide[wide_row : wide_row + 1], msg[beside : beside + 1]]
        parts += [far_phi, own_phi] if row < 2 else [own_phi, far_phi]
        for k, part in enumerate(parts):
            cells[k, row : row + 1] = part
    place = lax.broadcasted_iota(jnp.int32, (8, cols), 0)
    is_top = (place == 0) | (place == 2)
    sx = jnp.where(is_top, 1.0, -1.0)
    sy = jnp.where(place < 2, 1.0, -1.0)
    delta = jnp.where(is_top, planes.up_jump, planes.low_jump)
    site = Site([cells[k] for k in range(2, 6)], *[cells[k] for k in range(6, 11)])
    w = lattice_weight[7]
    p = sx * site.u[0] + sy * site.u[1]
    q = sx * site.force[0] + sy * site.force[1]
    change = delta * (3.0 * sy + 9.0 * (sy * p) - 3.0 * site.u[1]) + 3.0 * (delta * delta)
    rp, gp = site.r * p, site.g_scale * p
    f_post = w * (site.k + p * (4.5 * rp + 3.375 * q) + 3.0 * rp + 1.125 * q + site.rho * change)
    g_post = w * (site.g_base + 4.5 * (gp * p) + 3.0 * gp + site.phi * change)
    return f_post - 0.25 * cells[0], g_post - (1.0 / 9.0) * cells[1]


def moment_kernel(after_north, after_south, f_ref, g_ref, faces, rims):
    layers, rows = f_ref.shape[1], f_ref.shape[2]
    for s, x in enumerate((layers - 1, 0)):
        for k, part in enumerate(moments_of(lambda i: f_ref[i, x])):
            faces[s, k] = part
    for s, (edge, chosen) in enumerate(((rows - 1, north_going), (0, south_going))):
        for k, part in enumerate(moments_of(lambda i: f_ref[i, :, edge, :])):
            rims[s, k] = part
        for j, i in enumerate(chosen):
            rims[s, 4 + j] = f_ref[i, :, edge, :]
            rims[s, 9 + j] = g_ref[i, :, edge, :]


def half_rows(rows, first):
    return slice(0, rows // 2) if first else slice(rows // 2, rows)


def seam_rows(rows, up):
    return slice(rows // 2 - 2, rows // 2) if up else slice(rows // 2, rows // 2 + 2)


def rim_values(rims, s, phi_ref, minus, plus, south_msg, north_msg, line, edge, chosen, out):
    layers, rows, cols = phi_ref.shape
    phi = phi_ref[:, edge, :]
    with_halo(line, phi, minus[edge : edge + 1], plus[edge : edge + 1])
    if edge == 0:
        below, above = south_msg[rows : rows + layers], phi_ref[:, 1, :]
    else:
        below, above = phi_ref[:, rows - 2, :], north_msg[rows : rows + layers]
    site = Site(
        [rims[s, k] for k in range(4)],
        phi,
        line[7 : 7 + layers],
        line[9 : 9 + layers],
        below,
        above,
    )
    for j, i in enumerate(chosen):
        cz = lattice_velocity[i][2]
        even, odd = site.pair_f(i)
        out[s, j] = z_moved(even + odd - 0.25 * rims[s, 4 + j], cz)
        even, odd = site.pair_g(i)
        out[s, 5 + j] = z_moved(even + odd - (1.0 / 9.0) * rims[s, 9 + j], cz)


def face_kernel(
    sizes,
    offsets,
    f_ref,
    g_ref,
    face_moments,
    rims,
    phi_ref,
    rise,
    fall,
    south_msg,
    north_msg,
    mate,
    direct,
    direct_short,
    across,
    across_short,
    joint,
    cross,
    minus_out,
    plus_out,
    minus_wide,
    plus_wide,
    window,
    halo,
    line,
    rim_post,
    post,
    cells,
    corners,
    raw,
    wide,
):
    layers, rows, cols = phi_ref.shape
    planes = Planes(offsets, rows, sizes)
    shear = Shear(raw, wide, rows)
    window[...] = jnp.zeros_like(window)
    for up in (True, False):
        if up:
            first, second = rise, north_msg
            near, far, start = planes.low_far, planes.low_near, planes.low_rest
        else:
            first, second = south_msg, fall
            near, far, start = planes.up_far, planes.up_near, rows - 1 - planes.up_rest
        target = minus_wide if up else plus_wide
        for k in range(window.shape[0]):
            lanes = slice(LANES * k, LANES * k + LANES)
            window[k, 8 : 8 + rows] = first[0:rows, lanes]
            window[k, 8 + rows : 8 + 2 * rows] = second[0:rows, lanes]
            target[:, lanes] = (
                near * window[k, pl.ds(start, rows + 16)]
                + far * window[k, pl.ds(start + 1, rows + 16)]
            )
    minus_out[...] = minus_wide[8 : 8 + rows]
    plus_out[...] = plus_wide[8 : 8 + rows]
    corners[0], corners[1] = corner_values(
        cells, planes, phi_ref, south_msg, north_msg, minus_wide, plus_wide
    )
    for s, (edge, chosen) in enumerate(((rows - 1, north_going), (0, south_going))):
        rim_values(
            rims,
            s,
            phi_ref,
            minus_out,
            plus_out,
            south_msg,
            north_msg,
            line,
            edge,
            chosen,
            rim_post,
        )
    for side, up in enumerate((True, False)):
        x = layers - 1 if up else 0
        delta = planes.up_jump if up else planes.low_jump
        with_halo(
            halo, phi_ref[x], south_msg[rows + x : rows + x + 1], north_msg[rows + x : rows + x + 1]
        )
        for h in range(0, rows, 8):
            span = slice(h, h + 8)
            phi_h = phi_ref[x, span]
            if up:
                minus, plus = phi_ref[x - 1, span], plus_wide[8 + h : 16 + h]
            else:
                minus, plus = minus_wide[8 + h : 16 + h], phi_ref[x + 1, span]
            site = Site(
                [face_moments[side, k, span] for k in range(4)],
                phi_h,
                minus,
                plus,
                halo[7 + h : 15 + h],
                halo[9 + h : 17 + h],
            )
            for j, i in enumerate(rising if up else falling):
                cz = lattice_velocity[i][2]
                change = lattice_weight[i] * site.jump(i, delta)
                even, odd = site.pair_f(i)
                value = even + odd - 0.25 * f_ref[i, x, span] + site.rho * change
                post[side, j, span] = z_moved(value, cz)
                even, odd = site.pair_g(i)
                value = even + odd - (1.0 / 9.0) * g_ref[i, x, span] + phi_h * change
                post[side, 5 + j, span] = z_moved(value, cz)

    part = rows // 2
    seam = 10 * part

    def hand_out(is_odd):
        for side, up in enumerate((True, False)):
            if up:
                near, far, rest = planes.up_near, planes.up_far, planes.up_rest
            else:
                near, far, rest = planes.low_near, planes.low_far, planes.low_rest
            first, second = (direct, mate) if up == is_odd else (joint, across)
            shear.clear()
            for j in range(10):
                cy = lattice_velocity[(rising if up else falling)[j % 5]][1]
                shear.put(post[side, j], up, near, far)
                corner = side + (0 if cy == 1 else 2)
                if cy == 1:
                    gate = jnp.where(rest == (0 if up else rows - 1), near, 0.0)
                    at = rows + 7 if up else rows + 8
                if cy == -1:
                    gate = jnp.where(rest == (rows - 1 if up else 0), far, 0.0)
                    at = 2 * rows + 7 if up else 2 * rows + 8
                if cy != 0:
                    shear.add_row(at, gate * corners[j // 5, corner : corner + 1])
                shear.take(up, 0, rest, cy, first, j)
                shear.take(up, 1, rest, cy, second, j)
        for j in range(10):
            mate[j, rows : rows + layers] = rim_post[1 if is_odd else 0, j]
            cross[j] = rim_post[0 if is_odd else 1, j]
            direct_short[j] = direct[j, half_rows(rows, is_odd)]
            across_short[part * j : part * j + part] = across[j, half_rows(rows, is_odd)]
            across_short[seam + 2 * j : seam + 2 * j + 2] = across[j, seam_rows(rows, not is_odd)]
        across_short[seam + 20 : seam + 24] = jnp.zeros((4, cols), f32)

    pl.when(planes.odd)(lambda: hand_out(True))
    pl.when(jnp.logical_not(planes.odd))(lambda: hand_out(False))


def bulk_kernel(
    after,
    f_ref,
    g_ref,
    phi_ref,
    minus,
    plus,
    south_msg,
    north_msg,
    mate_rim,
    cross_rim,
    next_f,
    next_g,
    wide_phi,
    halo,
):
    layers, rows, cols = phi_ref.shape
    is_odd = lax.rem(lax.axis_index("gy"), 2) == 1
    wide_phi[0] = minus[...]
    wide_phi[layers + 1] = plus[...]
    for x in range(layers):
        wide_phi[x + 1] = phi_ref[x]

    def layer(x, carry):
        with_halo(halo, phi_ref[x], south_msg[pl.ds(rows + x, 1)], north_msg[pl.ds(rows + x, 1)])
        beyond = lax.rem(x + 1, layers)
        before = lax.rem(x + layers - 1, layers)
        for h in range(0, rows, 8):
            span = slice(h, h + 8)
            phi_h = phi_ref[x, span]
            site = Site(
                moments_of(lambda i: f_ref[i, x, span]),
                phi_h,
                wide_phi[x, span],
                wide_phi[x + 2, span],
                halo[7 + h : 15 + h],
                halo[9 + h : 17 + h],
            )

            def emit(out, slot, i, value):
                cx, cy, cz = lattice_velocity[i]
                value = z_moved(value, cz)
                at = beyond if cx == 1 else before if cx == -1 else x
                if cy == 0:
                    out[i, at, span] = value
                elif cy == 1:
                    if h == 0:
                        rim = slot * 5 + north_going.index(i)
                        out[i, at, 0:1] = jnp.where(
                            is_odd, mate_rim[rim, pl.ds(rows + x, 1)], cross_rim[rim, pl.ds(x, 1)]
                        )
                    if h + 8 < rows:
                        out[i, at, h + 1 : h + 9] = value
                    else:
                        out[i, at, h + 1 : h + 8] = value[0:7]
                else:
                    if h + 8 == rows:
                        rim = slot * 5 + south_going.index(i)
                        out[i, at, rows - 1 : rows] = jnp.where(
                            is_odd, cross_rim[rim, pl.ds(x, 1)], mate_rim[rim, pl.ds(rows + x, 1)]
                        )
                    if h > 0:
                        out[i, at, h - 1 : h + 7] = value
                    else:
                        out[i, at, 0:7] = value[1:8]

            emit(next_f, 0, 0, lattice_weight[0] * site.k - 0.25 * f_ref[0, x, span])
            rest_g = (phi_h - 2.0 * site.mu - 0.5 * (phi_h * site.uu)) * (1.0 / 0.9)
            emit(next_g, 1, 0, rest_g - (1.0 / 9.0) * g_ref[0, x, span])
            for i in range(1, 19, 2):
                even, odd = site.pair_f(i)
                emit(next_f, 0, i, (even + odd) - 0.25 * f_ref[i, x, span])
                emit(next_f, 0, i + 1, (even - odd) - 0.25 * f_ref[i + 1, x, span])
                even, odd = site.pair_g(i)
                emit(next_g, 1, i, (even + odd) - (1.0 / 9.0) * g_ref[i, x, span])
                emit(next_g, 1, i + 1, (even - odd) - (1.0 / 9.0) * g_ref[i + 1, x, span])
        return carry

    lax.fori_loop(0, layers, layer, 0)


def put_faces(buf, out_f, out_g, chosen, x, sems):
    copies = [
        pltpu.make_async_copy(buf.at[5 * family + j], out.at[i, x], sems.at[5 * family + j])
        for family, out in enumerate((out_f, out_g))
        for j, i in enumerate(chosen)
    ]
    for copy in copies:
        copy.start()
    for copy in copies:
        copy.wait()


def merge_fill_kernel(
    sizes,
    offsets,
    direct,
    direct_short,
    across,
    across_short,
    f_in,
    g_in,
    f_out,
    g_out,
    buf,
    sems,
):
    layers, rows = f_out.shape[1], f_out.shape[2]
    planes = Planes(offsets, rows, sizes)
    part = rows // 2
    seam = 10 * part

    def merge(rest, up):
        is_long = rest > part
        near, other, between = half_rows(rows, up), half_rows(rows, not up), seam_rows(rows, up)

        @pl.when(is_long)
        def _():
            buf[...] = across[...]
            for j in range(10):
                buf[j, near] = buf[j, near] + direct_short[j]

        @pl.when(jnp.logical_not(is_long))
        def _():
            buf[...] = direct[...]
            for j in range(10):
                buf[j, other] = buf[j, other] + across_short[part * j : part * j + part]
                at = seam + 2 * j
                buf[j, between] = buf[j, between] + across_short[at : at + 2]

        if up:
            put_faces(buf, f_out, g_out, rising, 0, sems)
        else:
            put_faces(buf, f_out, g_out, falling, layers - 1, sems)

    pl.when(planes.odd)(lambda: merge(planes.low_rest, True))
    pl.when(jnp.logical_not(planes.odd))(lambda: merge(planes.up_rest, False))


def joint_fill_kernel(joint, f_in, g_in, f_out, g_out, sems):
    odd = lax.rem(lax.axis_index("gy"), 2) == 1
    layers = f_out.shape[1]
    pl.when(odd)(lambda: put_faces(joint, f_out, g_out, falling, layers - 1, sems))
    pl.when(jnp.logical_not(odd))(lambda: put_faces(joint, f_out, g_out, rising, 0, sems))


def on_device(momentum_dist, order_dist, offsets):
    layers, rows, cols = momentum_dist.shape[1:]
    count_x, count_y = lax.axis_size("gx"), lax.axis_size("gy")
    per_plane = count_x // 4
    half = count_y // 2

    def hop(value, target):
        perm = []
        for x in range(count_x):
            for y in range(count_y):
                tx, ty = target(x, y)
                perm.append((x * count_y + y, tx % count_x * count_y + ty % count_y))
        return lax.ppermute(value, ("gx", "gy"), perm)

    def base_up(x):
        return half if (x + 1) % per_plane == 0 else 0

    def base_low(x):
        return half if x % per_plane == 0 else 0

    def hop_parity(value, odd_up, extra):
        def target(x, y):
            if (y % 2 == 1) == odd_up:
                return (x + 1, y - base_up(x) - extra)
            return (x - 1, y + base_low(x) + extra)

        return hop(value, target)

    def hop_y(value, step):
        return hop(value, lambda x, y: (x, y + step))

    smem, vmem, anywhere = spec_of(pltpu.SMEM), spec_of(VMEM), spec_of(pl.ANY)
    plane = jax.ShapeDtypeStruct((rows, cols), f32)
    top, bottom = jnp.sum(order_dist[:, layers - 1], axis=0), jnp.sum(order_dist[:, 0], axis=0)
    rise = hop(top, lambda x, y: (x + 1, y - base_up(x)))
    fall = hop(bottom, lambda x, y: (x - 1, y + base_low(x)))

    block = jax.ShapeDtypeStruct((layers + 16, cols), f32)
    phi, to_north, to_south, order_near = pl.pallas_call(
        phi_kernel,
        out_shape=[jax.ShapeDtypeStruct((layers, rows, cols), f32)]
        + [block] * 2
        + [jax.ShapeDtypeStruct(order_dist.shape, f32)],
        in_specs=[anywhere, anywhere, vmem, vmem],
        out_specs=[vmem] * 4,
        scratch_shapes=[
            VMEM((19, 2, rows, cols), f32),
            pltpu.SemaphoreType.DMA((layers + 2,)),
        ],
        compiler_params=params(52 << 20),
        name="phi_all",
    )(momentum_dist, order_dist, top, bottom)
    to_north = jnp.concatenate([fall, to_north], 0)
    to_south = jnp.concatenate([rise, to_south], 0)
    south_msg, north_msg = hop_y(to_north, 1), hop_y(to_south, -1)

    face_moments, rims = pl.pallas_call(
        moment_kernel,
        out_shape=[
            jax.ShapeDtypeStruct((2, 4, rows, cols), f32),
            jax.ShapeDtypeStruct((2, 14, layers, cols), f32),
        ],
        in_specs=[anywhere, anywhere, vmem, vmem],
        out_specs=[vmem] * 2,
        compiler_params=params(16 << 20),
        name="moments",
    )(to_north, to_south, momentum_dist, order_near)

    part = rows // 2
    ten = jax.ShapeDtypeStruct((10, rows, cols), f32)
    ten_short = jax.ShapeDtypeStruct((10, part, cols), f32)
    ten_seam = jax.ShapeDtypeStruct((10 * part + 24, cols), f32)
    side = jax.ShapeDtypeStruct((10, layers, cols), f32)
    ten_side = jax.ShapeDtypeStruct((10, rows + layers, cols), f32)
    *outgoing, minus, plus = pl.pallas_call(
        functools.partial(face_kernel, (count_x, count_y)),
        out_shape=[ten_side, ten, ten_short, ten, ten_seam, ten, side] + [plane] * 2,
        in_specs=[smem] + [vmem] * 9,
        out_specs=[vmem] * 9,
        scratch_shapes=[
            VMEM((rows + 16, cols), f32),
            VMEM((rows + 16, cols), f32),
            VMEM((cols // LANES, 2 * rows + 16, LANES), f32),
            VMEM((rows + 16, cols), f32),
            VMEM((layers + 16, cols), f32),
            VMEM((2, 10, layers, cols), f32),
            VMEM((2, 10, rows, cols), f32),
            VMEM((11, 8, cols), f32),
            VMEM((2, 8, cols), f32),
            VMEM((cols // LANES, rows + 16, LANES), f32),
            VMEM((cols // LANES, 3 * rows + 16, LANES), f32),
        ],
        compiler_params=params(24 << 20),
        name="faces",
    )(
        offsets,
        momentum_dist,
        order_near,
        face_moments,
        rims,
        phi,
        rise,
        fall,
        south_msg,
        north_msg,
    )
    around = (phi, minus, plus, south_msg, north_msg)
    whole = jax.ShapeDtypeStruct(momentum_dist.shape, f32)

    def finish(long_planes, mate, direct, direct_short, across, across_short, joint, cross):

        def is_long(x):
            return x % per_plane == 0 and x // per_plane % 4 in long_planes

        def hop_some(value, odd_up, extra, long):
            pairs = []
            for x in range(count_x):
                for y in range(count_y):
                    up = (y % 2 == 1) == odd_up
                    tx = (x + 1 if up else x - 1) % count_x
                    if is_long(tx if up else x) != long:
                        continue
                    ty = y - base_up(x) - extra if up else y + base_low(x) + extra
                    pairs.append((x * count_y + y, tx * count_y + ty % count_y))
            return lax.ppermute(value, ("gx", "gy"), pairs)

        cross = hop(cross, lambda x, y: (x, y + 1 if y % 2 == 1 else y - 1))
        mate = hop(mate, lambda x, y: (x, y ^ 1))
        direct, direct_short, across, across_short, cross = lax.optimization_barrier(
            (direct, direct_short, across, across_short, cross)
        )
        direct = hop_some(direct, True, 0, False)
        direct_short = hop_some(direct_short, True, 0, True)
        across = hop_some(across, False, 1, True)
        across_short = hop_some(across_short, False, 1, False)
        joint = joint + mate[:, :rows]
        after = joint
        joint = hop_parity(joint, False, 0)

        next_f, next_g = pl.pallas_call(
            bulk_kernel,
            out_shape=[whole, whole],
            in_specs=[anywhere] + [vmem] * 9,
            out_specs=[vmem] * 2,
            scratch_shapes=[
                VMEM((layers + 2, rows, cols), f32),
                VMEM((rows + 16, cols), f32),
            ],
            compiler_params=params(48 << 20),
            name="bulk",
        )(after, momentum_dist, order_near, *around, mate, cross)

        next_f, next_g = pl.pallas_call(
            joint_fill_kernel,
            out_shape=[whole, whole],
            in_specs=[vmem, anywhere, anywhere],
            out_specs=[anywhere, anywhere],
            scratch_shapes=[pltpu.SemaphoreType.DMA((10,))],
            input_output_aliases={1: 0, 2: 1},
            compiler_params=params(24 << 20),
            name="joint_fill",
        )(joint, next_f, next_g)

        return pl.pallas_call(
            functools.partial(merge_fill_kernel, (count_x, count_y)),
            out_shape=[whole, whole],
            in_specs=[smem] + [vmem] * 4 + [anywhere, anywhere],
            out_specs=[anywhere, anywhere],
            scratch_shapes=[VMEM((10, rows, cols), f32), pltpu.SemaphoreType.DMA((10,))],
            input_output_aliases={5: 0, 6: 1},
            compiler_params=params(24 << 20),
            name="merge_fill",
        )(offsets, direct, direct_short, across, across_short, next_f, next_g)

    is_long = [(offsets[k] - half * rows > part).astype(jnp.int32) for k in (1, 2)]
    branches = [
        functools.partial(finish, {3} | ({1} if k & 2 else set()) | ({2} if k & 1 else set()))
        for k in range(4)
    ]
    return lax.switch(2 * is_long[0] + is_long[1], branches, *outgoing)


def solution(mesh):
    return jax.shard_map(
        on_device,
        mesh=mesh,
        in_specs=(P(None, "gx", "gy", None), P(None, "gx", "gy", None), P()),
        out_specs=(P(None, "gx", "gy", None), P(None, "gx", "gy", None)),
        check_vma=False,
    )
```

```python
import functools

import jax
import jax.numpy as jnp
from jax import lax
from jax.experimental import pallas as pl
from jax.experimental.pallas import tpu as pltpu
from jax.sharding import PartitionSpec as P

lattice_velocity = [
    (0, 0, 0),
    (1, 0, 0),
    (-1, 0, 0),
    (0, 1, 0),
    (0, -1, 0),
    (0, 0, 1),
    (0, 0, -1),
    (1, 1, 0),
    (-1, -1, 0),
    (1, -1, 0),
    (-1, 1, 0),
    (1, 0, 1),
    (-1, 0, -1),
    (1, 0, -1),
    (-1, 0, 1),
    (0, 1, 1),
    (0, -1, -1),
    (0, 1, -1),
    (0, -1, 1),
]
lattice_weight = [1.0 / 3.0] + [1.0 / 18.0] * 6 + [1.0 / 36.0] * 12
plane_speed = 0.04
rising = [1, 7, 9, 11, 13]
falling = [2, 8, 10, 12, 14]
north_going = [i for i in range(19) if lattice_velocity[i][1] == 1]
south_going = [i for i in range(19) if lattice_velocity[i][1] == -1]
f32 = jnp.float32
VMEM = pltpu.VMEM
LANES = 128


def z_moved(value, step):
    if step == 0:
        return value
    return pltpu.roll(value, step % value.shape[-1], value.ndim - 1)


def spec_of(space):
    return pl.BlockSpec(memory_space=space)


def params(limit):
    return pltpu.CompilerParams(vmem_limit_bytes=limit)


def along(parts, c):
    total = None
    for sign, part in zip(c, parts):
        if sign == 0:
            continue
        if total is None:
            total = part if sign > 0 else -part
        else:
            total = total + part if sign > 0 else total - part
    return total


def signed_sum(load, axis):
    ups = [i for i in range(19) if lattice_velocity[i][axis] == 1]
    downs = [i for i in range(19) if lattice_velocity[i][axis] == -1]
    total = load(ups[0]) - load(downs[0])
    for i, j in zip(ups[1:], downs[1:]):
        total = total + (load(i) - load(j))
    return total


def moments_of(load):
    rho = load(0)
    for i in range(1, 19):
        rho = rho + load(i)
    return [rho] + [signed_sum(load, axis) for axis in range(3)]


class Site:
    def __init__(self, moments, phi, minus, plus, south, north):
        rho, momentum = moments[0], moments[1:]
        lower, upper = z_moved(phi, 1), z_moved(phi, -1)
        lap = (plus + minus) + (north + south) + (upper + lower) - 6.0 * phi
        mu = phi * (0.0625 * (phi * phi) - 0.0625) - 0.04 * lap
        half_mu = 0.5 * mu
        force = [half_mu * (plus - minus), half_mu * (north - south), half_mu * (upper - lower)]
        inverse = 1.0 / rho
        u = [(j + 0.5 * k) * inverse for j, k in zip(momentum, force)]
        uu = u[0] * u[0] + u[1] * u[1] + u[2] * u[2]
        uf = u[0] * force[0] + u[1] * force[1] + u[2] * force[2]
        self.rho, self.phi, self.mu, self.u, self.force, self.uu = rho, phi, mu, u, force, uu
        self.r = 1.25 * rho
        self.k = self.r * (1.0 - 1.5 * uu) - 1.125 * uf
        self.g_scale = phi * (1.0 / 0.9)
        self.g_base = (3.0 / 0.9) * mu - 1.5 * (self.g_scale * uu)

    def pair_f(self, i):
        p, q = along(self.u, lattice_velocity[i]), along(self.force, lattice_velocity[i])
        w = lattice_weight[i]
        rp = self.r * p
        even = w * (self.k + p * (4.5 * rp + 3.375 * q))
        odd = (3.0 * w) * rp + (1.125 * w) * q
        return even, odd

    def pair_g(self, i):
        p = along(self.u, lattice_velocity[i])
        w = lattice_weight[i]
        gp = self.g_scale * p
        return w * (self.g_base + 4.5 * (gp * p)), (3.0 * w) * gp

    def jump(self, i, delta):
        cy = lattice_velocity[i][1]
        uy = self.u[1]
        if cy == 0:
            return delta * (-3.0 * uy) - (1.5 * delta * delta)
        p = along(self.u, lattice_velocity[i])
        return delta * (3.0 * cy + (9.0 * cy) * p - 3.0 * uy) + (3.0 * delta * delta)


class Shear:
    def __init__(self, raw, wide, rows):
        self.raw, self.wide, self.rows = raw, wide, rows

    def clear(self):
        self.raw[...] = jnp.zeros_like(self.raw)
        self.wide[...] = jnp.zeros_like(self.wide)

    def put(self, value, up, near, far):
        n = self.rows
        for k in range(self.raw.shape[0]):
            self.raw[k, 8 : 8 + n] = value[:, LANES * k : LANES * k + LANES]
        for k in range(self.raw.shape[0]):
            if up:
                self.wide[k, n : n + n + 8] = (
                    near * self.raw[k, 0 : n + 8] + far * self.raw[k, 1 : n + 9]
                )
            else:
                self.wide[k, n + 8 : n + n + 16] = (
                    near * self.raw[k, 7 : n + 15] + far * self.raw[k, 8 : n + 16]
                )

    def add_row(self, at, row):
        for k in range(self.raw.shape[0]):
            lanes = slice(LANES * k, LANES * k + LANES)
            self.wide[k, at : at + 1] = self.wide[k, at : at + 1] + row[:, lanes]

    def take(self, up, block, rest, cy, ref, j):
        n = self.rows
        if up:
            start = (n + 8 if block == 0 else 8) + rest - cy
        else:
            start = (n + 8 if block == 0 else n + n + 8) - rest - cy
        for k in range(self.raw.shape[0]):
            ref[j, 0:n, LANES * k : LANES * k + LANES] = self.wide[k, pl.ds(start, n)]


class Planes:
    def __init__(self, offsets, rows, sizes):
        count_x, count_y = sizes
        per_plane, half = count_x // 4, count_y // 2
        a = lax.axis_index("gx")
        self.odd = lax.rem(lax.axis_index("gy"), 2) == 1

        def plane_of(column):
            is_plane = lax.rem(column, per_plane) == 0
            plane = lax.rem(lax.div(column, per_plane), 4)
            rest = jnp.where(is_plane, jnp.clip(offsets[plane] - half * rows, 0, rows - 1), 0)
            return is_plane, (2.0 * plane.astype(f32) + 1.0) * 0.125, rest

        up_is, up_part, self.up_rest = plane_of(lax.rem(a + 1, count_x))
        low_is, low_part, self.low_rest = plane_of(a)
        self.up_near = jnp.where(up_is, 1.0 - up_part, 1.0)
        self.up_far = jnp.where(up_is, up_part, 0.0)
        self.low_near = jnp.where(low_is, low_part, 0.0)
        self.low_far = jnp.where(low_is, 1.0 - low_part, 1.0)
        self.up_jump = jnp.where(up_is, -plane_speed, 0.0)
        self.low_jump = jnp.where(low_is, plane_speed, 0.0)


def order_sum(load):
    total = load(0)
    for i in range(1, 19):
        total = total + load(i)
    return total


def phi_faces_kernel(part, base, f_ref, g_ref, offsets, top, bottom, index, buf, sems):
    layers = g_ref.shape[1]
    copies = [
        pltpu.make_async_copy(g_ref.at[:, x], buf.at[s], sems.at[s])
        for s, x in enumerate((layers - 1, 0))
    ]
    for copy in copies:
        copy.start()
    first, second = offsets[1] - base > part, offsets[2] - base > part
    index[0] = 2 * first.astype(jnp.int32) + second.astype(jnp.int32)
    for s, (copy, out) in enumerate(zip(copies, (top, bottom))):
        copy.wait()
        out[...] = order_sum(lambda i: buf[s, i])


def phi_kernel(f_ref, g_ref, top, bottom, phi_ref, to_north, to_south):
    layers, rows = phi_ref.shape[0], phi_ref.shape[1]
    faces = (layers - 1, 0)
    phi_ref[layers - 1] = top[...]
    phi_ref[0] = bottom[...]
    for x in range(layers):
        if 0 < x < layers - 1:
            phi_ref[x] = order_sum(lambda i: g_ref[i, x])
        to_north[x : x + 1] = phi_ref[x, rows - 1 : rows]
        to_south[x : x + 1] = phi_ref[x, 0:1]
    for s, x in enumerate(faces):
        for out, edge, inner, chosen in (
            (to_north, rows - 1, rows - 2, (7, 10)),
            (to_south, 0, 1, (9, 8)),
        ):
            out[layers + s : layers + s + 1] = phi_ref[x, inner : inner + 1]
            at = layers + 2 + 6 * s
            out[at : at + 1] = f_ref[chosen[s], x, edge : edge + 1]
            out[at + 1 : at + 2] = g_ref[chosen[s], x, edge : edge + 1]
            for k, part in enumerate(moments_of(lambda i: f_ref[i, x, edge : edge + 1])):
                out[at + 2 + k : at + 3 + k] = part
    for out in (to_north, to_south):
        out[layers + 14 : layers + 16] = jnp.zeros((2, out.shape[1]), f32)


def with_halo(ref, layer, below, above):
    rows = layer.shape[0]
    ref[8 : 8 + rows] = layer
    ref[7:8] = below
    ref[8 + rows : 9 + rows] = above


def corner_values(cells, planes, phi_ref, south_msg, north_msg, minus_wide, plus_wide):
    layers, rows, cols = phi_ref.shape
    cells[...] = jnp.ones_like(cells)
    for row in range(4):
        msg = south_msg if row < 2 else north_msg
        x = layers - 1 if row % 2 == 0 else 0
        beside = rows + (layers - 2 if row % 2 == 0 else 1)
        wide_row = 7 if row < 2 else rows + 8
        at = rows + layers
        first = at + 2 + 6 * (row % 2)
        far_phi = msg[at + row % 2 : at + row % 2 + 1]
        own_phi = phi_ref[x, 0:1] if row < 2 else phi_ref[x, rows - 1 : rows]
        parts = [msg[first + k : first + k + 1] for k in range(6)]
        parts.append(msg[rows + x : rows + x + 1])
        if row % 2 == 0:
            parts += [msg[beside : beside + 1], plus_wide[wide_row : wide_row + 1]]
        else:
            parts += [minus_wide[wide_row : wide_row + 1], msg[beside : beside + 1]]
        parts += [far_phi, own_phi] if row < 2 else [own_phi, far_phi]
        for k, part in enumerate(parts):
            cells[k, row : row + 1] = part
    place = lax.broadcasted_iota(jnp.int32, (8, cols), 0)
    is_top = (place == 0) | (place == 2)
    sx = jnp.where(is_top, 1.0, -1.0)
    sy = jnp.where(place < 2, 1.0, -1.0)
    delta = jnp.where(is_top, planes.up_jump, planes.low_jump)
    site = Site([cells[k] for k in range(2, 6)], *[cells[k] for k in range(6, 11)])
    w = lattice_weight[7]
    p = sx * site.u[0] + sy * site.u[1]
    q = sx * site.force[0] + sy * site.force[1]
    change = delta * (3.0 * sy + 9.0 * (sy * p) - 3.0 * site.u[1]) + 3.0 * (delta * delta)
    rp, gp = site.r * p, site.g_scale * p
    f_post = w * (site.k + p * (4.5 * rp + 3.375 * q) + 3.0 * rp + 1.125 * q + site.rho * change)
    g_post = w * (site.g_base + 4.5 * (gp * p) + 3.0 * gp + site.phi * change)
    return f_post - 0.25 * cells[0], g_post - (1.0 / 9.0) * cells[1]


def moment_kernel(after_north, after_south, f_ref, g_ref, faces, rims):
    layers, rows = f_ref.shape[1], f_ref.shape[2]
    for s, x in enumerate((layers - 1, 0)):
        for k, part in enumerate(moments_of(lambda i: f_ref[i, x])):
            faces[s, k] = part
    for s, (edge, chosen) in enumerate(((rows - 1, north_going), (0, south_going))):
        for k, part in enumerate(moments_of(lambda i: f_ref[i, :, edge, :])):
            rims[s, k] = part
        for j, i in enumerate(chosen):
            rims[s, 4 + j] = f_ref[i, :, edge, :]
            rims[s, 9 + j] = g_ref[i, :, edge, :]


def half_rows(rows, first):
    return slice(0, rows // 2) if first else slice(rows // 2, rows)


def seam_rows(rows, up):
    return slice(rows // 2 - 2, rows // 2) if up else slice(rows // 2, rows // 2 + 2)


def rim_values(rims, s, phi_ref, minus, plus, south_msg, north_msg, line, edge, chosen, out):
    layers, rows, cols = phi_ref.shape
    phi = phi_ref[:, edge, :]
    with_halo(line, phi, minus[edge : edge + 1], plus[edge : edge + 1])
    if edge == 0:
        below, above = south_msg[rows : rows + layers], phi_ref[:, 1, :]
    else:
        below, above = phi_ref[:, rows - 2, :], north_msg[rows : rows + layers]
    site = Site(
        [rims[s, k] for k in range(4)],
        phi,
        line[7 : 7 + layers],
        line[9 : 9 + layers],
        below,
        above,
    )
    for j, i in enumerate(chosen):
        cz = lattice_velocity[i][2]
        even, odd = site.pair_f(i)
        out[s, j] = z_moved(even + odd - 0.25 * rims[s, 4 + j], cz)
        even, odd = site.pair_g(i)
        out[s, 5 + j] = z_moved(even + odd - (1.0 / 9.0) * rims[s, 9 + j], cz)


def face_kernel(
    sizes,
    offsets,
    f_ref,
    g_ref,
    face_moments,
    rims,
    phi_ref,
    rise,
    fall,
    south_msg,
    north_msg,
    mate,
    direct,
    direct_short,
    across,
    across_short,
    joint,
    cross,
    minus_out,
    plus_out,
    minus_wide,
    plus_wide,
    window,
    halo,
    line,
    rim_post,
    post,
    cells,
    corners,
    raw,
    wide,
):
    layers, rows, cols = phi_ref.shape
    planes = Planes(offsets, rows, sizes)
    shear = Shear(raw, wide, rows)
    window[...] = jnp.zeros_like(window)
    for up in (True, False):
        if up:
            first, second = rise, north_msg
            near, far, start = planes.low_far, planes.low_near, planes.low_rest
        else:
            first, second = south_msg, fall
            near, far, start = planes.up_far, planes.up_near, rows - 1 - planes.up_rest
        target = minus_wide if up else plus_wide
        for k in range(window.shape[0]):
            lanes = slice(LANES * k, LANES * k + LANES)
            window[k, 8 : 8 + rows] = first[0:rows, lanes]
            window[k, 8 + rows : 8 + 2 * rows] = second[0:rows, lanes]
            target[:, lanes] = (
                near * window[k, pl.ds(start, rows + 16)]
                + far * window[k, pl.ds(start + 1, rows + 16)]
            )
    minus_out[...] = minus_wide[8 : 8 + rows]
    plus_out[...] = plus_wide[8 : 8 + rows]
    corners[0], corners[1] = corner_values(
        cells, planes, phi_ref, south_msg, north_msg, minus_wide, plus_wide
    )
    for s, (edge, chosen) in enumerate(((rows - 1, north_going), (0, south_going))):
        rim_values(
            rims,
            s,
            phi_ref,
            minus_out,
            plus_out,
            south_msg,
            north_msg,
            line,
            edge,
            chosen,
            rim_post,
        )
    for side, up in enumerate((True, False)):
        x = layers - 1 if up else 0
        delta = planes.up_jump if up else planes.low_jump
        with_halo(
            halo, phi_ref[x], south_msg[rows + x : rows + x + 1], north_msg[rows + x : rows + x + 1]
        )
        for h in range(0, rows, 8):
            span = slice(h, h + 8)
            phi_h = phi_ref[x, span]
            if up:
                minus, plus = phi_ref[x - 1, span], plus_wide[8 + h : 16 + h]
            else:
                minus, plus = minus_wide[8 + h : 16 + h], phi_ref[x + 1, span]
            site = Site(
                [face_moments[side, k, span] for k in range(4)],
                phi_h,
                minus,
                plus,
                halo[7 + h : 15 + h],
                halo[9 + h : 17 + h],
            )
            for j, i in enumerate(rising if up else falling):
                cz = lattice_velocity[i][2]
                change = lattice_weight[i] * site.jump(i, delta)
                even, odd = site.pair_f(i)
                value = even + odd - 0.25 * f_ref[i, x, span] + site.rho * change
                post[side, j, span] = z_moved(value, cz)
                even, odd = site.pair_g(i)
                value = even + odd - (1.0 / 9.0) * g_ref[i, x, span] + phi_h * change
                post[side, 5 + j, span] = z_moved(value, cz)

    part = rows // 2
    seam = 10 * part

    def hand_out(is_odd):
        for side, up in enumerate((True, False)):
            if up:
                near, far, rest = planes.up_near, planes.up_far, planes.up_rest
            else:
                near, far, rest = planes.low_near, planes.low_far, planes.low_rest
            first, second = (direct, mate) if up == is_odd else (joint, across)
            shear.clear()
            for j in range(10):
                cy = lattice_velocity[(rising if up else falling)[j % 5]][1]
                shear.put(post[side, j], up, near, far)
                corner = side + (0 if cy == 1 else 2)
                if cy == 1:
                    gate = jnp.where(rest == (0 if up else rows - 1), near, 0.0)
                    at = rows + 7 if up else rows + 8
                if cy == -1:
                    gate = jnp.where(rest == (rows - 1 if up else 0), far, 0.0)
                    at = 2 * rows + 7 if up else 2 * rows + 8
                if cy != 0:
                    shear.add_row(at, gate * corners[j // 5, corner : corner + 1])
                shear.take(up, 0, rest, cy, first, j)
                shear.take(up, 1, rest, cy, second, j)
        for j in range(10):
            mate[j, rows : rows + layers] = rim_post[1 if is_odd else 0, j]
            cross[j] = rim_post[0 if is_odd else 1, j]
            direct_short[j] = direct[j, half_rows(rows, is_odd)]
            across_short[part * j : part * j + part] = across[j, half_rows(rows, is_odd)]
            across_short[seam + 2 * j : seam + 2 * j + 2] = across[j, seam_rows(rows, not is_odd)]
        across_short[seam + 20 : seam + 24] = jnp.zeros((4, cols), f32)

    pl.when(planes.odd)(lambda: hand_out(True))
    pl.when(jnp.logical_not(planes.odd))(lambda: hand_out(False))


def bulk_kernel(
    after,
    f_ref,
    g_ref,
    phi_ref,
    minus,
    plus,
    south_msg,
    north_msg,
    mate_rim,
    cross_rim,
    next_f,
    next_g,
    wide_phi,
    halo,
):
    layers, rows, cols = phi_ref.shape
    is_odd = lax.rem(lax.axis_index("gy"), 2) == 1
    wide_phi[0] = minus[...]
    wide_phi[layers + 1] = plus[...]
    for x in range(layers):
        wide_phi[x + 1] = phi_ref[x]

    def layer(x, carry):
        with_halo(halo, phi_ref[x], south_msg[pl.ds(rows + x, 1)], north_msg[pl.ds(rows + x, 1)])
        beyond = lax.rem(x + 1, layers)
        before = lax.rem(x + layers - 1, layers)
        for h in range(0, rows, 8):
            span = slice(h, h + 8)
            phi_h = phi_ref[x, span]
            site = Site(
                moments_of(lambda i: f_ref[i, x, span]),
                phi_h,
                wide_phi[x, span],
                wide_phi[x + 2, span],
                halo[7 + h : 15 + h],
                halo[9 + h : 17 + h],
            )

            def emit(out, slot, i, value):
                cx, cy, cz = lattice_velocity[i]
                value = z_moved(value, cz)
                at = beyond if cx == 1 else before if cx == -1 else x
                if cy == 0:
                    out[i, at, span] = value
                elif cy == 1:
                    if h == 0:
                        rim = slot * 5 + north_going.index(i)
                        out[i, at, 0:1] = jnp.where(
                            is_odd, mate_rim[rim, pl.ds(rows + x, 1)], cross_rim[rim, pl.ds(x, 1)]
                        )
                    if h + 8 < rows:
                        out[i, at, h + 1 : h + 9] = value
                    else:
                        out[i, at, h + 1 : h + 8] = value[0:7]
                else:
                    if h + 8 == rows:
                        rim = slot * 5 + south_going.index(i)
                        out[i, at, rows - 1 : rows] = jnp.where(
                            is_odd, cross_rim[rim, pl.ds(x, 1)], mate_rim[rim, pl.ds(rows + x, 1)]
                        )
                    if h > 0:
                        out[i, at, h - 1 : h + 7] = value
                    else:
                        out[i, at, 0:7] = value[1:8]

            emit(next_f, 0, 0, lattice_weight[0] * site.k - 0.25 * f_ref[0, x, span])
            rest_g = (phi_h - 2.0 * site.mu - 0.5 * (phi_h * site.uu)) * (1.0 / 0.9)
            emit(next_g, 1, 0, rest_g - (1.0 / 9.0) * g_ref[0, x, span])
            for i in range(1, 19, 2):
                even, odd = site.pair_f(i)
                emit(next_f, 0, i, (even + odd) - 0.25 * f_ref[i, x, span])
                emit(next_f, 0, i + 1, (even - odd) - 0.25 * f_ref[i + 1, x, span])
                even, odd = site.pair_g(i)
                emit(next_g, 1, i, (even + odd) - (1.0 / 9.0) * g_ref[i, x, span])
                emit(next_g, 1, i + 1, (even - odd) - (1.0 / 9.0) * g_ref[i + 1, x, span])
        return carry

    lax.fori_loop(0, layers, layer, 0)


def put_faces(buf, out_f, out_g, chosen, x, sems):
    copies = [
        pltpu.make_async_copy(buf.at[5 * family + j], out.at[i, x], sems.at[5 * family + j])
        for family, out in enumerate((out_f, out_g))
        for j, i in enumerate(chosen)
    ]
    for copy in copies:
        copy.start()
    for copy in copies:
        copy.wait()


def merge_fill_kernel(
    sizes,
    offsets,
    direct,
    direct_short,
    across,
    across_short,
    f_in,
    g_in,
    f_out,
    g_out,
    buf,
    sems,
):
    layers, rows = f_out.shape[1], f_out.shape[2]
    planes = Planes(offsets, rows, sizes)
    part = rows // 2
    seam = 10 * part

    def merge(rest, up):
        is_long = rest > part
        near, other, between = half_rows(rows, up), half_rows(rows, not up), seam_rows(rows, up)

        @pl.when(is_long)
        def _():
            buf[...] = across[...]
            for j in range(10):
                buf[j, near] = buf[j, near] + direct_short[j]

        @pl.when(jnp.logical_not(is_long))
        def _():
            buf[...] = direct[...]
            for j in range(10):
                buf[j, other] = buf[j, other] + across_short[part * j : part * j + part]
                at = seam + 2 * j
                buf[j, between] = buf[j, between] + across_short[at : at + 2]

        if up:
            put_faces(buf, f_out, g_out, rising, 0, sems)
        else:
            put_faces(buf, f_out, g_out, falling, layers - 1, sems)

    pl.when(planes.odd)(lambda: merge(planes.low_rest, True))
    pl.when(jnp.logical_not(planes.odd))(lambda: merge(planes.up_rest, False))


def joint_fill_kernel(joint, f_in, g_in, f_out, g_out, sems):
    odd = lax.rem(lax.axis_index("gy"), 2) == 1
    layers = f_out.shape[1]
    pl.when(odd)(lambda: put_faces(joint, f_out, g_out, falling, layers - 1, sems))
    pl.when(jnp.logical_not(odd))(lambda: put_faces(joint, f_out, g_out, rising, 0, sems))


def on_device(momentum_dist, order_dist, offsets):
    layers, rows, cols = momentum_dist.shape[1:]
    count_x, count_y = lax.axis_size("gx"), lax.axis_size("gy")
    per_plane = count_x // 4
    half = count_y // 2

    def hop(value, target):
        perm = []
        for x in range(count_x):
            for y in range(count_y):
                tx, ty = target(x, y)
                perm.append((x * count_y + y, tx % count_x * count_y + ty % count_y))
        return lax.ppermute(value, ("gx", "gy"), perm)

    def base_up(x):
        return half if (x + 1) % per_plane == 0 else 0

    def base_low(x):
        return half if x % per_plane == 0 else 0

    def hop_parity(value, odd_up, extra):
        def target(x, y):
            if (y % 2 == 1) == odd_up:
                return (x + 1, y - base_up(x) - extra)
            return (x - 1, y + base_low(x) + extra)

        return hop(value, target)

    def hop_y(value, step):
        return hop(value, lambda x, y: (x, y + step))

    smem, vmem, anywhere = spec_of(pltpu.SMEM), spec_of(VMEM), spec_of(pl.ANY)
    plane = jax.ShapeDtypeStruct((rows, cols), f32)
    part = rows // 2
    top, bottom, index = pl.pallas_call(
        functools.partial(phi_faces_kernel, part, half * rows),
        out_shape=[plane] * 2 + [jax.ShapeDtypeStruct((1,), jnp.int32)],
        in_specs=[anywhere, anywhere, smem],
        out_specs=[vmem] * 2 + [smem],
        scratch_shapes=[VMEM((2, 19, rows, cols), f32), pltpu.SemaphoreType.DMA((2,))],
        compiler_params=params(46 << 20),
        name="phi_faces",
    )(momentum_dist, order_dist, offsets)
    rise = hop(top, lambda x, y: (x + 1, y - base_up(x)))
    fall = hop(bottom, lambda x, y: (x - 1, y + base_low(x)))

    block = jax.ShapeDtypeStruct((layers + 16, cols), f32)
    phi, to_north, to_south = pl.pallas_call(
        phi_kernel,
        out_shape=[jax.ShapeDtypeStruct((layers, rows, cols), f32)] + [block] * 2,
        in_specs=[vmem] * 4,
        out_specs=[vmem] * 3,
        compiler_params=params(8 << 20),
        name="phi_all",
    )(momentum_dist, order_dist, top, bottom)
    to_north = jnp.concatenate([fall, to_north], 0)
    to_south = jnp.concatenate([rise, to_south], 0)
    south_msg, north_msg = hop_y(to_north, 1), hop_y(to_south, -1)

    face_moments, rims = pl.pallas_call(
        moment_kernel,
        out_shape=[
            jax.ShapeDtypeStruct((2, 4, rows, cols), f32),
            jax.ShapeDtypeStruct((2, 14, layers, cols), f32),
        ],
        in_specs=[anywhere, anywhere, vmem, vmem],
        out_specs=[vmem] * 2,
        compiler_params=params(16 << 20),
        name="moments",
    )(to_north, to_south, momentum_dist, order_dist)

    ten = jax.ShapeDtypeStruct((10, rows, cols), f32)
    ten_short = jax.ShapeDtypeStruct((10, part, cols), f32)
    ten_seam = jax.ShapeDtypeStruct((10 * part + 24, cols), f32)
    side = jax.ShapeDtypeStruct((10, layers, cols), f32)
    ten_side = jax.ShapeDtypeStruct((10, rows + layers, cols), f32)
    *outgoing, minus, plus = pl.pallas_call(
        functools.partial(face_kernel, (count_x, count_y)),
        out_shape=[ten_side, ten, ten_short, ten, ten_seam, ten, side] + [plane] * 2,
        in_specs=[smem] + [vmem] * 9,
        out_specs=[vmem] * 9,
        scratch_shapes=[
            VMEM((rows + 16, cols), f32),
            VMEM((rows + 16, cols), f32),
            VMEM((cols // LANES, 2 * rows + 16, LANES), f32),
            VMEM((rows + 16, cols), f32),
            VMEM((layers + 16, cols), f32),
            VMEM((2, 10, layers, cols), f32),
            VMEM((2, 10, rows, cols), f32),
            VMEM((11, 8, cols), f32),
            VMEM((2, 8, cols), f32),
            VMEM((cols // LANES, rows + 16, LANES), f32),
            VMEM((cols // LANES, 3 * rows + 16, LANES), f32),
        ],
        compiler_params=params(24 << 20),
        name="faces",
    )(
        offsets,
        momentum_dist,
        order_dist,
        face_moments,
        rims,
        phi,
        rise,
        fall,
        south_msg,
        north_msg,
    )
    around = (phi, minus, plus, south_msg, north_msg)
    whole = jax.ShapeDtypeStruct(momentum_dist.shape, f32)

    def finish(long_planes, mate, direct, direct_short, across, across_short, joint, cross):

        def is_long(x):
            return x % per_plane == 0 and x // per_plane % 4 in long_planes

        def hop_some(value, odd_up, extra, long):
            pairs = []
            for x in range(count_x):
                for y in range(count_y):
                    up = (y % 2 == 1) == odd_up
                    tx = (x + 1 if up else x - 1) % count_x
                    if is_long(tx if up else x) != long:
                        continue
                    ty = y - base_up(x) - extra if up else y + base_low(x) + extra
                    pairs.append((x * count_y + y, tx * count_y + ty % count_y))
            return lax.ppermute(value, ("gx", "gy"), pairs)

        cross = hop(cross, lambda x, y: (x, y + 1 if y % 2 == 1 else y - 1))
        mate = hop(mate, lambda x, y: (x, y ^ 1))
        direct, direct_short, across, across_short, cross = lax.optimization_barrier(
            (direct, direct_short, across, across_short, cross)
        )
        direct = hop_some(direct, True, 0, False)
        direct_short = hop_some(direct_short, True, 0, True)
        across = hop_some(across, False, 1, True)
        across_short = hop_some(across_short, False, 1, False)
        joint = joint + mate[:, :rows]
        after = joint
        joint = hop_parity(joint, False, 0)

        next_f, next_g = pl.pallas_call(
            bulk_kernel,
            out_shape=[whole, whole],
            in_specs=[anywhere] + [vmem] * 9,
            out_specs=[vmem] * 2,
            scratch_shapes=[
                VMEM((layers + 2, rows, cols), f32),
                VMEM((rows + 16, cols), f32),
            ],
            compiler_params=params(48 << 20),
            name="bulk",
        )(after, momentum_dist, order_dist, *around, mate, cross)

        next_f, next_g = pl.pallas_call(
            joint_fill_kernel,
            out_shape=[whole, whole],
            in_specs=[vmem, anywhere, anywhere],
            out_specs=[anywhere, anywhere],
            scratch_shapes=[pltpu.SemaphoreType.DMA((10,))],
            input_output_aliases={1: 0, 2: 1},
            compiler_params=params(24 << 20),
            name="joint_fill",
        )(joint, next_f, next_g)

        return pl.pallas_call(
            functools.partial(merge_fill_kernel, (count_x, count_y)),
            out_shape=[whole, whole],
            in_specs=[smem] + [vmem] * 4 + [anywhere, anywhere],
            out_specs=[anywhere, anywhere],
            scratch_shapes=[VMEM((10, rows, cols), f32), pltpu.SemaphoreType.DMA((10,))],
            input_output_aliases={5: 0, 6: 1},
            compiler_params=params(24 << 20),
            name="merge_fill",
        )(offsets, direct, direct_short, across, across_short, next_f, next_g)

    branches = [
        functools.partial(finish, {3} | ({1} if k & 2 else set()) | ({2} if k & 1 else set()))
        for k in range(4)
    ]
    return lax.switch(index[0], branches, *outgoing)


def solution(mesh):
    return jax.shard_map(
        on_device,
        mesh=mesh,
        in_specs=(P(None, "gx", "gy", None), P(None, "gx", "gy", None), P()),
        out_specs=(P(None, "gx", "gy", None), P(None, "gx", "gy", None)),
        check_vma=False,
    )
```

```python
import functools

import jax
import jax.numpy as jnp
from jax import lax
from jax.experimental import pallas as pl
from jax.experimental.pallas import tpu as pltpu
from jax.sharding import PartitionSpec as P

lattice_velocity = [
    (0, 0, 0),
    (1, 0, 0),
    (-1, 0, 0),
    (0, 1, 0),
    (0, -1, 0),
    (0, 0, 1),
    (0, 0, -1),
    (1, 1, 0),
    (-1, -1, 0),
    (1, -1, 0),
    (-1, 1, 0),
    (1, 0, 1),
    (-1, 0, -1),
    (1, 0, -1),
    (-1, 0, 1),
    (0, 1, 1),
    (0, -1, -1),
    (0, 1, -1),
    (0, -1, 1),
]
lattice_weight = [1.0 / 3.0] + [1.0 / 18.0] * 6 + [1.0 / 36.0] * 12
plane_speed = 0.04
rising = [1, 7, 9, 11, 13]
falling = [2, 8, 10, 12, 14]
north_going = [i for i in range(19) if lattice_velocity[i][1] == 1]
south_going = [i for i in range(19) if lattice_velocity[i][1] == -1]
f32 = jnp.float32
VMEM = pltpu.VMEM
LANES = 128


def z_moved(value, step):
    if step == 0:
        return value
    return pltpu.roll(value, step % value.shape[-1], value.ndim - 1)


def spec_of(space):
    return pl.BlockSpec(memory_space=space)


def params(limit):
    return pltpu.CompilerParams(vmem_limit_bytes=limit)


def along(parts, c):
    total = None
    for sign, part in zip(c, parts):
        if sign == 0:
            continue
        if total is None:
            total = part if sign > 0 else -part
        else:
            total = total + part if sign > 0 else total - part
    return total


def signed_sum(load, axis):
    ups = [i for i in range(19) if lattice_velocity[i][axis] == 1]
    downs = [i for i in range(19) if lattice_velocity[i][axis] == -1]
    total = load(ups[0]) - load(downs[0])
    for i, j in zip(ups[1:], downs[1:]):
        total = total + (load(i) - load(j))
    return total


def moments_of(load):
    rho = load(0)
    for i in range(1, 19):
        rho = rho + load(i)
    return [rho] + [signed_sum(load, axis) for axis in range(3)]


class Site:
    def __init__(self, moments, phi, minus, plus, south, north):
        rho, momentum = moments[0], moments[1:]
        lower, upper = z_moved(phi, 1), z_moved(phi, -1)
        lap = (plus + minus) + (north + south) + (upper + lower) - 6.0 * phi
        mu = phi * (0.0625 * (phi * phi) - 0.0625) - 0.04 * lap
        half_mu = 0.5 * mu
        force = [half_mu * (plus - minus), half_mu * (north - south), half_mu * (upper - lower)]
        inverse = 1.0 / rho
        u = [(j + 0.5 * k) * inverse for j, k in zip(momentum, force)]
        uu = u[0] * u[0] + u[1] * u[1] + u[2] * u[2]
        uf = u[0] * force[0] + u[1] * force[1] + u[2] * force[2]
        self.rho, self.phi, self.mu, self.u, self.force, self.uu = rho, phi, mu, u, force, uu
        self.r = 1.25 * rho
        self.k = self.r * (1.0 - 1.5 * uu) - 1.125 * uf
        self.g_scale = phi * (1.0 / 0.9)
        self.g_base = (3.0 / 0.9) * mu - 1.5 * (self.g_scale * uu)

    def pair_f(self, i):
        p, q = along(self.u, lattice_velocity[i]), along(self.force, lattice_velocity[i])
        w = lattice_weight[i]
        rp = self.r * p
        even = w * (self.k + p * (4.5 * rp + 3.375 * q))
        odd = (3.0 * w) * rp + (1.125 * w) * q
        return even, odd

    def pair_g(self, i):
        p = along(self.u, lattice_velocity[i])
        w = lattice_weight[i]
        gp = self.g_scale * p
        return w * (self.g_base + 4.5 * (gp * p)), (3.0 * w) * gp

    def jump(self, i, delta):
        cy = lattice_velocity[i][1]
        uy = self.u[1]
        if cy == 0:
            return delta * (-3.0 * uy) - (1.5 * delta * delta)
        p = along(self.u, lattice_velocity[i])
        return delta * (3.0 * cy + (9.0 * cy) * p - 3.0 * uy) + (3.0 * delta * delta)


class Shear:
    def __init__(self, raw, wide, rows):
        self.raw, self.wide, self.rows = raw, wide, rows

    def clear(self):
        self.raw[...] = jnp.zeros_like(self.raw)
        self.wide[...] = jnp.zeros_like(self.wide)

    def put(self, value, up, near, far):
        n = self.rows
        for k in range(self.raw.shape[0]):
            self.raw[k, 8 : 8 + n] = value[:, LANES * k : LANES * k + LANES]
        for k in range(self.raw.shape[0]):
            if up:
                self.wide[k, n : n + n + 8] = (
                    near * self.raw[k, 0 : n + 8] + far * self.raw[k, 1 : n + 9]
                )
            else:
                self.wide[k, n + 8 : n + n + 16] = (
                    near * self.raw[k, 7 : n + 15] + far * self.raw[k, 8 : n + 16]
                )

    def add_row(self, at, row):
        for k in range(self.raw.shape[0]):
            lanes = slice(LANES * k, LANES * k + LANES)
            self.wide[k, at : at + 1] = self.wide[k, at : at + 1] + row[:, lanes]

    def take(self, up, block, rest, cy, ref, j):
        n = self.rows
        if up:
            start = (n + 8 if block == 0 else 8) + rest - cy
        else:
            start = (n + 8 if block == 0 else n + n + 8) - rest - cy
        for k in range(self.raw.shape[0]):
            ref[j, 0:n, LANES * k : LANES * k + LANES] = self.wide[k, pl.ds(start, n)]


class Planes:
    def __init__(self, offsets, rows, sizes):
        count_x, count_y = sizes
        per_plane, half = count_x // 4, count_y // 2
        a = lax.axis_index("gx")
        self.odd = lax.rem(lax.axis_index("gy"), 2) == 1

        def plane_of(column):
            is_plane = lax.rem(column, per_plane) == 0
            plane = lax.rem(lax.div(column, per_plane), 4)
            rest = jnp.where(is_plane, jnp.clip(offsets[plane] - half * rows, 0, rows - 1), 0)
            return is_plane, (2.0 * plane.astype(f32) + 1.0) * 0.125, rest

        up_is, up_part, self.up_rest = plane_of(lax.rem(a + 1, count_x))
        low_is, low_part, self.low_rest = plane_of(a)
        self.up_near = jnp.where(up_is, 1.0 - up_part, 1.0)
        self.up_far = jnp.where(up_is, up_part, 0.0)
        self.low_near = jnp.where(low_is, low_part, 0.0)
        self.low_far = jnp.where(low_is, 1.0 - low_part, 1.0)
        self.up_jump = jnp.where(up_is, -plane_speed, 0.0)
        self.low_jump = jnp.where(low_is, plane_speed, 0.0)


def order_sum(load):
    total = load(0)
    for i in range(1, 19):
        total = total + load(i)
    return total


def phi_kernel(
    base, offsets, f_ref, g_ref, top, bottom, phi_ref, to_north, to_south, gbuf, index, fbuf, sems
):
    layers, rows = phi_ref.shape[0], phi_ref.shape[1]
    faces = (layers - 1, 0)
    f_copies = [
        pltpu.make_async_copy(f_ref.at[:, x], fbuf.at[:, s], sems.at[layers + s])
        for s, x in enumerate(faces)
    ]
    g_copies = [
        pltpu.make_async_copy(g_ref.at[:, x], gbuf.at[:, x], sems.at[x]) for x in range(layers)
    ]
    for copy in f_copies + g_copies:
        copy.start()
    is_long = [(offsets[k] - base > rows // 2).astype(jnp.int32) for k in (1, 2)]
    index[0] = 2 * is_long[0] + is_long[1]
    phi_ref[layers - 1] = top[...]
    phi_ref[0] = bottom[...]
    edges = ((to_north, rows - 1, rows - 2, (7, 10)), (to_south, 0, 1, (9, 8)))
    for s, x in enumerate(faces):
        f_copies[s].wait()
        for out, edge, inner, chosen in edges:
            out[layers + s : layers + s + 1] = phi_ref[x, inner : inner + 1]
            at = layers + 2 + 6 * s
            out[at : at + 1] = fbuf[chosen[s], s, edge : edge + 1]
            for k, part in enumerate(moments_of(lambda i: fbuf[i, s, edge : edge + 1])):
                out[at + 2 + k : at + 3 + k] = part
    for x in range(layers):
        g_copies[x].wait()
        if 0 < x < layers - 1:
            phi_ref[x] = order_sum(lambda i: gbuf[i, x])
        to_north[x : x + 1] = phi_ref[x, rows - 1 : rows]
        to_south[x : x + 1] = phi_ref[x, 0:1]
    for s, x in enumerate(faces):
        for out, edge, inner, chosen in edges:
            at = layers + 3 + 6 * s
            out[at : at + 1] = gbuf[chosen[s], x, edge : edge + 1]
    for out in (to_north, to_south):
        out[layers + 14 : layers + 16] = jnp.zeros((2, out.shape[1]), f32)


def with_halo(ref, layer, below, above):
    rows = layer.shape[0]
    ref[8 : 8 + rows] = layer
    ref[7:8] = below
    ref[8 + rows : 9 + rows] = above


def corner_values(cells, planes, phi_ref, south_msg, north_msg, minus_wide, plus_wide):
    layers, rows, cols = phi_ref.shape
    cells[...] = jnp.ones_like(cells)
    for row in range(4):
        msg = south_msg if row < 2 else north_msg
        x = layers - 1 if row % 2 == 0 else 0
        beside = rows + (layers - 2 if row % 2 == 0 else 1)
        wide_row = 7 if row < 2 else rows + 8
        at = rows + layers
        first = at + 2 + 6 * (row % 2)
        far_phi = msg[at + row % 2 : at + row % 2 + 1]
        own_phi = phi_ref[x, 0:1] if row < 2 else phi_ref[x, rows - 1 : rows]
        parts = [msg[first + k : first + k + 1] for k in range(6)]
        parts.append(msg[rows + x : rows + x + 1])
        if row % 2 == 0:
            parts += [msg[beside : beside + 1], plus_wide[wide_row : wide_row + 1]]
        else:
            parts += [minus_wide[wide_row : wide_row + 1], msg[beside : beside + 1]]
        parts += [far_phi, own_phi] if row < 2 else [own_phi, far_phi]
        for k, part in enumerate(parts):
            cells[k, row : row + 1] = part
    place = lax.broadcasted_iota(jnp.int32, (8, cols), 0)
    is_top = (place == 0) | (place == 2)
    sx = jnp.where(is_top, 1.0, -1.0)
    sy = jnp.where(place < 2, 1.0, -1.0)
    delta = jnp.where(is_top, planes.up_jump, planes.low_jump)
    site = Site([cells[k] for k in range(2, 6)], *[cells[k] for k in range(6, 11)])
    w = lattice_weight[7]
    p = sx * site.u[0] + sy * site.u[1]
    q = sx * site.force[0] + sy * site.force[1]
    change = delta * (3.0 * sy + 9.0 * (sy * p) - 3.0 * site.u[1]) + 3.0 * (delta * delta)
    rp, gp = site.r * p, site.g_scale * p
    f_post = w * (site.k + p * (4.5 * rp + 3.375 * q) + 3.0 * rp + 1.125 * q + site.rho * change)
    g_post = w * (site.g_base + 4.5 * (gp * p) + 3.0 * gp + site.phi * change)
    return f_post - 0.25 * cells[0], g_post - (1.0 / 9.0) * cells[1]


def moment_kernel(after_north, after_south, f_ref, g_ref, faces, rims):
    layers, rows = f_ref.shape[1], f_ref.shape[2]
    for s, x in enumerate((layers - 1, 0)):
        for k, part in enumerate(moments_of(lambda i: f_ref[i, x])):
            faces[s, k] = part
    for s, (edge, chosen) in enumerate(((rows - 1, north_going), (0, south_going))):
        for k, part in enumerate(moments_of(lambda i: f_ref[i, :, edge, :])):
            rims[s, k] = part
        for j, i in enumerate(chosen):
            rims[s, 4 + j] = f_ref[i, :, edge, :]
            rims[s, 9 + j] = g_ref[i, :, edge, :]


def half_rows(rows, first):
    return slice(0, rows // 2) if first else slice(rows // 2, rows)


def seam_rows(rows, up):
    return slice(rows // 2 - 2, rows // 2) if up else slice(rows // 2, rows // 2 + 2)


def rim_values(rims, s, phi_ref, minus, plus, south_msg, north_msg, line, edge, chosen, out):
    layers, rows, cols = phi_ref.shape
    phi = phi_ref[:, edge, :]
    with_halo(line, phi, minus[edge : edge + 1], plus[edge : edge + 1])
    if edge == 0:
        below, above = south_msg[rows : rows + layers], phi_ref[:, 1, :]
    else:
        below, above = phi_ref[:, rows - 2, :], north_msg[rows : rows + layers]
    site = Site(
        [rims[s, k] for k in range(4)],
        phi,
        line[7 : 7 + layers],
        line[9 : 9 + layers],
        below,
        above,
    )
    for j, i in enumerate(chosen):
        cz = lattice_velocity[i][2]
        even, odd = site.pair_f(i)
        out[s, j] = z_moved(even + odd - 0.25 * rims[s, 4 + j], cz)
        even, odd = site.pair_g(i)
        out[s, 5 + j] = z_moved(even + odd - (1.0 / 9.0) * rims[s, 9 + j], cz)


def face_kernel(
    sizes,
    offsets,
    f_ref,
    g_ref,
    face_moments,
    rims,
    phi_ref,
    rise,
    fall,
    south_msg,
    north_msg,
    mate,
    direct,
    direct_short,
    across,
    across_short,
    joint,
    cross,
    minus_out,
    plus_out,
    minus_wide,
    plus_wide,
    window,
    halo,
    line,
    rim_post,
    post,
    cells,
    corners,
    raw,
    wide,
):
    layers, rows, cols = phi_ref.shape
    planes = Planes(offsets, rows, sizes)
    shear = Shear(raw, wide, rows)
    window[...] = jnp.zeros_like(window)
    for up in (True, False):
        if up:
            first, second = rise, north_msg
            near, far, start = planes.low_far, planes.low_near, planes.low_rest
        else:
            first, second = south_msg, fall
            near, far, start = planes.up_far, planes.up_near, rows - 1 - planes.up_rest
        target = minus_wide if up else plus_wide
        for k in range(window.shape[0]):
            lanes = slice(LANES * k, LANES * k + LANES)
            window[k, 8 : 8 + rows] = first[0:rows, lanes]
            window[k, 8 + rows : 8 + 2 * rows] = second[0:rows, lanes]
            target[:, lanes] = (
                near * window[k, pl.ds(start, rows + 16)]
                + far * window[k, pl.ds(start + 1, rows + 16)]
            )
    minus_out[...] = minus_wide[8 : 8 + rows]
    plus_out[...] = plus_wide[8 : 8 + rows]
    corners[0], corners[1] = corner_values(
        cells, planes, phi_ref, south_msg, north_msg, minus_wide, plus_wide
    )
    for s, (edge, chosen) in enumerate(((rows - 1, north_going), (0, south_going))):
        rim_values(
            rims,
            s,
            phi_ref,
            minus_out,
            plus_out,
            south_msg,
            north_msg,
            line,
            edge,
            chosen,
            rim_post,
        )
    for side, up in enumerate((True, False)):
        x = layers - 1 if up else 0
        delta = planes.up_jump if up else planes.low_jump
        with_halo(
            halo, phi_ref[x], south_msg[rows + x : rows + x + 1], north_msg[rows + x : rows + x + 1]
        )
        for h in range(0, rows, 8):
            span = slice(h, h + 8)
            phi_h = phi_ref[x, span]
            if up:
                minus, plus = phi_ref[x - 1, span], plus_wide[8 + h : 16 + h]
            else:
                minus, plus = minus_wide[8 + h : 16 + h], phi_ref[x + 1, span]
            site = Site(
                [face_moments[side, k, span] for k in range(4)],
                phi_h,
                minus,
                plus,
                halo[7 + h : 15 + h],
                halo[9 + h : 17 + h],
            )
            for j, i in enumerate(rising if up else falling):
                cz = lattice_velocity[i][2]
                change = lattice_weight[i] * site.jump(i, delta)
                even, odd = site.pair_f(i)
                value = even + odd - 0.25 * f_ref[i, x, span] + site.rho * change
                post[side, j, span] = z_moved(value, cz)
                even, odd = site.pair_g(i)
                value = even + odd - (1.0 / 9.0) * g_ref[i, x, span] + phi_h * change
                post[side, 5 + j, span] = z_moved(value, cz)

    part = rows // 2
    seam = 10 * part

    def hand_out(is_odd):
        for side, up in enumerate((True, False)):
            if up:
                near, far, rest = planes.up_near, planes.up_far, planes.up_rest
            else:
                near, far, rest = planes.low_near, planes.low_far, planes.low_rest
            first, second = (direct, mate) if up == is_odd else (joint, across)
            shear.clear()
            for j in range(10):
                cy = lattice_velocity[(rising if up else falling)[j % 5]][1]
                shear.put(post[side, j], up, near, far)
                corner = side + (0 if cy == 1 else 2)
                if cy == 1:
                    gate = jnp.where(rest == (0 if up else rows - 1), near, 0.0)
                    at = rows + 7 if up else rows + 8
                if cy == -1:
                    gate = jnp.where(rest == (rows - 1 if up else 0), far, 0.0)
                    at = 2 * rows + 7 if up else 2 * rows + 8
                if cy != 0:
                    shear.add_row(at, gate * corners[j // 5, corner : corner + 1])
                shear.take(up, 0, rest, cy, first, j)
                shear.take(up, 1, rest, cy, second, j)
        for j in range(10):
            mate[j, rows : rows + layers] = rim_post[1 if is_odd else 0, j]
            cross[j] = rim_post[0 if is_odd else 1, j]
            direct_short[j] = direct[j, half_rows(rows, is_odd)]
            across_short[part * j : part * j + part] = across[j, half_rows(rows, is_odd)]
            across_short[seam + 2 * j : seam + 2 * j + 2] = across[j, seam_rows(rows, not is_odd)]
        across_short[seam + 20 : seam + 24] = jnp.zeros((4, cols), f32)

    pl.when(planes.odd)(lambda: hand_out(True))
    pl.when(jnp.logical_not(planes.odd))(lambda: hand_out(False))


def bulk_kernel(
    after,
    f_ref,
    g_ref,
    phi_ref,
    minus,
    plus,
    south_msg,
    north_msg,
    mate_rim,
    cross_rim,
    next_f,
    next_g,
    wide_phi,
    halo,
):
    layers, rows, cols = phi_ref.shape
    is_odd = lax.rem(lax.axis_index("gy"), 2) == 1
    wide_phi[0] = minus[...]
    wide_phi[layers + 1] = plus[...]
    for x in range(layers):
        wide_phi[x + 1] = phi_ref[x]

    def layer(x, carry):
        with_halo(halo, phi_ref[x], south_msg[pl.ds(rows + x, 1)], north_msg[pl.ds(rows + x, 1)])
        beyond = lax.rem(x + 1, layers)
        before = lax.rem(x + layers - 1, layers)
        for h in range(0, rows, 8):
            span = slice(h, h + 8)
            phi_h = phi_ref[x, span]
            site = Site(
                moments_of(lambda i: f_ref[i, x, span]),
                phi_h,
                wide_phi[x, span],
                wide_phi[x + 2, span],
                halo[7 + h : 15 + h],
                halo[9 + h : 17 + h],
            )

            def emit(out, slot, i, value):
                cx, cy, cz = lattice_velocity[i]
                value = z_moved(value, cz)
                at = beyond if cx == 1 else before if cx == -1 else x
                if cy == 0:
                    out[i, at, span] = value
                elif cy == 1:
                    if h == 0:
                        rim = slot * 5 + north_going.index(i)
                        out[i, at, 0:1] = jnp.where(
                            is_odd, mate_rim[rim, pl.ds(rows + x, 1)], cross_rim[rim, pl.ds(x, 1)]
                        )
                    if h + 8 < rows:
                        out[i, at, h + 1 : h + 9] = value
                    else:
                        out[i, at, h + 1 : h + 8] = value[0:7]
                else:
                    if h + 8 == rows:
                        rim = slot * 5 + south_going.index(i)
                        out[i, at, rows - 1 : rows] = jnp.where(
                            is_odd, cross_rim[rim, pl.ds(x, 1)], mate_rim[rim, pl.ds(rows + x, 1)]
                        )
                    if h > 0:
                        out[i, at, h - 1 : h + 7] = value
                    else:
                        out[i, at, 0:7] = value[1:8]

            emit(next_f, 0, 0, lattice_weight[0] * site.k - 0.25 * f_ref[0, x, span])
            rest_g = (phi_h - 2.0 * site.mu - 0.5 * (phi_h * site.uu)) * (1.0 / 0.9)
            emit(next_g, 1, 0, rest_g - (1.0 / 9.0) * g_ref[0, x, span])
            for i in range(1, 19, 2):
                even, odd = site.pair_f(i)
                emit(next_f, 0, i, (even + odd) - 0.25 * f_ref[i, x, span])
                emit(next_f, 0, i + 1, (even - odd) - 0.25 * f_ref[i + 1, x, span])
                even, odd = site.pair_g(i)
                emit(next_g, 1, i, (even + odd) - (1.0 / 9.0) * g_ref[i, x, span])
                emit(next_g, 1, i + 1, (even - odd) - (1.0 / 9.0) * g_ref[i + 1, x, span])
        return carry

    lax.fori_loop(0, layers, layer, 0)


def put_faces(buf, out_f, out_g, chosen, x, sems):
    copies = [
        pltpu.make_async_copy(buf.at[5 * family + j], out.at[i, x], sems.at[5 * family + j])
        for family, out in enumerate((out_f, out_g))
        for j, i in enumerate(chosen)
    ]
    for copy in copies:
        copy.start()
    for copy in copies:
        copy.wait()


def merge_fill_kernel(
    sizes,
    offsets,
    direct,
    direct_short,
    across,
    across_short,
    f_in,
    g_in,
    f_out,
    g_out,
    buf,
    sems,
):
    layers, rows = f_out.shape[1], f_out.shape[2]
    planes = Planes(offsets, rows, sizes)
    part = rows // 2
    seam = 10 * part

    def merge(rest, up):
        near, other, between = half_rows(rows, up), half_rows(rows, not up), seam_rows(rows, up)
        chosen, x = (rising, 0) if up else (falling, layers - 1)
        copies = [
            pltpu.make_async_copy(
                buf.at[j], (f_out if j < 5 else g_out).at[chosen[j % 5], x], sems.at[j]
            )
            for j in range(10)
        ]

        def long():
            for j in range(10):
                buf[j, near] = across[j, near] + direct_short[j]
                buf[j, other] = across[j, other]
                copies[j].start()

        def short():
            for j in range(10):
                at = seam + 2 * j
                buf[j, near] = direct[j, near]
                buf[j, between] = direct[j, between] + across_short[at : at + 2]
                buf[j, other] = direct[j, other] + across_short[part * j : part * j + part]
                copies[j].start()

        is_long = rest > part
        pl.when(is_long)(long)
        pl.when(jnp.logical_not(is_long))(short)
        for copy in copies:
            copy.wait()

    pl.when(planes.odd)(lambda: merge(planes.low_rest, True))
    pl.when(jnp.logical_not(planes.odd))(lambda: merge(planes.up_rest, False))


def joint_fill_kernel(joint, f_in, g_in, f_out, g_out, sems):
    odd = lax.rem(lax.axis_index("gy"), 2) == 1
    layers = f_out.shape[1]
    pl.when(odd)(lambda: put_faces(joint, f_out, g_out, falling, layers - 1, sems))
    pl.when(jnp.logical_not(odd))(lambda: put_faces(joint, f_out, g_out, rising, 0, sems))


def on_device(momentum_dist, order_dist, offsets):
    layers, rows, cols = momentum_dist.shape[1:]
    count_x, count_y = lax.axis_size("gx"), lax.axis_size("gy")
    per_plane = count_x // 4
    half = count_y // 2

    def hop(value, target):
        perm = []
        for x in range(count_x):
            for y in range(count_y):
                tx, ty = target(x, y)
                perm.append((x * count_y + y, tx % count_x * count_y + ty % count_y))
        return lax.ppermute(value, ("gx", "gy"), perm)

    def base_up(x):
        return half if (x + 1) % per_plane == 0 else 0

    def base_low(x):
        return half if x % per_plane == 0 else 0

    def hop_parity(value, odd_up, extra):
        def target(x, y):
            if (y % 2 == 1) == odd_up:
                return (x + 1, y - base_up(x) - extra)
            return (x - 1, y + base_low(x) + extra)

        return hop(value, target)

    def hop_y(value, step):
        return hop(value, lambda x, y: (x, y + step))

    smem, vmem, anywhere = spec_of(pltpu.SMEM), spec_of(VMEM), spec_of(pl.ANY)
    plane = jax.ShapeDtypeStruct((rows, cols), f32)
    top, bottom = jnp.sum(order_dist[:, layers - 1], axis=0), jnp.sum(order_dist[:, 0], axis=0)
    rise = hop(top, lambda x, y: (x + 1, y - base_up(x)))
    fall = hop(bottom, lambda x, y: (x - 1, y + base_low(x)))

    block = jax.ShapeDtypeStruct((layers + 16, cols), f32)
    phi, to_north, to_south, order_near, index = pl.pallas_call(
        functools.partial(phi_kernel, half * rows),
        out_shape=[jax.ShapeDtypeStruct((layers, rows, cols), f32)]
        + [block] * 2
        + [jax.ShapeDtypeStruct(order_dist.shape, f32), jax.ShapeDtypeStruct((1,), jnp.int32)],
        in_specs=[smem, anywhere, anywhere, vmem, vmem],
        out_specs=[vmem] * 4 + [smem],
        scratch_shapes=[
            VMEM((19, 2, rows, cols), f32),
            pltpu.SemaphoreType.DMA((layers + 2,)),
        ],
        compiler_params=params(52 << 20),
        name="phi_all",
    )(offsets, momentum_dist, order_dist, top, bottom)
    to_north = jnp.concatenate([fall, to_north], 0)
    to_south = jnp.concatenate([rise, to_south], 0)
    south_msg, north_msg = hop_y(to_north, 1), hop_y(to_south, -1)

    face_moments, rims = pl.pallas_call(
        moment_kernel,
        out_shape=[
            jax.ShapeDtypeStruct((2, 4, rows, cols), f32),
            jax.ShapeDtypeStruct((2, 14, layers, cols), f32),
        ],
        in_specs=[anywhere, anywhere, vmem, vmem],
        out_specs=[vmem] * 2,
        compiler_params=params(16 << 20),
        name="moments",
    )(to_north, to_south, momentum_dist, order_near)

    part = rows // 2
    ten = jax.ShapeDtypeStruct((10, rows, cols), f32)
    ten_short = jax.ShapeDtypeStruct((10, part, cols), f32)
    ten_seam = jax.ShapeDtypeStruct((10 * part + 24, cols), f32)
    side = jax.ShapeDtypeStruct((10, layers, cols), f32)
    ten_side = jax.ShapeDtypeStruct((10, rows + layers, cols), f32)
    *outgoing, minus, plus = pl.pallas_call(
        functools.partial(face_kernel, (count_x, count_y)),
        out_shape=[ten_side, ten, ten_short, ten, ten_seam, ten, side] + [plane] * 2,
        in_specs=[smem] + [vmem] * 9,
        out_specs=[vmem] * 9,
        scratch_shapes=[
            VMEM((rows + 16, cols), f32),
            VMEM((rows + 16, cols), f32),
            VMEM((cols // LANES, 2 * rows + 16, LANES), f32),
            VMEM((rows + 16, cols), f32),
            VMEM((layers + 16, cols), f32),
            VMEM((2, 10, layers, cols), f32),
            VMEM((2, 10, rows, cols), f32),
            VMEM((11, 8, cols), f32),
            VMEM((2, 8, cols), f32),
            VMEM((cols // LANES, rows + 16, LANES), f32),
            VMEM((cols // LANES, 3 * rows + 16, LANES), f32),
        ],
        compiler_params=params(24 << 20),
        name="faces",
    )(
        offsets,
        momentum_dist,
        order_near,
        face_moments,
        rims,
        phi,
        rise,
        fall,
        south_msg,
        north_msg,
    )
    around = (phi, minus, plus, south_msg, north_msg)
    whole = jax.ShapeDtypeStruct(momentum_dist.shape, f32)

    def finish(long_planes, mate, direct, direct_short, across, across_short, joint, cross):

        def is_long(x):
            return x % per_plane == 0 and x // per_plane % 4 in long_planes

        def hop_some(value, odd_up, extra, long):
            pairs = []
            for x in range(count_x):
                for y in range(count_y):
                    up = (y % 2 == 1) == odd_up
                    tx = (x + 1 if up else x - 1) % count_x
                    if is_long(tx if up else x) != long:
                        continue
                    ty = y - base_up(x) - extra if up else y + base_low(x) + extra
                    pairs.append((x * count_y + y, tx * count_y + ty % count_y))
            return lax.ppermute(value, ("gx", "gy"), pairs)

        cross = hop(cross, lambda x, y: (x, y + 1 if y % 2 == 1 else y - 1))
        mate = hop(mate, lambda x, y: (x, y ^ 1))
        direct, direct_short, across, across_short, cross = lax.optimization_barrier(
            (direct, direct_short, across, across_short, cross)
        )
        direct = hop_some(direct, True, 0, False)
        direct_short = hop_some(direct_short, True, 0, True)
        across = hop_some(across, False, 1, True)
        across_short = hop_some(across_short, False, 1, False)
        joint = joint + mate[:, :rows]
        after = joint
        joint = hop_parity(joint, False, 0)

        next_f, next_g = pl.pallas_call(
            bulk_kernel,
            out_shape=[whole, whole],
            in_specs=[anywhere] + [vmem] * 9,
            out_specs=[vmem] * 2,
            scratch_shapes=[
                VMEM((layers + 2, rows, cols), f32),
                VMEM((rows + 16, cols), f32),
            ],
            compiler_params=params(48 << 20),
            name="bulk",
        )(after, momentum_dist, order_near, *around, mate, cross)

        next_f, next_g = pl.pallas_call(
            joint_fill_kernel,
            out_shape=[whole, whole],
            in_specs=[vmem, anywhere, anywhere],
            out_specs=[anywhere, anywhere],
            scratch_shapes=[pltpu.SemaphoreType.DMA((10,))],
            input_output_aliases={1: 0, 2: 1},
            compiler_params=params(24 << 20),
            name="joint_fill",
        )(joint, next_f, next_g)

        return pl.pallas_call(
            functools.partial(merge_fill_kernel, (count_x, count_y)),
            out_shape=[whole, whole],
            in_specs=[smem] + [vmem] * 4 + [anywhere, anywhere],
            out_specs=[anywhere, anywhere],
            scratch_shapes=[VMEM((10, rows, cols), f32), pltpu.SemaphoreType.DMA((10,))],
            input_output_aliases={5: 0, 6: 1},
            compiler_params=params(24 << 20),
            name="merge_fill",
        )(offsets, direct, direct_short, across, across_short, next_f, next_g)

    branches = [
        functools.partial(finish, {3} | ({1} if k & 2 else set()) | ({2} if k & 1 else set()))
        for k in range(4)
    ]
    return lax.switch(index[0], branches, *outgoing)


def solution(mesh):
    return jax.shard_map(
        on_device,
        mesh=mesh,
        in_specs=(P(None, "gx", "gy", None), P(None, "gx", "gy", None), P()),
        out_specs=(P(None, "gx", "gy", None), P(None, "gx", "gy", None)),
        check_vma=False,
    )
```

```python
import functools

import jax
import jax.numpy as jnp
from jax import lax
from jax.experimental import pallas as pl
from jax.experimental.pallas import tpu as pltpu
from jax.sharding import PartitionSpec as P

lattice_velocity = [
    (0, 0, 0),
    (1, 0, 0),
    (-1, 0, 0),
    (0, 1, 0),
    (0, -1, 0),
    (0, 0, 1),
    (0, 0, -1),
    (1, 1, 0),
    (-1, -1, 0),
    (1, -1, 0),
    (-1, 1, 0),
    (1, 0, 1),
    (-1, 0, -1),
    (1, 0, -1),
    (-1, 0, 1),
    (0, 1, 1),
    (0, -1, -1),
    (0, 1, -1),
    (0, -1, 1),
]
lattice_weight = [1.0 / 3.0] + [1.0 / 18.0] * 6 + [1.0 / 36.0] * 12
plane_speed = 0.04
rising = [1, 7, 9, 11, 13]
falling = [2, 8, 10, 12, 14]
north_going = [i for i in range(19) if lattice_velocity[i][1] == 1]
south_going = [i for i in range(19) if lattice_velocity[i][1] == -1]
f32 = jnp.float32
VMEM = pltpu.VMEM
LANES = 128


def z_moved(value, step):
    if step == 0:
        return value
    return pltpu.roll(value, step % value.shape[-1], value.ndim - 1)


def spec_of(space):
    return pl.BlockSpec(memory_space=space)


def params(limit):
    return pltpu.CompilerParams(vmem_limit_bytes=limit)


def along(parts, c):
    total = None
    for sign, part in zip(c, parts):
        if sign == 0:
            continue
        if total is None:
            total = part if sign > 0 else -part
        else:
            total = total + part if sign > 0 else total - part
    return total


def signed_sum(load, axis):
    ups = [i for i in range(19) if lattice_velocity[i][axis] == 1]
    downs = [i for i in range(19) if lattice_velocity[i][axis] == -1]
    total = load(ups[0]) - load(downs[0])
    for i, j in zip(ups[1:], downs[1:]):
        total = total + (load(i) - load(j))
    return total


def moments_of(load):
    rho = load(0)
    for i in range(1, 19):
        rho = rho + load(i)
    return [rho] + [signed_sum(load, axis) for axis in range(3)]


class Site:
    def __init__(self, moments, phi, minus, plus, south, north):
        rho, momentum = moments[0], moments[1:]
        lower, upper = z_moved(phi, 1), z_moved(phi, -1)
        lap = (plus + minus) + (north + south) + (upper + lower) - 6.0 * phi
        mu = phi * (0.0625 * (phi * phi) - 0.0625) - 0.04 * lap
        half_mu = 0.5 * mu
        force = [half_mu * (plus - minus), half_mu * (north - south), half_mu * (upper - lower)]
        inverse = 1.0 / rho
        u = [(j + 0.5 * k) * inverse for j, k in zip(momentum, force)]
        uu = u[0] * u[0] + u[1] * u[1] + u[2] * u[2]
        uf = u[0] * force[0] + u[1] * force[1] + u[2] * force[2]
        self.rho, self.phi, self.mu, self.u, self.force, self.uu = rho, phi, mu, u, force, uu
        self.r = 1.25 * rho
        self.k = self.r * (1.0 - 1.5 * uu) - 1.125 * uf
        self.g_scale = phi * (1.0 / 0.9)
        self.g_base = (3.0 / 0.9) * mu - 1.5 * (self.g_scale * uu)

    def pair_f(self, i):
        p, q = along(self.u, lattice_velocity[i]), along(self.force, lattice_velocity[i])
        w = lattice_weight[i]
        rp = self.r * p
        even = w * (self.k + p * (4.5 * rp + 3.375 * q))
        odd = (3.0 * w) * rp + (1.125 * w) * q
        return even, odd

    def pair_g(self, i):
        p = along(self.u, lattice_velocity[i])
        w = lattice_weight[i]
        gp = self.g_scale * p
        return w * (self.g_base + 4.5 * (gp * p)), (3.0 * w) * gp

    def jump(self, i, delta):
        cy = lattice_velocity[i][1]
        uy = self.u[1]
        if cy == 0:
            return delta * (-3.0 * uy) - (1.5 * delta * delta)
        p = along(self.u, lattice_velocity[i])
        return delta * (3.0 * cy + (9.0 * cy) * p - 3.0 * uy) + (3.0 * delta * delta)


class Shear:
    def __init__(self, raw, wide, rows):
        self.raw, self.wide, self.rows = raw, wide, rows

    def clear(self):
        self.raw[...] = jnp.zeros_like(self.raw)
        self.wide[...] = jnp.zeros_like(self.wide)

    def put(self, value, up, near, far):
        n = self.rows
        for k in range(self.raw.shape[0]):
            self.raw[k, 8 : 8 + n] = value[:, LANES * k : LANES * k + LANES]
        for k in range(self.raw.shape[0]):
            if up:
                self.wide[k, n : n + n + 8] = (
                    near * self.raw[k, 0 : n + 8] + far * self.raw[k, 1 : n + 9]
                )
            else:
                self.wide[k, n + 8 : n + n + 16] = (
                    near * self.raw[k, 7 : n + 15] + far * self.raw[k, 8 : n + 16]
                )

    def add_row(self, at, row):
        for k in range(self.raw.shape[0]):
            lanes = slice(LANES * k, LANES * k + LANES)
            self.wide[k, at : at + 1] = self.wide[k, at : at + 1] + row[:, lanes]

    def take(self, up, block, rest, cy, ref, j):
        n = self.rows
        if up:
            start = (n + 8 if block == 0 else 8) + rest - cy
        else:
            start = (n + 8 if block == 0 else n + n + 8) - rest - cy
        for k in range(self.raw.shape[0]):
            ref[j, 0:n, LANES * k : LANES * k + LANES] = self.wide[k, pl.ds(start, n)]


class Planes:
    def __init__(self, offsets, rows, sizes):
        count_x, count_y = sizes
        per_plane, half = count_x // 4, count_y // 2
        a = lax.axis_index("gx")
        self.odd = lax.rem(lax.axis_index("gy"), 2) == 1

        def plane_of(column):
            is_plane = lax.rem(column, per_plane) == 0
            plane = lax.rem(lax.div(column, per_plane), 4)
            rest = jnp.where(is_plane, jnp.clip(offsets[plane] - half * rows, 0, rows - 1), 0)
            return is_plane, (2.0 * plane.astype(f32) + 1.0) * 0.125, rest

        up_is, up_part, self.up_rest = plane_of(lax.rem(a + 1, count_x))
        low_is, low_part, self.low_rest = plane_of(a)
        self.up_near = jnp.where(up_is, 1.0 - up_part, 1.0)
        self.up_far = jnp.where(up_is, up_part, 0.0)
        self.low_near = jnp.where(low_is, low_part, 0.0)
        self.low_far = jnp.where(low_is, 1.0 - low_part, 1.0)
        self.up_jump = jnp.where(up_is, -plane_speed, 0.0)
        self.low_jump = jnp.where(low_is, plane_speed, 0.0)


def order_sum(load):
    total = load(0)
    for i in range(1, 19):
        total = total + load(i)
    return total


def phi_kernel(f_ref, g_ref, top, bottom, phi_ref, to_north, to_south, gbuf, fbuf, sems):
    layers, rows = phi_ref.shape[0], phi_ref.shape[1]
    faces = (layers - 1, 0)
    f_copies = [
        pltpu.make_async_copy(f_ref.at[:, x], fbuf.at[:, s], sems.at[layers + s])
        for s, x in enumerate(faces)
    ]
    g_copies = [
        pltpu.make_async_copy(g_ref.at[:, x], gbuf.at[:, x], sems.at[x]) for x in range(layers)
    ]
    for copy in f_copies + g_copies:
        copy.start()
    phi_ref[layers - 1] = top[...]
    phi_ref[0] = bottom[...]
    edges = ((to_north, rows - 1, rows - 2, (7, 10)), (to_south, 0, 1, (9, 8)))
    for s, x in enumerate(faces):
        f_copies[s].wait()
        for out, edge, inner, chosen in edges:
            out[layers + s : layers + s + 1] = phi_ref[x, inner : inner + 1]
            at = layers + 2 + 6 * s
            out[at : at + 1] = fbuf[chosen[s], s, edge : edge + 1]
            for k, part in enumerate(moments_of(lambda i: fbuf[i, s, edge : edge + 1])):
                out[at + 2 + k : at + 3 + k] = part
    for x in range(layers):
        g_copies[x].wait()
        if 0 < x < layers - 1:
            phi_ref[x] = order_sum(lambda i: gbuf[i, x])
        to_north[x : x + 1] = phi_ref[x, rows - 1 : rows]
        to_south[x : x + 1] = phi_ref[x, 0:1]
    for s, x in enumerate(faces):
        for out, edge, inner, chosen in edges:
            at = layers + 3 + 6 * s
            out[at : at + 1] = gbuf[chosen[s], x, edge : edge + 1]
    for out in (to_north, to_south):
        out[layers + 14 : layers + 16] = jnp.zeros((2, out.shape[1]), f32)


def with_halo(ref, layer, below, above):
    rows = layer.shape[0]
    ref[8 : 8 + rows] = layer
    ref[7:8] = below
    ref[8 + rows : 9 + rows] = above


def corner_values(cells, planes, phi_ref, south_msg, north_msg, minus_wide, plus_wide):
    layers, rows, cols = phi_ref.shape
    cells[...] = jnp.ones_like(cells)
    for row in range(4):
        msg = south_msg if row < 2 else north_msg
        x = layers - 1 if row % 2 == 0 else 0
        beside = rows + (layers - 2 if row % 2 == 0 else 1)
        wide_row = 7 if row < 2 else rows + 8
        at = rows + layers
        first = at + 2 + 6 * (row % 2)
        far_phi = msg[at + row % 2 : at + row % 2 + 1]
        own_phi = phi_ref[x, 0:1] if row < 2 else phi_ref[x, rows - 1 : rows]
        parts = [msg[first + k : first + k + 1] for k in range(6)]
        parts.append(msg[rows + x : rows + x + 1])
        if row % 2 == 0:
            parts += [msg[beside : beside + 1], plus_wide[wide_row : wide_row + 1]]
        else:
            parts += [minus_wide[wide_row : wide_row + 1], msg[beside : beside + 1]]
        parts += [far_phi, own_phi] if row < 2 else [own_phi, far_phi]
        for k, part in enumerate(parts):
            cells[k, row : row + 1] = part
    place = lax.broadcasted_iota(jnp.int32, (8, cols), 0)
    is_top = (place == 0) | (place == 2)
    sx = jnp.where(is_top, 1.0, -1.0)
    sy = jnp.where(place < 2, 1.0, -1.0)
    delta = jnp.where(is_top, planes.up_jump, planes.low_jump)
    site = Site([cells[k] for k in range(2, 6)], *[cells[k] for k in range(6, 11)])
    w = lattice_weight[7]
    p = sx * site.u[0] + sy * site.u[1]
    q = sx * site.force[0] + sy * site.force[1]
    change = delta * (3.0 * sy + 9.0 * (sy * p) - 3.0 * site.u[1]) + 3.0 * (delta * delta)
    rp, gp = site.r * p, site.g_scale * p
    f_post = w * (site.k + p * (4.5 * rp + 3.375 * q) + 3.0 * rp + 1.125 * q + site.rho * change)
    g_post = w * (site.g_base + 4.5 * (gp * p) + 3.0 * gp + site.phi * change)
    return f_post - 0.25 * cells[0], g_post - (1.0 / 9.0) * cells[1]


def moment_kernel(after_north, after_south, f_ref, g_ref, faces, rims):
    layers, rows = f_ref.shape[1], f_ref.shape[2]
    for s, x in enumerate((layers - 1, 0)):
        for k, part in enumerate(moments_of(lambda i: f_ref[i, x])):
            faces[s, k] = part
    for s, (edge, chosen) in enumerate(((rows - 1, north_going), (0, south_going))):
        for k, part in enumerate(moments_of(lambda i: f_ref[i, :, edge, :])):
            rims[s, k] = part
        for j, i in enumerate(chosen):
            rims[s, 4 + j] = f_ref[i, :, edge, :]
            rims[s, 9 + j] = g_ref[i, :, edge, :]


def half_rows(rows, first):
    return slice(0, rows // 2) if first else slice(rows // 2, rows)


def seam_rows(rows, up):
    return slice(rows // 2 - 2, rows // 2) if up else slice(rows // 2, rows // 2 + 2)


def rim_values(rims, s, phi_ref, minus, plus, south_msg, north_msg, line, edge, chosen, out):
    layers, rows, cols = phi_ref.shape
    phi = phi_ref[:, edge, :]
    with_halo(line, phi, minus[edge : edge + 1], plus[edge : edge + 1])
    if edge == 0:
        below, above = south_msg[rows : rows + layers], phi_ref[:, 1, :]
    else:
        below, above = phi_ref[:, rows - 2, :], north_msg[rows : rows + layers]
    site = Site(
        [rims[s, k] for k in range(4)],
        phi,
        line[7 : 7 + layers],
        line[9 : 9 + layers],
        below,
        above,
    )
    for j, i in enumerate(chosen):
        cz = lattice_velocity[i][2]
        even, odd = site.pair_f(i)
        out[s, j] = z_moved(even + odd - 0.25 * rims[s, 4 + j], cz)
        even, odd = site.pair_g(i)
        out[s, 5 + j] = z_moved(even + odd - (1.0 / 9.0) * rims[s, 9 + j], cz)


def face_kernel(
    sizes,
    offsets,
    f_ref,
    g_ref,
    face_moments,
    rims,
    phi_ref,
    rise,
    fall,
    south_msg,
    north_msg,
    mate,
    direct,
    direct_short,
    across,
    across_short,
    joint,
    cross,
    minus_out,
    plus_out,
    minus_wide,
    plus_wide,
    window,
    halo,
    line,
    rim_post,
    post,
    cells,
    corners,
    raw,
    wide,
):
    layers, rows, cols = phi_ref.shape
    planes = Planes(offsets, rows, sizes)
    shear = Shear(raw, wide, rows)
    window[...] = jnp.zeros_like(window)
    for up in (True, False):
        if up:
            first, second = rise, north_msg
            near, far, start = planes.low_far, planes.low_near, planes.low_rest
        else:
            first, second = south_msg, fall
            near, far, start = planes.up_far, planes.up_near, rows - 1 - planes.up_rest
        target = minus_wide if up else plus_wide
        for k in range(window.shape[0]):
            lanes = slice(LANES * k, LANES * k + LANES)
            window[k, 8 : 8 + rows] = first[0:rows, lanes]
            window[k, 8 + rows : 8 + 2 * rows] = second[0:rows, lanes]
            target[:, lanes] = (
                near * window[k, pl.ds(start, rows + 16)]
                + far * window[k, pl.ds(start + 1, rows + 16)]
            )
    minus_out[...] = minus_wide[8 : 8 + rows]
    plus_out[...] = plus_wide[8 : 8 + rows]
    corners[0], corners[1] = corner_values(
        cells, planes, phi_ref, south_msg, north_msg, minus_wide, plus_wide
    )
    for s, (edge, chosen) in enumerate(((rows - 1, north_going), (0, south_going))):
        rim_values(
            rims,
            s,
            phi_ref,
            minus_out,
            plus_out,
            south_msg,
            north_msg,
            line,
            edge,
            chosen,
            rim_post,
        )
    for side, up in enumerate((True, False)):
        x = layers - 1 if up else 0
        delta = planes.up_jump if up else planes.low_jump
        with_halo(
            halo, phi_ref[x], south_msg[rows + x : rows + x + 1], north_msg[rows + x : rows + x + 1]
        )
        for h in range(0, rows, 8):
            span = slice(h, h + 8)
            phi_h = phi_ref[x, span]
            if up:
                minus, plus = phi_ref[x - 1, span], plus_wide[8 + h : 16 + h]
            else:
                minus, plus = minus_wide[8 + h : 16 + h], phi_ref[x + 1, span]
            site = Site(
                [face_moments[side, k, span] for k in range(4)],
                phi_h,
                minus,
                plus,
                halo[7 + h : 15 + h],
                halo[9 + h : 17 + h],
            )
            for j, i in enumerate(rising if up else falling):
                cz = lattice_velocity[i][2]
                change = lattice_weight[i] * site.jump(i, delta)
                even, odd = site.pair_f(i)
                value = even + odd - 0.25 * f_ref[i, x, span] + site.rho * change
                post[side, j, span] = z_moved(value, cz)
                even, odd = site.pair_g(i)
                value = even + odd - (1.0 / 9.0) * g_ref[i, x, span] + phi_h * change
                post[side, 5 + j, span] = z_moved(value, cz)

    part = rows // 2
    seam = 10 * part

    def hand_out(is_odd):
        for side, up in enumerate((True, False)):
            if up:
                near, far, rest = planes.up_near, planes.up_far, planes.up_rest
            else:
                near, far, rest = planes.low_near, planes.low_far, planes.low_rest
            first, second = (direct, mate) if up == is_odd else (joint, across)
            shear.clear()
            for j in range(10):
                cy = lattice_velocity[(rising if up else falling)[j % 5]][1]
                shear.put(post[side, j], up, near, far)
                corner = side + (0 if cy == 1 else 2)
                if cy == 1:
                    gate = jnp.where(rest == (0 if up else rows - 1), near, 0.0)
                    at = rows + 7 if up else rows + 8
                if cy == -1:
                    gate = jnp.where(rest == (rows - 1 if up else 0), far, 0.0)
                    at = 2 * rows + 7 if up else 2 * rows + 8
                if cy != 0:
                    shear.add_row(at, gate * corners[j // 5, corner : corner + 1])
                shear.take(up, 0, rest, cy, first, j)
                shear.take(up, 1, rest, cy, second, j)
        for j in range(10):
            mate[j, rows : rows + layers] = rim_post[1 if is_odd else 0, j]
            cross[j] = rim_post[0 if is_odd else 1, j]
            direct_short[j] = direct[j, half_rows(rows, is_odd)]
            across_short[part * j : part * j + part] = across[j, half_rows(rows, is_odd)]
            across_short[seam + 2 * j : seam + 2 * j + 2] = across[j, seam_rows(rows, not is_odd)]
        across_short[seam + 20 : seam + 24] = jnp.zeros((4, cols), f32)

    pl.when(planes.odd)(lambda: hand_out(True))
    pl.when(jnp.logical_not(planes.odd))(lambda: hand_out(False))


def bulk_kernel(
    after,
    f_ref,
    g_ref,
    phi_ref,
    minus,
    plus,
    south_msg,
    north_msg,
    mate_rim,
    cross_rim,
    next_f,
    next_g,
    wide_phi,
    halo,
):
    layers, rows, cols = phi_ref.shape
    is_odd = lax.rem(lax.axis_index("gy"), 2) == 1
    wide_phi[0] = minus[...]
    wide_phi[layers + 1] = plus[...]
    for x in range(layers):
        wide_phi[x + 1] = phi_ref[x]

    def layer(x, carry):
        with_halo(halo, phi_ref[x], south_msg[pl.ds(rows + x, 1)], north_msg[pl.ds(rows + x, 1)])
        beyond = lax.rem(x + 1, layers)
        before = lax.rem(x + layers - 1, layers)
        for h in range(0, rows, 8):
            span = slice(h, h + 8)
            phi_h = phi_ref[x, span]
            site = Site(
                moments_of(lambda i: f_ref[i, x, span]),
                phi_h,
                wide_phi[x, span],
                wide_phi[x + 2, span],
                halo[7 + h : 15 + h],
                halo[9 + h : 17 + h],
            )

            def emit(out, slot, i, value):
                cx, cy, cz = lattice_velocity[i]
                value = z_moved(value, cz)
                at = beyond if cx == 1 else before if cx == -1 else x
                if cy == 0:
                    out[i, at, span] = value
                elif cy == 1:
                    if h == 0:
                        rim = slot * 5 + north_going.index(i)
                        out[i, at, 0:1] = jnp.where(
                            is_odd, mate_rim[rim, pl.ds(rows + x, 1)], cross_rim[rim, pl.ds(x, 1)]
                        )
                    if h + 8 < rows:
                        out[i, at, h + 1 : h + 9] = value
                    else:
                        out[i, at, h + 1 : h + 8] = value[0:7]
                else:
                    if h + 8 == rows:
                        rim = slot * 5 + south_going.index(i)
                        out[i, at, rows - 1 : rows] = jnp.where(
                            is_odd, cross_rim[rim, pl.ds(x, 1)], mate_rim[rim, pl.ds(rows + x, 1)]
                        )
                    if h > 0:
                        out[i, at, h - 1 : h + 7] = value
                    else:
                        out[i, at, 0:7] = value[1:8]

            emit(next_f, 0, 0, lattice_weight[0] * site.k - 0.25 * f_ref[0, x, span])
            rest_g = (phi_h - 2.0 * site.mu - 0.5 * (phi_h * site.uu)) * (1.0 / 0.9)
            emit(next_g, 1, 0, rest_g - (1.0 / 9.0) * g_ref[0, x, span])
            for i in range(1, 19, 2):
                even, odd = site.pair_f(i)
                emit(next_f, 0, i, (even + odd) - 0.25 * f_ref[i, x, span])
                emit(next_f, 0, i + 1, (even - odd) - 0.25 * f_ref[i + 1, x, span])
                even, odd = site.pair_g(i)
                emit(next_g, 1, i, (even + odd) - (1.0 / 9.0) * g_ref[i, x, span])
                emit(next_g, 1, i + 1, (even - odd) - (1.0 / 9.0) * g_ref[i + 1, x, span])
        return carry

    lax.fori_loop(0, layers, layer, 0)


def put_faces(buf, out_f, out_g, chosen, x, sems):
    copies = [
        pltpu.make_async_copy(buf.at[5 * family + j], out.at[i, x], sems.at[5 * family + j])
        for family, out in enumerate((out_f, out_g))
        for j, i in enumerate(chosen)
    ]
    for copy in copies:
        copy.start()
    for copy in copies:
        copy.wait()


def merge_fill_kernel(
    count_x,
    long_planes,
    direct,
    direct_short,
    across,
    across_short,
    f_in,
    g_in,
    f_out,
    g_out,
    buf,
    sems,
):
    layers, rows = f_out.shape[1], f_out.shape[2]
    per_plane = count_x // 4
    a = lax.axis_index("gx")
    odd = lax.rem(lax.axis_index("gy"), 2) == 1
    part = rows // 2
    seam = 10 * part

    def merge(column, up):
        near, other, between = half_rows(rows, up), half_rows(rows, not up), seam_rows(rows, up)
        chosen, x = (rising, 0) if up else (falling, layers - 1)
        copies = [
            pltpu.make_async_copy(
                buf.at[j], (f_out if j < 5 else g_out).at[chosen[j % 5], x], sems.at[j]
            )
            for j in range(10)
        ]

        def long():
            for j in range(10):
                buf[j, near] = across[j, near] + direct_short[j]
                buf[j, other] = across[j, other]
                copies[j].start()

        def short():
            for j in range(10):
                at = seam + 2 * j
                buf[j, near] = direct[j, near]
                buf[j, between] = direct[j, between] + across_short[at : at + 2]
                buf[j, other] = direct[j, other] + across_short[part * j : part * j + part]
                copies[j].start()

        plane = lax.rem(lax.div(column, per_plane), 4)
        in_set = plane == long_planes[0]
        for k in long_planes[1:]:
            in_set = jnp.logical_or(in_set, plane == k)
        is_long = jnp.logical_and(lax.rem(column, per_plane) == 0, in_set)
        pl.when(is_long)(long)
        pl.when(jnp.logical_not(is_long))(short)
        for copy in copies:
            copy.wait()

    pl.when(odd)(lambda: merge(a, True))
    pl.when(jnp.logical_not(odd))(lambda: merge(lax.rem(a + 1, count_x), False))


def joint_fill_kernel(joint, f_in, g_in, f_out, g_out, sems):
    odd = lax.rem(lax.axis_index("gy"), 2) == 1
    layers = f_out.shape[1]
    pl.when(odd)(lambda: put_faces(joint, f_out, g_out, falling, layers - 1, sems))
    pl.when(jnp.logical_not(odd))(lambda: put_faces(joint, f_out, g_out, rising, 0, sems))


def on_device(momentum_dist, order_dist, offsets):
    layers, rows, cols = momentum_dist.shape[1:]
    count_x, count_y = lax.axis_size("gx"), lax.axis_size("gy")
    per_plane = count_x // 4
    half = count_y // 2

    def hop(value, target):
        perm = []
        for x in range(count_x):
            for y in range(count_y):
                tx, ty = target(x, y)
                perm.append((x * count_y + y, tx % count_x * count_y + ty % count_y))
        return lax.ppermute(value, ("gx", "gy"), perm)

    def base_up(x):
        return half if (x + 1) % per_plane == 0 else 0

    def base_low(x):
        return half if x % per_plane == 0 else 0

    def hop_parity(value, odd_up, extra):
        def target(x, y):
            if (y % 2 == 1) == odd_up:
                return (x + 1, y - base_up(x) - extra)
            return (x - 1, y + base_low(x) + extra)

        return hop(value, target)

    def hop_y(value, step):
        return hop(value, lambda x, y: (x, y + step))

    smem, vmem, anywhere = spec_of(pltpu.SMEM), spec_of(VMEM), spec_of(pl.ANY)
    plane = jax.ShapeDtypeStruct((rows, cols), f32)
    top, bottom = jnp.sum(order_dist[:, layers - 1], axis=0), jnp.sum(order_dist[:, 0], axis=0)
    rise = hop(top, lambda x, y: (x + 1, y - base_up(x)))
    fall = hop(bottom, lambda x, y: (x - 1, y + base_low(x)))

    block = jax.ShapeDtypeStruct((layers + 16, cols), f32)
    phi, to_north, to_south, order_near = pl.pallas_call(
        phi_kernel,
        out_shape=[jax.ShapeDtypeStruct((layers, rows, cols), f32)]
        + [block] * 2
        + [jax.ShapeDtypeStruct(order_dist.shape, f32)],
        in_specs=[anywhere, anywhere, vmem, vmem],
        out_specs=[vmem] * 4,
        scratch_shapes=[
            VMEM((19, 2, rows, cols), f32),
            pltpu.SemaphoreType.DMA((layers + 2,)),
        ],
        compiler_params=params(52 << 20),
        name="phi_all",
    )(momentum_dist, order_dist, top, bottom)
    to_north = jnp.concatenate([fall, to_north], 0)
    to_south = jnp.concatenate([rise, to_south], 0)
    south_msg, north_msg = hop_y(to_north, 1), hop_y(to_south, -1)

    face_moments, rims = pl.pallas_call(
        moment_kernel,
        out_shape=[
            jax.ShapeDtypeStruct((2, 4, rows, cols), f32),
            jax.ShapeDtypeStruct((2, 14, layers, cols), f32),
        ],
        in_specs=[anywhere, anywhere, vmem, vmem],
        out_specs=[vmem] * 2,
        compiler_params=params(16 << 20),
        name="moments",
    )(to_north, to_south, momentum_dist, order_near)

    part = rows // 2
    ten = jax.ShapeDtypeStruct((10, rows, cols), f32)
    ten_short = jax.ShapeDtypeStruct((10, part, cols), f32)
    ten_seam = jax.ShapeDtypeStruct((10 * part + 24, cols), f32)
    side = jax.ShapeDtypeStruct((10, layers, cols), f32)
    ten_side = jax.ShapeDtypeStruct((10, rows + layers, cols), f32)
    *outgoing, minus, plus = pl.pallas_call(
        functools.partial(face_kernel, (count_x, count_y)),
        out_shape=[ten_side, ten, ten_short, ten, ten_seam, ten, side] + [plane] * 2,
        in_specs=[smem] + [vmem] * 9,
        out_specs=[vmem] * 9,
        scratch_shapes=[
            VMEM((rows + 16, cols), f32),
            VMEM((rows + 16, cols), f32),
            VMEM((cols // LANES, 2 * rows + 16, LANES), f32),
            VMEM((rows + 16, cols), f32),
            VMEM((layers + 16, cols), f32),
            VMEM((2, 10, layers, cols), f32),
            VMEM((2, 10, rows, cols), f32),
            VMEM((11, 8, cols), f32),
            VMEM((2, 8, cols), f32),
            VMEM((cols // LANES, rows + 16, LANES), f32),
            VMEM((cols // LANES, 3 * rows + 16, LANES), f32),
        ],
        compiler_params=params(24 << 20),
        name="faces",
    )(
        offsets,
        momentum_dist,
        order_near,
        face_moments,
        rims,
        phi,
        rise,
        fall,
        south_msg,
        north_msg,
    )
    around = (phi, minus, plus, south_msg, north_msg)
    whole = jax.ShapeDtypeStruct(momentum_dist.shape, f32)

    def finish(long_planes, mate, direct, direct_short, across, across_short, joint, cross):

        def is_long(x):
            return x % per_plane == 0 and x // per_plane % 4 in long_planes

        def hop_some(value, odd_up, extra, long):
            pairs = []
            for x in range(count_x):
                for y in range(count_y):
                    up = (y % 2 == 1) == odd_up
                    tx = (x + 1 if up else x - 1) % count_x
                    if is_long(tx if up else x) != long:
                        continue
                    ty = y - base_up(x) - extra if up else y + base_low(x) + extra
                    pairs.append((x * count_y + y, tx * count_y + ty % count_y))
            return lax.ppermute(value, ("gx", "gy"), pairs)

        cross = hop(cross, lambda x, y: (x, y + 1 if y % 2 == 1 else y - 1))
        mate = hop(mate, lambda x, y: (x, y ^ 1))
        direct, direct_short, across, across_short, cross = lax.optimization_barrier(
            (direct, direct_short, across, across_short, cross)
        )
        direct = hop_some(direct, True, 0, False)
        direct_short = hop_some(direct_short, True, 0, True)
        across = hop_some(across, False, 1, True)
        across_short = hop_some(across_short, False, 1, False)
        joint = joint + mate[:, :rows]
        after = joint
        joint = hop_parity(joint, False, 0)

        next_f, next_g = pl.pallas_call(
            bulk_kernel,
            out_shape=[whole, whole],
            in_specs=[anywhere] + [vmem] * 9,
            out_specs=[vmem] * 2,
            scratch_shapes=[
                VMEM((layers + 2, rows, cols), f32),
                VMEM((rows + 16, cols), f32),
            ],
            compiler_params=params(48 << 20),
            name="bulk",
        )(after, momentum_dist, order_near, *around, mate, cross)

        next_f, next_g = pl.pallas_call(
            joint_fill_kernel,
            out_shape=[whole, whole],
            in_specs=[vmem, anywhere, anywhere],
            out_specs=[anywhere, anywhere],
            scratch_shapes=[pltpu.SemaphoreType.DMA((10,))],
            input_output_aliases={1: 0, 2: 1},
            compiler_params=params(24 << 20),
            name="joint_fill",
        )(joint, next_f, next_g)

        return pl.pallas_call(
            functools.partial(merge_fill_kernel, count_x, sorted(long_planes)),
            out_shape=[whole, whole],
            in_specs=[vmem] * 4 + [anywhere, anywhere],
            out_specs=[anywhere, anywhere],
            scratch_shapes=[VMEM((10, rows, cols), f32), pltpu.SemaphoreType.DMA((10,))],
            input_output_aliases={4: 0, 5: 1},
            compiler_params=params(24 << 20),
            name="merge_fill",
        )(direct, direct_short, across, across_short, next_f, next_g)

    is_long = [(offsets[k] - half * rows > part).astype(jnp.int32) for k in (1, 2)]
    branches = [
        functools.partial(finish, {3} | ({1} if k & 2 else set()) | ({2} if k & 1 else set()))
        for k in range(4)
    ]
    return lax.switch(2 * is_long[0] + is_long[1], branches, *outgoing)


def solution(mesh):
    return jax.shard_map(
        on_device,
        mesh=mesh,
        in_specs=(P(None, "gx", "gy", None), P(None, "gx", "gy", None), P()),
        out_specs=(P(None, "gx", "gy", None), P(None, "gx", "gy", None)),
        check_vma=False,
    )
```

```python
import functools

import jax
import jax.numpy as jnp
from jax import lax
from jax.experimental import pallas as pl
from jax.experimental.pallas import tpu as pltpu
from jax.sharding import PartitionSpec as P

lattice_velocity = [
    (0, 0, 0),
    (1, 0, 0),
    (-1, 0, 0),
    (0, 1, 0),
    (0, -1, 0),
    (0, 0, 1),
    (0, 0, -1),
    (1, 1, 0),
    (-1, -1, 0),
    (1, -1, 0),
    (-1, 1, 0),
    (1, 0, 1),
    (-1, 0, -1),
    (1, 0, -1),
    (-1, 0, 1),
    (0, 1, 1),
    (0, -1, -1),
    (0, 1, -1),
    (0, -1, 1),
]
lattice_weight = [1.0 / 3.0] + [1.0 / 18.0] * 6 + [1.0 / 36.0] * 12
plane_speed = 0.04
rising = [1, 7, 9, 11, 13]
falling = [2, 8, 10, 12, 14]
north_going = [i for i in range(19) if lattice_velocity[i][1] == 1]
south_going = [i for i in range(19) if lattice_velocity[i][1] == -1]
f32 = jnp.float32
VMEM = pltpu.VMEM
LANES = 128


def z_moved(value, step):
    if step == 0:
        return value
    return pltpu.roll(value, step % value.shape[-1], value.ndim - 1)


def spec_of(space):
    return pl.BlockSpec(memory_space=space)


def params(limit):
    return pltpu.CompilerParams(vmem_limit_bytes=limit)


def along(parts, c):
    total = None
    for sign, part in zip(c, parts):
        if sign == 0:
            continue
        if total is None:
            total = part if sign > 0 else -part
        else:
            total = total + part if sign > 0 else total - part
    return total


def signed_sum(load, axis):
    ups = [i for i in range(19) if lattice_velocity[i][axis] == 1]
    downs = [i for i in range(19) if lattice_velocity[i][axis] == -1]
    total = load(ups[0]) - load(downs[0])
    for i, j in zip(ups[1:], downs[1:]):
        total = total + (load(i) - load(j))
    return total


def moments_of(load):
    rho = load(0)
    for i in range(1, 19):
        rho = rho + load(i)
    return [rho] + [signed_sum(load, axis) for axis in range(3)]


class Site:
    def __init__(self, moments, phi, minus, plus, south, north):
        rho, momentum = moments[0], moments[1:]
        lower, upper = z_moved(phi, 1), z_moved(phi, -1)
        lap = (plus + minus) + (north + south) + (upper + lower) - 6.0 * phi
        mu = phi * (0.0625 * (phi * phi) - 0.0625) - 0.04 * lap
        half_mu = 0.5 * mu
        force = [half_mu * (plus - minus), half_mu * (north - south), half_mu * (upper - lower)]
        inverse = 1.0 / rho
        u = [(j + 0.5 * k) * inverse for j, k in zip(momentum, force)]
        uu = u[0] * u[0] + u[1] * u[1] + u[2] * u[2]
        uf = u[0] * force[0] + u[1] * force[1] + u[2] * force[2]
        self.rho, self.phi, self.mu, self.u, self.force, self.uu = rho, phi, mu, u, force, uu
        self.r = 1.25 * rho
        self.k = self.r * (1.0 - 1.5 * uu) - 1.125 * uf
        self.g_scale = phi * (1.0 / 0.9)
        self.g_base = (3.0 / 0.9) * mu - 1.5 * (self.g_scale * uu)

    def pair_f(self, i):
        p, q = along(self.u, lattice_velocity[i]), along(self.force, lattice_velocity[i])
        w = lattice_weight[i]
        rp = self.r * p
        even = w * (self.k + p * (4.5 * rp + 3.375 * q))
        odd = (3.0 * w) * rp + (1.125 * w) * q
        return even, odd

    def pair_g(self, i):
        p = along(self.u, lattice_velocity[i])
        w = lattice_weight[i]
        gp = self.g_scale * p
        return w * (self.g_base + 4.5 * (gp * p)), (3.0 * w) * gp

    def jump(self, i, delta):
        cy = lattice_velocity[i][1]
        uy = self.u[1]
        if cy == 0:
            return delta * (-3.0 * uy) - (1.5 * delta * delta)
        p = along(self.u, lattice_velocity[i])
        return delta * (3.0 * cy + (9.0 * cy) * p - 3.0 * uy) + (3.0 * delta * delta)


class Shear:
    def __init__(self, raw, wide, rows):
        self.raw, self.wide, self.rows = raw, wide, rows

    def clear(self):
        self.raw[...] = jnp.zeros_like(self.raw)
        self.wide[...] = jnp.zeros_like(self.wide)

    def put(self, value, up, near, far):
        n = self.rows
        for k in range(self.raw.shape[0]):
            self.raw[k, 8 : 8 + n] = value[:, LANES * k : LANES * k + LANES]
        for k in range(self.raw.shape[0]):
            if up:
                self.wide[k, n : n + n + 8] = (
                    near * self.raw[k, 0 : n + 8] + far * self.raw[k, 1 : n + 9]
                )
            else:
                self.wide[k, n + 8 : n + n + 16] = (
                    near * self.raw[k, 7 : n + 15] + far * self.raw[k, 8 : n + 16]
                )

    def add_row(self, at, row):
        for k in range(self.raw.shape[0]):
            lanes = slice(LANES * k, LANES * k + LANES)
            self.wide[k, at : at + 1] = self.wide[k, at : at + 1] + row[:, lanes]

    def take(self, up, block, rest, cy, ref, j):
        n = self.rows
        if up:
            start = (n + 8 if block == 0 else 8) + rest - cy
        else:
            start = (n + 8 if block == 0 else n + n + 8) - rest - cy
        for k in range(self.raw.shape[0]):
            ref[j, 0:n, LANES * k : LANES * k + LANES] = self.wide[k, pl.ds(start, n)]


def plane_at(column, count_x):
    per_plane = count_x // 4
    is_plane = lax.rem(column, per_plane) == 0
    return is_plane, lax.rem(lax.div(column, per_plane), 4)


class Planes:
    def __init__(self, rests, count_x):
        self.up_rest, self.low_rest = rests
        self.odd = lax.rem(lax.axis_index("gy"), 2) == 1
        a = lax.axis_index("gx")

        def part_of(column):
            is_plane, plane = plane_at(column, count_x)
            return is_plane, (2.0 * plane.astype(f32) + 1.0) * 0.125

        up_is, up_part = part_of(lax.rem(a + 1, count_x))
        low_is, low_part = part_of(a)
        self.up_near = jnp.where(up_is, 1.0 - up_part, 1.0)
        self.up_far = jnp.where(up_is, up_part, 0.0)
        self.low_near = jnp.where(low_is, low_part, 0.0)
        self.low_far = jnp.where(low_is, 1.0 - low_part, 1.0)
        self.up_jump = jnp.where(up_is, -plane_speed, 0.0)
        self.low_jump = jnp.where(low_is, plane_speed, 0.0)


def order_sum(load):
    total = load(0)
    for i in range(1, 19):
        total = total + load(i)
    return total


def phi_kernel(f_ref, g_ref, top, bottom, phi_ref, to_north, to_south, gbuf, fbuf, sems):
    layers, rows = phi_ref.shape[0], phi_ref.shape[1]
    faces = (layers - 1, 0)
    f_copies = [
        pltpu.make_async_copy(f_ref.at[:, x], fbuf.at[:, s], sems.at[layers + s])
        for s, x in enumerate(faces)
    ]
    g_copies = [
        pltpu.make_async_copy(g_ref.at[:, x], gbuf.at[:, x], sems.at[x]) for x in range(layers)
    ]
    for copy in f_copies + g_copies:
        copy.start()
    phi_ref[layers - 1] = top[...]
    phi_ref[0] = bottom[...]
    edges = ((to_north, rows - 1, rows - 2, (7, 10)), (to_south, 0, 1, (9, 8)))
    for s, x in enumerate(faces):
        f_copies[s].wait()
        for out, edge, inner, chosen in edges:
            out[layers + s : layers + s + 1] = phi_ref[x, inner : inner + 1]
            at = layers + 2 + 6 * s
            out[at : at + 1] = fbuf[chosen[s], s, edge : edge + 1]
            for k, part in enumerate(moments_of(lambda i: fbuf[i, s, edge : edge + 1])):
                out[at + 2 + k : at + 3 + k] = part
    for x in range(layers):
        g_copies[x].wait()
        if 0 < x < layers - 1:
            phi_ref[x] = order_sum(lambda i: gbuf[i, x])
        to_north[x : x + 1] = phi_ref[x, rows - 1 : rows]
        to_south[x : x + 1] = phi_ref[x, 0:1]
    for s, x in enumerate(faces):
        for out, edge, inner, chosen in edges:
            at = layers + 3 + 6 * s
            out[at : at + 1] = gbuf[chosen[s], x, edge : edge + 1]
    for out in (to_north, to_south):
        out[layers + 14 : layers + 16] = jnp.zeros((2, out.shape[1]), f32)


def with_halo(ref, layer, below, above):
    rows = layer.shape[0]
    ref[8 : 8 + rows] = layer
    ref[7:8] = below
    ref[8 + rows : 9 + rows] = above


def corner_values(cells, planes, phi_ref, south_msg, north_msg, minus_wide, plus_wide):
    layers, rows, cols = phi_ref.shape
    cells[...] = jnp.ones_like(cells)
    for row in range(4):
        msg = south_msg if row < 2 else north_msg
        x = layers - 1 if row % 2 == 0 else 0
        beside = rows + (layers - 2 if row % 2 == 0 else 1)
        wide_row = 7 if row < 2 else rows + 8
        at = rows + layers
        first = at + 2 + 6 * (row % 2)
        far_phi = msg[at + row % 2 : at + row % 2 + 1]
        own_phi = phi_ref[x, 0:1] if row < 2 else phi_ref[x, rows - 1 : rows]
        parts = [msg[first + k : first + k + 1] for k in range(6)]
        parts.append(msg[rows + x : rows + x + 1])
        if row % 2 == 0:
            parts += [msg[beside : beside + 1], plus_wide[wide_row : wide_row + 1]]
        else:
            parts += [minus_wide[wide_row : wide_row + 1], msg[beside : beside + 1]]
        parts += [far_phi, own_phi] if row < 2 else [own_phi, far_phi]
        for k, part in enumerate(parts):
            cells[k, row : row + 1] = part
    place = lax.broadcasted_iota(jnp.int32, (8, cols), 0)
    is_top = (place == 0) | (place == 2)
    sx = jnp.where(is_top, 1.0, -1.0)
    sy = jnp.where(place < 2, 1.0, -1.0)
    delta = jnp.where(is_top, planes.up_jump, planes.low_jump)
    site = Site([cells[k] for k in range(2, 6)], *[cells[k] for k in range(6, 11)])
    w = lattice_weight[7]
    p = sx * site.u[0] + sy * site.u[1]
    q = sx * site.force[0] + sy * site.force[1]
    change = delta * (3.0 * sy + 9.0 * (sy * p) - 3.0 * site.u[1]) + 3.0 * (delta * delta)
    rp, gp = site.r * p, site.g_scale * p
    f_post = w * (site.k + p * (4.5 * rp + 3.375 * q) + 3.0 * rp + 1.125 * q + site.rho * change)
    g_post = w * (site.g_base + 4.5 * (gp * p) + 3.0 * gp + site.phi * change)
    return f_post - 0.25 * cells[0], g_post - (1.0 / 9.0) * cells[1]


def moment_kernel(
    sizes, after_north, after_south, offsets, f_ref, g_ref, faces, rims, rests
):
    layers, rows = f_ref.shape[1], f_ref.shape[2]
    count_x, count_y = sizes
    a = lax.axis_index("gx")
    for k, column in enumerate((lax.rem(a + 1, count_x), a)):
        is_plane, plane = plane_at(column, count_x)
        rest = jnp.clip(offsets[plane] - count_y // 2 * rows, 0, rows - 1)
        rest = jnp.where(is_plane, rest, 0).astype(f32)
        rests[k] = jnp.full(rests.shape[1:], rest, f32)
    for s, x in enumerate((layers - 1, 0)):
        for k, part in enumerate(moments_of(lambda i: f_ref[i, x])):
            faces[s, k] = part
    for s, (edge, chosen) in enumerate(((rows - 1, north_going), (0, south_going))):
        for k, part in enumerate(moments_of(lambda i: f_ref[i, :, edge, :])):
            rims[s, k] = part
        for j, i in enumerate(chosen):
            rims[s, 4 + j] = f_ref[i, :, edge, :]
            rims[s, 9 + j] = g_ref[i, :, edge, :]


def half_rows(rows, first):
    return slice(0, rows // 2) if first else slice(rows // 2, rows)


def seam_rows(rows, up):
    return slice(rows // 2 - 2, rows // 2) if up else slice(rows // 2, rows // 2 + 2)


def rim_values(rims, s, phi_ref, minus, plus, south_msg, north_msg, line, edge, chosen, out):
    layers, rows, cols = phi_ref.shape
    phi = phi_ref[:, edge, :]
    with_halo(line, phi, minus[edge : edge + 1], plus[edge : edge + 1])
    if edge == 0:
        below, above = south_msg[rows : rows + layers], phi_ref[:, 1, :]
    else:
        below, above = phi_ref[:, rows - 2, :], north_msg[rows : rows + layers]
    site = Site(
        [rims[s, k] for k in range(4)],
        phi,
        line[7 : 7 + layers],
        line[9 : 9 + layers],
        below,
        above,
    )
    for j, i in enumerate(chosen):
        cz = lattice_velocity[i][2]
        even, odd = site.pair_f(i)
        out[s, j] = z_moved(even + odd - 0.25 * rims[s, 4 + j], cz)
        even, odd = site.pair_g(i)
        out[s, 5 + j] = z_moved(even + odd - (1.0 / 9.0) * rims[s, 9 + j], cz)


def face_kernel(
    count_x,
    rests,
    f_ref,
    g_ref,
    face_moments,
    rims,
    phi_ref,
    rise,
    fall,
    south_msg,
    north_msg,
    mate,
    direct,
    direct_short,
    across,
    across_short,
    joint,
    cross,
    minus_out,
    plus_out,
    minus_wide,
    plus_wide,
    window,
    halo,
    line,
    rim_post,
    post,
    cells,
    corners,
    raw,
    wide,
):
    layers, rows, cols = phi_ref.shape
    planes = Planes([jnp.max(rests[k]).astype(jnp.int32) for k in range(2)], count_x)
    shear = Shear(raw, wide, rows)
    window[...] = jnp.zeros_like(window)
    for up in (True, False):
        if up:
            first, second = rise, north_msg
            near, far, start = planes.low_far, planes.low_near, planes.low_rest
        else:
            first, second = south_msg, fall
            near, far, start = planes.up_far, planes.up_near, rows - 1 - planes.up_rest
        target = minus_wide if up else plus_wide
        for k in range(window.shape[0]):
            lanes = slice(LANES * k, LANES * k + LANES)
            window[k, 8 : 8 + rows] = first[0:rows, lanes]
            window[k, 8 + rows : 8 + 2 * rows] = second[0:rows, lanes]
            target[:, lanes] = (
                near * window[k, pl.ds(start, rows + 16)]
                + far * window[k, pl.ds(start + 1, rows + 16)]
            )
    minus_out[...] = minus_wide[8 : 8 + rows]
    plus_out[...] = plus_wide[8 : 8 + rows]
    corners[0], corners[1] = corner_values(
        cells, planes, phi_ref, south_msg, north_msg, minus_wide, plus_wide
    )
    for s, (edge, chosen) in enumerate(((rows - 1, north_going), (0, south_going))):
        rim_values(
            rims,
            s,
            phi_ref,
            minus_out,
            plus_out,
            south_msg,
            north_msg,
            line,
            edge,
            chosen,
            rim_post,
        )
    for side, up in enumerate((True, False)):
        x = layers - 1 if up else 0
        delta = planes.up_jump if up else planes.low_jump
        with_halo(
            halo, phi_ref[x], south_msg[rows + x : rows + x + 1], north_msg[rows + x : rows + x + 1]
        )
        for h in range(0, rows, 8):
            span = slice(h, h + 8)
            phi_h = phi_ref[x, span]
            if up:
                minus, plus = phi_ref[x - 1, span], plus_wide[8 + h : 16 + h]
            else:
                minus, plus = minus_wide[8 + h : 16 + h], phi_ref[x + 1, span]
            site = Site(
                [face_moments[side, k, span] for k in range(4)],
                phi_h,
                minus,
                plus,
                halo[7 + h : 15 + h],
                halo[9 + h : 17 + h],
            )
            for j, i in enumerate(rising if up else falling):
                cz = lattice_velocity[i][2]
                change = lattice_weight[i] * site.jump(i, delta)
                even, odd = site.pair_f(i)
                value = even + odd - 0.25 * f_ref[i, x, span] + site.rho * change
                post[side, j, span] = z_moved(value, cz)
                even, odd = site.pair_g(i)
                value = even + odd - (1.0 / 9.0) * g_ref[i, x, span] + phi_h * change
                post[side, 5 + j, span] = z_moved(value, cz)

    part = rows // 2
    seam = 10 * part

    def hand_out(is_odd):
        for side, up in enumerate((True, False)):
            if up:
                near, far, rest = planes.up_near, planes.up_far, planes.up_rest
            else:
                near, far, rest = planes.low_near, planes.low_far, planes.low_rest
            first, second = (direct, mate) if up == is_odd else (joint, across)
            shear.clear()
            for j in range(10):
                cy = lattice_velocity[(rising if up else falling)[j % 5]][1]
                shear.put(post[side, j], up, near, far)
                corner = side + (0 if cy == 1 else 2)
                if cy == 1:
                    gate = jnp.where(rest == (0 if up else rows - 1), near, 0.0)
                    at = rows + 7 if up else rows + 8
                if cy == -1:
                    gate = jnp.where(rest == (rows - 1 if up else 0), far, 0.0)
                    at = 2 * rows + 7 if up else 2 * rows + 8
                if cy != 0:
                    shear.add_row(at, gate * corners[j // 5, corner : corner + 1])
                shear.take(up, 0, rest, cy, first, j)
                shear.take(up, 1, rest, cy, second, j)
        for j in range(10):
            mate[j, rows : rows + layers] = rim_post[1 if is_odd else 0, j]
            cross[j] = rim_post[0 if is_odd else 1, j]
            direct_short[j] = direct[j, half_rows(rows, is_odd)]
            across_short[part * j : part * j + part] = across[j, half_rows(rows, is_odd)]
            across_short[seam + 2 * j : seam + 2 * j + 2] = across[j, seam_rows(rows, not is_odd)]
        across_short[seam + 20 : seam + 24] = jnp.zeros((4, cols), f32)

    pl.when(planes.odd)(lambda: hand_out(True))
    pl.when(jnp.logical_not(planes.odd))(lambda: hand_out(False))


def bulk_kernel(
    after,
    f_ref,
    g_ref,
    phi_ref,
    minus,
    plus,
    south_msg,
    north_msg,
    mate_rim,
    cross_rim,
    next_f,
    next_g,
    wide_phi,
    halo,
):
    layers, rows, cols = phi_ref.shape
    is_odd = lax.rem(lax.axis_index("gy"), 2) == 1
    wide_phi[0] = minus[...]
    wide_phi[layers + 1] = plus[...]
    for x in range(layers):
        wide_phi[x + 1] = phi_ref[x]

    def layer(x, carry):
        with_halo(halo, phi_ref[x], south_msg[pl.ds(rows + x, 1)], north_msg[pl.ds(rows + x, 1)])
        beyond = lax.rem(x + 1, layers)
        before = lax.rem(x + layers - 1, layers)
        for h in range(0, rows, 8):
            span = slice(h, h + 8)
            phi_h = phi_ref[x, span]
            site = Site(
                moments_of(lambda i: f_ref[i, x, span]),
                phi_h,
                wide_phi[x, span],
                wide_phi[x + 2, span],
                halo[7 + h : 15 + h],
                halo[9 + h : 17 + h],
            )

            def emit(out, slot, i, value):
                cx, cy, cz = lattice_velocity[i]
                value = z_moved(value, cz)
                at = beyond if cx == 1 else before if cx == -1 else x
                if cy == 0:
                    out[i, at, span] = value
                elif cy == 1:
                    if h == 0:
                        rim = slot * 5 + north_going.index(i)
                        out[i, at, 0:1] = jnp.where(
                            is_odd, mate_rim[rim, pl.ds(rows + x, 1)], cross_rim[rim, pl.ds(x, 1)]
                        )
                    if h + 8 < rows:
                        out[i, at, h + 1 : h + 9] = value
                    else:
                        out[i, at, h + 1 : h + 8] = value[0:7]
                else:
                    if h + 8 == rows:
                        rim = slot * 5 + south_going.index(i)
                        out[i, at, rows - 1 : rows] = jnp.where(
                            is_odd, cross_rim[rim, pl.ds(x, 1)], mate_rim[rim, pl.ds(rows + x, 1)]
                        )
                    if h > 0:
                        out[i, at, h - 1 : h + 7] = value
                    else:
                        out[i, at, 0:7] = value[1:8]

            emit(next_f, 0, 0, lattice_weight[0] * site.k - 0.25 * f_ref[0, x, span])
            rest_g = (phi_h - 2.0 * site.mu - 0.5 * (phi_h * site.uu)) * (1.0 / 0.9)
            emit(next_g, 1, 0, rest_g - (1.0 / 9.0) * g_ref[0, x, span])
            for i in range(1, 19, 2):
                even, odd = site.pair_f(i)
                emit(next_f, 0, i, (even + odd) - 0.25 * f_ref[i, x, span])
                emit(next_f, 0, i + 1, (even - odd) - 0.25 * f_ref[i + 1, x, span])
                even, odd = site.pair_g(i)
                emit(next_g, 1, i, (even + odd) - (1.0 / 9.0) * g_ref[i, x, span])
                emit(next_g, 1, i + 1, (even - odd) - (1.0 / 9.0) * g_ref[i + 1, x, span])
        return carry

    lax.fori_loop(0, layers, layer, 0)


def put_faces(buf, out_f, out_g, chosen, x, sems):
    copies = [
        pltpu.make_async_copy(buf.at[5 * family + j], out.at[i, x], sems.at[5 * family + j])
        for family, out in enumerate((out_f, out_g))
        for j, i in enumerate(chosen)
    ]
    for copy in copies:
        copy.start()
    for copy in copies:
        copy.wait()


def merge_fill_kernel(
    count_x,
    long_planes,
    direct,
    direct_short,
    across,
    across_short,
    f_in,
    g_in,
    f_out,
    g_out,
    buf,
    sems,
):
    layers, rows = f_out.shape[1], f_out.shape[2]
    a = lax.axis_index("gx")
    odd = lax.rem(lax.axis_index("gy"), 2) == 1
    part = rows // 2
    seam = 10 * part

    def merge(column, up):
        near, other, between = half_rows(rows, up), half_rows(rows, not up), seam_rows(rows, up)
        chosen, x = (rising, 0) if up else (falling, layers - 1)
        copies = [
            pltpu.make_async_copy(
                buf.at[j], (f_out if j < 5 else g_out).at[chosen[j % 5], x], sems.at[j]
            )
            for j in range(10)
        ]

        def long():
            for j in range(10):
                buf[j, near] = across[j, near] + direct_short[j]
                buf[j, other] = across[j, other]
                copies[j].start()

        def short():
            for j in range(10):
                at = seam + 2 * j
                buf[j, near] = direct[j, near]
                buf[j, between] = direct[j, between] + across_short[at : at + 2]
                buf[j, other] = direct[j, other] + across_short[part * j : part * j + part]
                copies[j].start()

        is_plane, plane = plane_at(column, count_x)
        in_set = plane == long_planes[0]
        for k in long_planes[1:]:
            in_set = jnp.logical_or(in_set, plane == k)
        is_long = jnp.logical_and(is_plane, in_set)
        pl.when(is_long)(long)
        pl.when(jnp.logical_not(is_long))(short)
        for copy in copies:
            copy.wait()

    pl.when(odd)(lambda: merge(a, True))
    pl.when(jnp.logical_not(odd))(lambda: merge(lax.rem(a + 1, count_x), False))


def joint_fill_kernel(joint, f_in, g_in, f_out, g_out, sems):
    odd = lax.rem(lax.axis_index("gy"), 2) == 1
    layers = f_out.shape[1]
    pl.when(odd)(lambda: put_faces(joint, f_out, g_out, falling, layers - 1, sems))
    pl.when(jnp.logical_not(odd))(lambda: put_faces(joint, f_out, g_out, rising, 0, sems))


def on_device(momentum_dist, order_dist, offsets):
    layers, rows, cols = momentum_dist.shape[1:]
    count_x, count_y = lax.axis_size("gx"), lax.axis_size("gy")
    per_plane = count_x // 4
    half = count_y // 2

    def hop(value, target):
        perm = []
        for x in range(count_x):
            for y in range(count_y):
                tx, ty = target(x, y)
                perm.append((x * count_y + y, tx % count_x * count_y + ty % count_y))
        return lax.ppermute(value, ("gx", "gy"), perm)

    def base_up(x):
        return half if (x + 1) % per_plane == 0 else 0

    def base_low(x):
        return half if x % per_plane == 0 else 0

    def hop_parity(value, odd_up, extra):
        def target(x, y):
            if (y % 2 == 1) == odd_up:
                return (x + 1, y - base_up(x) - extra)
            return (x - 1, y + base_low(x) + extra)

        return hop(value, target)

    def hop_y(value, step):
        return hop(value, lambda x, y: (x, y + step))

    smem, vmem, anywhere = spec_of(pltpu.SMEM), spec_of(VMEM), spec_of(pl.ANY)
    plane = jax.ShapeDtypeStruct((rows, cols), f32)
    top, bottom = jnp.sum(order_dist[:, layers - 1], axis=0), jnp.sum(order_dist[:, 0], axis=0)
    rise = hop(top, lambda x, y: (x + 1, y - base_up(x)))
    fall = hop(bottom, lambda x, y: (x - 1, y + base_low(x)))

    block = jax.ShapeDtypeStruct((layers + 16, cols), f32)
    phi, to_north, to_south, order_near = pl.pallas_call(
        phi_kernel,
        out_shape=[jax.ShapeDtypeStruct((layers, rows, cols), f32)]
        + [block] * 2
        + [jax.ShapeDtypeStruct(order_dist.shape, f32)],
        in_specs=[anywhere, anywhere, vmem, vmem],
        out_specs=[vmem] * 4,
        scratch_shapes=[
            VMEM((19, 2, rows, cols), f32),
            pltpu.SemaphoreType.DMA((layers + 2,)),
        ],
        compiler_params=params(52 << 20),
        name="phi_all",
    )(momentum_dist, order_dist, top, bottom)
    to_north = jnp.concatenate([fall, to_north], 0)
    to_south = jnp.concatenate([rise, to_south], 0)
    south_msg, north_msg = hop_y(to_north, 1), hop_y(to_south, -1)

    face_moments, rims, rests = pl.pallas_call(
        functools.partial(moment_kernel, (count_x, count_y)),
        out_shape=[
            jax.ShapeDtypeStruct((2, 4, rows, cols), f32),
            jax.ShapeDtypeStruct((2, 14, layers, cols), f32),
            jax.ShapeDtypeStruct((2, 8, LANES), f32),
        ],
        in_specs=[anywhere, anywhere, smem, vmem, vmem],
        out_specs=[vmem] * 3,
        compiler_params=params(16 << 20),
        name="moments",
    )(to_north, to_south, offsets, momentum_dist, order_near)

    part = rows // 2
    ten = jax.ShapeDtypeStruct((10, rows, cols), f32)
    ten_short = jax.ShapeDtypeStruct((10, part, cols), f32)
    ten_seam = jax.ShapeDtypeStruct((10 * part + 24, cols), f32)
    side = jax.ShapeDtypeStruct((10, layers, cols), f32)
    ten_side = jax.ShapeDtypeStruct((10, rows + layers, cols), f32)
    *outgoing, minus, plus = pl.pallas_call(
        functools.partial(face_kernel, count_x),
        out_shape=[ten_side, ten, ten_short, ten, ten_seam, ten, side] + [plane] * 2,
        in_specs=[vmem] * 10,
        out_specs=[vmem] * 9,
        scratch_shapes=[
            VMEM((rows + 16, cols), f32),
            VMEM((rows + 16, cols), f32),
            VMEM((cols // LANES, 2 * rows + 16, LANES), f32),
            VMEM((rows + 16, cols), f32),
            VMEM((layers + 16, cols), f32),
            VMEM((2, 10, layers, cols), f32),
            VMEM((2, 10, rows, cols), f32),
            VMEM((11, 8, cols), f32),
            VMEM((2, 8, cols), f32),
            VMEM((cols // LANES, rows + 16, LANES), f32),
            VMEM((cols // LANES, 3 * rows + 16, LANES), f32),
        ],
        compiler_params=params(24 << 20),
        name="faces",
    )(
        rests,
        momentum_dist,
        order_near,
        face_moments,
        rims,
        phi,
        rise,
        fall,
        south_msg,
        north_msg,
    )
    around = (phi, minus, plus, south_msg, north_msg)
    whole = jax.ShapeDtypeStruct(momentum_dist.shape, f32)

    def finish(long_planes, mate, direct, direct_short, across, across_short, joint, cross):

        def is_long(x):
            return x % per_plane == 0 and x // per_plane % 4 in long_planes

        def hop_some(value, odd_up, extra, long):
            pairs = []
            for x in range(count_x):
                for y in range(count_y):
                    up = (y % 2 == 1) == odd_up
                    tx = (x + 1 if up else x - 1) % count_x
                    if is_long(tx if up else x) != long:
                        continue
                    ty = y - base_up(x) - extra if up else y + base_low(x) + extra
                    pairs.append((x * count_y + y, tx * count_y + ty % count_y))
            return lax.ppermute(value, ("gx", "gy"), pairs)

        cross = hop(cross, lambda x, y: (x, y + 1 if y % 2 == 1 else y - 1))
        mate = hop(mate, lambda x, y: (x, y ^ 1))
        direct, direct_short, across, across_short, cross = lax.optimization_barrier(
            (direct, direct_short, across, across_short, cross)
        )
        direct = hop_some(direct, True, 0, False)
        direct_short = hop_some(direct_short, True, 0, True)
        across = hop_some(across, False, 1, True)
        across_short = hop_some(across_short, False, 1, False)
        joint = joint + mate[:, :rows]
        after = joint
        joint = hop_parity(joint, False, 0)

        next_f, next_g = pl.pallas_call(
            bulk_kernel,
            out_shape=[whole, whole],
            in_specs=[anywhere] + [vmem] * 9,
            out_specs=[vmem] * 2,
            scratch_shapes=[
                VMEM((layers + 2, rows, cols), f32),
                VMEM((rows + 16, cols), f32),
            ],
            compiler_params=params(48 << 20),
            name="bulk",
        )(after, momentum_dist, order_near, *around, mate, cross)

        next_f, next_g = pl.pallas_call(
            joint_fill_kernel,
            out_shape=[whole, whole],
            in_specs=[vmem, anywhere, anywhere],
            out_specs=[anywhere, anywhere],
            scratch_shapes=[pltpu.SemaphoreType.DMA((10,))],
            input_output_aliases={1: 0, 2: 1},
            compiler_params=params(24 << 20),
            name="joint_fill",
        )(joint, next_f, next_g)

        return pl.pallas_call(
            functools.partial(merge_fill_kernel, count_x, sorted(long_planes)),
            out_shape=[whole, whole],
            in_specs=[vmem] * 4 + [anywhere, anywhere],
            out_specs=[anywhere, anywhere],
            scratch_shapes=[VMEM((10, rows, cols), f32), pltpu.SemaphoreType.DMA((10,))],
            input_output_aliases={4: 0, 5: 1},
            compiler_params=params(24 << 20),
            name="merge_fill",
        )(direct, direct_short, across, across_short, next_f, next_g)

    is_long = [(offsets[k] - half * rows > part).astype(jnp.int32) for k in (1, 2)]
    branches = [
        functools.partial(finish, {3} | ({1} if k & 2 else set()) | ({2} if k & 1 else set()))
        for k in range(4)
    ]
    return lax.switch(2 * is_long[0] + is_long[1], branches, *outgoing)


def solution(mesh):
    return jax.shard_map(
        on_device,
        mesh=mesh,
        in_specs=(P(None, "gx", "gy", None), P(None, "gx", "gy", None), P()),
        out_specs=(P(None, "gx", "gy", None), P(None, "gx", "gy", None)),
        check_vma=False,
    )
```

```python
import functools

import jax
import jax.numpy as jnp
from jax import lax
from jax.experimental import pallas as pl
from jax.experimental.pallas import tpu as pltpu
from jax.sharding import PartitionSpec as P

lattice_velocity = [
    (0, 0, 0),
    (1, 0, 0),
    (-1, 0, 0),
    (0, 1, 0),
    (0, -1, 0),
    (0, 0, 1),
    (0, 0, -1),
    (1, 1, 0),
    (-1, -1, 0),
    (1, -1, 0),
    (-1, 1, 0),
    (1, 0, 1),
    (-1, 0, -1),
    (1, 0, -1),
    (-1, 0, 1),
    (0, 1, 1),
    (0, -1, -1),
    (0, 1, -1),
    (0, -1, 1),
]
lattice_weight = [1.0 / 3.0] + [1.0 / 18.0] * 6 + [1.0 / 36.0] * 12
plane_speed = 0.04
rising = [1, 7, 9, 11, 13]
falling = [2, 8, 10, 12, 14]
north_going = [i for i in range(19) if lattice_velocity[i][1] == 1]
south_going = [i for i in range(19) if lattice_velocity[i][1] == -1]
f32 = jnp.float32
VMEM = pltpu.VMEM
LANES = 128


def z_moved(value, step):
    if step == 0:
        return value
    return pltpu.roll(value, step % value.shape[-1], value.ndim - 1)


def spec_of(space):
    return pl.BlockSpec(memory_space=space)


def params(limit):
    return pltpu.CompilerParams(vmem_limit_bytes=limit)


def along(parts, c):
    total = None
    for sign, part in zip(c, parts):
        if sign == 0:
            continue
        if total is None:
            total = part if sign > 0 else -part
        else:
            total = total + part if sign > 0 else total - part
    return total


def signed_sum(load, axis):
    ups = [i for i in range(19) if lattice_velocity[i][axis] == 1]
    downs = [i for i in range(19) if lattice_velocity[i][axis] == -1]
    total = load(ups[0]) - load(downs[0])
    for i, j in zip(ups[1:], downs[1:]):
        total = total + (load(i) - load(j))
    return total


def moments_of(load):
    rho = load(0)
    for i in range(1, 19):
        rho = rho + load(i)
    return [rho] + [signed_sum(load, axis) for axis in range(3)]


class Site:
    def __init__(self, moments, phi, minus, plus, south, north):
        rho, momentum = moments[0], moments[1:]
        lower, upper = z_moved(phi, 1), z_moved(phi, -1)
        lap = (plus + minus) + (north + south) + (upper + lower) - 6.0 * phi
        mu = phi * (0.0625 * (phi * phi) - 0.0625) - 0.04 * lap
        half_mu = 0.5 * mu
        force = [half_mu * (plus - minus), half_mu * (north - south), half_mu * (upper - lower)]
        inverse = 1.0 / rho
        u = [(j + 0.5 * k) * inverse for j, k in zip(momentum, force)]
        uu = u[0] * u[0] + u[1] * u[1] + u[2] * u[2]
        uf = u[0] * force[0] + u[1] * force[1] + u[2] * force[2]
        self.rho, self.phi, self.mu, self.u, self.force, self.uu = rho, phi, mu, u, force, uu
        self.r = 1.25 * rho
        self.k = self.r * (1.0 - 1.5 * uu) - 1.125 * uf
        self.g_scale = phi * (1.0 / 0.9)
        self.g_base = (3.0 / 0.9) * mu - 1.5 * (self.g_scale * uu)

    def pair_f(self, i):
        p, q = along(self.u, lattice_velocity[i]), along(self.force, lattice_velocity[i])
        w = lattice_weight[i]
        rp = self.r * p
        even = w * (self.k + p * (4.5 * rp + 3.375 * q))
        odd = (3.0 * w) * rp + (1.125 * w) * q
        return even, odd

    def pair_g(self, i):
        p = along(self.u, lattice_velocity[i])
        w = lattice_weight[i]
        gp = self.g_scale * p
        return w * (self.g_base + 4.5 * (gp * p)), (3.0 * w) * gp

    def jump(self, i, delta):
        cy = lattice_velocity[i][1]
        uy = self.u[1]
        if cy == 0:
            return delta * (-3.0 * uy) - (1.5 * delta * delta)
        p = along(self.u, lattice_velocity[i])
        return delta * (3.0 * cy + (9.0 * cy) * p - 3.0 * uy) + (3.0 * delta * delta)


class Shear:
    def __init__(self, raw, wide, rows):
        self.raw, self.wide, self.rows = raw, wide, rows

    def clear(self):
        self.raw[...] = jnp.zeros_like(self.raw)
        self.wide[...] = jnp.zeros_like(self.wide)

    def put(self, value, up, near, far):
        n = self.rows
        for k in range(self.raw.shape[0]):
            self.raw[k, 8 : 8 + n] = value[:, LANES * k : LANES * k + LANES]
        for k in range(self.raw.shape[0]):
            if up:
                self.wide[k, n : n + n + 8] = (
                    near * self.raw[k, 0 : n + 8] + far * self.raw[k, 1 : n + 9]
                )
            else:
                self.wide[k, n + 8 : n + n + 16] = (
                    near * self.raw[k, 7 : n + 15] + far * self.raw[k, 8 : n + 16]
                )

    def add_row(self, at, row):
        for k in range(self.raw.shape[0]):
            lanes = slice(LANES * k, LANES * k + LANES)
            self.wide[k, at : at + 1] = self.wide[k, at : at + 1] + row[:, lanes]

    def take(self, up, block, rest, cy, ref, j):
        n = self.rows
        if up:
            start = (n + 8 if block == 0 else 8) + rest - cy
        else:
            start = (n + 8 if block == 0 else n + n + 8) - rest - cy
        for k in range(self.raw.shape[0]):
            ref[j, 0:n, LANES * k : LANES * k + LANES] = self.wide[k, pl.ds(start, n)]


def plane_at(column, count_x):
    per_plane = count_x // 4
    is_plane = lax.rem(column, per_plane) == 0
    return is_plane, lax.rem(lax.div(column, per_plane), 4)


class Planes:
    def __init__(self, rests, count_x):
        self.up_rest, self.low_rest = rests
        self.odd = lax.rem(lax.axis_index("gy"), 2) == 1
        a = lax.axis_index("gx")

        def part_of(column):
            is_plane, plane = plane_at(column, count_x)
            return is_plane, (2.0 * plane.astype(f32) + 1.0) * 0.125

        up_is, up_part = part_of(lax.rem(a + 1, count_x))
        low_is, low_part = part_of(a)
        self.up_near = jnp.where(up_is, 1.0 - up_part, 1.0)
        self.up_far = jnp.where(up_is, up_part, 0.0)
        self.low_near = jnp.where(low_is, low_part, 0.0)
        self.low_far = jnp.where(low_is, 1.0 - low_part, 1.0)
        self.up_jump = jnp.where(up_is, -plane_speed, 0.0)
        self.low_jump = jnp.where(low_is, plane_speed, 0.0)


def order_sum(load):
    total = load(0)
    for i in range(1, 19):
        total = total + load(i)
    return total


def gate_kernel(g_ref, out):
    out[...] = jnp.zeros_like(out)


def phi_kernel(gate, f_ref, g_ref, top, bottom, phi_ref, to_north, to_south, fbuf, sems):
    layers, rows = phi_ref.shape[0], phi_ref.shape[1]
    faces = (layers - 1, 0)
    copies = [
        pltpu.make_async_copy(f_ref.at[:, x], fbuf.at[:, s], sems.at[s])
        for s, x in enumerate(faces)
    ]
    for copy in copies:
        copy.start()
    phi_ref[layers - 1] = top[...]
    phi_ref[0] = bottom[...]
    for x in range(layers):
        if 0 < x < layers - 1:
            phi_ref[x] = order_sum(lambda i: g_ref[i, x])
        to_north[x : x + 1] = phi_ref[x, rows - 1 : rows]
        to_south[x : x + 1] = phi_ref[x, 0:1]
    for s, x in enumerate(faces):
        copies[s].wait()
        for out, edge, inner, chosen in (
            (to_north, rows - 1, rows - 2, (7, 10)),
            (to_south, 0, 1, (9, 8)),
        ):
            out[layers + s : layers + s + 1] = phi_ref[x, inner : inner + 1]
            at = layers + 2 + 6 * s
            out[at : at + 1] = fbuf[chosen[s], s, edge : edge + 1]
            out[at + 1 : at + 2] = g_ref[chosen[s], x, edge : edge + 1]
            for k, part in enumerate(moments_of(lambda i: fbuf[i, s, edge : edge + 1])):
                out[at + 2 + k : at + 3 + k] = part
    for out in (to_north, to_south):
        out[layers + 14 : layers + 16] = jnp.zeros((2, out.shape[1]), f32)


def with_halo(ref, layer, below, above):
    rows = layer.shape[0]
    ref[8 : 8 + rows] = layer
    ref[7:8] = below
    ref[8 + rows : 9 + rows] = above


def corner_values(cells, planes, phi_ref, south_msg, north_msg, minus_wide, plus_wide):
    layers, rows, cols = phi_ref.shape
    cells[...] = jnp.ones_like(cells)
    for row in range(4):
        msg = south_msg if row < 2 else north_msg
        x = layers - 1 if row % 2 == 0 else 0
        beside = rows + (layers - 2 if row % 2 == 0 else 1)
        wide_row = 7 if row < 2 else rows + 8
        at = rows + layers
        first = at + 2 + 6 * (row % 2)
        far_phi = msg[at + row % 2 : at + row % 2 + 1]
        own_phi = phi_ref[x, 0:1] if row < 2 else phi_ref[x, rows - 1 : rows]
        parts = [msg[first + k : first + k + 1] for k in range(6)]
        parts.append(msg[rows + x : rows + x + 1])
        if row % 2 == 0:
            parts += [msg[beside : beside + 1], plus_wide[wide_row : wide_row + 1]]
        else:
            parts += [minus_wide[wide_row : wide_row + 1], msg[beside : beside + 1]]
        parts += [far_phi, own_phi] if row < 2 else [own_phi, far_phi]
        for k, part in enumerate(parts):
            cells[k, row : row + 1] = part
    place = lax.broadcasted_iota(jnp.int32, (8, cols), 0)
    is_top = (place == 0) | (place == 2)
    sx = jnp.where(is_top, 1.0, -1.0)
    sy = jnp.where(place < 2, 1.0, -1.0)
    delta = jnp.where(is_top, planes.up_jump, planes.low_jump)
    site = Site([cells[k] for k in range(2, 6)], *[cells[k] for k in range(6, 11)])
    w = lattice_weight[7]
    p = sx * site.u[0] + sy * site.u[1]
    q = sx * site.force[0] + sy * site.force[1]
    change = delta * (3.0 * sy + 9.0 * (sy * p) - 3.0 * site.u[1]) + 3.0 * (delta * delta)
    rp, gp = site.r * p, site.g_scale * p
    f_post = w * (site.k + p * (4.5 * rp + 3.375 * q) + 3.0 * rp + 1.125 * q + site.rho * change)
    g_post = w * (site.g_base + 4.5 * (gp * p) + 3.0 * gp + site.phi * change)
    return f_post - 0.25 * cells[0], g_post - (1.0 / 9.0) * cells[1]


def moment_kernel(
    sizes, after_north, after_south, offsets, f_ref, g_ref, faces, rims, rests
):
    layers, rows = f_ref.shape[1], f_ref.shape[2]
    count_x, count_y = sizes
    a = lax.axis_index("gx")
    for k, column in enumerate((lax.rem(a + 1, count_x), a)):
        is_plane, plane = plane_at(column, count_x)
        rest = jnp.clip(offsets[plane] - count_y // 2 * rows, 0, rows - 1)
        rest = jnp.where(is_plane, rest, 0).astype(f32)
        rests[k] = jnp.full(rests.shape[1:], rest, f32)
    for s, x in enumerate((layers - 1, 0)):
        for k, part in enumerate(moments_of(lambda i: f_ref[i, x])):
            faces[s, k] = part
    for s, (edge, chosen) in enumerate(((rows - 1, north_going), (0, south_going))):
        for k, part in enumerate(moments_of(lambda i: f_ref[i, :, edge, :])):
            rims[s, k] = part
        for j, i in enumerate(chosen):
            rims[s, 4 + j] = f_ref[i, :, edge, :]
            rims[s, 9 + j] = g_ref[i, :, edge, :]


def half_rows(rows, first):
    return slice(0, rows // 2) if first else slice(rows // 2, rows)


def seam_rows(rows, up):
    return slice(rows // 2 - 2, rows // 2) if up else slice(rows // 2, rows // 2 + 2)


def rim_values(rims, s, phi_ref, minus, plus, south_msg, north_msg, line, edge, chosen, out):
    layers, rows, cols = phi_ref.shape
    phi = phi_ref[:, edge, :]
    with_halo(line, phi, minus[edge : edge + 1], plus[edge : edge + 1])
    if edge == 0:
        below, above = south_msg[rows : rows + layers], phi_ref[:, 1, :]
    else:
        below, above = phi_ref[:, rows - 2, :], north_msg[rows : rows + layers]
    site = Site(
        [rims[s, k] for k in range(4)],
        phi,
        line[7 : 7 + layers],
        line[9 : 9 + layers],
        below,
        above,
    )
    for j, i in enumerate(chosen):
        cz = lattice_velocity[i][2]
        even, odd = site.pair_f(i)
        out[s, j] = z_moved(even + odd - 0.25 * rims[s, 4 + j], cz)
        even, odd = site.pair_g(i)
        out[s, 5 + j] = z_moved(even + odd - (1.0 / 9.0) * rims[s, 9 + j], cz)


def face_kernel(
    count_x,
    rests,
    f_ref,
    g_ref,
    face_moments,
    rims,
    phi_ref,
    rise,
    fall,
    south_msg,
    north_msg,
    mate,
    direct,
    direct_short,
    across,
    across_short,
    joint,
    cross,
    minus_out,
    plus_out,
    minus_wide,
    plus_wide,
    window,
    halo,
    line,
    rim_post,
    post,
    cells,
    corners,
    raw,
    wide,
):
    layers, rows, cols = phi_ref.shape
    planes = Planes([jnp.max(rests[k]).astype(jnp.int32) for k in range(2)], count_x)
    shear = Shear(raw, wide, rows)
    window[...] = jnp.zeros_like(window)
    for up in (True, False):
        if up:
            first, second = rise, north_msg
            near, far, start = planes.low_far, planes.low_near, planes.low_rest
        else:
            first, second = south_msg, fall
            near, far, start = planes.up_far, planes.up_near, rows - 1 - planes.up_rest
        target = minus_wide if up else plus_wide
        for k in range(window.shape[0]):
            lanes = slice(LANES * k, LANES * k + LANES)
            window[k, 8 : 8 + rows] = first[0:rows, lanes]
            window[k, 8 + rows : 8 + 2 * rows] = second[0:rows, lanes]
            target[:, lanes] = (
                near * window[k, pl.ds(start, rows + 16)]
                + far * window[k, pl.ds(start + 1, rows + 16)]
            )
    minus_out[...] = minus_wide[8 : 8 + rows]
    plus_out[...] = plus_wide[8 : 8 + rows]
    corners[0], corners[1] = corner_values(
        cells, planes, phi_ref, south_msg, north_msg, minus_wide, plus_wide
    )
    for s, (edge, chosen) in enumerate(((rows - 1, north_going), (0, south_going))):
        rim_values(
            rims,
            s,
            phi_ref,
            minus_out,
            plus_out,
            south_msg,
            north_msg,
            line,
            edge,
            chosen,
            rim_post,
        )
    for side, up in enumerate((True, False)):
        x = layers - 1 if up else 0
        delta = planes.up_jump if up else planes.low_jump
        with_halo(
            halo, phi_ref[x], south_msg[rows + x : rows + x + 1], north_msg[rows + x : rows + x + 1]
        )
        for h in range(0, rows, 8):
            span = slice(h, h + 8)
            phi_h = phi_ref[x, span]
            if up:
                minus, plus = phi_ref[x - 1, span], plus_wide[8 + h : 16 + h]
            else:
                minus, plus = minus_wide[8 + h : 16 + h], phi_ref[x + 1, span]
            site = Site(
                [face_moments[side, k, span] for k in range(4)],
                phi_h,
                minus,
                plus,
                halo[7 + h : 15 + h],
                halo[9 + h : 17 + h],
            )
            for j, i in enumerate(rising if up else falling):
                cz = lattice_velocity[i][2]
                change = lattice_weight[i] * site.jump(i, delta)
                even, odd = site.pair_f(i)
                value = even + odd - 0.25 * f_ref[i, x, span] + site.rho * change
                post[side, j, span] = z_moved(value, cz)
                even, odd = site.pair_g(i)
                value = even + odd - (1.0 / 9.0) * g_ref[i, x, span] + phi_h * change
                post[side, 5 + j, span] = z_moved(value, cz)

    part = rows // 2
    seam = 10 * part

    def hand_out(is_odd):
        for side, up in enumerate((True, False)):
            if up:
                near, far, rest = planes.up_near, planes.up_far, planes.up_rest
            else:
                near, far, rest = planes.low_near, planes.low_far, planes.low_rest
            first, second = (direct, mate) if up == is_odd else (joint, across)
            shear.clear()
            for j in range(10):
                cy = lattice_velocity[(rising if up else falling)[j % 5]][1]
                shear.put(post[side, j], up, near, far)
                corner = side + (0 if cy == 1 else 2)
                if cy == 1:
                    gate = jnp.where(rest == (0 if up else rows - 1), near, 0.0)
                    at = rows + 7 if up else rows + 8
                if cy == -1:
                    gate = jnp.where(rest == (rows - 1 if up else 0), far, 0.0)
                    at = 2 * rows + 7 if up else 2 * rows + 8
                if cy != 0:
                    shear.add_row(at, gate * corners[j // 5, corner : corner + 1])
                shear.take(up, 0, rest, cy, first, j)
                shear.take(up, 1, rest, cy, second, j)
        for j in range(10):
            mate[j, rows : rows + layers] = rim_post[1 if is_odd else 0, j]
            cross[j] = rim_post[0 if is_odd else 1, j]
            direct_short[j] = direct[j, half_rows(rows, is_odd)]
            across_short[part * j : part * j + part] = across[j, half_rows(rows, is_odd)]
            across_short[seam + 2 * j : seam + 2 * j + 2] = across[j, seam_rows(rows, not is_odd)]
        across_short[seam + 20 : seam + 24] = jnp.zeros((4, cols), f32)

    pl.when(planes.odd)(lambda: hand_out(True))
    pl.when(jnp.logical_not(planes.odd))(lambda: hand_out(False))


def bulk_kernel(
    after,
    f_ref,
    g_ref,
    phi_ref,
    minus,
    plus,
    south_msg,
    north_msg,
    mate_rim,
    cross_rim,
    next_f,
    next_g,
    wide_phi,
    halo,
):
    layers, rows, cols = phi_ref.shape
    is_odd = lax.rem(lax.axis_index("gy"), 2) == 1
    wide_phi[0] = minus[...]
    wide_phi[layers + 1] = plus[...]
    for x in range(layers):
        wide_phi[x + 1] = phi_ref[x]

    def layer(x, carry):
        with_halo(halo, phi_ref[x], south_msg[pl.ds(rows + x, 1)], north_msg[pl.ds(rows + x, 1)])
        beyond = lax.rem(x + 1, layers)
        before = lax.rem(x + layers - 1, layers)
        for h in range(0, rows, 8):
            span = slice(h, h + 8)
            phi_h = phi_ref[x, span]
            site = Site(
                moments_of(lambda i: f_ref[i, x, span]),
                phi_h,
                wide_phi[x, span],
                wide_phi[x + 2, span],
                halo[7 + h : 15 + h],
                halo[9 + h : 17 + h],
            )

            def emit(out, slot, i, value):
                cx, cy, cz = lattice_velocity[i]
                value = z_moved(value, cz)
                at = beyond if cx == 1 else before if cx == -1 else x
                if cy == 0:
                    out[i, at, span] = value
                elif cy == 1:
                    if h == 0:
                        rim = slot * 5 + north_going.index(i)
                        out[i, at, 0:1] = jnp.where(
                            is_odd, mate_rim[rim, pl.ds(rows + x, 1)], cross_rim[rim, pl.ds(x, 1)]
                        )
                    if h + 8 < rows:
                        out[i, at, h + 1 : h + 9] = value
                    else:
                        out[i, at, h + 1 : h + 8] = value[0:7]
                else:
                    if h + 8 == rows:
                        rim = slot * 5 + south_going.index(i)
                        out[i, at, rows - 1 : rows] = jnp.where(
                            is_odd, cross_rim[rim, pl.ds(x, 1)], mate_rim[rim, pl.ds(rows + x, 1)]
                        )
                    if h > 0:
                        out[i, at, h - 1 : h + 7] = value
                    else:
                        out[i, at, 0:7] = value[1:8]

            emit(next_f, 0, 0, lattice_weight[0] * site.k - 0.25 * f_ref[0, x, span])
            rest_g = (phi_h - 2.0 * site.mu - 0.5 * (phi_h * site.uu)) * (1.0 / 0.9)
            emit(next_g, 1, 0, rest_g - (1.0 / 9.0) * g_ref[0, x, span])
            for i in range(1, 19, 2):
                even, odd = site.pair_f(i)
                emit(next_f, 0, i, (even + odd) - 0.25 * f_ref[i, x, span])
                emit(next_f, 0, i + 1, (even - odd) - 0.25 * f_ref[i + 1, x, span])
                even, odd = site.pair_g(i)
                emit(next_g, 1, i, (even + odd) - (1.0 / 9.0) * g_ref[i, x, span])
                emit(next_g, 1, i + 1, (even - odd) - (1.0 / 9.0) * g_ref[i + 1, x, span])
        return carry

    lax.fori_loop(0, layers, layer, 0)


def put_faces(buf, out_f, out_g, chosen, x, sems):
    copies = [
        pltpu.make_async_copy(buf.at[5 * family + j], out.at[i, x], sems.at[5 * family + j])
        for family, out in enumerate((out_f, out_g))
        for j, i in enumerate(chosen)
    ]
    for copy in copies:
        copy.start()
    for copy in copies:
        copy.wait()


def merge_fill_kernel(
    count_x,
    long_planes,
    direct,
    direct_short,
    across,
    across_short,
    f_in,
    g_in,
    f_out,
    g_out,
    buf,
    sems,
):
    layers, rows = f_out.shape[1], f_out.shape[2]
    a = lax.axis_index("gx")
    odd = lax.rem(lax.axis_index("gy"), 2) == 1
    part = rows // 2
    seam = 10 * part

    def merge(column, up):
        near, other, between = half_rows(rows, up), half_rows(rows, not up), seam_rows(rows, up)
        chosen, x = (rising, 0) if up else (falling, layers - 1)
        copies = [
            pltpu.make_async_copy(
                buf.at[j], (f_out if j < 5 else g_out).at[chosen[j % 5], x], sems.at[j]
            )
            for j in range(10)
        ]

        def long():
            for j in range(10):
                buf[j, near] = across[j, near] + direct_short[j]
                buf[j, other] = across[j, other]
                copies[j].start()

        def short():
            for j in range(10):
                at = seam + 2 * j
                buf[j, near] = direct[j, near]
                buf[j, between] = direct[j, between] + across_short[at : at + 2]
                buf[j, other] = direct[j, other] + across_short[part * j : part * j + part]
                copies[j].start()

        is_plane, plane = plane_at(column, count_x)
        in_set = plane == long_planes[0]
        for k in long_planes[1:]:
            in_set = jnp.logical_or(in_set, plane == k)
        is_long = jnp.logical_and(is_plane, in_set)
        pl.when(is_long)(long)
        pl.when(jnp.logical_not(is_long))(short)
        for copy in copies:
            copy.wait()

    pl.when(odd)(lambda: merge(a, True))
    pl.when(jnp.logical_not(odd))(lambda: merge(lax.rem(a + 1, count_x), False))


def joint_fill_kernel(joint, f_in, g_in, f_out, g_out, sems):
    odd = lax.rem(lax.axis_index("gy"), 2) == 1
    layers = f_out.shape[1]
    pl.when(odd)(lambda: put_faces(joint, f_out, g_out, falling, layers - 1, sems))
    pl.when(jnp.logical_not(odd))(lambda: put_faces(joint, f_out, g_out, rising, 0, sems))


def on_device(momentum_dist, order_dist, offsets):
    layers, rows, cols = momentum_dist.shape[1:]
    count_x, count_y = lax.axis_size("gx"), lax.axis_size("gy")
    per_plane = count_x // 4
    half = count_y // 2

    def hop(value, target):
        perm = []
        for x in range(count_x):
            for y in range(count_y):
                tx, ty = target(x, y)
                perm.append((x * count_y + y, tx % count_x * count_y + ty % count_y))
        return lax.ppermute(value, ("gx", "gy"), perm)

    def base_up(x):
        return half if (x + 1) % per_plane == 0 else 0

    def base_low(x):
        return half if x % per_plane == 0 else 0

    def hop_parity(value, odd_up, extra):
        def target(x, y):
            if (y % 2 == 1) == odd_up:
                return (x + 1, y - base_up(x) - extra)
            return (x - 1, y + base_low(x) + extra)

        return hop(value, target)

    def hop_y(value, step):
        return hop(value, lambda x, y: (x, y + step))

    smem, vmem, anywhere = spec_of(pltpu.SMEM), spec_of(VMEM), spec_of(pl.ANY)
    plane = jax.ShapeDtypeStruct((rows, cols), f32)
    top, bottom = jnp.sum(order_dist[:, layers - 1], axis=0), jnp.sum(order_dist[:, 0], axis=0)
    rise = hop(top, lambda x, y: (x + 1, y - base_up(x)))
    fall = hop(bottom, lambda x, y: (x - 1, y + base_low(x)))

    block = jax.ShapeDtypeStruct((layers + 16, cols), f32)
    gate = pl.pallas_call(
        gate_kernel,
        out_shape=jax.ShapeDtypeStruct((8, LANES), f32),
        in_specs=[anywhere],
        out_specs=vmem,
        compiler_params=params(50 << 20),
        name="gate",
    )(order_dist)
    phi, to_north, to_south = pl.pallas_call(
        phi_kernel,
        out_shape=[jax.ShapeDtypeStruct((layers, rows, cols), f32)] + [block] * 2,
        in_specs=[anywhere, anywhere, vmem, vmem, vmem],
        out_specs=[vmem] * 3,
        scratch_shapes=[VMEM((19, 2, rows, cols), f32), pltpu.SemaphoreType.DMA((2,))],
        compiler_params=params(8 << 20),
        name="phi_all",
    )(gate, momentum_dist, order_dist, top, bottom)
    to_north = jnp.concatenate([fall, to_north], 0)
    to_south = jnp.concatenate([rise, to_south], 0)
    south_msg, north_msg = hop_y(to_north, 1), hop_y(to_south, -1)

    face_moments, rims, rests = pl.pallas_call(
        functools.partial(moment_kernel, (count_x, count_y)),
        out_shape=[
            jax.ShapeDtypeStruct((2, 4, rows, cols), f32),
            jax.ShapeDtypeStruct((2, 14, layers, cols), f32),
            jax.ShapeDtypeStruct((2, 8, LANES), f32),
        ],
        in_specs=[anywhere, anywhere, smem, vmem, vmem],
        out_specs=[vmem] * 3,
        compiler_params=params(16 << 20),
        name="moments",
    )(to_north, to_south, offsets, momentum_dist, order_dist)

    part = rows // 2
    ten = jax.ShapeDtypeStruct((10, rows, cols), f32)
    ten_short = jax.ShapeDtypeStruct((10, part, cols), f32)
    ten_seam = jax.ShapeDtypeStruct((10 * part + 24, cols), f32)
    side = jax.ShapeDtypeStruct((10, layers, cols), f32)
    ten_side = jax.ShapeDtypeStruct((10, rows + layers, cols), f32)
    *outgoing, minus, plus = pl.pallas_call(
        functools.partial(face_kernel, count_x),
        out_shape=[ten_side, ten, ten_short, ten, ten_seam, ten, side] + [plane] * 2,
        in_specs=[vmem] * 10,
        out_specs=[vmem] * 9,
        scratch_shapes=[
            VMEM((rows + 16, cols), f32),
            VMEM((rows + 16, cols), f32),
            VMEM((cols // LANES, 2 * rows + 16, LANES), f32),
            VMEM((rows + 16, cols), f32),
            VMEM((layers + 16, cols), f32),
            VMEM((2, 10, layers, cols), f32),
            VMEM((2, 10, rows, cols), f32),
            VMEM((11, 8, cols), f32),
            VMEM((2, 8, cols), f32),
            VMEM((cols // LANES, rows + 16, LANES), f32),
            VMEM((cols // LANES, 3 * rows + 16, LANES), f32),
        ],
        compiler_params=params(24 << 20),
        name="faces",
    )(
        rests,
        momentum_dist,
        order_dist,
        face_moments,
        rims,
        phi,
        rise,
        fall,
        south_msg,
        north_msg,
    )
    around = (phi, minus, plus, south_msg, north_msg)
    whole = jax.ShapeDtypeStruct(momentum_dist.shape, f32)

    def finish(long_planes, mate, direct, direct_short, across, across_short, joint, cross):

        def is_long(x):
            return x % per_plane == 0 and x // per_plane % 4 in long_planes

        def hop_some(value, odd_up, extra, long):
            pairs = []
            for x in range(count_x):
                for y in range(count_y):
                    up = (y % 2 == 1) == odd_up
                    tx = (x + 1 if up else x - 1) % count_x
                    if is_long(tx if up else x) != long:
                        continue
                    ty = y - base_up(x) - extra if up else y + base_low(x) + extra
                    pairs.append((x * count_y + y, tx * count_y + ty % count_y))
            return lax.ppermute(value, ("gx", "gy"), pairs)

        cross = hop(cross, lambda x, y: (x, y + 1 if y % 2 == 1 else y - 1))
        mate = hop(mate, lambda x, y: (x, y ^ 1))
        direct, direct_short, across, across_short, cross = lax.optimization_barrier(
            (direct, direct_short, across, across_short, cross)
        )
        direct = hop_some(direct, True, 0, False)
        direct_short = hop_some(direct_short, True, 0, True)
        across = hop_some(across, False, 1, True)
        across_short = hop_some(across_short, False, 1, False)
        joint = joint + mate[:, :rows]
        after = joint
        joint = hop_parity(joint, False, 0)

        next_f, next_g = pl.pallas_call(
            bulk_kernel,
            out_shape=[whole, whole],
            in_specs=[anywhere] + [vmem] * 9,
            out_specs=[vmem] * 2,
            scratch_shapes=[
                VMEM((layers + 2, rows, cols), f32),
                VMEM((rows + 16, cols), f32),
            ],
            compiler_params=params(48 << 20),
            name="bulk",
        )(after, momentum_dist, order_dist, *around, mate, cross)

        next_f, next_g = pl.pallas_call(
            joint_fill_kernel,
            out_shape=[whole, whole],
            in_specs=[vmem, anywhere, anywhere],
            out_specs=[anywhere, anywhere],
            scratch_shapes=[pltpu.SemaphoreType.DMA((10,))],
            input_output_aliases={1: 0, 2: 1},
            compiler_params=params(24 << 20),
            name="joint_fill",
        )(joint, next_f, next_g)

        return pl.pallas_call(
            functools.partial(merge_fill_kernel, count_x, sorted(long_planes)),
            out_shape=[whole, whole],
            in_specs=[vmem] * 4 + [anywhere, anywhere],
            out_specs=[anywhere, anywhere],
            scratch_shapes=[VMEM((10, rows, cols), f32), pltpu.SemaphoreType.DMA((10,))],
            input_output_aliases={4: 0, 5: 1},
            compiler_params=params(24 << 20),
            name="merge_fill",
        )(direct, direct_short, across, across_short, next_f, next_g)

    is_long = [(offsets[k] - half * rows > part).astype(jnp.int32) for k in (1, 2)]
    branches = [
        functools.partial(finish, {3} | ({1} if k & 2 else set()) | ({2} if k & 1 else set()))
        for k in range(4)
    ]
    return lax.switch(2 * is_long[0] + is_long[1], branches, *outgoing)


def solution(mesh):
    return jax.shard_map(
        on_device,
        mesh=mesh,
        in_specs=(P(None, "gx", "gy", None), P(None, "gx", "gy", None), P()),
        out_specs=(P(None, "gx", "gy", None), P(None, "gx", "gy", None)),
        check_vma=False,
    )
```

```python
import functools

import jax
import jax.numpy as jnp
from jax import lax
from jax.experimental import pallas as pl
from jax.experimental.pallas import tpu as pltpu
from jax.sharding import PartitionSpec as P

lattice_velocity = [
    (0, 0, 0),
    (1, 0, 0),
    (-1, 0, 0),
    (0, 1, 0),
    (0, -1, 0),
    (0, 0, 1),
    (0, 0, -1),
    (1, 1, 0),
    (-1, -1, 0),
    (1, -1, 0),
    (-1, 1, 0),
    (1, 0, 1),
    (-1, 0, -1),
    (1, 0, -1),
    (-1, 0, 1),
    (0, 1, 1),
    (0, -1, -1),
    (0, 1, -1),
    (0, -1, 1),
]
lattice_weight = [1.0 / 3.0] + [1.0 / 18.0] * 6 + [1.0 / 36.0] * 12
plane_speed = 0.04
rising = [1, 7, 9, 11, 13]
falling = [2, 8, 10, 12, 14]
north_going = [i for i in range(19) if lattice_velocity[i][1] == 1]
south_going = [i for i in range(19) if lattice_velocity[i][1] == -1]
f32 = jnp.float32
VMEM = pltpu.VMEM
LANES = 128


def z_moved(value, step):
    if step == 0:
        return value
    return pltpu.roll(value, step % value.shape[-1], value.ndim - 1)


def spec_of(space):
    return pl.BlockSpec(memory_space=space)


def params(limit):
    return pltpu.CompilerParams(vmem_limit_bytes=limit)


def along(parts, c):
    total = None
    for sign, part in zip(c, parts):
        if sign == 0:
            continue
        if total is None:
            total = part if sign > 0 else -part
        else:
            total = total + part if sign > 0 else total - part
    return total


def signed_sum(load, axis):
    ups = [i for i in range(19) if lattice_velocity[i][axis] == 1]
    downs = [i for i in range(19) if lattice_velocity[i][axis] == -1]
    total = load(ups[0]) - load(downs[0])
    for i, j in zip(ups[1:], downs[1:]):
        total = total + (load(i) - load(j))
    return total


def moments_of(load):
    rho = load(0)
    for i in range(1, 19):
        rho = rho + load(i)
    return [rho] + [signed_sum(load, axis) for axis in range(3)]


class Site:
    def __init__(self, moments, phi, minus, plus, south, north):
        rho, momentum = moments[0], moments[1:]
        lower, upper = z_moved(phi, 1), z_moved(phi, -1)
        lap = (plus + minus) + (north + south) + (upper + lower) - 6.0 * phi
        mu = phi * (0.0625 * (phi * phi) - 0.0625) - 0.04 * lap
        half_mu = 0.5 * mu
        force = [half_mu * (plus - minus), half_mu * (north - south), half_mu * (upper - lower)]
        inverse = 1.0 / rho
        u = [(j + 0.5 * k) * inverse for j, k in zip(momentum, force)]
        uu = u[0] * u[0] + u[1] * u[1] + u[2] * u[2]
        uf = u[0] * force[0] + u[1] * force[1] + u[2] * force[2]
        self.rho, self.phi, self.mu, self.u, self.force, self.uu = rho, phi, mu, u, force, uu
        self.r = 1.25 * rho
        self.k = self.r * (1.0 - 1.5 * uu) - 1.125 * uf
        self.g_scale = phi * (1.0 / 0.9)
        self.g_base = (3.0 / 0.9) * mu - 1.5 * (self.g_scale * uu)

    def pair_f(self, i):
        p, q = along(self.u, lattice_velocity[i]), along(self.force, lattice_velocity[i])
        w = lattice_weight[i]
        rp = self.r * p
        even = w * (self.k + p * (4.5 * rp + 3.375 * q))
        odd = (3.0 * w) * rp + (1.125 * w) * q
        return even, odd

    def pair_g(self, i):
        p = along(self.u, lattice_velocity[i])
        w = lattice_weight[i]
        gp = self.g_scale * p
        return w * (self.g_base + 4.5 * (gp * p)), (3.0 * w) * gp

    def jump(self, i, delta):
        cy = lattice_velocity[i][1]
        uy = self.u[1]
        if cy == 0:
            return delta * (-3.0 * uy) - (1.5 * delta * delta)
        p = along(self.u, lattice_velocity[i])
        return delta * (3.0 * cy + (9.0 * cy) * p - 3.0 * uy) + (3.0 * delta * delta)


class Shear:
    def __init__(self, raw, wide, rows):
        self.raw, self.wide, self.rows = raw, wide, rows

    def clear(self):
        self.raw[...] = jnp.zeros_like(self.raw)
        self.wide[...] = jnp.zeros_like(self.wide)

    def put(self, value, up, near, far):
        n = self.rows
        for k in range(self.raw.shape[0]):
            self.raw[k, 8 : 8 + n] = value[:, LANES * k : LANES * k + LANES]
        for k in range(self.raw.shape[0]):
            if up:
                self.wide[k, n : n + n + 8] = (
                    near * self.raw[k, 0 : n + 8] + far * self.raw[k, 1 : n + 9]
                )
            else:
                self.wide[k, n + 8 : n + n + 16] = (
                    near * self.raw[k, 7 : n + 15] + far * self.raw[k, 8 : n + 16]
                )

    def add_row(self, at, row):
        for k in range(self.raw.shape[0]):
            lanes = slice(LANES * k, LANES * k + LANES)
            self.wide[k, at : at + 1] = self.wide[k, at : at + 1] + row[:, lanes]

    def take(self, up, block, rest, cy, ref, j):
        n = self.rows
        if up:
            start = (n + 8 if block == 0 else 8) + rest - cy
        else:
            start = (n + 8 if block == 0 else n + n + 8) - rest - cy
        for k in range(self.raw.shape[0]):
            ref[j, 0:n, LANES * k : LANES * k + LANES] = self.wide[k, pl.ds(start, n)]


def plane_at(column, count_x):
    per_plane = count_x // 4
    is_plane = lax.rem(column, per_plane) == 0
    return is_plane, lax.rem(lax.div(column, per_plane), 4)


class Planes:
    def __init__(self, rests, count_x):
        self.up_rest, self.low_rest = rests
        self.odd = lax.rem(lax.axis_index("gy"), 2) == 1
        a = lax.axis_index("gx")

        def part_of(column):
            is_plane, plane = plane_at(column, count_x)
            return is_plane, (2.0 * plane.astype(f32) + 1.0) * 0.125

        up_is, up_part = part_of(lax.rem(a + 1, count_x))
        low_is, low_part = part_of(a)
        self.up_near = jnp.where(up_is, 1.0 - up_part, 1.0)
        self.up_far = jnp.where(up_is, up_part, 0.0)
        self.low_near = jnp.where(low_is, low_part, 0.0)
        self.low_far = jnp.where(low_is, 1.0 - low_part, 1.0)
        self.up_jump = jnp.where(up_is, -plane_speed, 0.0)
        self.low_jump = jnp.where(low_is, plane_speed, 0.0)


def order_sum(load):
    total = load(0)
    for i in range(1, 19):
        total = total + load(i)
    return total


def gate_kernel(g_ref, out):
    out[...] = jnp.zeros_like(out)


def phi_kernel(gate, f_ref, g_ref, top, bottom, phi_ref, to_north, to_south, fbuf, sems):
    layers, rows = phi_ref.shape[0], phi_ref.shape[1]
    faces = (layers - 1, 0)
    copies = [
        pltpu.make_async_copy(f_ref.at[:, x], fbuf.at[:, s], sems.at[s])
        for s, x in enumerate(faces)
    ]
    for copy in copies:
        copy.start()
    phi_ref[layers - 1] = top[...]
    phi_ref[0] = bottom[...]
    for x in range(layers):
        if 0 < x < layers - 1:
            phi_ref[x] = order_sum(lambda i: g_ref[i, x])
        to_north[x : x + 1] = phi_ref[x, rows - 1 : rows]
        to_south[x : x + 1] = phi_ref[x, 0:1]
    for s, x in enumerate(faces):
        copies[s].wait()
        for out, edge, inner, chosen in (
            (to_north, rows - 1, rows - 2, (7, 10)),
            (to_south, 0, 1, (9, 8)),
        ):
            out[layers + s : layers + s + 1] = phi_ref[x, inner : inner + 1]
            at = layers + 2 + 6 * s
            out[at : at + 1] = fbuf[chosen[s], s, edge : edge + 1]
            out[at + 1 : at + 2] = g_ref[chosen[s], x, edge : edge + 1]
            for k, part in enumerate(moments_of(lambda i: fbuf[i, s, edge : edge + 1])):
                out[at + 2 + k : at + 3 + k] = part
    for out in (to_north, to_south):
        out[layers + 14 : layers + 16] = jnp.zeros((2, out.shape[1]), f32)


def with_halo(ref, layer, below, above):
    rows = layer.shape[0]
    ref[8 : 8 + rows] = layer
    ref[7:8] = below
    ref[8 + rows : 9 + rows] = above


def corner_values(cells, planes, phi_ref, south_msg, north_msg, minus_wide, plus_wide):
    layers, rows, cols = phi_ref.shape
    cells[...] = jnp.ones_like(cells)
    for row in range(4):
        msg = south_msg if row < 2 else north_msg
        x = layers - 1 if row % 2 == 0 else 0
        beside = rows + (layers - 2 if row % 2 == 0 else 1)
        wide_row = 7 if row < 2 else rows + 8
        at = rows + layers
        first = at + 2 + 6 * (row % 2)
        far_phi = msg[at + row % 2 : at + row % 2 + 1]
        own_phi = phi_ref[x, 0:1] if row < 2 else phi_ref[x, rows - 1 : rows]
        parts = [msg[first + k : first + k + 1] for k in range(6)]
        parts.append(msg[rows + x : rows + x + 1])
        if row % 2 == 0:
            parts += [msg[beside : beside + 1], plus_wide[wide_row : wide_row + 1]]
        else:
            parts += [minus_wide[wide_row : wide_row + 1], msg[beside : beside + 1]]
        parts += [far_phi, own_phi] if row < 2 else [own_phi, far_phi]
        for k, part in enumerate(parts):
            cells[k, row : row + 1] = part
    place = lax.broadcasted_iota(jnp.int32, (8, cols), 0)
    is_top = (place == 0) | (place == 2)
    sx = jnp.where(is_top, 1.0, -1.0)
    sy = jnp.where(place < 2, 1.0, -1.0)
    delta = jnp.where(is_top, planes.up_jump, planes.low_jump)
    site = Site([cells[k] for k in range(2, 6)], *[cells[k] for k in range(6, 11)])
    w = lattice_weight[7]
    p = sx * site.u[0] + sy * site.u[1]
    q = sx * site.force[0] + sy * site.force[1]
    change = delta * (3.0 * sy + 9.0 * (sy * p) - 3.0 * site.u[1]) + 3.0 * (delta * delta)
    rp, gp = site.r * p, site.g_scale * p
    f_post = w * (site.k + p * (4.5 * rp + 3.375 * q) + 3.0 * rp + 1.125 * q + site.rho * change)
    g_post = w * (site.g_base + 4.5 * (gp * p) + 3.0 * gp + site.phi * change)
    return f_post - 0.25 * cells[0], g_post - (1.0 / 9.0) * cells[1]


def moment_kernel(
    sizes, after_north, after_south, offsets, f_ref, g_ref, faces, rims, rests
):
    layers, rows = f_ref.shape[1], f_ref.shape[2]
    count_x, count_y = sizes
    a = lax.axis_index("gx")
    for k, column in enumerate((lax.rem(a + 1, count_x), a)):
        is_plane, plane = plane_at(column, count_x)
        rest = jnp.clip(offsets[plane] - count_y // 2 * rows, 0, rows - 1)
        rest = jnp.where(is_plane, rest, 0).astype(f32)
        rests[k] = jnp.full(rests.shape[1:], rest, f32)
    for s, x in enumerate((layers - 1, 0)):
        for k, part in enumerate(moments_of(lambda i: f_ref[i, x])):
            faces[s, k] = part
    for s, (edge, chosen) in enumerate(((rows - 1, north_going), (0, south_going))):
        for k, part in enumerate(moments_of(lambda i: f_ref[i, :, edge, :])):
            rims[s, k] = part
        for j, i in enumerate(chosen):
            rims[s, 4 + j] = f_ref[i, :, edge, :]
            rims[s, 9 + j] = g_ref[i, :, edge, :]


displacement_classes = ((0, 5), (6, 10), (11, 15))


def rows_needed(rest, rows):
    return min(rows, rows + 1 - rest), min(rows, rest + 2)


def message_rows(count, rows):
    if count >= rows:
        return 10 * rows
    half = rows // 2
    full = half if count >= half else 0
    return 10 * full + -(-10 * (count - full) // 8) * 8


def split_sizes(first, second, rows):
    groups = [(0, 0), displacement_classes[first], displacement_classes[second], (rows - 1, rows - 1)]
    direct = [max(rows_needed(r, rows)[0] for r in range(low, high + 1)) for low, high in groups]
    across = [max(rows_needed(r, rows)[1] for r in range(low, high + 1)) for low, high in groups]

    def options(needs):
        for mask in range(16):
            small = [k for k in range(4) if mask >> k & 1]
            size = max([needs[k] for k in small], default=0)
            if size < rows:
                yield size, small

    best = None
    for d_size, d_small in options(direct):
        for a_size, a_small in options(across):
            costs = []
            for k in range(4):
                d_rows = message_rows(d_size if k in d_small else rows, rows)
                a_rows = message_rows(a_size if k in a_small else rows, rows)
                costs.append(2 * d_rows + a_rows)
            pairs = [costs[k] + costs[(k + 1) % 4] for k in range(4)]
            rank = (max(pairs), sum(pairs), d_size, a_size, d_small, a_small)
            if best is None or rank < best:
                best = rank
    return best[2], best[4], best[3], best[5]


def pieces(count, rows, first):
    half = rows // 2
    if count >= half:
        tile = slice(0, half) if first else slice(half, rows)
        rest = slice(half, count) if first else slice(rows - count, half)
    else:
        tile = None
        rest = slice(0, count) if first else slice(rows - count, rows)
    length = rest.stop - rest.start
    base = 10 * half if tile else 0
    places = []
    if tile:
        places.append((tile, lambda j: slice(half * j, half * j + half)))
    if length:
        places.append((rest, lambda j: slice(base + length * j, base + length * j + length)))
    return places, base + 10 * length


def pack(out, source, count, rows, first):
    places, used = pieces(count, rows, first)
    for j in range(10):
        for window, place in places:
            out[place(j)] = source[j, window]
    if used < out.shape[0]:
        out[used:] = jnp.zeros((out.shape[0] - used, out.shape[1]), f32)


def unpack_add(buf, j, message, count, rows, first):
    for window, place in pieces(count, rows, first)[0]:
        buf[j, window] = buf[j, window] + message[place(j)]


def rim_values(rims, s, phi_ref, minus, plus, south_msg, north_msg, line, edge, chosen, out):
    layers, rows, cols = phi_ref.shape
    phi = phi_ref[:, edge, :]
    with_halo(line, phi, minus[edge : edge + 1], plus[edge : edge + 1])
    if edge == 0:
        below, above = south_msg[rows : rows + layers], phi_ref[:, 1, :]
    else:
        below, above = phi_ref[:, rows - 2, :], north_msg[rows : rows + layers]
    site = Site(
        [rims[s, k] for k in range(4)],
        phi,
        line[7 : 7 + layers],
        line[9 : 9 + layers],
        below,
        above,
    )
    for j, i in enumerate(chosen):
        cz = lattice_velocity[i][2]
        even, odd = site.pair_f(i)
        out[s, j] = z_moved(even + odd - 0.25 * rims[s, 4 + j], cz)
        even, odd = site.pair_g(i)
        out[s, 5 + j] = z_moved(even + odd - (1.0 / 9.0) * rims[s, 9 + j], cz)


def face_kernel(
    count_x,
    sizes,
    rests,
    f_ref,
    g_ref,
    face_moments,
    rims,
    phi_ref,
    rise,
    fall,
    south_msg,
    north_msg,
    mate,
    direct,
    direct_short,
    across,
    across_short,
    joint,
    cross,
    minus_out,
    plus_out,
    minus_wide,
    plus_wide,
    window,
    halo,
    line,
    rim_post,
    post,
    cells,
    corners,
    raw,
    wide,
):
    layers, rows, cols = phi_ref.shape
    planes = Planes([jnp.max(rests[k]).astype(jnp.int32) for k in range(2)], count_x)
    shear = Shear(raw, wide, rows)
    window[...] = jnp.zeros_like(window)
    for up in (True, False):
        if up:
            first, second = rise, north_msg
            near, far, start = planes.low_far, planes.low_near, planes.low_rest
        else:
            first, second = south_msg, fall
            near, far, start = planes.up_far, planes.up_near, rows - 1 - planes.up_rest
        target = minus_wide if up else plus_wide
        for k in range(window.shape[0]):
            lanes = slice(LANES * k, LANES * k + LANES)
            window[k, 8 : 8 + rows] = first[0:rows, lanes]
            window[k, 8 + rows : 8 + 2 * rows] = second[0:rows, lanes]
            target[:, lanes] = (
                near * window[k, pl.ds(start, rows + 16)]
                + far * window[k, pl.ds(start + 1, rows + 16)]
            )
    minus_out[...] = minus_wide[8 : 8 + rows]
    plus_out[...] = plus_wide[8 : 8 + rows]
    corners[0], corners[1] = corner_values(
        cells, planes, phi_ref, south_msg, north_msg, minus_wide, plus_wide
    )
    for s, (edge, chosen) in enumerate(((rows - 1, north_going), (0, south_going))):
        rim_values(
            rims,
            s,
            phi_ref,
            minus_out,
            plus_out,
            south_msg,
            north_msg,
            line,
            edge,
            chosen,
            rim_post,
        )
    for side, up in enumerate((True, False)):
        x = layers - 1 if up else 0
        delta = planes.up_jump if up else planes.low_jump
        with_halo(
            halo, phi_ref[x], south_msg[rows + x : rows + x + 1], north_msg[rows + x : rows + x + 1]
        )
        for h in range(0, rows, 8):
            span = slice(h, h + 8)
            phi_h = phi_ref[x, span]
            if up:
                minus, plus = phi_ref[x - 1, span], plus_wide[8 + h : 16 + h]
            else:
                minus, plus = minus_wide[8 + h : 16 + h], phi_ref[x + 1, span]
            site = Site(
                [face_moments[side, k, span] for k in range(4)],
                phi_h,
                minus,
                plus,
                halo[7 + h : 15 + h],
                halo[9 + h : 17 + h],
            )
            for j, i in enumerate(rising if up else falling):
                cz = lattice_velocity[i][2]
                change = lattice_weight[i] * site.jump(i, delta)
                even, odd = site.pair_f(i)
                value = even + odd - 0.25 * f_ref[i, x, span] + site.rho * change
                post[side, j, span] = z_moved(value, cz)
                even, odd = site.pair_g(i)
                value = even + odd - (1.0 / 9.0) * g_ref[i, x, span] + phi_h * change
                post[side, 5 + j, span] = z_moved(value, cz)

    def hand_out(is_odd):
        for side, up in enumerate((True, False)):
            if up:
                near, far, rest = planes.up_near, planes.up_far, planes.up_rest
            else:
                near, far, rest = planes.low_near, planes.low_far, planes.low_rest
            first, second = (direct, mate) if up == is_odd else (joint, across)
            shear.clear()
            for j in range(10):
                cy = lattice_velocity[(rising if up else falling)[j % 5]][1]
                shear.put(post[side, j], up, near, far)
                corner = side + (0 if cy == 1 else 2)
                if cy == 1:
                    gate = jnp.where(rest == (0 if up else rows - 1), near, 0.0)
                    at = rows + 7 if up else rows + 8
                if cy == -1:
                    gate = jnp.where(rest == (rows - 1 if up else 0), far, 0.0)
                    at = 2 * rows + 7 if up else 2 * rows + 8
                if cy != 0:
                    shear.add_row(at, gate * corners[j // 5, corner : corner + 1])
                shear.take(up, 0, rest, cy, first, j)
                shear.take(up, 1, rest, cy, second, j)
        for j in range(10):
            mate[j, rows : rows + layers] = rim_post[1 if is_odd else 0, j]
            cross[j] = rim_post[0 if is_odd else 1, j]
        pack(direct_short, direct, sizes[0], rows, is_odd)
        pack(across_short, across, sizes[1], rows, is_odd)

    pl.when(planes.odd)(lambda: hand_out(True))
    pl.when(jnp.logical_not(planes.odd))(lambda: hand_out(False))


def bulk_kernel(
    after,
    f_ref,
    g_ref,
    phi_ref,
    minus,
    plus,
    south_msg,
    north_msg,
    mate_rim,
    cross_rim,
    next_f,
    next_g,
    wide_phi,
    halo,
):
    layers, rows, cols = phi_ref.shape
    is_odd = lax.rem(lax.axis_index("gy"), 2) == 1
    wide_phi[0] = minus[...]
    wide_phi[layers + 1] = plus[...]
    for x in range(layers):
        wide_phi[x + 1] = phi_ref[x]

    def layer(x, carry):
        with_halo(halo, phi_ref[x], south_msg[pl.ds(rows + x, 1)], north_msg[pl.ds(rows + x, 1)])
        beyond = lax.rem(x + 1, layers)
        before = lax.rem(x + layers - 1, layers)
        for h in range(0, rows, 8):
            span = slice(h, h + 8)
            phi_h = phi_ref[x, span]
            site = Site(
                moments_of(lambda i: f_ref[i, x, span]),
                phi_h,
                wide_phi[x, span],
                wide_phi[x + 2, span],
                halo[7 + h : 15 + h],
                halo[9 + h : 17 + h],
            )

            def emit(out, slot, i, value):
                cx, cy, cz = lattice_velocity[i]
                value = z_moved(value, cz)
                at = beyond if cx == 1 else before if cx == -1 else x
                if cy == 0:
                    out[i, at, span] = value
                elif cy == 1:
                    if h == 0:
                        rim = slot * 5 + north_going.index(i)
                        out[i, at, 0:1] = jnp.where(
                            is_odd, mate_rim[rim, pl.ds(rows + x, 1)], cross_rim[rim, pl.ds(x, 1)]
                        )
                    if h + 8 < rows:
                        out[i, at, h + 1 : h + 9] = value
                    else:
                        out[i, at, h + 1 : h + 8] = value[0:7]
                else:
                    if h + 8 == rows:
                        rim = slot * 5 + south_going.index(i)
                        out[i, at, rows - 1 : rows] = jnp.where(
                            is_odd, cross_rim[rim, pl.ds(x, 1)], mate_rim[rim, pl.ds(rows + x, 1)]
                        )
                    if h > 0:
                        out[i, at, h - 1 : h + 7] = value
                    else:
                        out[i, at, 0:7] = value[1:8]

            emit(next_f, 0, 0, lattice_weight[0] * site.k - 0.25 * f_ref[0, x, span])
            rest_g = (phi_h - 2.0 * site.mu - 0.5 * (phi_h * site.uu)) * (1.0 / 0.9)
            emit(next_g, 1, 0, rest_g - (1.0 / 9.0) * g_ref[0, x, span])
            for i in range(1, 19, 2):
                even, odd = site.pair_f(i)
                emit(next_f, 0, i, (even + odd) - 0.25 * f_ref[i, x, span])
                emit(next_f, 0, i + 1, (even - odd) - 0.25 * f_ref[i + 1, x, span])
                even, odd = site.pair_g(i)
                emit(next_g, 1, i, (even + odd) - (1.0 / 9.0) * g_ref[i, x, span])
                emit(next_g, 1, i + 1, (even - odd) - (1.0 / 9.0) * g_ref[i + 1, x, span])
        return carry

    lax.fori_loop(0, layers, layer, 0)


def put_faces(buf, out_f, out_g, chosen, x, sems):
    copies = [
        pltpu.make_async_copy(buf.at[5 * family + j], out.at[i, x], sems.at[5 * family + j])
        for family, out in enumerate((out_f, out_g))
        for j, i in enumerate(chosen)
    ]
    for copy in copies:
        copy.start()
    for copy in copies:
        copy.wait()


def merge_fill_kernel(
    count_x,
    split,
    direct,
    direct_short,
    across,
    across_short,
    f_in,
    g_in,
    f_out,
    g_out,
    buf,
    sems,
):
    layers, rows = f_out.shape[1], f_out.shape[2]
    d_size, d_small, a_size, a_small = split
    a = lax.axis_index("gx")
    odd = lax.rem(lax.axis_index("gy"), 2) == 1

    def merge(column, up):
        chosen, x = (rising, 0) if up else (falling, layers - 1)
        copies = [
            pltpu.make_async_copy(
                buf.at[j], (f_out if j < 5 else g_out).at[chosen[j % 5], x], sems.at[j]
            )
            for j in range(10)
        ]

        def fill(short_direct, short_across):
            for j in range(10):
                if short_direct and short_across:
                    buf[j] = jnp.zeros(buf.shape[1:], f32)
                elif short_direct:
                    buf[j] = across[j]
                elif short_across:
                    buf[j] = direct[j]
                else:
                    buf[j] = direct[j] + across[j]
                if short_direct:
                    unpack_add(buf, j, direct_short, d_size, rows, up)
                if short_across:
                    unpack_add(buf, j, across_short, a_size, rows, not up)
                copies[j].start()

        is_plane, plane = plane_at(column, count_x)
        plane = jnp.where(is_plane, plane, 0)
        modes = [(k in d_small, k in a_small) for k in range(4)]
        for mode in sorted(set(modes)):
            members = [k for k in range(4) if modes[k] == mode]
            inside = plane == members[0]
            for k in members[1:]:
                inside = jnp.logical_or(inside, plane == k)
            pl.when(inside)(functools.partial(fill, *mode))
        for copy in copies:
            copy.wait()

    pl.when(odd)(lambda: merge(a, True))
    pl.when(jnp.logical_not(odd))(lambda: merge(lax.rem(a + 1, count_x), False))


def joint_fill_kernel(joint, f_in, g_in, f_out, g_out, sems):
    odd = lax.rem(lax.axis_index("gy"), 2) == 1
    layers = f_out.shape[1]
    pl.when(odd)(lambda: put_faces(joint, f_out, g_out, falling, layers - 1, sems))
    pl.when(jnp.logical_not(odd))(lambda: put_faces(joint, f_out, g_out, rising, 0, sems))


def on_device(momentum_dist, order_dist, offsets):
    layers, rows, cols = momentum_dist.shape[1:]
    count_x, count_y = lax.axis_size("gx"), lax.axis_size("gy")
    per_plane = count_x // 4
    half = count_y // 2

    def hop(value, target):
        perm = []
        for x in range(count_x):
            for y in range(count_y):
                tx, ty = target(x, y)
                perm.append((x * count_y + y, tx % count_x * count_y + ty % count_y))
        return lax.ppermute(value, ("gx", "gy"), perm)

    def base_up(x):
        return half if (x + 1) % per_plane == 0 else 0

    def base_low(x):
        return half if x % per_plane == 0 else 0

    def hop_parity(value, odd_up, extra):
        def target(x, y):
            if (y % 2 == 1) == odd_up:
                return (x + 1, y - base_up(x) - extra)
            return (x - 1, y + base_low(x) + extra)

        return hop(value, target)

    def hop_y(value, step):
        return hop(value, lambda x, y: (x, y + step))

    smem, vmem, anywhere = spec_of(pltpu.SMEM), spec_of(VMEM), spec_of(pl.ANY)
    plane = jax.ShapeDtypeStruct((rows, cols), f32)
    top, bottom = jnp.sum(order_dist[:, layers - 1], axis=0), jnp.sum(order_dist[:, 0], axis=0)
    rise = hop(top, lambda x, y: (x + 1, y - base_up(x)))
    fall = hop(bottom, lambda x, y: (x - 1, y + base_low(x)))

    block = jax.ShapeDtypeStruct((layers + 16, cols), f32)
    gate = pl.pallas_call(
        gate_kernel,
        out_shape=jax.ShapeDtypeStruct((8, LANES), f32),
        in_specs=[anywhere],
        out_specs=vmem,
        compiler_params=params(50 << 20),
        name="gate",
    )(order_dist)
    phi, to_north, to_south = pl.pallas_call(
        phi_kernel,
        out_shape=[jax.ShapeDtypeStruct((layers, rows, cols), f32)] + [block] * 2,
        in_specs=[anywhere, anywhere, vmem, vmem, vmem],
        out_specs=[vmem] * 3,
        scratch_shapes=[VMEM((19, 2, rows, cols), f32), pltpu.SemaphoreType.DMA((2,))],
        compiler_params=params(8 << 20),
        name="phi_all",
    )(gate, momentum_dist, order_dist, top, bottom)
    to_north = jnp.concatenate([fall, to_north], 0)
    to_south = jnp.concatenate([rise, to_south], 0)
    south_msg, north_msg = hop_y(to_north, 1), hop_y(to_south, -1)

    face_moments, rims, rests = pl.pallas_call(
        functools.partial(moment_kernel, (count_x, count_y)),
        out_shape=[
            jax.ShapeDtypeStruct((2, 4, rows, cols), f32),
            jax.ShapeDtypeStruct((2, 14, layers, cols), f32),
            jax.ShapeDtypeStruct((2, 8, LANES), f32),
        ],
        in_specs=[anywhere, anywhere, smem, vmem, vmem],
        out_specs=[vmem] * 3,
        compiler_params=params(16 << 20),
        name="moments",
    )(to_north, to_south, offsets, momentum_dist, order_dist)

    ten = jax.ShapeDtypeStruct((10, rows, cols), f32)
    side = jax.ShapeDtypeStruct((10, layers, cols), f32)
    ten_side = jax.ShapeDtypeStruct((10, rows + layers, cols), f32)
    whole = jax.ShapeDtypeStruct(momentum_dist.shape, f32)

    def finish(first, second):
        split = split_sizes(first, second, rows)
        d_size, d_small, a_size, a_small = split
        d_short = jax.ShapeDtypeStruct((max(8, message_rows(d_size, rows)), cols), f32)
        a_short = jax.ShapeDtypeStruct((max(8, message_rows(a_size, rows)), cols), f32)

        def hop_some(value, odd_up, extra, planes):
            pairs = []
            for x in range(count_x):
                for y in range(count_y):
                    up = (y % 2 == 1) == odd_up
                    tx = (x + 1 if up else x - 1) % count_x
                    column = tx if up else x
                    if (column // per_plane % 4 if column % per_plane == 0 else 0) not in planes:
                        continue
                    ty = y - base_up(x) - extra if up else y + base_low(x) + extra
                    pairs.append((x * count_y + y, tx * count_y + ty % count_y))
            return lax.ppermute(value, ("gx", "gy"), pairs) if pairs else value

        mate, direct, direct_short, across, across_short, joint, cross, minus, plus = pl.pallas_call(
            functools.partial(face_kernel, count_x, (d_size, a_size)),
            out_shape=[ten_side, ten, d_short, ten, a_short, ten, side] + [plane] * 2,
            in_specs=[vmem] * 10,
            out_specs=[vmem] * 9,
            scratch_shapes=[
                VMEM((rows + 16, cols), f32),
                VMEM((rows + 16, cols), f32),
                VMEM((cols // LANES, 2 * rows + 16, LANES), f32),
                VMEM((rows + 16, cols), f32),
                VMEM((layers + 16, cols), f32),
                VMEM((2, 10, layers, cols), f32),
                VMEM((2, 10, rows, cols), f32),
                VMEM((11, 8, cols), f32),
                VMEM((2, 8, cols), f32),
                VMEM((cols // LANES, rows + 16, LANES), f32),
                VMEM((cols // LANES, 3 * rows + 16, LANES), f32),
            ],
            compiler_params=params(24 << 20),
            name="faces",
        )(
            rests,
            momentum_dist,
            order_dist,
            face_moments,
            rims,
            phi,
            rise,
            fall,
            south_msg,
            north_msg,
        )
        around = (phi, minus, plus, south_msg, north_msg)
        cross = hop(cross, lambda x, y: (x, y + 1 if y % 2 == 1 else y - 1))
        mate = hop(mate, lambda x, y: (x, y ^ 1))
        direct, direct_short, across, across_short, cross = lax.optimization_barrier(
            (direct, direct_short, across, across_short, cross)
        )
        d_full = [k for k in range(4) if k not in d_small]
        a_full = [k for k in range(4) if k not in a_small]
        direct = hop_some(direct, True, 0, d_full)
        direct_short = hop_some(direct_short, True, 0, d_small)
        across = hop_some(across, False, 1, a_full)
        across_short = hop_some(across_short, False, 1, a_small)
        joint = joint + mate[:, :rows]
        after = joint
        joint = hop_parity(joint, False, 0)

        next_f, next_g = pl.pallas_call(
            bulk_kernel,
            out_shape=[whole, whole],
            in_specs=[anywhere] + [vmem] * 9,
            out_specs=[vmem] * 2,
            scratch_shapes=[
                VMEM((layers + 2, rows, cols), f32),
                VMEM((rows + 16, cols), f32),
            ],
            compiler_params=params(48 << 20),
            name="bulk",
        )(after, momentum_dist, order_dist, *around, mate, cross)

        next_f, next_g = pl.pallas_call(
            joint_fill_kernel,
            out_shape=[whole, whole],
            in_specs=[vmem, anywhere, anywhere],
            out_specs=[anywhere, anywhere],
            scratch_shapes=[pltpu.SemaphoreType.DMA((10,))],
            input_output_aliases={1: 0, 2: 1},
            compiler_params=params(24 << 20),
            name="joint_fill",
        )(joint, next_f, next_g)

        return pl.pallas_call(
            functools.partial(merge_fill_kernel, count_x, split),
            out_shape=[whole, whole],
            in_specs=[vmem] * 4 + [anywhere, anywhere],
            out_specs=[anywhere, anywhere],
            scratch_shapes=[VMEM((10, rows, cols), f32), pltpu.SemaphoreType.DMA((10,))],
            input_output_aliases={4: 0, 5: 1},
            compiler_params=params(24 << 20),
            name="merge_fill",
        )(direct, direct_short, across, across_short, next_f, next_g)

    edges = [high for _, high in displacement_classes[:-1]]
    kinds = [
        sum((offsets[k] - half * rows > edge).astype(jnp.int32) for edge in edges) for k in (1, 2)
    ]
    count = len(displacement_classes)
    branches = [functools.partial(finish, k // count, k % count) for k in range(count * count)]
    return lax.switch(count * kinds[0] + kinds[1], branches)


def solution(mesh):
    return jax.shard_map(
        on_device,
        mesh=mesh,
        in_specs=(P(None, "gx", "gy", None), P(None, "gx", "gy", None), P()),
        out_specs=(P(None, "gx", "gy", None), P(None, "gx", "gy", None)),
        check_vma=False,
    )
```
